32 devices in a mesh: batch: 8 (over y, x, core), seq: 4 (over z).
Axes of the slice: x: 2, y: 2, z: 4, core: 2. Of those that a mesh axis runs over, the one named last changes fastest.
Arguments:
- inputs: bfloat16 [16, 1024, 1280], P('batch', 'seq'), may hold values from -6 to 6
- lengths: int32 [16], P('batch'), may hold values from 1 to 1024, as said below
- query_key_value_weight: bfloat16 [2, 1280, 3840], P(None, 'batch'), may hold values from -0.15625 to 0.15625
- output_weight: bfloat16 [2, 1280, 1280], P(None, 'batch'), may hold values from -0.625 to 0.625
- up_weight: bfloat16 [2, 1280, 1280], P(None, 'batch'), may hold values from -0.15625 to 0.15625
- down_weight: bfloat16 [2, 1280, 1280], P(None, 'batch'), may hold values from -0.15625 to 0.15625
- gain_attn: bfloat16 [2, 1280], P(None, 'batch'), may hold values from 0.099609375 to 1.8984375
- gain_mlp: bfloat16 [2, 1280], P(None, 'batch'), may hold values from 0.099609375 to 1.8984375
- cotangent: bfloat16 [16, 1024, 1280], P('batch', 'seq'), may hold values from -6 to 6
Outputs:
- hidden_states: bfloat16 [2, 16, 1024, 1280], P(None, 'batch', 'seq')
- input_grad: float32 [16, 1024, 1280], P('batch', 'seq')
- grad_qkv: float32 [2, 1280, 3840], P(None, 'batch')
- grad_out: float32 [2, 1280, 1280], P(None, 'batch')
- grad_up: float32 [2, 1280, 1280], P(None, 'batch')
- grad_down: float32 [2, 1280, 1280], P(None, 'batch')
- grad_gain_attn: float32 [2, 1280], P(None, 'batch')
- grad_gain_mlp: float32 [2, 1280], P(None, 'batch')
The draws below stay inside these ranges and needn't reach their ends.
Inputs may be any that keep to these rules, and one draw needn't show every extreme that they name: The last lengths of the 1024 slots of a series are its real patches, the slots before are padding.
All inputs are finite; a program needn't handle non-finite values.
Results may differ from the reference program's by a relative error of at most 0.025.
Values may be sent and summed in bfloat16 or wider, within the bound.
A program may use at most 384 MiB of HBM per device.

```python
import math
import jax
import jax.numpy as jnp
from jax import lax

D = 1280
HEADS = 16
HEAD_DIM = 80
FF = 1280
LAYERS = 2
SLOTS = 1024
SER_DEV = 2
SERIES = 16


def draw_lengths(key, part):
    key = jax.random.fold_in(key, 11)
    base_key, pick_key = jax.random.split(key)
    base_len = jax.random.randint(base_key, (SERIES,), 1, SLOTS + 1)
    picked = jax.random.randint(pick_key, (SERIES // SER_DEV,), 0, SER_DEV)
    series_ids = jnp.arange(SERIES)
    is_full = series_ids % SER_DEV == picked[series_ids // SER_DEV]
    return jnp.where(is_full, SLOTS, base_len).astype(jnp.int32)


def steps_of(rng, extent, cuts, low, top_value):
    loudness, own = 1.0, jax.random.fold_in(rng, 6)
    for dim, blocks in cuts:
        steps = jnp.exp(jax.random.uniform(jax.random.fold_in(own, dim), (blocks,), jnp.float32, low / len(cuts), top_value / len(cuts)))
        loudness = loudness * jnp.repeat(steps, extent[dim] // blocks).reshape([-1 if axis == dim else 1 for axis in range(len(extent))])
    return loudness


def gaussian(key, shape, deviation, bound, cuts=(), held_as=jnp.bfloat16):
    array = jax.random.normal(key, shape, jnp.float32) * deviation
    if len(cuts) > 0:
        array = steps_of(key, shape, cuts, -0.22, 0.18) * array
    return jnp.clip(array, min=-bound, max=bound).astype(held_as)


def setup_inputs(seed: int = 0) -> dict:
    keys = jax.random.split(jax.random.key(seed), 10)
    inputs = gaussian(keys[0], (SERIES, SLOTS, D), 1.0, 6.0, ((0, 8), (1, 4)))
    lengths = draw_lengths(jax.random.fold_in(keys[9], 71), 0)
    query_key_value_weight = gaussian(keys[2], (LAYERS, D, 3 * D), D ** -0.5, 0.15625, ((1, 8),))
    output_weight = gaussian(keys[3], (LAYERS, D, D), (D // 16) ** -0.5, 0.625, ((1, 8),))
    up_weight = gaussian(keys[4], (LAYERS, D, FF), D ** -0.5, 0.15625, ((1, 8),))
    down_weight = gaussian(keys[5], (LAYERS, FF, D), FF ** -0.5, 0.15625, ((1, 8),))
    gain_attn = jnp.clip(1.0 + 0.18 * jax.random.normal(keys[6], (LAYERS, D), jnp.float32), 0.099609375, 1.8984375).astype(jnp.bfloat16)
    gain_mlp = jnp.clip(1.0 + 0.18 * jax.random.normal(keys[7], (LAYERS, D), jnp.float32), 0.099609375, 1.8984375).astype(jnp.bfloat16)
    cotangent = gaussian(keys[8], (SERIES, SLOTS, D), 1.0, 6.0, ((0, 8), (1, 4)))
    return {"inputs": inputs, "lengths": lengths, "query_key_value_weight": query_key_value_weight, "output_weight": output_weight, "up_weight": up_weight, "down_weight": down_weight, "gain_attn": gain_attn, "gain_mlp": gain_mlp, "cotangent": cotangent}


@jax.custom_vjp
def low(v):
    return lax.optimization_barrier(v.astype(jnp.bfloat16)).astype(jnp.float32)

@jax.custom_vjp
def lower_backward(v):
    return v

def low_keep(v):
    return (low(v), None)

def low_pass(kept, grad):
    return (grad,)

def back_keep(v):
    return (v, None)

def back_low(kept, grad):
    return (low(grad),)
low.defvjp(low_keep, low_pass)
lower_backward.defvjp(back_keep, back_low)

def norm_rows(hidden_rows, gain):
    return hidden_rows * lax.rsqrt(lax.optimization_barrier(jnp.mean(hidden_rows * hidden_rows, axis=-1, keepdims=True)) + 1e-06) * gain

def rotate(tensor, cos_table, sin_table):
    half_dim = tensor.shape[-1] // 2
    front_half = tensor[..., :half_dim]
    back_half = tensor[..., half_dim:]
    return jnp.concatenate([front_half * cos_table - back_half * sin_table, back_half * cos_table + front_half * sin_table], axis=-1)

def rope_tables(slot_ids, pad_start):
    frequency = jnp.exp(jnp.arange(HEAD_DIM // 2, dtype=jnp.float32) * (-2.0 * math.log(10000.0) / HEAD_DIM))
    positions = slot_ids.astype(jnp.float32)[None, :] - pad_start.astype(jnp.float32)[:, None]
    angles = positions[:, :, None, None] * frequency
    return (jnp.cos(angles), jnp.sin(angles))

def allowed(query_slots, key_slots, pad_start):
    causal = query_slots[:, None] >= key_slots[None, :]
    same_slot = query_slots[:, None] == key_slots[None, :]
    live_key = key_slots[None, None, :] >= pad_start[:, None, None]
    return causal[None] & live_key | same_slot[None]

def layer_forward(hidden_rows, params, cos_table, sin_table, allow_mask):
    query_key_value_weight, output_weight, up_weight, down_weight, gain_attn, gain_mlp = params
    series_count, slot_count, model_width = hidden_rows.shape
    highest_precision = lax.Precision.HIGHEST
    split_shape = (series_count, slot_count, HEADS, HEAD_DIM)
    attention_normed = low(norm_rows(hidden_rows, gain_attn))
    projected_rows = lower_backward(jnp.einsum('nfk,ku->nfu', attention_normed, query_key_value_weight, precision=highest_precision))
    queries = low(rotate(projected_rows[..., :model_width].reshape(split_shape), cos_table, sin_table))
    keys_rot = low(rotate(projected_rows[..., model_width:2 * model_width].reshape(split_shape), cos_table, sin_table))
    values = low(projected_rows[..., 2 * model_width:].reshape(split_shape))
    scores = lower_backward(jnp.einsum('sqhe,skhe->shqk', queries, keys_rot, precision=highest_precision) / math.sqrt(HEAD_DIM))
    scores = jnp.where(allow_mask[:, None], scores, -1e+30)
    attn_weights = low(jax.nn.softmax(scores, axis=-1))
    attention_output = jnp.einsum('shqk,skhe->sqhe', attn_weights, values, precision=highest_precision).reshape(series_count, slot_count, model_width)
    attention_output = lower_backward(low(attention_output))
    middle_hidden = hidden_rows + lower_backward(jnp.einsum('nfk,ku->nfu', attention_output, output_weight, precision=highest_precision))
    feedforward_normed = low(norm_rows(middle_hidden, gain_mlp))
    before_activation = lower_backward(jnp.einsum('nqr,rb->nqb', feedforward_normed, up_weight, precision=highest_precision))
    silu_output = low(jax.nn.silu(before_activation))
    return middle_hidden + lower_backward(jnp.einsum('zje,eq->zjq', silu_output, down_weight, precision=highest_precision))

def forward(hidden_rows, params_all, cos_table, sin_table, allow_mask):
    layer_outs = []
    for layer_index in range(LAYERS):
        params = tuple((weight[layer_index] for weight in params_all))
        hidden_rows = layer_forward(hidden_rows, params, cos_table, sin_table, allow_mask)
        layer_outs.append(hidden_rows)
    return jnp.stack(layer_outs)

def reference(inputs, lengths, query_key_value_weight, output_weight, up_weight, down_weight, gain_attn, gain_mlp, cotangent):
    params_all = tuple((weight.astype(jnp.float32) for weight in (query_key_value_weight, output_weight, up_weight, down_weight, gain_attn, gain_mlp)))
    group_size = math.gcd(SERIES, max(1, 4096 // SLOTS))
    group_count = SERIES // group_size
    grouped_inputs = inputs.astype(jnp.float32).reshape(group_count, group_size, SLOTS, D)
    grouped_lengths = lengths.reshape(group_count, group_size)
    grouped_cot = cotangent.astype(jnp.float32).reshape(group_count, group_size, SLOTS, D)
    slot_ids = jnp.arange(SLOTS, dtype=jnp.int32)

    def scan_step(totals, group_item):
        group_inputs, group_lengths, group_cot = group_item
        pad_start = SLOTS - group_lengths
        cos_table, sin_table = rope_tables(slot_ids, pad_start)
        allow_mask = allowed(slot_ids, slot_ids, pad_start)

        def stacked(layer_input, layer_params):
            return forward(layer_input, layer_params, cos_table, sin_table, allow_mask)
        layer_outs, pullback = jax.vjp(stacked, group_inputs, params_all)
        cotangent_seed = jnp.zeros_like(layer_outs).at[LAYERS - 1].set(group_cot)
        input_grad, param_grads = pullback(cotangent_seed)
        totals = tuple((running + addend for running, addend in zip(totals, param_grads)))
        return (totals, (layer_outs.astype(jnp.bfloat16), input_grad))
    init_grads = tuple((jnp.zeros_like(weight) for weight in params_all))
    totals, (layer_outs, input_grads) = lax.scan(scan_step, init_grads, (grouped_inputs, grouped_lengths, grouped_cot))
    hidden_states = jnp.transpose(layer_outs, (1, 0, 2, 3, 4)).reshape(LAYERS, SERIES, SLOTS, D)
    input_grad = input_grads.reshape(SERIES, SLOTS, D)
    return (hidden_states, input_grad, totals[0], totals[1], totals[2], totals[3], totals[4], totals[5])
```

```python
import math, functools
import jax, jax.numpy as jnp
from jax import lax
from jax.experimental import pallas as pl
from jax.experimental.pallas import tpu as pltpu
from jax.sharding import PartitionSpec as P
HEAD_DIM=80
C2 = math.log2(math.e)/math.sqrt(HEAD_DIM)
NEG=-1e30

def dot00(a,b): return lax.dot_general(a,b,(((0,),(0,)),((),())),preferred_element_type=jnp.float32)
def dot10(a,b): return lax.dot_general(a,b,(((1,),(0,)),((),())),preferred_element_type=jnp.float32)
def dot11(a,b): return lax.dot_general(a,b,(((1,),(1,)),((),())),preferred_element_type=jnp.float32)

def plans(core):
    if core == 0:
        return [(0,[("o",0,0)]),(1,[("o",0,0),("x",0,1),("x",1,2),("o",1,3)])]
    return [(0,[("x",0,0),("o",0,1)]),(1,[("x",0,0),("o",0,1),("o",1,2)])]

def masked(s, quarter, diag, pad, Q):
    row=lax.broadcasted_iota(jnp.int32,s.shape,0)
    live = row >= pad - quarter*Q
    if diag:
        col=lax.broadcasted_iota(jnp.int32,s.shape,1)
        ok=((row<=col)&live)|(row==col)
    else: ok=live
    return jnp.where(ok,s,NEG)

def fwd_kernel(HB,Q,meta,q,k,v,kx,vx,o_ref,lse_ref):
    pad=meta[1]
    def run(core):
        for hh in range(HB):
            hs=slice(hh*80,hh*80+80)
            for qb,blocks in plans(core):
                qs=slice(qb*Q,qb*Q+Q)
                qT=q[hs,qs]
                s=[]
                for i,(src,half,quarter) in enumerate(blocks):
                    kr=k if src=="o" else kx
                    sT=dot00(kr[hs,half*Q:half*Q+Q],qT)
                    s.append(masked(sT,quarter,i==len(blocks)-1,pad,Q))
                m=functools.reduce(jnp.maximum,[jnp.max(t,axis=0,keepdims=True) for t in s])
                l=0.;o=0.
                for t,(src,half,quarter) in zip(s,blocks):
                    vr=v if src=="o" else vx
                    p=jnp.exp2((t-m)*C2)
                    l=l+jnp.sum(p,axis=0,keepdims=True)
                    o=o+dot10(vr[hs,half*Q:half*Q+Q],p.astype(jnp.bfloat16))
                o_ref[hs,qs]=(o*(1.0/l)).astype(o_ref.dtype)
                lse_ref[0,hh:hh+1,qs]=m*C2+jnp.log2(l)
    for core in (0,1):
        pl.when(meta[0]==core)(functools.partial(run,core))

def attn_fwd(meta,qkvT,kvxT,heads,HB=4):
    R=qkvT.shape[1]; Q=R//2; D=heads*80; n=heads//HB
    blk=lambda off: pl.BlockSpec((HB*80,R),lambda h,off=off:(h+off*n,0))
    flops=2*2*5*Q*Q*heads*256
    return pl.pallas_call(
        functools.partial(fwd_kernel,HB,Q),
        grid=(n,),
        in_specs=[pl.BlockSpec(memory_space=pltpu.SMEM),blk(0),blk(1),blk(2),blk(0),blk(1)],
        out_specs=[blk(0),pl.BlockSpec((1,HB,R),lambda h:(h,0,0))],
        out_shape=[jax.ShapeDtypeStruct((D,R),jnp.bfloat16),jax.ShapeDtypeStruct((n,HB,R),jnp.float32)],
        compiler_params=pltpu.CompilerParams(vmem_limit_bytes=48*2**20),
        cost_estimate=pl.CostEstimate(flops=flops,bytes_accessed=R*D*2*6,transcendentals=5*Q*Q*heads),
        name="attention_forward",
    )(meta,qkvT,qkvT,qkvT,kvxT,kvxT)

def bwd_kernel(HB,Q,meta,q,k,v,kx,vx,do,o,lse,cos,sin,cosx,sinx,dq_ref,dk_ref,dv_ref,dkx_ref,dvx_ref):
    pad=meta[1]
    scale=1.0/math.sqrt(HEAD_DIM)
    def unrot(t,ct,st):
        a,b=t[:40],t[40:]
        return jnp.concatenate([a*ct+b*st,b*ct-a*st],axis=0)
    def run(core):
        for hh in range(HB):
            hs=slice(hh*80,hh*80+80)
            dk={};dv={}
            for qb,blocks in plans(core):
                qs=slice(qb*Q,qb*Q+Q)
                qT=q[hs,qs]; doT=do[hs,qs]
                delta=jnp.sum(doT.astype(jnp.float32)*o[hs,qs].astype(jnp.float32),axis=0,keepdims=True)
                L=lse[0,hh:hh+1,qs]
                dq=0.
                for i,(src,half,quarter) in enumerate(blocks):
                    kr,vr=(k,v) if src=="o" else (kx,vx)
                    ks=slice(half*Q,half*Q+Q)
                    kT=kr[hs,ks]; vT=vr[hs,ks]
                    s=masked(dot00(kT,qT),quarter,i==len(blocks)-1,pad,Q)
                    p=jnp.exp2(s*C2-L)
                    dp=dot00(vT,doT)
                    ds=(p*(dp-delta)).astype(jnp.bfloat16)
                    pb=p.astype(jnp.bfloat16)
                    dq=dq+dot10(kT,ds)
                    key=(src,half)
                    a=dot11(qT,ds); c=dot11(doT,pb)
                    dk[key]=dk[key]+a if key in dk else a
                    dv[key]=dv[key]+c if key in dv else c
                dq_ref[hs,qs]=unrot(dq*scale,cos[:,qs],sin[:,qs]).astype(jnp.bfloat16)
            for src,kref,vref,ct,st in (("o",dk_ref,dv_ref,cos,sin),("x",dkx_ref,dvx_ref,cosx,sinx)):
                for half in (0,1):
                    ks=slice(half*Q,half*Q+Q)
                    if (src,half) in dk:
                        kref[hs,ks]=unrot(dk[src,half]*scale,ct[:,ks],st[:,ks]).astype(jnp.bfloat16)
                        vref[hs,ks]=dv[src,half].astype(jnp.bfloat16)
                    else:
                        kref[hs,ks]=jnp.zeros((80,Q),jnp.bfloat16)
                        vref[hs,ks]=jnp.zeros((80,Q),jnp.bfloat16)
    for core in (0,1):
        pl.when(meta[0]==core)(functools.partial(run,core))

def attn_bwd(meta,qkvT,kvxT,doT,oT,lse,cos,sin,cosx,sinx,heads,HB=4):
    R=qkvT.shape[1]; Q=R//2; D=heads*80; n=heads//HB
    blk=lambda off: pl.BlockSpec((HB*80,R),lambda h,off=off:(h+off*n,0))
    tab=pl.BlockSpec((40,R),lambda h:(0,0))
    out=jax.ShapeDtypeStruct((D,R),jnp.bfloat16)
    return pl.pallas_call(
        functools.partial(bwd_kernel,HB,Q),
        grid=(n,),
        in_specs=[pl.BlockSpec(memory_space=pltpu.SMEM),blk(0),blk(1),blk(2),blk(0),blk(1),blk(0),blk(0),
                  pl.BlockSpec((1,HB,R),lambda h:(h,0,0)),tab,tab,tab,tab],
        out_specs=[blk(0)]*5,
        out_shape=[out]*5,
        compiler_params=pltpu.CompilerParams(vmem_limit_bytes=48*2**20),
        cost_estimate=pl.CostEstimate(flops=5*2*5*Q*Q*heads*256,bytes_accessed=R*D*2*12,transcendentals=5*Q*Q*heads),
        name="attention_backward",
    )(meta,qkvT,qkvT,qkvT,kvxT,kvxT,doT,oT,lse,cos,sin,cosx,sinx)


LAYERS = 2
SLOTS = 1024
BF = jnp.bfloat16
F32 = jnp.float32
AXES = ("batch", "seq")


def local(nb, ns, inputs, lengths, wqkv, wout, wup, wdown, gain_attn, gain_mlp, cotangent):
    ser, quarter, width = inputs.shape
    heads = width // HEAD_DIM
    rows = 2 * quarter
    shard = wout.shape[1]
    batch = lax.axis_index("batch")
    z = lax.axis_index("seq")
    core = batch % 2
    chip = batch // 2
    chips = nb // 2
    side = math.isqrt(chips)

    def send(array, move):
        pairs = []
        for b in range(nb):
            for s in range(ns):
                b2, s2 = move(b, s)
                pairs.append((b * ns + s, b2 * ns + s2))
        return lax.ppermute(array, AXES, pairs)

    def by_batch(array, mask):
        return send(array, lambda b, s: (b ^ mask, s))

    def by_seq(array, mask):
        return send(array, lambda b, s: (b, s ^ mask))

    def owner(quarter_index):
        return (0, 1, 1, 0)[quarter_index]

    def spread(b, s, turn):
        return (b & ~1) | owner(s), 2 * (b & 1) + (turn if s < 2 else 1 - turn)

    late = (z >= 2).astype(jnp.int32)
    odd = z % 2

    def to_series(array):
        first = lax.dynamic_index_in_dim(array, late, 0, keepdims=False)
        second = lax.dynamic_index_in_dim(array, 1 - late, 0, keepdims=False)
        got0 = send(first, lambda b, s: spread(b, s, 0))
        got1 = send(second, lambda b, s: spread(b, s, 1))
        swap = odd == 1
        return jnp.concatenate([jnp.where(swap, got1, got0), jnp.where(swap, got0, got1)], axis=0)

    def back(b, s, turn):
        for b0 in range(b & ~1, (b & ~1) + 2):
            for s0 in range(ns):
                if spread(b0, s0, turn) == (b, s):
                    return b0, s0

    def from_series(array):
        swap = odd == 1
        low, high = array[:quarter], array[quarter:]
        got0 = send(jnp.where(swap, high, low), lambda b, s: back(b, s, 0))
        got1 = send(jnp.where(swap, low, high), lambda b, s: back(b, s, 1))
        swap2 = late == 1
        return jnp.stack([jnp.where(swap2, got1, got0), jnp.where(swap2, got0, got1)])

    xbit, ybit = 2, 4

    def gather(array):
        if nb != 8:
            return lax.all_gather(array, "batch", axis=0, tiled=True)
        half = array.shape[0] // 2
        got_x = by_batch(array, xbit)
        got_y = by_batch(array, ybit)
        diag_a = by_batch(got_y[:half], xbit)
        diag_b = by_batch(got_x[half:], ybit)
        mine = jnp.stack([array, got_x, got_y, jnp.concatenate([diag_a, diag_b], axis=0)])
        other = by_batch(mine, 1)
        order = jnp.arange(4) ^ chip
        mine = jnp.take(mine, order, axis=0, mode="clip")
        other = jnp.take(other, order, axis=0, mode="clip")
        low = jnp.where(core == 0, mine, other)
        high = jnp.where(core == 0, other, mine)
        return jnp.stack([low, high], axis=1).reshape((nb * array.shape[0],) + array.shape[1:])

    def scatter(grad):
        if nb != 8:
            part = lax.psum_scatter(grad, "batch", scatter_dimension=0, tiled=True)
        else:
            four = grad.reshape((chips, 2, shard) + grad.shape[1:])
            away = lax.dynamic_index_in_dim(four, 1 - core, 1, keepdims=False)
            keep = lax.dynamic_index_in_dim(four, core, 1, keepdims=False)
            keep = keep + by_batch(away, 1)
            pick = lambda m: lax.dynamic_index_in_dim(keep, chip ^ m, 0, keepdims=False)
            own, tox, toy, tod = pick(0), pick(1), pick(2), pick(3)
            half = shard // 2
            got_a = by_batch(jnp.concatenate([tox[:half], tod[:half]], axis=0), xbit)
            got_b = by_batch(jnp.concatenate([toy[half:], tod[half:]], axis=0), ybit)
            own_a = own[:half] + got_a[:half]
            y_a = toy[:half] + got_a[half:]
            own_b = own[half:] + got_b[:half]
            x_b = tox[half:] + got_b[half:]
            own_a = own_a + by_batch(y_a, ybit)
            own_b = own_b + by_batch(x_b, xbit)
            part = jnp.concatenate([own_a, own_b], axis=0)
        return sum_seq(part)

    def sum_seq(part):
        if ns != 4 or part.shape[0] % 4:
            return lax.psum(part, "seq")
        half = part.shape[0] // 2
        z0 = z % 2
        z1 = z // 2
        two = part.reshape((2, half) + part.shape[1:])
        keep = lax.dynamic_index_in_dim(two, z0, 0, keepdims=False) + by_seq(
            lax.dynamic_index_in_dim(two, 1 - z0, 0, keepdims=False), 1
        )
        four = keep.reshape((2, half // 2) + part.shape[1:])
        keep = lax.dynamic_index_in_dim(four, z1, 0, keepdims=False) + by_seq(
            lax.dynamic_index_in_dim(four, 1 - z1, 0, keepdims=False), 2
        )
        got = by_seq(keep, 2)
        first = z1 == 0
        piece = jnp.concatenate([jnp.where(first, keep, got), jnp.where(first, got, keep)], axis=0)
        got = by_seq(piece, 1)
        first = z0 == 0
        return jnp.concatenate([jnp.where(first, piece, got), jnp.where(first, got, piece)], axis=0)

    both = jnp.stack([lengths, by_batch(lengths, 1)])
    both = jnp.where(core == 0, both, both[::-1]).reshape(-1)
    pad_start = SLOTS - lax.dynamic_index_in_dim(both, z, 0, keepdims=False)
    meta = jnp.stack([core, pad_start]).astype(jnp.int32)
    frequency = jnp.exp(
        jnp.arange(HEAD_DIM // 2, dtype=F32) * (-2.0 * math.log(10000.0) / HEAD_DIM)
    )

    def tables(which):
        low = jnp.where(which == 0, 0, quarter)
        high = jnp.where(which == 0, 3 * quarter, 2 * quarter)
        offset = jnp.arange(quarter, dtype=jnp.int32)
        slots = jnp.concatenate([low + offset, high + offset])
        angle = frequency[:, None] * (slots - pad_start).astype(F32)[None, :]
        return jnp.cos(angle), jnp.sin(angle)

    cos, sin = tables(core)
    cosx, sinx = tables(1 - core)

    def rotate(t):
        t = t.reshape(heads, 2, HEAD_DIM // 2, rows)
        a, b = t[:, 0], t[:, 1]
        return jnp.stack([a * cos - b * sin, b * cos + a * sin], axis=1).reshape(width, rows)

    gains = jnp.concatenate([gain_attn, gain_mlp], axis=0)
    gains = lax.all_gather(gains, "batch", axis=1, tiled=True).astype(F32)

    def normed(h, gain):
        r = lax.rsqrt(jnp.mean(h * h, axis=-1, keepdims=True) + 1e-6)
        return (h * r * gain).astype(BF)

    dot = lambda a, b, i, j: lax.dot_general(
        a, b, (((i,), (j,)), ((), ())), preferred_element_type=F32
    )

    full = []
    for layer in range(LAYERS):
        full.append((gather(wqkv[layer]), gather(wout[layer]), gather(wup[layer]), gather(wdown[layer])))

    h = to_series(inputs).astype(F32)
    saved = []
    hidden = []
    for layer in range(LAYERS):
        fqkv, fout, fup, fdown = full[layer]
        xn = normed(h, gains[layer])
        proj = dot(fqkv, xn, 0, 1)
        qkv = jnp.concatenate(
            [rotate(proj[:width]), rotate(proj[width : 2 * width]), proj[2 * width :]], axis=0
        ).astype(BF)
        kvx = by_batch(qkv[width:], 1)
        att, lse = attn_fwd(meta, qkv, kvx, heads)
        middle = h + dot(att, fout, 0, 0)
        mn = normed(middle, gains[LAYERS + layer])
        pre = dot(mn, fup, 1, 0)
        act = (pre * jax.nn.sigmoid(pre)).astype(BF)
        out = middle + dot(act, fdown, 1, 0)
        saved.append((h, xn, qkv, kvx, att, lse, middle, mn, pre, act))
        h = out
        hidden.append(from_series(h.astype(BF)))

    def norm_back(e, h, gain, g):
        r = lax.rsqrt(jnp.mean(h * h, axis=-1, keepdims=True) + 1e-6)
        n = h * r
        eg = e * gain
        dgain = jnp.sum(e * n, axis=0)
        return g + r * (eg - n * jnp.mean(eg * n, axis=-1, keepdims=True)), dgain

    g = to_series(cotangent).astype(F32)
    grads = [None] * LAYERS
    dgains = [None] * (2 * LAYERS)
    for layer in reversed(range(LAYERS)):
        fqkv, fout, fup, fdown = full[layer]
        h, xn, qkv, kvx, att, lse, middle, mn, pre, act = saved[layer]
        gb = g.astype(BF)
        d_down = scatter(dot(act, gb, 0, 0).astype(BF))
        da = dot(gb, fdown, 1, 1)
        s = jax.nn.sigmoid(pre)
        dpre = (da * (s + pre * s * (1.0 - s))).astype(BF)
        d_up = scatter(dot(mn, dpre, 0, 0).astype(BF))
        e = dot(dpre, fup, 1, 1)
        mg, dgains[LAYERS + layer] = norm_back(e, middle, gains[LAYERS + layer], g)
        mb = mg.astype(BF)
        d_out = scatter(dot(att, mb, 1, 0).astype(BF))
        datt = dot(fout, mb, 1, 1).astype(BF)
        dq, dk, dv, dkx, dvx = attn_bwd(meta, qkv, kvx, datt, att, lse, cos, sin, cosx, sinx, heads)
        got = by_batch(jnp.concatenate([dkx, dvx], axis=0), 1)
        pg = jnp.concatenate([dq, dk + got[:width], dv + got[width:]], axis=0)
        d_qkv = scatter(dot(xn, pg, 0, 1).astype(BF))
        e = dot(pg, fqkv, 0, 1)
        g, dgains[layer] = norm_back(e, h, gains[layer], mg)
        grads[layer] = (d_qkv, d_out, d_up, d_down)
    input_grad = from_series(g.astype(BF)).astype(F32)
    dgain = jnp.stack(dgains).astype(BF)
    dgain = lax.psum(lax.psum_scatter(dgain, "batch", scatter_dimension=1, tiled=True), "seq").astype(F32)
    stacked = [
        jnp.stack([grads[layer][k] for layer in range(LAYERS)]).astype(F32) for k in range(4)
    ]
    return (jnp.stack(hidden), input_grad, *stacked, dgain[:LAYERS], dgain[LAYERS:])


def solution(mesh):
    nb, ns = mesh.shape["batch"], mesh.shape["seq"]
    rows = P("batch", "seq", None)
    weight = P(None, "batch", None)
    gain = P(None, "batch")
    return jax.shard_map(
        functools.partial(local, nb, ns),
        mesh=mesh,
        in_specs=(rows, P("batch"), weight, weight, weight, weight, gain, gain, rows),
        out_specs=(P(None, "batch", "seq", None), rows, weight, weight, weight, weight, gain, gain),
        check_vma=False,
    )
```

```python
import functools
import math

import jax
import jax.numpy as jnp
from jax import lax
from jax.experimental import pallas as pl
from jax.experimental.pallas import tpu as pltpu
from jax.sharding import PartitionSpec as P

HEAD_DIM = 80
HALF = HEAD_DIM // 2
LAYERS = 2
SLOTS = 1024
BF = jnp.bfloat16
F32 = jnp.float32
AXES = ("batch", "seq")
LOG2_SCALE = math.log2(math.e) / math.sqrt(HEAD_DIM)
NEG = -1e30
EPS = 1e-6
TILE = 256
MESH = pl.DeviceIdType.MESH
ANY = pl.BlockSpec(memory_space=pl.ANY)
VM = pl.BlockSpec(memory_space=pltpu.VMEM)
SM = pl.BlockSpec(memory_space=pltpu.SMEM)
GROUP = 4


def dot(a, b, i, j):
    return lax.dot_general(a, b, (((i,), (j,)), ((), ())), preferred_element_type=F32)


def struct(shape, dtype=BF):
    return jax.ShapeDtypeStruct(shape, dtype)


def tiles(extent):
    return [slice(at, at + TILE) for at in range(0, extent, TILE)]


class Place:
    def __init__(self):
        self.batch = lax.axis_index("batch")
        self.z = lax.axis_index("seq")
        self.core = self.batch % 2
        self.chip = self.batch // 2
        x = self.chip % 2
        y = (self.chip // 2) % 2
        self.to_x = 2 - 4 * x
        self.to_y = 4 - 8 * y
        self.x = self.batch + self.to_x
        self.y = self.batch + self.to_y
        self.diag = self.batch + self.to_x + self.to_y
        self.sibling = self.batch + 1 - 2 * self.core
        self.inner = (self.z == 1) | (self.z == 2)
        self.pair_z = self.z + 1 - 2 * (self.z % 2)
        self.owner = ((self.z + 1) // 2) % 2
        self.part = self.z // 2

    def id(self, batch):
        return (batch, self.z)

    def workers(self):
        return [
            (2 * self.chip + self.owner, (1 - self.core) * (1 + j) + self.core * 3 * j) for j in (0, 1)
        ]

    def holders(self):
        return [(2 * self.chip + 1 - self.owner, at) for at in (self.core, 3 - self.core)]


def greet(place, signals, line=False):
    barrier = pltpu.get_barrier_semaphore()
    for device in signals:
        pl.semaphore_signal(barrier, inc=1, device_id=device, device_id_type=MESH)
    if line:
        pl.semaphore_signal(barrier, inc=1, device_id=(place.batch, place.pair_z), device_id_type=MESH)

        @pl.when(place.inner)
        def _():
            pl.semaphore_signal(barrier, inc=1, device_id=(place.batch, 3 - place.z), device_id_type=MESH)

        pl.semaphore_wait(barrier, len(signals) + 1 + place.part + place.z % 2 - 2 * place.part * (place.z % 2))
    else:
        pl.semaphore_wait(barrier, len(signals))


class Swap:
    def __init__(self, place, to_workers, src, landing, send, recv):
        self.src, self.landing, self.send, self.recv = src, landing, send, recv
        self.to = place.workers() if to_workers else place.holders()
        self.came_from = place.holders() if to_workers else place.workers()
        self.part = place.part

    def copy(self, k):
        return remote(
            self.src.at[k], self.landing.at[self.part], self.send.at[k], self.recv.at[self.part], self.to[k]
        )

    def start(self):
        for k in (0, 1):
            self.copy(k).start()

    def arrive(self):
        for k in (0, 1):
            remote(
                self.src.at[k], self.landing.at[k], self.send.at[k], self.recv.at[k], self.to[k]
            ).wait_recv()

    def drain(self):
        for k in (0, 1):
            self.copy(k).wait_send()


def swap_scratch():
    return [pltpu.SemaphoreType.DMA((2,)), pltpu.SemaphoreType.DMA((2,))]


def remote(src, dst, send_sem, recv_sem, device):
    return pltpu.make_async_remote_copy(
        src_ref=src, dst_ref=dst, send_sem=send_sem, recv_sem=recv_sem, device_id=device,
        device_id_type=MESH,
    )


class Gather:
    SEMS = 9

    def __init__(self, place, spread, shards, full, send, recv, local):
        self.place, self.spread = place, spread
        self.shards, self.full = shards, full
        self.send, self.recv, self.local = send, recv, local

    def rows(self, unit, index, part=None):
        size = self.shards[unit].shape[0]
        start, count = index * size, size
        if part is not None:
            count = size // 2
            start = start + part * count
        return self.full.at[unit, pl.ds(pl.multiple_of(start, 16), count)]

    def copy(self, unit, k):
        p = self.place
        mine, of_x, of_y, of_d = p.batch, p.x, p.y, p.diag
        src, index, part, to = (
            (self.shards[unit], mine, None, p.x),
            (self.shards[unit], mine, None, p.y),
            (self.shards[unit], mine, None, p.sibling),
            (None, of_y, 0, p.x),
            (None, of_x, 1, p.y),
            (None, of_x, None, p.sibling),
            (None, of_y, None, p.sibling),
            (None, of_d, 0, p.sibling),
            (None, of_d, 1, p.sibling),
        )[k]
        dst = self.rows(unit, index, part)
        return remote(dst if src is None else src, dst, self.send.at[unit, k], self.recv.at[unit, k], p.id(to))

    def own(self, unit):
        dst = self.rows(unit, self.place.batch) if self.spread else self.full.at[unit]
        return pltpu.make_async_copy(self.shards[unit], dst, self.local.at[unit])

    def open(self, unit):
        self.own(unit).start()
        if self.spread:
            for k in (0, 1, 2):
                self.copy(unit, k).start()

    def relay(self, unit):
        if self.spread:
            self.copy(unit, 0).wait_recv()
            self.copy(unit, 1).wait_recv()
            for k in (3, 4, 5, 6):
                self.copy(unit, k).start()

    def share(self, unit):
        if self.spread:
            for k in (3, 4):
                self.copy(unit, k).wait_recv()
                self.copy(unit, k + 4).start()

    def finish(self, unit):
        self.own(unit).wait()
        if self.spread:
            for k in (2, 5, 6, 7, 8):
                self.copy(unit, k).wait_recv()

    def drain(self, unit):
        if self.spread:
            for k in range(self.SEMS):
                self.copy(unit, k).wait_send()


def gather_scratch(units, width):
    return [
        pltpu.VMEM((units, width, width), BF),
        pltpu.SemaphoreType.DMA((units, Gather.SEMS)),
        pltpu.SemaphoreType.DMA((units, Gather.SEMS)),
        pltpu.SemaphoreType.DMA((units,)),
    ]


class Scatter:
    SEMS = 7

    def __init__(self, place, grads, out, keep, got_core, got_x, got_y, last_x, last_y, send, recv, local):
        self.p, self.grads, self.out = place, grads, out
        self.room, self.got_core = keep, got_core
        self.got_x, self.got_y, self.last_x, self.last_y = got_x, got_y, last_x, last_y
        self.send, self.recv, self.local = send, recv, local
        p = place
        self.chip_x = p.x // 2
        self.chip_y = p.y // 2
        self.chip_d = p.diag // 2

    def keep(self, unit):
        far, near = self.grads[unit]
        if far is None:
            return near.at[:, self.p.core]
        return self.room.at[unit]

    def piece(self, unit, chip, part):
        half = self.last_x.shape[1]
        return self.keep(unit).at[chip, pl.ds(part * half, half)]

    def copy(self, unit, k):
        p = self.p
        src, dst, to = (
            lambda: (self.source(unit).at[:, 1 - p.core], self.got_core.at[unit], p.sibling),
            lambda: (self.piece(unit, self.chip_x, 0), self.got_x.at[unit, 0], p.x),
            lambda: (self.piece(unit, self.chip_d, 0), self.got_x.at[unit, 1], p.x),
            lambda: (self.piece(unit, self.chip_y, 1), self.got_y.at[unit, 0], p.y),
            lambda: (self.piece(unit, self.chip_d, 1), self.got_y.at[unit, 1], p.y),
            lambda: (self.piece(unit, self.chip_y, 0), self.last_y.at[unit], p.y),
            lambda: (self.piece(unit, self.chip_x, 1), self.last_x.at[unit], p.x),
        )[k]()
        return remote(src, dst, self.send.at[unit, k], self.recv.at[unit, k], p.id(to))

    def source(self, unit):
        far, near = self.grads[unit]
        return near if far is None else far

    def load(self, unit):
        return pltpu.make_async_copy(self.grads[unit][0].at[:, self.p.core], self.room.at[unit], self.local.at[unit, 0])

    def store(self, unit):
        return pltpu.make_async_copy(self.keep(unit).at[self.p.chip], self.out.at[unit], self.local.at[unit, 1])

    def open(self, unit):
        self.copy(unit, 0).start()
        if self.grads[unit][0] is not None:
            self.load(unit).start()

    def add(self, ref, other):
        ref[...] = (ref[...].astype(F32) + other[...].astype(F32)).astype(BF)

    def first(self, unit):
        if self.grads[unit][0] is not None:
            self.load(unit).wait()
        self.copy(unit, 0).wait_recv()
        self.add(self.keep(unit), self.got_core.at[unit])
        for k in (1, 2, 3, 4):
            self.copy(unit, k).start()

    def second(self, unit):
        p = self.p
        self.copy(unit, 2).wait_recv()
        self.add(self.piece(unit, self.chip_y, 0), self.got_x.at[unit, 1])
        self.copy(unit, 5).start()
        self.copy(unit, 4).wait_recv()
        self.add(self.piece(unit, self.chip_x, 1), self.got_y.at[unit, 1])
        self.copy(unit, 6).start()
        self.copy(unit, 1).wait_recv()
        self.add(self.piece(unit, p.chip, 0), self.got_x.at[unit, 0])
        self.copy(unit, 3).wait_recv()
        self.add(self.piece(unit, p.chip, 1), self.got_y.at[unit, 0])

    def third(self, unit):
        p = self.p
        self.copy(unit, 5).wait_recv()
        self.add(self.piece(unit, p.chip, 0), self.last_y.at[unit])
        self.copy(unit, 6).wait_recv()
        self.add(self.piece(unit, p.chip, 1), self.last_x.at[unit])
        if self.out is not None:
            self.store(unit).start()

    def drain(self, unit):
        for k in range(self.SEMS):
            self.copy(unit, k).wait_send()
        if self.out is not None:
            self.store(unit).wait()


def scatter_scratch(units, loaded, shard, width):
    half = shard // 2
    return [
        pltpu.VMEM((max(loaded, 1), 4, shard, width) if loaded else (1, 1, 16, width), BF),
        pltpu.VMEM((units, 4, shard, width), BF),
        pltpu.VMEM((units, 2, half, width), BF),
        pltpu.VMEM((units, 2, half, width), BF),
        pltpu.VMEM((units, half, width), BF),
        pltpu.VMEM((units, half, width), BF),
        pltpu.SemaphoreType.DMA((units, Scatter.SEMS)),
        pltpu.SemaphoreType.DMA((units, Scatter.SEMS)),
        pltpu.SemaphoreType.DMA((units, 2)),
    ]


class Line:
    def __init__(self, place, shares, out, mine, got, other, send, recv, local):
        self.p, self.shares, self.out = place, shares, out
        self.room, self.got, self.other = mine, got, other
        self.send, self.recv, self.local = send, recv, local

    def copy(self, item, half, k):
        p = self.p
        size = self.got.shape[1] // 2
        part = lambda ref: ref.at[pl.ds(half * size, size)]
        mine, got, other = self.mine(item), self.got.at[item], self.other.at[item]
        src, dst, to_z = ((mine, got, p.pair_z), (mine, other, 3 - p.z), (got, got, p.pair_z))[k]
        at = 3 * half + k
        return remote(part(src), part(dst), self.send.at[item, at], self.recv.at[item, at], (p.batch, to_z))

    def mine(self, item):
        far, near = self.shares[item]
        return self.room.at[item] if near is None else near

    def part(self, ref, half):
        size = self.got.shape[1] // 2
        return ref.at[pl.ds(half * size, size)]

    def load(self, item):
        return pltpu.make_async_copy(self.shares[item][0], self.room.at[item], self.local.at[item, 0])

    def store(self, item):
        return pltpu.make_async_copy(self.got.at[item], self.out.at[item], self.local.at[item, 1])

    def start(self, item):
        if self.shares[item][0] is not None:
            self.load(item).wait()

        @pl.when(jnp.logical_not(self.p.inner))
        def _():
            for half in (0, 1):
                self.copy(item, half, 0).start()

    def middle(self, item):
        @pl.when(self.p.inner)
        def _():
            for half in (0, 1):
                mine = self.part(self.mine(item), half)
                got = self.part(self.got.at[item], half)
                self.copy(item, half, 0).wait_recv()
                mine[...] = (mine[...].astype(F32) + got[...].astype(F32)).astype(BF)
                self.copy(item, half, 1).start()

    def last(self, item):
        @pl.when(self.p.inner)
        def _():
            for half in (0, 1):
                mine = self.part(self.mine(item), half)
                got = self.part(self.got.at[item], half)
                other = self.part(self.other.at[item], half)
                self.copy(item, half, 1).wait_recv()
                got[...] = (mine[...].astype(F32) + other[...].astype(F32)).astype(BF)
                self.copy(item, half, 2).start()

    def end(self, item):
        @pl.when(jnp.logical_not(self.p.inner))
        def _():
            for half in (0, 1):
                self.copy(item, half, 2).wait_recv()

        self.store(item).start()

    def drain(self, item):
        @pl.when(self.p.inner)
        def _():
            for half in (0, 1):
                self.copy(item, half, 1).wait_send()
                self.copy(item, half, 2).wait_send()

        @pl.when(jnp.logical_not(self.p.inner))
        def _():
            for half in (0, 1):
                self.copy(item, half, 0).wait_send()

        self.store(item).wait()


def line_scratch(items, loaded, shard, width):
    return [
        pltpu.VMEM((loaded, shard, width) if loaded else (1, 16, width), BF),
        pltpu.VMEM((items, shard, width), BF),
        pltpu.VMEM((items, shard, width), BF),
        pltpu.SemaphoreType.DMA((items, 6)),
        pltpu.SemaphoreType.DMA((items, 6)),
        pltpu.SemaphoreType.DMA((items, 2)),
    ]


class Plan:
    def __init__(self, xy, xy_arrays, z, z_arrays, shard, width):
        self.xy, self.xy_arrays, self.z, self.z_arrays = xy, xy_arrays, z, z_arrays
        self.shard, self.width = shard, width
        self.keep_sums = bool(xy) and not any(src == "sum" for src, _ in z)

    def args(self):
        return [*self.xy_arrays, *self.z_arrays]

    def outs(self):
        out = []
        if self.keep_sums:
            out.append(struct((len(self.xy), self.shard, self.width)))
        if self.z:
            out.append(struct((len(self.z), self.shard, self.width)))
        return out

    def scratch(self):
        loaded = sum(src != "own" for src, _ in self.xy)
        shares = sum(src != "sum" for src, _ in self.z)
        return (scatter_scratch(len(self.xy), loaded, self.shard, self.width) if self.xy else []) + (
            line_scratch(len(self.z), shares, self.shard, self.width) if self.z else []
        )

    def signals(self, p):
        return [p.id(p.sibling), p.id(p.x), p.id(p.y)] if self.xy else []

    def open(self, p, inputs, outputs, scratch, own=None):
        outputs, scratch = list(outputs), list(scratch)
        arrays = inputs[: len(self.xy_arrays)]
        shares = inputs[len(self.xy_arrays) :]
        sums_out = outputs.pop(0) if self.keep_sums else None
        scatter = line = None
        if self.xy:
            grads = [
                (None, own.at[unit]) if src == "own" else (arrays[src].at[unit], None) for src, unit in self.xy
            ]
            scatter = Scatter(p, grads, sums_out, *scratch[:9])
            scratch = scratch[9:]
        if self.z:
            items = [
                (None, scatter.keep(i).at[p.chip]) if src == "sum" else (shares[src].at[i], None)
                for src, i in self.z
            ]
            line = Line(p, items, outputs.pop(0), *scratch)
        return scatter, line


class Copies:
    def __init__(self, sems):
        self.sems, self.used, self.open = sems, 0, []

    def start(self, src, dst):
        copy = pltpu.make_async_copy(src, dst, self.sems.at[self.used])
        self.used += 1
        copy.start()
        return copy

    def save(self, src, dst):
        self.open.append(self.start(src, dst))

    def finish(self):
        for copy in self.open:
            copy.wait()


def rms(rows):
    return lax.rsqrt(jnp.mean(rows * rows, axis=-1, keepdims=True) + EPS)


def project_kernel(first, spread, *refs):
    refs = list(refs)
    take = lambda n: [refs.pop(0) for _ in range(n)]
    shard, rows_in, cos, sin = take(4)
    hid_in = None if first else take(1)[0]
    w_out, qkv_out, kvx_out, xt_out, swap_out = take(5)
    full, g_send, g_recv, g_local, h, xhat, xt, qkv, kvx, x_send, x_recv, copy_sems, s_send, s_recv = take(14)
    landing = take(1)[0] if first else swap_out
    p = Place()
    width = xhat.shape[1]
    rows = xhat.shape[0]
    quarter = rows // 2
    copies = Copies(copy_sems)
    swap = Swap(p, first, rows_in if first else hid_in, landing, s_send, s_recv)
    signals = [p.id(p.sibling)] + ([p.id(p.x), p.id(p.y)] if spread else [])
    greet(p, signals + swap.came_from)
    order = (1, 2, 0)
    gather = Gather(
        p, spread,
        [shard.at[:, pl.ds(u * width, width)] for u in range(3)],
        full, g_send, g_recv, g_local,
    )
    swap.start()
    if not first:
        load = copies.start(rows_in, h)
    gather.open(order[0])
    gather.open(order[1])
    if first:
        swap.arrive()
        for k in (0, 1):
            h[k * quarter : (k + 1) * quarter, :] = landing[k].astype(F32)
        copies.save(h, swap_out)
    else:
        load.wait()
    xhat[...] = (h[...] * rms(h[...])).astype(BF)
    xt[...] = xhat[...].T
    copies.save(xt, xt_out)

    def work(unit):
        step = 8 * HEAD_DIM
        for at in range(0, width, step):
            y = dot(xhat[...], full[unit, :, at : at + step], 1, 0).T
            for head in range(0, step, HEAD_DIM):
                to = unit * width + at + head
                if unit == 2:
                    qkv[to : to + HEAD_DIM, :] = y[head : head + HEAD_DIM].astype(BF)
                else:
                    a, b = y[head : head + HALF], y[head + HALF : head + HEAD_DIM]
                    qkv[to : to + HEAD_DIM, :] = jnp.concatenate(
                        [a * cos[...] - b * sin[...], b * cos[...] + a * sin[...]], axis=0
                    ).astype(BF)

    def exchange(unit):
        k = unit - 1
        return remote(
            qkv.at[pl.ds(unit * width, width)], kvx.at[pl.ds(k * width, width)],
            x_send.at[k], x_recv.at[k], p.id(p.sibling),
        )

    gather.relay(order[0])
    gather.open(order[2])
    gather.relay(order[1])
    gather.share(order[0])
    for i, unit in enumerate(order):
        gather.finish(unit)
        copies.save(full.at[unit], w_out.at[unit])
        work(unit)
        if unit:
            exchange(unit).start()
        if i == 0:
            gather.relay(order[2])
            gather.share(order[1])
        if i == 1:
            gather.share(order[2])
    copies.save(qkv, qkv_out)
    for unit in (1, 2):
        exchange(unit).wait_recv()
    copies.save(kvx, kvx_out)
    for unit in (1, 2):
        exchange(unit).wait_send()
    for unit in order:
        gather.drain(unit)
    if not first:
        swap.arrive()
    swap.drain()
    copies.finish()


def project(first, spread, name, collective, shard, rows_in, cos, sin, hid, rows, width):
    nat = (rows, width)
    outs = [
        struct((3, width, width)), struct((3 * width, rows)), struct((2 * width, rows)), struct((width, rows)),
        struct(nat, F32) if first else struct((2, rows // 2, width)),
    ]
    scratch = gather_scratch(3, width) + [
        pltpu.VMEM(nat, F32),
        pltpu.VMEM(nat, BF),
        pltpu.VMEM((width, rows), BF),
        pltpu.VMEM((3 * width, rows), BF),
        pltpu.VMEM((2 * width, rows), BF),
        pltpu.SemaphoreType.DMA((2,)),
        pltpu.SemaphoreType.DMA((2,)),
        pltpu.SemaphoreType.DMA((8,)),
    ] + swap_scratch()
    if first:
        scratch += [pltpu.VMEM((2, rows // 2, width), BF)]
    args = [shard, rows_in, cos, sin] + ([] if first else [hid])
    return pl.pallas_call(
        functools.partial(project_kernel, first, spread),
        in_specs=[ANY, ANY, VM, VM] + [ANY] * (len(args) - 4),
        out_specs=[ANY] * len(outs),
        out_shape=outs,
        scratch_shapes=scratch,
        compiler_params=pltpu.CompilerParams(
            collective_id=collective, has_side_effects=True, vmem_limit_bytes=56 * 2**20
        ),
        cost_estimate=pl.CostEstimate(flops=45 * 10**9, bytes_accessed=30 * 10**6, transcendentals=0),
        name=name,
    )(*args)


def key_blocks(core):
    if core == 0:
        return [(0, [("o", 0, 0)]), (1, [("o", 0, 0), ("x", 0, 1), ("x", 1, 2), ("o", 1, 3)])]
    return [(0, [("x", 0, 0), ("o", 0, 1)]), (1, [("x", 0, 0), ("o", 0, 1), ("o", 1, 2)])]


def masked(scores, quarter, diagonal, pad):
    size = scores.shape[0]
    key = lax.broadcasted_iota(jnp.int32, scores.shape, 0)
    ok = key >= pad - quarter * size
    if diagonal:
        query = lax.broadcasted_iota(jnp.int32, scores.shape, 1)
        ok = ((key <= query) & ok) | (key == query)
    return jnp.where(ok, scores, NEG)


def attend_heads(core, base, pad, qkv, kvx, o_ref, lse_ref):
    width, rows = o_ref.shape
    size = rows // 2
    at = lambda off, hh: pl.ds(pl.multiple_of(off * width + (base + hh) * HEAD_DIM, 16), HEAD_DIM)
    for hh in range(GROUP):
        for block, keys in key_blocks(core):
            cols = slice(block * size, block * size + size)
            q = qkv[at(0, hh), cols]
            scores = []
            for i, (src, half, quarter) in enumerate(keys):
                span = slice(half * size, half * size + size)
                k = qkv[at(1, hh), span] if src == "o" else kvx[at(0, hh), span]
                scores.append(masked(dot(k, q, 0, 0), quarter, i == len(keys) - 1, pad))
            top = functools.reduce(jnp.maximum, [jnp.max(s, axis=0, keepdims=True) for s in scores])
            total = 0.0
            out = 0.0
            for s, (src, half, quarter) in zip(scores, keys):
                span = slice(half * size, half * size + size)
                v = qkv[at(2, hh), span] if src == "o" else kvx[at(1, hh), span]
                weight = jnp.exp2((s - top) * LOG2_SCALE)
                total = total + jnp.sum(weight, axis=0, keepdims=True)
                out = out + dot(v, weight.astype(BF), 1, 0)
            o_ref[at(0, hh), cols] = (out * (1.0 / total)).astype(BF)
            lse_ref[base // GROUP, hh : hh + 1, cols] = top * LOG2_SCALE + jnp.log2(total)


def block_kernel(spread, swapping, pad_ref, qkv_in, kvx_in, h_in, out_shard, up_shard, down_shard, *refs):
    refs = list(refs)
    rows_in = refs.pop(0) if swapping else None
    swap_out = refs.pop(9) if swapping else None
    (w_out, h_out, hid_out, att_out, lse_out, mid_out, mt_out, pre_out, at_out, full, g_send, g_recv, g_local,
     qkv, kvx, h, att, lse, mid, mhat, mt, pre, act, act_t, hid, copy_sems, *swap_sems) = refs
    p = Place()
    copies = Copies(copy_sems)
    signals = [p.id(p.sibling), p.id(p.x), p.id(p.y)] if spread else []
    if swapping:
        swap = Swap(p, True, rows_in, swap_out, *swap_sems)
        signals += swap.came_from
    if signals:
        greet(p, signals)
    gather = Gather(p, spread, [out_shard, up_shard, down_shard], full, g_send, g_recv, g_local)
    loads = [copies.start(qkv_in, qkv), copies.start(kvx_in, kvx)]
    gather.open(0)
    gather.open(1)
    if swapping:
        swap.start()
    load_h = copies.start(h_in, h)
    for load in loads:
        load.wait()
    pad = pad_ref[0]
    groups = att.shape[0] // (HEAD_DIM * GROUP)

    def body(group, carry):
        base = group * GROUP
        for core in (0, 1):
            pl.when(p.core == core)(
                functools.partial(attend_heads, core, base, pad, qkv, kvx, att, lse)
            )

        @pl.when(group == 2)
        def _():
            gather.relay(0)
            gather.open(2)

        return carry

    lax.fori_loop(0, groups, body, 0)
    copies.save(att, att_out)
    copies.save(lse, lse_out)
    gather.share(0)
    gather.relay(1)
    gather.finish(0)
    copies.save(full.at[0], w_out.at[0])
    load_h.wait()
    width = att.shape[0]
    square = 0.0
    for cols in tiles(width):
        m = h[:, cols] + dot(att[...], full[0, :, cols], 0, 0)
        mid[:, cols] = m
        square = square + jnp.sum(m * m, axis=1, keepdims=True)
    copies.save(mid, mid_out)
    scale = lax.rsqrt(square / width + EPS)
    for cols in tiles(width):
        m = (mid[:, cols] * scale).astype(BF)
        mhat[:, cols] = m
        mt[cols, :] = m.T
    copies.save(mt, mt_out)
    gather.share(1)
    gather.finish(1)
    copies.save(full.at[1], w_out.at[1])
    for cols in tiles(width):
        v = dot(mhat[...], full[1, :, cols], 1, 0)
        pre[:, cols] = v
        a = (v / (1.0 + jnp.exp(-v))).astype(BF)
        act[:, cols] = a
        act_t[cols, :] = a.T
    copies.save(pre, pre_out)
    copies.save(act_t, at_out)
    gather.relay(2)
    gather.share(2)
    gather.finish(2)
    copies.save(full.at[2], w_out.at[2])
    for cols in tiles(width):
        v = mid[:, cols] + dot(act[...], full[2, :, cols], 1, 0)
        h[:, cols] = v
        hid[:, cols] = v.astype(BF)
    copies.save(h, h_out)
    copies.save(hid, hid_out)
    for unit in range(3):
        gather.drain(unit)
    if swapping:
        swap.arrive()
        swap.drain()
    copies.finish()


def block(spread, name, collective, pad, qkv, kvx, h, out_shard, up_shard, down_shard, rows_in, heads):
    swapping = rows_in is not None
    rows, width = h.shape
    lse_shape = (heads // GROUP, GROUP, rows)
    nat, tr = (rows, width), (width, rows)
    outs = [
        struct((3, width, width)), struct(nat, F32), struct(nat), struct(tr), struct(lse_shape, F32), struct(nat, F32),
        struct(tr), struct(nat, F32), struct(tr),
    ]
    scratch = gather_scratch(3, width) + [
        pltpu.VMEM((3 * width, rows), BF),
        pltpu.VMEM((2 * width, rows), BF),
        pltpu.VMEM(nat, F32),
        pltpu.VMEM(tr, BF),
        pltpu.VMEM(lse_shape, F32),
        pltpu.VMEM(nat, F32),
        pltpu.VMEM(nat, BF),
        pltpu.VMEM(tr, BF),
        pltpu.VMEM(nat, F32),
        pltpu.VMEM(nat, BF),
        pltpu.VMEM(tr, BF),
        pltpu.VMEM(nat, BF),
        pltpu.SemaphoreType.DMA((16,)),
    ]
    args = [pad, qkv, kvx, h, out_shard, up_shard, down_shard]
    if swapping:
        args.append(rows_in)
        outs.append(struct((2, rows // 2, width)))
        scratch += swap_scratch()
    params = dict(vmem_limit_bytes=56 * 2**20)
    if spread or swapping:
        params.update(collective_id=collective, has_side_effects=True)
    return pl.pallas_call(
        functools.partial(block_kernel, spread, swapping),
        in_specs=[SM] + [ANY] * (len(args) - 1),
        out_specs=[ANY] * len(outs),
        out_shape=outs,
        scratch_shapes=scratch,
        compiler_params=pltpu.CompilerParams(**params),
        cost_estimate=pl.CostEstimate(flops=45 * 10**9, bytes_accessed=30 * 10**6, transcendentals=0),
        name=name,
    )(*args)


def feed_back_kernel(plan, *refs):
    refs = list(refs)
    take = lambda n: [refs.pop(0) for _ in range(n)]
    g_in, w_in, act_t_in, mt_in, pre_in, mid_in, att_in = take(7)
    inputs = take(len(plan.args())) if plan else []
    dw_out, mg_out, do_out = take(3)
    outputs = take(len(plan.outs())) if plan else []
    g, w, act_t, mt, pre, mid, att, gb, dpre, eg, do, dw, copy_sems = take(13)
    copies = Copies(copy_sems)
    width = w.shape[1]
    shard = dw.shape[3]
    if plan:
        p = Place()
        greet(p, plan.signals(p), bool(plan.z))
        scatter, line = plan.open(p, inputs, outputs, refs, dw)
        if line:
            line.load(0).start()
        if plan.xy[0][0] != "own":
            scatter.open(0)
    load_g = copies.start(g_in, gb if g_in.dtype == BF else g)
    load_act = copies.start(act_t_in, act_t)
    load_w = [copies.start(w_in.at[2], w.at[2])]
    load_pre = copies.start(pre_in, pre)
    load_mt = copies.start(mt_in, mt)
    load_w += [copies.start(w_in.at[1], w.at[1])]
    load_mid = copies.start(mid_in, mid)
    load_att = copies.start(att_in, att)
    load_w += [copies.start(w_in.at[0], w.at[0])]

    def put(unit, cols, value):
        for k in range(dw.shape[1]):
            for c in range(2):
                at = (2 * k + c) * shard
                dw[unit, k, c, :, cols] = value[at : at + shard].astype(BF)

    load_g.wait()
    if g_in.dtype == BF:
        g[...] = gb[...].astype(F32)
    else:
        gb[...] = g[...].astype(BF)
    load_act.wait()
    for cols in tiles(width):
        put(2, cols, dot(act_t[...], gb[:, cols], 1, 0))
    if plan and plan.xy[0][0] == "own":
        scatter.open(0)
    else:
        copies.save(dw.at[2], dw_out.at[2])
    if plan:
        if line:
            line.start(0)
    load_w[0].wait()
    load_pre.wait()
    for cols in tiles(width):
        da = dot(gb[...], w[2, cols, :], 1, 1)
        v = pre[:, cols]
        s = 1.0 / (1.0 + jnp.exp(-v))
        dpre[:, cols] = (da * (s + v * s * (1.0 - s))).astype(BF)
    if plan:
        scatter.first(0)
    load_mt.wait()
    for cols in tiles(width):
        put(1, cols, dot(mt[...], dpre[:, cols], 1, 0))
    copies.save(dw.at[1], dw_out.at[1])
    load_w[1].wait()
    load_mid.wait()
    r = rms(mid[...])
    total = 0.0
    for cols in tiles(width):
        e = dot(dpre[...], w[1, cols, :], 1, 1)
        eg[:, cols] = e
        total = total + jnp.sum(e * (mid[:, cols] * r), axis=1, keepdims=True)
    total = total / width
    if plan and line:
        line.middle(0)
    for cols in tiles(width):
        m = g[:, cols] + r * (eg[:, cols] - mid[:, cols] * r * total)
        g[:, cols] = m
        gb[:, cols] = m.astype(BF)
    copies.save(g, mg_out)
    load_att.wait()
    for cols in tiles(width):
        put(0, cols, dot(att[...], gb[:, cols], 1, 0))
    copies.save(dw.at[0], dw_out.at[0])
    load_w[2].wait()
    if plan:
        scatter.second(0)
        if line:
            line.last(0)
    for cols in tiles(width):
        do[cols, :] = dot(w[0, cols, :], gb[...], 1, 1).astype(BF)
    copies.save(do, do_out)
    if plan:
        scatter.third(0)
        if line:
            line.end(0)
            line.drain(0)
        scatter.drain(0)
    copies.finish()


def kernel_params(collective):
    params = dict(vmem_limit_bytes=63 * 2**20)
    if collective is not None:
        params.update(collective_id=collective, has_side_effects=True)
    return pltpu.CompilerParams(**params)


def feed_back(name, collective, g, w, act_t, mt, pre, mid, att, chips, shard, plan):
    width, rows = act_t.shape
    nat, tr = (rows, width), (width, rows)
    grad = (3, chips, 2, shard, width)
    args = [g, w, act_t, mt, pre, mid, att] + (plan.args() if plan else [])
    outs = [struct(grad), struct(nat, F32), struct(tr)] + (plan.outs() if plan else [])
    return pl.pallas_call(
        functools.partial(feed_back_kernel, plan),
        in_specs=[ANY] * len(args),
        out_specs=[ANY] * len(outs),
        out_shape=outs,
        scratch_shapes=[
            pltpu.VMEM(nat, F32),
            pltpu.VMEM((3, width, width), BF),
            pltpu.VMEM(tr, BF),
            pltpu.VMEM(tr, BF),
            pltpu.VMEM(nat, F32),
            pltpu.VMEM(nat, F32),
            pltpu.VMEM(tr, BF),
            pltpu.VMEM(nat, BF),
            pltpu.VMEM(nat, BF),
            pltpu.VMEM(nat, F32),
            pltpu.VMEM(tr, BF),
            pltpu.VMEM(grad, BF),
            pltpu.SemaphoreType.DMA((16,)),
        ] + (plan.scratch() if plan else []),
        compiler_params=kernel_params(collective if plan else None),
        cost_estimate=pl.CostEstimate(flops=16 * 10**9, bytes_accessed=30 * 10**6, transcendentals=0),
        name=name,
    )(*args)


def unrotate(t, cos, sin):
    a, b = t[:HALF], t[HALF:]
    return jnp.concatenate([a * cos + b * sin, b * cos - a * sin], axis=0)


def attend_back_heads(core, base, pad, qkv, kvx, do, o, lse, tables, dqkv, dkvx):
    width, rows = o.shape
    size = rows // 2
    scale = 1.0 / math.sqrt(HEAD_DIM)
    cos, sin, cosx, sinx = tables
    at = lambda off, hh: pl.ds(pl.multiple_of(off * width + (base + hh) * HEAD_DIM, 16), HEAD_DIM)
    for hh in range(GROUP):
        dk, dv = {}, {}
        for block, keys in key_blocks(core):
            cols = slice(block * size, block * size + size)
            q = qkv[at(0, hh), cols]
            d_out = do[at(0, hh), cols]
            delta = jnp.sum(d_out.astype(F32) * o[at(0, hh), cols].astype(F32), axis=0, keepdims=True)
            norm = lse[base // GROUP, hh : hh + 1, cols]
            dq = 0.0
            for i, (src, half, quarter) in enumerate(keys):
                span = slice(half * size, half * size + size)
                k = qkv[at(1, hh), span] if src == "o" else kvx[at(0, hh), span]
                v = qkv[at(2, hh), span] if src == "o" else kvx[at(1, hh), span]
                s = masked(dot(k, q, 0, 0), quarter, i == len(keys) - 1, pad)
                weight = jnp.exp2(s * LOG2_SCALE - norm)
                ds = (weight * (dot(v, d_out, 0, 0) - delta)).astype(BF)
                dq = dq + dot(k, ds, 1, 0)
                a, b = dot(q, ds, 1, 1), dot(d_out, weight.astype(BF), 1, 1)
                key = (src, half)
                dk[key] = dk[key] + a if key in dk else a
                dv[key] = dv[key] + b if key in dv else b
            dqkv[at(0, hh), cols] = unrotate(dq * scale, cos[:, cols], sin[:, cols]).astype(BF)
        for src, ref, k_off, ct, st in (("o", dqkv, 1, cos, sin), ("x", dkvx, 0, cosx, sinx)):
            for half in (0, 1):
                span = slice(half * size, half * size + size)
                if (src, half) in dk:
                    a = unrotate(dk[src, half] * scale, ct[:, span], st[:, span]).astype(BF)
                    b = dv[src, half].astype(BF)
                else:
                    a = b = jnp.zeros((HEAD_DIM, size), BF)
                ref[at(k_off, hh), span] = a
                ref[at(k_off + 1, hh), span] = b


def attend_back_kernel(plan, swapping, *refs):
    refs = list(refs)
    take = lambda n: [refs.pop(0) for _ in range(n)]
    pad_ref, qkv_in, kvx_in, do_in, att_in, lse, cos, sin, cosx, sinx = take(10)
    hid_in = take(1)[0] if swapping else None
    inputs = take(len(plan.args())) if plan else []
    pg_out = take(1)[0]
    swap_out = take(1)[0] if swapping else None
    outputs = take(len(plan.outs())) if plan else []
    qkv, kvx, do, att, dqkv, dkvx, got, x_send, x_recv, copy_sems = take(10)
    p = Place()
    copies = Copies(copy_sems)
    signals = [p.id(p.sibling)]
    if plan:
        signals = plan.signals(p)
    if swapping:
        swap = Swap(p, False, hid_in, swap_out, *take(2))
        signals = signals + swap.came_from
    greet(p, signals, bool(plan and plan.z))
    loads = [copies.start(a, b) for a, b in ((qkv_in, qkv), (kvx_in, kvx), (do_in, do), (att_in, att))]
    units = items = 0
    if plan:
        scatter, line = plan.open(p, inputs, outputs, refs)
        units, items = len(plan.xy), len(plan.z)
        for i in range(units):
            scatter.open(i)
        for i in range(items):
            line.load(i).start()
        for i in range(items):
            line.start(i)
    if swapping:
        swap.start()
    for load in loads:
        load.wait()
    for i in range(units):
        scatter.first(i)
    pad = pad_ref[0]
    width = att.shape[0]
    span = GROUP * HEAD_DIM
    groups = width // span

    def exchange(group, k):
        part = pl.ds(pl.multiple_of(k * width + group * span, 16), span)
        return remote(dkvx.at[part], got.at[part], x_send.at[group, k], x_recv.at[group, k], p.id(p.sibling))

    def body(group, carry):
        for core in (0, 1):
            pl.when(p.core == core)(
                functools.partial(
                    attend_back_heads, core, group * GROUP, pad, qkv, kvx, do, att, lse,
                    (cos, sin, cosx, sinx), dqkv, dkvx,
                )
            )
        for k in (0, 1):
            exchange(group, k).start()
        if plan:

            @pl.when(group == 1)
            def _():
                for i in range(items):
                    line.middle(i)
                scatter.second(0)

            @pl.when(group == 2)
            def _():
                for i in range(1, units):
                    scatter.second(i)
                for i in range(items):
                    line.last(i)

        return carry

    lax.fori_loop(0, groups, body, 0)
    for i in range(units):
        scatter.third(i)
    for group in range(groups):
        for k in (0, 1):
            exchange(group, k).wait_recv()
    own = dqkv.at[pl.ds(width, 2 * width)]
    own[...] = (own[...].astype(F32) + got[...].astype(F32)).astype(BF)
    copies.save(dqkv, pg_out)
    for i in range(items):
        line.end(i)
    for i in range(items):
        line.drain(i)
    for i in range(units):
        scatter.drain(i)
    for group in range(groups):
        for k in (0, 1):
            exchange(group, k).wait_send()
    if swapping:
        swap.arrive()
        swap.drain()
    copies.finish()


def attend_back(name, collective, pad, qkv, kvx, do, att, lse, tables, hid, plan):
    width, rows = att.shape
    swapping = hid is not None
    args = [pad, qkv, kvx, do, att, lse, *tables] + ([hid] if swapping else []) + (plan.args() if plan else [])
    specs = [SM] + [ANY] * 4 + [VM] * 5 + [ANY] * (len(args) - 10)
    outs = [struct((3 * width, rows))]
    if swapping:
        outs.append(struct(hid.shape))
    outs += plan.outs() if plan else []
    scratch = [
        pltpu.VMEM((3 * width, rows), BF),
        pltpu.VMEM((2 * width, rows), BF),
        pltpu.VMEM((width, rows), BF),
        pltpu.VMEM((width, rows), BF),
        pltpu.VMEM((3 * width, rows), BF),
        pltpu.VMEM((2 * width, rows), BF),
        pltpu.VMEM((2 * width, rows), BF),
        pltpu.SemaphoreType.DMA((lse.shape[0], 2)),
        pltpu.SemaphoreType.DMA((lse.shape[0], 2)),
        pltpu.SemaphoreType.DMA((8,)),
    ]
    if swapping:
        scratch += swap_scratch()
    return pl.pallas_call(
        functools.partial(attend_back_kernel, plan, swapping),
        in_specs=specs,
        out_specs=[ANY] * len(outs),
        out_shape=outs,
        scratch_shapes=scratch + (plan.scratch() if plan else []),
        compiler_params=kernel_params(collective),
        cost_estimate=pl.CostEstimate(flops=35 * 10**9, bytes_accessed=30 * 10**6, transcendentals=0),
        name=name,
    )(*args)


def project_back_kernel(plan, swapping, *refs):
    refs = list(refs)
    take = lambda n: [refs.pop(0) for _ in range(n)]
    pg_in, xt_in, w_in, h_in, mg_in = take(5)
    inputs = take(len(plan.args())) if plan else []
    dw_out = None if swapping and plan else take(1)[0]
    g_out = take(1)[0]
    outputs = take(len(plan.outs())) if plan else []
    pg, xt, w, h, g, eg, dw, copy_sems = take(8)
    gb = take(1)[0] if swapping else None
    swap_sems = take(2) if swapping else None
    copies = Copies(copy_sems)
    width = xt.shape[0]
    quarter = xt.shape[1] // 2
    shard = dw.shape[3]
    p = Place()
    signals = plan.signals(p) if plan else []
    if swapping:
        swap = Swap(p, False, gb, g_out, *swap_sems)
        signals = signals + swap.came_from
    if signals:
        greet(p, signals, bool(plan and plan.z))
    load_pg = copies.start(pg_in, pg)
    load_xt = copies.start(xt_in, xt)
    held = earlier = shares = 0
    scatter = line = None
    if plan:
        scatter, line = plan.open(p, inputs, outputs, refs, dw)
        held = len(plan.xy)
        earlier = sum(src != "own" for src, _ in plan.xy)
        shares = sum(src != "sum" for src, _ in plan.z)
    for i in range(earlier):
        scatter.open(i)
    for i in range(shares):
        line.load(i).start()
    load_w = copies.start(w_in, w)
    load_h = copies.start(h_in, h)
    load_g = copies.start(mg_in, g)
    load_pg.wait()
    load_xt.wait()
    for i in range(shares):
        line.start(i)
    for i in range(min(earlier, 1)):
        scatter.first(i)

    def weight_grad(unit):
        for cols in tiles(width):
            value = dot(xt[...], pg[unit * width + cols.start : unit * width + cols.stop, :], 1, 1)
            for k in range(dw.shape[1]):
                for c in range(2):
                    at = (2 * k + c) * shard
                    dw[unit, k, c, :, cols] = value[at : at + shard].astype(BF)
        if dw_out is not None and not (plan and ("own", unit) in plan.xy):
            copies.save(dw.at[unit], dw_out.at[unit])

    own = earlier
    weight_grad(1)
    for i in range(1, earlier):
        scatter.first(i)
    if own < held:
        scatter.open(own)
    weight_grad(2)
    if own < held:
        scatter.first(own)
    for i in range(shares):
        line.middle(i)
    if own + 1 < held:
        scatter.open(own + 1)
    weight_grad(0)
    if own + 2 < held:
        scatter.open(own + 2)
    for i in range(min(earlier, 1)):
        scatter.second(i)
    load_w.wait()
    load_h.wait()
    r = rms(h[...])
    total = 0.0
    for n, cols in enumerate(tiles(width)):
        e = 0.0
        for unit in range(3):
            e = e + dot(pg[unit * width : (unit + 1) * width, :], w[unit, cols, :], 0, 1)
        eg[:, cols] = e
        total = total + jnp.sum(e * (h[:, cols] * r), axis=1, keepdims=True)
        if n == 1:
            for i in range(1, earlier):
                scatter.second(i)
        if n == 2 and own + 1 < held:
            scatter.first(own + 1)
        if n == 3:
            for i in range(shares):
                line.last(i)
    total = total / width
    load_g.wait()
    for cols in tiles(width):
        v = g[:, cols] + r * (eg[:, cols] - h[:, cols] * r * total)
        if swapping:
            for k in (0, 1):
                gb[k, :, cols] = v[k * quarter : (k + 1) * quarter].astype(BF)
        else:
            g[:, cols] = v
    if swapping:
        swap.start()
    else:
        copies.save(g, g_out)
    chain = bool(plan) and len(plan.z) > shares
    for i in range(own + 2, held):
        scatter.first(i)
    for i in range(earlier):
        scatter.third(i)
    steps = [[] for _ in range(held + 6)]
    for i in range(held):
        if i >= earlier:
            steps[i].append(functools.partial(scatter.second, i))
            steps[i + 1].append(functools.partial(scatter.third, i))
        if chain:
            j = shares + i
            base = i + 1
            steps[base].append(functools.partial(line.start, j))
            steps[base + 1].append(functools.partial(line.middle, j))
            steps[base + 2].append(functools.partial(line.last, j))
            steps[base + 3].append(functools.partial(line.end, j))
    for group in steps:
        for step in group:
            step()
    for i in range(shares):
        line.end(i)
    for i in range(len(plan.z) if plan else 0):
        line.drain(i)
    for i in range(held):
        scatter.drain(i)
    if swapping:
        swap.arrive()
        swap.drain()
    copies.finish()


def project_back(name, collective, pg, xt, w, h, mg, chips, shard, swapping, plan):
    rows, width = h.shape
    nat, tr = (rows, width), (width, rows)
    grad = (3, chips, 2, shard, width)
    args = [pg, xt, w, h, mg] + (plan.args() if plan else [])
    outs = [] if swapping and plan else [struct(grad)]
    outs.append(struct((2, rows // 2, width)) if swapping else struct(nat, F32))
    outs += plan.outs() if plan else []
    scratch = [
        pltpu.VMEM((3 * width, rows), BF),
        pltpu.VMEM(tr, BF),
        pltpu.VMEM((3, width, width), BF),
        pltpu.VMEM(nat, F32),
        pltpu.VMEM(nat, F32),
        pltpu.VMEM(nat, F32),
        pltpu.VMEM(grad, BF),
        pltpu.SemaphoreType.DMA((8,)),
    ]
    if swapping:
        scratch += [pltpu.VMEM((2, rows // 2, width), BF)] + swap_scratch()
    return pl.pallas_call(
        functools.partial(project_back_kernel, plan, swapping),
        in_specs=[ANY] * len(args),
        out_specs=[ANY] * len(outs),
        out_shape=outs,
        scratch_shapes=scratch + (plan.scratch() if plan else []),
        compiler_params=kernel_params(collective if plan or swapping else None),
        cost_estimate=pl.CostEstimate(flops=16 * 10**9, bytes_accessed=30 * 10**6, transcendentals=0),
        name=name,
    )(*args)


def local(nb, ns, inputs, lengths, wqkv, wout, wup, wdown, gain_attn, gain_mlp, cotangent):
    series, quarter, width = inputs.shape
    heads = width // HEAD_DIM
    rows = 2 * quarter
    shard = wout.shape[1]
    chips = nb // 2
    spread = nb == 8
    z = lax.axis_index("seq")
    core = lax.axis_index("batch") % 2

    other = lax.ppermute(
        lengths, AXES, [(b * ns + s, (b ^ 1) * ns + s) for b in range(nb) for s in range(ns)]
    )
    both = jnp.where(core == 0, jnp.concatenate([lengths, other]), jnp.concatenate([other, lengths]))
    which = jnp.where((z == 0) | (z == 3), 2, 0) + z // 2
    pad = SLOTS - lax.dynamic_index_in_dim(both, which, 0, keepdims=True)
    angle = (
        jnp.exp(jnp.arange(HALF, dtype=F32) * (-2.0 * math.log(10000.0) / HEAD_DIM))[:, None]
        * jnp.arange(SLOTS, dtype=F32)[None, :]
    )
    cos_all, sin_all = jnp.cos(angle), jnp.sin(angle)
    cos_pad = lax.dynamic_slice_in_dim(cos_all, pad[0], 1, axis=1)
    sin_pad = lax.dynamic_slice_in_dim(sin_all, pad[0], 1, axis=1)
    cos_four = (cos_all * cos_pad + sin_all * sin_pad).reshape(HALF, 4, quarter)
    sin_four = (sin_all * cos_pad - cos_all * sin_pad).reshape(HALF, 4, quarter)

    def pick(table):
        even = jnp.concatenate([table[:, 0], table[:, 3]], axis=1)
        odd = jnp.concatenate([table[:, 1], table[:, 2]], axis=1)
        return jnp.where(core == 0, even, odd), jnp.where(core == 0, odd, even)

    cos, cosx = pick(cos_four)
    sin, sinx = pick(sin_four)

    wqkv_g = (wqkv.astype(F32) * gain_attn.astype(F32)[:, :, None]).astype(BF)
    wup_g = (wup.astype(F32) * gain_mlp.astype(F32)[:, :, None]).astype(BF)

    def shards(array, layer):
        if spread:
            return array[layer]
        return lax.all_gather(array[layer], "batch", axis=0, tiled=True)

    halves = lambda array: array.reshape(2, quarter, width)
    saved = []
    rows_in = inputs
    hid = None
    for layer in range(LAYERS):
        first = layer == 0
        w_qkv, qkv, kvx, xt, swapped = project(
            first, spread, f"project_{layer}", layer, shards(wqkv_g, layer), rows_in, cos, sin, hid, rows, width
        )
        h = swapped if first else rows_in
        hidden_0 = swapped
        w_ff, rows_in, hid, att, lse, mid, mt, pre, act_t, *rest = block(
            spread, f"block_{layer}", 2 + layer, pad, qkv, kvx, h,
            shards(wout, layer), shards(wup_g, layer), shards(wdown, layer), cotangent if first else None, heads,
        )
        hid = halves(hid)
        if first:
            g = rest[0].reshape(rows, width)
        saved.append((w_qkv, qkv, kvx, xt, h, w_ff, att, lse, mid, mt, pre, act_t))

    def plan(xy, xy_arrays, z, z_arrays):
        return Plan(xy, xy_arrays, z, z_arrays, shard, width) if spread else None

    tables = (cos, sin, cosx, sinx)
    w_qkv, qkv, kvx, xt, h, w_ff, att, lse, mid, mt, pre, act_t = saved[1]
    ff_1, mg, do, *p_d1 = feed_back(
        "feed_back_1", 4, g, w_ff, act_t, mt, pre, mid, att, chips, shard, plan([("own", 2)], [], [], [])
    )
    pg, hidden_1, *sums = attend_back(
        "attend_back_1", 5, pad, qkv, kvx, do, att, lse, tables, hid,
        plan([(0, 1), (0, 0)], [ff_1], [(0, 0)], p_d1),
    )
    p_uo1, r_d1 = sums if spread else (None, None)
    qkv_1, g, *sums = project_back(
        "project_back_1", 6, pg, xt, w_qkv, h, mg, chips, shard, False,
        plan([("own", 1)], [], [(0, 0)], [p_uo1]),
    )
    p_k1, r_u1 = sums if spread else (None, None)
    w_qkv, qkv, kvx, xt, h, w_ff, att, lse, mid, mt, pre, act_t = saved[0]
    ff_0, mg, do, *sums = feed_back(
        "feed_back_0", 7, g, w_ff, act_t, mt, pre, mid, att, chips, shard,
        plan([(0, 0)], [qkv_1], [(0, 1)], [p_uo1]),
    )
    p_q1, r_o1 = sums if spread else (None, None)
    pg, *sums = attend_back(
        "attend_back_0", 8, pad, qkv, kvx, do, att, lse, tables, None,
        plan([(0, 2), (1, 2)], [qkv_1, ff_0], [(0, 0), (1, 0)], [p_k1, p_q1]),
    )
    p_vd, r_kq1 = sums if spread else (None, None)
    tail = project_back(
        "project_back_0", 9, pg, xt, w_qkv, h, mg, chips, shard, True,
        plan(
            [(0, 1), (0, 0), ("own", 1), ("own", 2), ("own", 0)], [ff_0],
            [(0, 0), (0, 1)] + [("sum", i) for i in range(5)], [p_vd],
        ),
    )
    if spread:
        input_grad, r = tail
        s_qkv = [[r[6], r[4], r[5]], [r_kq1[1], r_kq1[0], r[0]]]
        s_ff = [[r[3], r[2], r[1]], [r_o1[0], r_u1[0], r_d1[0]]]
    else:
        qkv_0, input_grad = tail

        def over_all(grads):
            flat = grads.reshape(3, nb * shard, width)
            return lax.psum(lax.psum_scatter(flat, "batch", scatter_dimension=1, tiled=True), "seq")

        s_qkv = [over_all(qkv_0), over_all(qkv_1)]
        s_ff = [over_all(ff_0), over_all(ff_1)]
    input_grad = input_grad.astype(F32)
    hidden = [hidden_0, hidden_1]

    grad_qkv, grad_out, grad_up, grad_down, grad_ga, grad_gm = [], [], [], [], [], []
    for layer in range(LAYERS):
        ff = [part.astype(F32) for part in s_ff[layer]]
        qkv_sum = jnp.concatenate([part.astype(F32) for part in s_qkv[layer]], axis=1)
        grad_qkv.append(qkv_sum * gain_attn[layer].astype(F32)[:, None])
        grad_ga.append(jnp.sum(qkv_sum * wqkv[layer].astype(F32), axis=1))
        grad_out.append(ff[0])
        grad_up.append(ff[1] * gain_mlp[layer].astype(F32)[:, None])
        grad_gm.append(jnp.sum(ff[1] * wup[layer].astype(F32), axis=1))
        grad_down.append(ff[2])
    stack = jnp.stack
    return (
        stack(hidden), input_grad, stack(grad_qkv), stack(grad_out), stack(grad_up), stack(grad_down),
        stack(grad_ga), stack(grad_gm),
    )


def solution(mesh):
    nb, ns = mesh.shape["batch"], mesh.shape["seq"]
    rows = P("batch", "seq", None)
    weight = P(None, "batch", None)
    gain = P(None, "batch")
    return jax.shard_map(
        functools.partial(local, nb, ns),
        mesh=mesh,
        in_specs=(rows, P("batch"), weight, weight, weight, weight, gain, gain, rows),
        out_specs=(P(None, "batch", "seq", None), rows, weight, weight, weight, weight, gain, gain),
        check_vma=False,
    )
```

```python
import functools
import math

import jax
import jax.numpy as jnp
from jax import lax
from jax.experimental import pallas as pl
from jax.experimental.pallas import tpu as pltpu
from jax.sharding import PartitionSpec as P

HEAD_DIM = 80
HALF = HEAD_DIM // 2
LAYERS = 2
SLOTS = 1024
BF = jnp.bfloat16
F32 = jnp.float32
AXES = ("batch", "seq")
LOG2_SCALE = math.log2(math.e) / math.sqrt(HEAD_DIM)
NEG = -1e30
EPS = 1e-6
TILE = 256
MESH = pl.DeviceIdType.MESH
ANY = pl.BlockSpec(memory_space=pl.ANY)
VM = pl.BlockSpec(memory_space=pltpu.VMEM)
SM = pl.BlockSpec(memory_space=pltpu.SMEM)
GROUP = 4
LAG = 2
RATE = 2
DIRECT = (0, 1)
AHEAD = 2


def dot(a, b, i, j):
    return lax.dot_general(a, b, (((i,), (j,)), ((), ())), preferred_element_type=F32)


def struct(shape, dtype=BF):
    return jax.ShapeDtypeStruct(shape, dtype)


def tiles(extent):
    return [slice(at, at + TILE) for at in range(0, extent, TILE)]


class Place:
    def __init__(self):
        self.batch = lax.axis_index("batch")
        self.z = lax.axis_index("seq")
        self.core = self.batch % 2
        self.chip = self.batch // 2
        x = self.chip % 2
        y = (self.chip // 2) % 2
        self.to_x = 2 - 4 * x
        self.to_y = 4 - 8 * y
        self.x = self.batch + self.to_x
        self.y = self.batch + self.to_y
        self.diag = self.batch + self.to_x + self.to_y
        self.sibling = self.batch + 1 - 2 * self.core
        self.inner = (self.z == 1) | (self.z == 2)
        self.pair_z = self.z + 1 - 2 * (self.z % 2)
        self.owner = ((self.z + 1) // 2) % 2
        self.part = self.z // 2

    def id(self, batch):
        return (batch, self.z)

    def workers(self):
        return [
            (2 * self.chip + self.owner, (1 - self.core) * (1 + j) + self.core * 3 * j) for j in (0, 1)
        ]

    def holders(self):
        return [(2 * self.chip + 1 - self.owner, at) for at in (self.core, 3 - self.core)]


def greet(place, signals, line=False):
    barrier = pltpu.get_barrier_semaphore()
    for device in signals:
        pl.semaphore_signal(barrier, inc=1, device_id=device, device_id_type=MESH)
    if line:
        pl.semaphore_signal(barrier, inc=1, device_id=(place.batch, place.pair_z), device_id_type=MESH)

        @pl.when(place.inner)
        def _():
            pl.semaphore_signal(barrier, inc=1, device_id=(place.batch, 3 - place.z), device_id_type=MESH)

        pl.semaphore_wait(barrier, len(signals) + 1 + place.part + place.z % 2 - 2 * place.part * (place.z % 2))
    else:
        pl.semaphore_wait(barrier, len(signals))


class Swap:
    PIECES = 8

    def __init__(self, place, to_workers, src, landing, send, recv):
        self.src, self.landing, self.send, self.recv = src, landing, send, recv
        self.to = place.workers() if to_workers else place.holders()
        self.came_from = place.holders() if to_workers else place.workers()
        self.part = place.part
        self.sent = 0

    def copy(self, k, piece, part):
        count = self.src.shape[1] // self.PIECES
        rows = pl.ds(piece * count, count)
        return remote(
            self.src.at[k, rows], self.landing.at[part, rows], self.send.at[k, piece], self.recv.at[part, piece],
            self.to[k],
        )

    def start(self, pieces=PIECES):
        for _ in range(pieces):
            if self.sent < self.PIECES:
                for k in (0, 1):
                    self.copy(k, self.sent, self.part).start()
                self.sent += 1

    def arrive(self):
        for piece in range(self.PIECES):
            for k in (0, 1):
                self.copy(k, piece, k).wait_recv()

    def drain(self):
        for piece in range(self.PIECES):
            for k in (0, 1):
                self.copy(k, piece, self.part).wait_send()


def swap_scratch():
    return [pltpu.SemaphoreType.DMA((2, Swap.PIECES)), pltpu.SemaphoreType.DMA((2, Swap.PIECES))]


def remote(src, dst, send_sem, recv_sem, device):
    return pltpu.make_async_remote_copy(
        src_ref=src, dst_ref=dst, send_sem=send_sem, recv_sem=recv_sem, device_id=device,
        device_id_type=MESH,
    )


class Gather:
    SEMS = 13

    def __init__(self, place, spread, shards, full, slots, direct, send, recv, local):
        self.place, self.spread, self.direct = place, spread, direct
        self.shards, self.full, self.slots = shards, full, slots
        self.send, self.recv, self.local = send, recv, local
        self.stage = {}

    def rows(self, unit, index, start=0, count=None):
        size = self.shards[unit].shape[0]
        count = size if count is None else count
        return self.full.at[self.slots[unit], pl.ds(pl.multiple_of(index * size + start, 16), count)]

    def span(self, unit):
        size = self.shards[unit].shape[0]
        if unit in self.direct:
            return 0, 0, size
        hz = self.place.z % 2
        return hz * (size // 2), (1 - hz) * (size // 2), size // 2

    def cut(self, unit):
        _, _, half = self.span(unit)
        small = half // 32 * 16
        return small if unit % 2 else half - small

    def copy(self, unit, k):
        p = self.place
        near, far, half = self.span(unit)
        cut = self.cut(unit)
        src = self.shards[unit]
        whole = lambda index: self.rows(unit, index)
        x_part = lambda index, at: self.rows(unit, index, at, cut)
        y_part = lambda index, at: self.rows(unit, index, at + cut, half - cut)
        dst, to = (
            lambda: (whole(p.batch), p.id(p.x)),
            lambda: (whole(p.batch), p.id(p.y)),
            lambda: (whole(p.batch), p.id(p.sibling)),
            lambda: (x_part(p.y, near), p.id(p.x)),
            lambda: (y_part(p.x, near), p.id(p.y)),
            lambda: (whole(p.x), p.id(p.sibling)),
            lambda: (whole(p.y), p.id(p.sibling)),
            lambda: (x_part(p.diag, near), p.id(p.sibling)),
            lambda: (y_part(p.diag, near), p.id(p.sibling)),
            lambda: (x_part(p.diag, near), (p.batch, p.pair_z)),
            lambda: (y_part(p.diag, near), (p.batch, p.pair_z)),
            lambda: (x_part(p.diag, far), p.id(p.sibling)),
            lambda: (y_part(p.diag, far), p.id(p.sibling)),
        )[k]()
        return remote(src if k < 3 else dst, dst, self.send.at[unit, k], self.recv.at[unit, k], to)

    def own(self, unit):
        dst = self.rows(unit, self.place.batch) if self.spread else self.full.at[self.slots[unit]]
        return pltpu.make_async_copy(self.shards[unit], dst, self.local.at[unit])

    def at_stage(self, unit, stage):
        if self.stage.get(unit, 0) >= stage:
            return False
        assert self.stage.get(unit, 0) == stage - 1
        self.stage[unit] = stage
        return self.spread

    def open(self, unit):
        self.own(unit).start()
        if self.at_stage(unit, 1):
            for k in (0, 1, 2):
                self.copy(unit, k).start()

    def relay(self, unit):
        if self.at_stage(unit, 2):
            self.copy(unit, 0).wait_recv()
            self.copy(unit, 1).wait_recv()
            for k in (3, 4, 5, 6):
                self.copy(unit, k).start()

    def share(self, unit):
        if self.at_stage(unit, 3):
            for k in (3, 4):
                self.copy(unit, k).wait_recv()
                if unit not in self.direct:
                    self.copy(unit, k + 6).start()
                self.copy(unit, k + 4).start()

    def pass_on(self, unit):
        if self.at_stage(unit, 4) and unit not in self.direct:
            for k in (9, 10):
                self.arrival(unit, k).wait_recv()
                self.copy(unit, k + 2).start()

    def arrival(self, unit, k):
        p = self.place
        _, far, half = self.span(unit)
        cut = self.cut(unit)
        start, count = ((far, cut), (far + cut, half - cut))[k - 9]
        dst = self.rows(unit, p.diag, start, count)
        return remote(dst, dst, self.send.at[unit, k], self.recv.at[unit, k], (p.batch, p.pair_z))

    def need(self, unit):
        self.relay(unit)
        self.share(unit)
        self.pass_on(unit)
        self.own(unit).wait()
        if self.spread:
            for k in (2, 5, 6, 7, 8) + (() if unit in self.direct else (11, 12)):
                self.copy(unit, k).wait_recv()

    def drain(self, unit):
        if self.spread:
            for k in range(9 if unit in self.direct else self.SEMS):
                self.copy(unit, k).wait_send()


class Scatter:
    SEMS = 7

    def __init__(self, place, grads, out, keep, got_core, got_x, got_y, last_x, last_y, send, recv, local):
        self.p, self.grads, self.out = place, grads, out
        self.room, self.got_core = keep, got_core
        self.got_x, self.got_y, self.last_x, self.last_y = got_x, got_y, last_x, last_y
        self.send, self.recv, self.local = send, recv, local
        p = place
        self.chip_x = p.x // 2
        self.chip_y = p.y // 2
        self.chip_d = p.diag // 2

    def keep(self, unit):
        far, near = self.grads[unit]
        if far is None:
            return near.at[:, self.p.core]
        return self.room.at[unit]

    def piece(self, unit, chip, part):
        half = self.last_x.shape[1]
        return self.keep(unit).at[chip, pl.ds(part * half, half)]

    def copy(self, unit, k):
        p = self.p
        src, dst, to = (
            lambda: (self.source(unit).at[:, 1 - p.core], self.got_core.at[unit], p.sibling),
            lambda: (self.piece(unit, self.chip_x, 0), self.got_x.at[unit, 0], p.x),
            lambda: (self.piece(unit, self.chip_d, 0), self.got_x.at[unit, 1], p.x),
            lambda: (self.piece(unit, self.chip_y, 1), self.got_y.at[unit, 0], p.y),
            lambda: (self.piece(unit, self.chip_d, 1), self.got_y.at[unit, 1], p.y),
            lambda: (self.piece(unit, self.chip_y, 0), self.last_y.at[unit], p.y),
            lambda: (self.piece(unit, self.chip_x, 1), self.last_x.at[unit], p.x),
        )[k]()
        return remote(src, dst, self.send.at[unit, k], self.recv.at[unit, k], p.id(to))

    def source(self, unit):
        far, near = self.grads[unit]
        return near if far is None else far

    def load(self, unit):
        return pltpu.make_async_copy(self.grads[unit][0].at[:, self.p.core], self.room.at[unit], self.local.at[unit, 0])

    def store(self, unit):
        return pltpu.make_async_copy(self.keep(unit).at[self.p.chip], self.out.at[unit], self.local.at[unit, 1])

    def open(self, unit):
        self.copy(unit, 0).start()
        if self.grads[unit][0] is not None:
            self.load(unit).start()

    def add(self, ref, other):
        ref[...] = (ref[...].astype(F32) + other[...].astype(F32)).astype(BF)

    def first(self, unit):
        if self.grads[unit][0] is not None:
            self.load(unit).wait()
        self.copy(unit, 0).wait_recv()
        self.add(self.keep(unit), self.got_core.at[unit])
        for k in (1, 2, 3, 4):
            self.copy(unit, k).start()

    def second(self, unit):
        p = self.p
        self.copy(unit, 2).wait_recv()
        self.add(self.piece(unit, self.chip_y, 0), self.got_x.at[unit, 1])
        self.copy(unit, 5).start()
        self.copy(unit, 4).wait_recv()
        self.add(self.piece(unit, self.chip_x, 1), self.got_y.at[unit, 1])
        self.copy(unit, 6).start()
        self.copy(unit, 1).wait_recv()
        self.add(self.piece(unit, p.chip, 0), self.got_x.at[unit, 0])
        self.copy(unit, 3).wait_recv()
        self.add(self.piece(unit, p.chip, 1), self.got_y.at[unit, 0])

    def third(self, unit):
        p = self.p
        self.copy(unit, 5).wait_recv()
        self.add(self.piece(unit, p.chip, 0), self.last_y.at[unit])
        self.copy(unit, 6).wait_recv()
        self.add(self.piece(unit, p.chip, 1), self.last_x.at[unit])
        if self.out is not None:
            self.store(unit).start()

    def drain(self, unit):
        for k in range(self.SEMS):
            self.copy(unit, k).wait_send()
        if self.out is not None:
            self.store(unit).wait()


def scatter_scratch(units, loaded, shard, width):
    half = shard // 2
    return [
        pltpu.VMEM((max(loaded, 1), 4, shard, width) if loaded else (1, 1, 16, width), BF),
        pltpu.VMEM((units, 4, shard, width), BF),
        pltpu.VMEM((units, 2, half, width), BF),
        pltpu.VMEM((units, 2, half, width), BF),
        pltpu.VMEM((units, half, width), BF),
        pltpu.VMEM((units, half, width), BF),
        pltpu.SemaphoreType.DMA((units, Scatter.SEMS)),
        pltpu.SemaphoreType.DMA((units, Scatter.SEMS)),
        pltpu.SemaphoreType.DMA((units, 2)),
    ]


class Line:
    def __init__(self, place, shares, out, mine, got, other, send, recv, local):
        self.p, self.shares, self.out = place, shares, out
        self.room, self.got, self.other = mine, got, other
        self.send, self.recv, self.local = send, recv, local

    def copy(self, item, half, k):
        p = self.p
        size = self.got.shape[1] // 2
        part = lambda ref: ref.at[pl.ds(half * size, size)]
        mine, got, other = self.mine(item), self.got.at[item], self.other.at[item]
        src, dst, to_z = ((mine, got, p.pair_z), (mine, other, 3 - p.z), (got, got, p.pair_z))[k]
        at = 3 * half + k
        return remote(part(src), part(dst), self.send.at[item, at], self.recv.at[item, at], (p.batch, to_z))

    def mine(self, item):
        far, near = self.shares[item]
        return self.room.at[item] if near is None else near

    def part(self, ref, half):
        size = self.got.shape[1] // 2
        return ref.at[pl.ds(half * size, size)]

    def load(self, item):
        return pltpu.make_async_copy(self.shares[item][0], self.room.at[item], self.local.at[item, 0])

    def store(self, item):
        return pltpu.make_async_copy(self.got.at[item], self.out.at[item], self.local.at[item, 1])

    def start(self, item):
        if self.shares[item][0] is not None:
            self.load(item).wait()

        @pl.when(jnp.logical_not(self.p.inner))
        def _():
            for half in (0, 1):
                self.copy(item, half, 0).start()

    def middle(self, item):
        @pl.when(self.p.inner)
        def _():
            for half in (0, 1):
                mine = self.part(self.mine(item), half)
                got = self.part(self.got.at[item], half)
                self.copy(item, half, 0).wait_recv()
                mine[...] = (mine[...].astype(F32) + got[...].astype(F32)).astype(BF)
                self.copy(item, half, 1).start()

    def last(self, item):
        @pl.when(self.p.inner)
        def _():
            for half in (0, 1):
                mine = self.part(self.mine(item), half)
                got = self.part(self.got.at[item], half)
                other = self.part(self.other.at[item], half)
                self.copy(item, half, 1).wait_recv()
                got[...] = (mine[...].astype(F32) + other[...].astype(F32)).astype(BF)
                self.copy(item, half, 2).start()

    def end(self, item):
        @pl.when(jnp.logical_not(self.p.inner))
        def _():
            for half in (0, 1):
                self.copy(item, half, 2).wait_recv()

        self.store(item).start()

    def drain(self, item):
        @pl.when(self.p.inner)
        def _():
            for half in (0, 1):
                self.copy(item, half, 1).wait_send()
                self.copy(item, half, 2).wait_send()

        @pl.when(jnp.logical_not(self.p.inner))
        def _():
            for half in (0, 1):
                self.copy(item, half, 0).wait_send()

        self.store(item).wait()


def line_scratch(items, loaded, shard, width):
    return [
        pltpu.VMEM((loaded, shard, width) if loaded else (1, 16, width), BF),
        pltpu.VMEM((items, shard, width), BF),
        pltpu.VMEM((items, shard, width), BF),
        pltpu.SemaphoreType.DMA((items, 6)),
        pltpu.SemaphoreType.DMA((items, 6)),
        pltpu.SemaphoreType.DMA((items, 2)),
    ]


class Plan:
    def __init__(self, xy, xy_arrays, z, z_arrays, shard, width):
        self.xy, self.xy_arrays, self.z, self.z_arrays = xy, xy_arrays, z, z_arrays
        self.shard, self.width = shard, width
        self.keep_sums = bool(xy) and not any(src == "sum" for src, _ in z)

    def args(self):
        return [*self.xy_arrays, *self.z_arrays]

    def outs(self):
        out = []
        if self.keep_sums:
            out.append(struct((len(self.xy), self.shard, self.width)))
        if self.z:
            out.append(struct((len(self.z), self.shard, self.width)))
        return out

    def scratch(self):
        loaded = sum(src != "own" for src, _ in self.xy)
        shares = sum(src != "sum" for src, _ in self.z)
        return (scatter_scratch(len(self.xy), loaded, self.shard, self.width) if self.xy else []) + (
            line_scratch(len(self.z), shares, self.shard, self.width) if self.z else []
        )

    def signals(self, p):
        return [p.id(p.sibling), p.id(p.x), p.id(p.y)] if self.xy else []

    def open(self, p, inputs, outputs, scratch, own=None):
        outputs, scratch = list(outputs), list(scratch)
        arrays = inputs[: len(self.xy_arrays)]
        shares = inputs[len(self.xy_arrays) :]
        sums_out = outputs.pop(0) if self.keep_sums else None
        scatter = line = None
        if self.xy:
            grads = [
                (None, own.at[unit]) if src == "own" else (arrays[src].at[unit], None) for src, unit in self.xy
            ]
            scatter = Scatter(p, grads, sums_out, *scratch[:9])
            scratch = scratch[9:]
        if self.z:
            items = [
                (None, scatter.keep(i).at[p.chip]) if src == "sum" else (shares[src].at[i], None)
                for src, i in self.z
            ]
            line = Line(p, items, outputs.pop(0), *scratch)
        return scatter, line


def kernel_params(collective):
    params = dict(vmem_limit_bytes=63 * 2**20)
    if collective is not None:
        params.update(collective_id=collective, has_side_effects=True)
    return pltpu.CompilerParams(**params)


def rms(rows):
    return lax.rsqrt(jnp.mean(rows * rows, axis=-1, keepdims=True) + EPS)


def key_blocks(core):
    if core == 0:
        return [(0, [("o", 0, 0)]), (1, [("o", 0, 0), ("x", 0, 1), ("x", 1, 2), ("o", 1, 3)])]
    return [(0, [("x", 0, 0), ("o", 0, 1)]), (1, [("x", 0, 0), ("o", 0, 1), ("o", 1, 2)])]


def masked(scores, quarter, diagonal, pad):
    size = scores.shape[0]
    key = lax.broadcasted_iota(jnp.int32, scores.shape, 0)
    ok = key >= pad - quarter * size
    if diagonal:
        query = lax.broadcasted_iota(jnp.int32, scores.shape, 1)
        ok = ((key <= query) & ok) | (key == query)
    return jnp.where(ok, scores, NEG)


def attend_heads(core, base, pad, qkv, kvx, o_ref, lse_ref):
    width, rows = o_ref.shape
    size = rows // 2
    at = lambda off, hh: pl.ds(pl.multiple_of(off * width + (base + hh) * HEAD_DIM, 16), HEAD_DIM)
    for hh in range(GROUP):
        for block, keys in key_blocks(core):
            cols = slice(block * size, block * size + size)
            q = qkv[at(0, hh), cols]
            scores = []
            for i, (src, half, quarter) in enumerate(keys):
                span = slice(half * size, half * size + size)
                k = qkv[at(1, hh), span] if src == "o" else kvx[at(0, hh), span]
                scores.append(masked(dot(k, q, 0, 0), quarter, i == len(keys) - 1, pad))
            top = functools.reduce(jnp.maximum, [jnp.max(s, axis=0, keepdims=True) for s in scores])
            total = 0.0
            out = 0.0
            for s, (src, half, quarter) in zip(scores, keys):
                span = slice(half * size, half * size + size)
                v = qkv[at(2, hh), span] if src == "o" else kvx[at(1, hh), span]
                weight = jnp.exp2((s - top) * LOG2_SCALE)
                total = total + jnp.sum(weight, axis=0, keepdims=True)
                out = out + dot(v, weight.astype(BF), 1, 0)
            o_ref[at(0, hh), cols] = (out * (1.0 / total)).astype(BF)
            lse_ref[base // GROUP, hh : hh + 1, cols] = top * LOG2_SCALE + jnp.log2(total)


class Copies:
    def __init__(self, sems):
        self.sems, self.used, self.open = sems, 0, {}

    def start(self, src, dst):
        copy = pltpu.make_async_copy(src, dst, self.sems.at[self.used])
        self.used += 1
        copy.start()
        return copy

    def save(self, name, src, dst):
        self.open.setdefault(name, []).append(self.start(src, dst))

    def ready(self, *names):
        for name in names:
            for copy in self.open.pop(name, []):
                copy.wait()

    def finish(self):
        self.ready(*list(self.open))


def forward_kernel(spread, *refs):
    refs = list(refs)
    take = lambda n: [refs.pop(0) for _ in range(n)]
    pad_ref, cos, sin, rows_in, cot_in, wqkv, wout, wup, wdown = take(9)
    (w_out, cot_out, hid0_out, hid1_out, h_out, xt_out, qkv_out, kvx_out, att_out, lse_out, mid_out, mt_out, pre_out,
     act_out) = take(14)
    (full, g_send, g_recv, g_local, qkv, kvx, h, att, lse, mid, xhat, tp, tq, act, rows_buf, x_send, x_recv, s_send, s_recv,
     free, copy_sems) = refs
    p = Place()
    width = xhat.shape[1]
    rows = xhat.shape[0]
    quarter = rows // 2
    groups = width // (HEAD_DIM * GROUP)
    copies = Copies(copy_sems)
    swap_in = Swap(p, True, rows_in, rows_buf, s_send.at[0], s_recv.at[0])
    swap_cot = Swap(p, True, cot_in, cot_out, s_send.at[1], s_recv.at[1])
    swap_hid = Swap(p, False, rows_buf, hid0_out, s_send.at[2], s_recv.at[2])
    others = [p.id(p.x), p.id(p.y), p.id(p.sibling), (p.batch, p.pair_z)] if spread else [p.id(p.sibling)]
    greet(p, others + swap_in.came_from + swap_hid.came_from)
    shards = []
    for layer in range(LAYERS):
        shards += [wqkv.at[layer, :, pl.ds(u * width, width)] for u in (1, 2, 0)]
        shards += [w.at[layer] for w in (wout, wup, wdown)]
    units = len(shards)
    room = full.shape[0]
    slots = [unit % room for unit in range(units)]
    gather = Gather(p, spread, shards, full, slots, DIRECT, g_send, g_recv, g_local)

    moving = []

    def release():
        for unit in range(units - room):
            gather.drain(unit)
            copies.ready(("w", unit))
        if spread:
            for k, device in enumerate(others):
                pl.semaphore_signal(free.at[k], inc=1, device_id=device, device_id_type=MESH)

    def tick(unit):
        gather.relay(unit)
        if unit + AHEAD < units:
            if unit + AHEAD == room and spread:
                for k in range(len(others)):
                    pl.semaphore_wait(free.at[k], 1)
            gather.open(unit + AHEAD)
        if unit:
            gather.share(unit - 1)
        if unit >= LAG:
            gather.pass_on(unit - LAG)
        for swap in moving:
            swap.start(RATE)

    def need(unit):
        gather.need(unit)
        copies.save(("w", unit), full.at[slots[unit]], w_out.at[unit])

    swap_in.start()
    for unit in range(AHEAD):
        gather.open(unit)
    tick(0)
    swap_in.arrive()
    for k in (0, 1):
        h[k * quarter : (k + 1) * quarter, :] = rows_buf[k].astype(F32)
    pad = pad_ref[0]

    for layer in range(LAYERS):
        base = 6 * layer
        copies.save("h", h, h_out.at[layer])
        copies.ready("tp", "tq")
        xhat[...] = (h[...] * rms(h[...])).astype(BF)
        tp[...] = xhat[...].T
        copies.save("tp", tp, xt_out.at[layer])
        copies.ready("qkv")
        if layer == 0:
            tick(1)
            tick(2)

        def exchange(k):
            return remote(
                qkv.at[pl.ds((1 + k) * width, width)], kvx.at[layer, pl.ds(k * width, width)],
                x_send.at[layer, k], x_recv.at[layer, k], p.id(p.sibling),
            )

        for i, part in enumerate((1, 2, 0)):
            need(base + i)
            step = 8 * HEAD_DIM
            for at in range(0, width, step):
                y = dot(xhat[...], full[slots[base + i], :, at : at + step], 1, 0).T
                for head in range(0, step, HEAD_DIM):
                    to = part * width + at + head
                    if part == 2:
                        qkv[to : to + HEAD_DIM, :] = y[head : head + HEAD_DIM].astype(BF)
                    else:
                        a, b = y[head : head + HALF], y[head + HALF : head + HEAD_DIM]
                        qkv[to : to + HEAD_DIM, :] = jnp.concatenate(
                            [a * cos[...] - b * sin[...], b * cos[...] + a * sin[...]], axis=0
                        ).astype(BF)
            if i < 2:
                exchange(i).start()
                tick(base + 3 + i)
        copies.save("qkv", qkv, qkv_out.at[layer])
        if layer == 0:
            moving.append(swap_cot)
        for k in (0, 1):
            exchange(k).wait_recv()
        copies.save("kvx", kvx.at[layer], kvx_out.at[layer])
        copies.ready("att", "lse")

        def body(group, carry):
            for core in (0, 1):
                pl.when(p.core == core)(
                    functools.partial(attend_heads, core, group * GROUP, pad, qkv, kvx.at[layer], att, lse)
                )

            @pl.when(group == 1)
            def _():
                tick(base + 5)

            return carry

        lax.fori_loop(0, groups, body, 0)
        if layer == 0:
            release()
        if layer == 0:
            tick(base + 6)
        copies.save("att", att, att_out.at[layer])
        copies.save("lse", lse, lse_out.at[layer])
        for k in (0, 1):
            exchange(k).wait_send()
        copies.ready("mid")
        need(base + 3)
        square = 0.0
        for cols in tiles(width):
            m = h[:, cols] + dot(att[...], full[slots[base + 3], :, cols], 0, 0)
            mid[:, cols] = m
            square = square + jnp.sum(m * m, axis=1, keepdims=True)
        copies.save("mid", mid, mid_out.at[layer])
        scale = lax.rsqrt(square / width + EPS)
        for cols in tiles(width):
            m = (mid[:, cols] * scale).astype(BF)
            xhat[:, cols] = m
            tq[cols, :] = m.T
        copies.save("tq", tq, mt_out.at[layer])
        need(base + 4)
        copies.ready("h", "tp")
        for cols in tiles(width):
            v = dot(xhat[...], full[slots[base + 4], :, cols], 1, 0)
            h[:, cols] = v
            a = (v / (1.0 + jnp.exp(-v))).astype(BF)
            act[:, cols] = a
            tp[cols, :] = a.T
        copies.save("pre", h, pre_out.at[layer])
        copies.save("tp", tp, act_out.at[layer])
        last = layer == LAYERS - 1
        if not last:
            tick(base + 7)
        need(base + 5)
        copies.ready("pre")
        if last:
            swap_hid.start()
            swap_hid.drain()
        for cols in tiles(width):
            v = mid[:, cols] + dot(act[...], full[slots[base + 5], :, cols], 1, 0)
            if not last:
                h[:, cols] = v
            for k in (0, 1):
                rows_buf[k, :, cols] = v[k * quarter : (k + 1) * quarter].astype(BF)
        if last:
            copies.save("hid", rows_buf, hid1_out)
        else:
            moving.append(swap_hid)
            tick(base + 8)
    for unit in range(units - room, units):
        gather.drain(unit)
    for swap in moving:
        swap.start()
    swap_in.drain()
    swap_cot.arrive()
    swap_cot.drain()
    swap_hid.arrive()
    copies.finish()


def forward(spread, collective, pad, cos, sin, inputs, cotangent, wqkv, wout, wup, wdown, shard):
    _, quarter, width = inputs.shape
    rows = 2 * quarter
    groups = width // (HEAD_DIM * GROUP)
    nat, tr = (rows, width), (width, rows)
    lse = (groups, GROUP, rows)
    two = lambda shape, dtype=BF: struct((LAYERS,) + shape, dtype)
    units = 6 * LAYERS
    room = units - 3
    swapped = struct((2, quarter, width))
    outs = [
        struct((units, width, width)), swapped, swapped, swapped, two(nat, F32), two(tr), two((3 * width, rows)),
        two((2 * width, rows)), two(tr), two(lse, F32), two(nat, F32), two(tr), two(nat, F32), two(tr),
    ]
    scratch = [
        pltpu.VMEM((room, width, width), BF),
        pltpu.SemaphoreType.DMA((units, Gather.SEMS)),
        pltpu.SemaphoreType.DMA((units, Gather.SEMS)),
        pltpu.SemaphoreType.DMA((units,)),
        pltpu.VMEM((3 * width, rows), BF),
        pltpu.VMEM((LAYERS, 2 * width, rows), BF),
        pltpu.VMEM(nat, F32),
        pltpu.VMEM(tr, BF),
        pltpu.VMEM(lse, F32),
        pltpu.VMEM(nat, F32),
        pltpu.VMEM(nat, BF),
        pltpu.VMEM(tr, BF),
        pltpu.VMEM(tr, BF),
        pltpu.VMEM(nat, BF),
        pltpu.VMEM((2, quarter, width), BF),
        pltpu.SemaphoreType.DMA((LAYERS, 2)),
        pltpu.SemaphoreType.DMA((LAYERS, 2)),
        pltpu.SemaphoreType.DMA((3, 2, Swap.PIECES)),
        pltpu.SemaphoreType.DMA((3, 2, Swap.PIECES)),
        pltpu.SemaphoreType.REGULAR((4,)),
        pltpu.SemaphoreType.DMA((units + 10 * LAYERS + 2,)),
    ]
    return pl.pallas_call(
        functools.partial(forward_kernel, spread),
        in_specs=[SM, VM, VM] + [ANY] * 6,
        out_specs=[ANY] * len(outs),
        out_shape=outs,
        scratch_shapes=scratch,
        compiler_params=kernel_params(collective),
        cost_estimate=pl.CostEstimate(flops=180 * 10**9, bytes_accessed=100 * 10**6, transcendentals=0),
        name="forward",
    )(pad, cos, sin, inputs, cotangent, wqkv, wout, wup, wdown)


def feed_back_kernel(plan, layer, *refs):
    refs = list(refs)
    take = lambda n: [refs.pop(0) for _ in range(n)]
    g_in, w_in, *held = take(7)
    act_t_in, mt_in, pre_in, mid_in, att_in = [ref.at[layer] for ref in held]
    inputs = take(len(plan.args())) if plan else []
    dw_out, mg_out, do_out = take(3)
    outputs = take(len(plan.outs())) if plan else []
    g, w, act_t, mt, pre, mid, att, gb, dpre, eg, do, dw, copy_sems = take(13)
    copies = Copies(copy_sems)
    width = w.shape[1]
    shard = dw.shape[3]
    if plan:
        p = Place()
        greet(p, plan.signals(p), bool(plan.z))
        scatter, line = plan.open(p, inputs, outputs, refs, dw)
        if line:
            line.load(0).start()
        if plan.xy[0][0] != "own":
            scatter.open(0)
    load_g = copies.start(g_in, gb if g_in.dtype == BF else g)
    load_act = copies.start(act_t_in, act_t)
    load_w = [copies.start(w_in.at[6 * layer + 5], w.at[2])]
    load_pre = copies.start(pre_in, pre)
    load_mt = copies.start(mt_in, mt)
    load_w += [copies.start(w_in.at[6 * layer + 4], w.at[1])]
    load_mid = copies.start(mid_in, mid)
    load_att = copies.start(att_in, att)
    load_w += [copies.start(w_in.at[6 * layer + 3], w.at[0])]

    def put(unit, cols, value):
        for k in range(dw.shape[1]):
            for c in range(2):
                at = (2 * k + c) * shard
                dw[unit, k, c, :, cols] = value[at : at + shard].astype(BF)

    load_g.wait()
    if g_in.dtype == BF:
        g[...] = gb[...].astype(F32)
    else:
        gb[...] = g[...].astype(BF)
    load_act.wait()
    for cols in tiles(width):
        put(2, cols, dot(act_t[...], gb[:, cols], 1, 0))
    if plan and plan.xy[0][0] == "own":
        scatter.open(0)
    else:
        copies.save("dw", dw.at[2], dw_out.at[2])
    if plan:
        if line:
            line.start(0)
    load_w[0].wait()
    load_pre.wait()
    for cols in tiles(width):
        da = dot(gb[...], w[2, cols, :], 1, 1)
        v = pre[:, cols]
        s = 1.0 / (1.0 + jnp.exp(-v))
        dpre[:, cols] = (da * (s + v * s * (1.0 - s))).astype(BF)
    if plan:
        scatter.first(0)
    load_mt.wait()
    for cols in tiles(width):
        put(1, cols, dot(mt[...], dpre[:, cols], 1, 0))
    copies.save("dw", dw.at[1], dw_out.at[1])
    load_w[1].wait()
    load_mid.wait()
    r = rms(mid[...])
    total = 0.0
    for cols in tiles(width):
        e = dot(dpre[...], w[1, cols, :], 1, 1)
        eg[:, cols] = e
        total = total + jnp.sum(e * (mid[:, cols] * r), axis=1, keepdims=True)
    total = total / width
    if plan and line:
        line.middle(0)
    for cols in tiles(width):
        m = g[:, cols] + r * (eg[:, cols] - mid[:, cols] * r * total)
        g[:, cols] = m
        gb[:, cols] = m.astype(BF)
    copies.save("g", g, mg_out)
    load_att.wait()
    for cols in tiles(width):
        put(0, cols, dot(att[...], gb[:, cols], 1, 0))
    copies.save("dw", dw.at[0], dw_out.at[0])
    load_w[2].wait()
    if plan:
        scatter.second(0)
        if line:
            line.last(0)
    for cols in tiles(width):
        do[cols, :] = dot(w[0, cols, :], gb[...], 1, 1).astype(BF)
    copies.save("do", do, do_out)
    if plan:
        scatter.third(0)
        if line:
            line.end(0)
            line.drain(0)
        scatter.drain(0)
    copies.finish()


def feed_back(name, collective, layer, g, w, act_t, mt, pre, mid, att, chips, shard, plan):
    _, width, rows = act_t.shape
    nat, tr = (rows, width), (width, rows)
    grad = (3, chips, 2, shard, width)
    args = [g, w, act_t, mt, pre, mid, att] + (plan.args() if plan else [])
    outs = [struct(grad), struct(nat, F32), struct(tr)] + (plan.outs() if plan else [])
    return pl.pallas_call(
        functools.partial(feed_back_kernel, plan, layer),
        in_specs=[ANY] * len(args),
        out_specs=[ANY] * len(outs),
        out_shape=outs,
        scratch_shapes=[
            pltpu.VMEM(nat, F32),
            pltpu.VMEM((3, width, width), BF),
            pltpu.VMEM(tr, BF),
            pltpu.VMEM(tr, BF),
            pltpu.VMEM(nat, F32),
            pltpu.VMEM(nat, F32),
            pltpu.VMEM(tr, BF),
            pltpu.VMEM(nat, BF),
            pltpu.VMEM(nat, BF),
            pltpu.VMEM(nat, F32),
            pltpu.VMEM(tr, BF),
            pltpu.VMEM(grad, BF),
            pltpu.SemaphoreType.DMA((16,)),
        ] + (plan.scratch() if plan else []),
        compiler_params=kernel_params(collective if plan else None),
        cost_estimate=pl.CostEstimate(flops=16 * 10**9, bytes_accessed=30 * 10**6, transcendentals=0),
        name=name,
    )(*args)


def unrotate(t, cos, sin):
    a, b = t[:HALF], t[HALF:]
    return jnp.concatenate([a * cos + b * sin, b * cos - a * sin], axis=0)


def attend_back_heads(core, base, pad, qkv, kvx, do, o, lse, tables, dqkv, dkvx):
    width, rows = o.shape
    size = rows // 2
    scale = 1.0 / math.sqrt(HEAD_DIM)
    cos, sin, cosx, sinx = tables
    at = lambda off, hh: pl.ds(pl.multiple_of(off * width + (base + hh) * HEAD_DIM, 16), HEAD_DIM)
    for hh in range(GROUP):
        dk, dv = {}, {}
        for block, keys in key_blocks(core):
            cols = slice(block * size, block * size + size)
            q = qkv[at(0, hh), cols]
            d_out = do[at(0, hh), cols]
            delta = jnp.sum(d_out.astype(F32) * o[at(0, hh), cols].astype(F32), axis=0, keepdims=True)
            norm = lse[base // GROUP, hh : hh + 1, cols]
            dq = 0.0
            for i, (src, half, quarter) in enumerate(keys):
                span = slice(half * size, half * size + size)
                k = qkv[at(1, hh), span] if src == "o" else kvx[at(0, hh), span]
                v = qkv[at(2, hh), span] if src == "o" else kvx[at(1, hh), span]
                s = masked(dot(k, q, 0, 0), quarter, i == len(keys) - 1, pad)
                weight = jnp.exp2(s * LOG2_SCALE - norm)
                ds = (weight * (dot(v, d_out, 0, 0) - delta)).astype(BF)
                dq = dq + dot(k, ds, 1, 0)
                a, b = dot(q, ds, 1, 1), dot(d_out, weight.astype(BF), 1, 1)
                key = (src, half)
                dk[key] = dk[key] + a if key in dk else a
                dv[key] = dv[key] + b if key in dv else b
            dqkv[at(0, hh), cols] = unrotate(dq * scale, cos[:, cols], sin[:, cols]).astype(BF)
        for src, ref, k_off, ct, st in (("o", dqkv, 1, cos, sin), ("x", dkvx, 0, cosx, sinx)):
            for half in (0, 1):
                span = slice(half * size, half * size + size)
                if (src, half) in dk:
                    a = unrotate(dk[src, half] * scale, ct[:, span], st[:, span]).astype(BF)
                    b = dv[src, half].astype(BF)
                else:
                    a = b = jnp.zeros((HEAD_DIM, size), BF)
                ref[at(k_off, hh), span] = a
                ref[at(k_off + 1, hh), span] = b


def attend_back_kernel(plan, layer, swapping, *refs):
    refs = list(refs)
    take = lambda n: [refs.pop(0) for _ in range(n)]
    pad_ref, qkv_in, kvx_in, do_in, att_in, lse, cos, sin, cosx, sinx = take(10)
    qkv_in, kvx_in, att_in = qkv_in.at[layer], kvx_in.at[layer], att_in.at[layer]
    hid_in = take(1)[0] if swapping else None
    inputs = take(len(plan.args())) if plan else []
    pg_out = take(1)[0]
    swap_out = take(1)[0] if swapping else None
    outputs = take(len(plan.outs())) if plan else []
    qkv, kvx, do, att, dqkv, dkvx, got, x_send, x_recv, copy_sems = take(10)
    p = Place()
    copies = Copies(copy_sems)
    signals = [p.id(p.sibling)]
    if plan:
        signals = plan.signals(p)
    if swapping:
        swap = Swap(p, False, hid_in, swap_out, *take(2))
        signals = signals + swap.came_from
    greet(p, signals, bool(plan and plan.z))
    loads = [copies.start(a, b) for a, b in ((qkv_in, qkv), (kvx_in, kvx), (do_in, do), (att_in, att))]
    units = items = 0
    if plan:
        scatter, line = plan.open(p, inputs, outputs, refs)
        units, items = len(plan.xy), len(plan.z)
        for i in range(units):
            scatter.open(i)
        for i in range(items):
            line.load(i).start()
        for i in range(items):
            line.start(i)
    if swapping:
        swap.start()
    for load in loads:
        load.wait()
    for i in range(units):
        scatter.first(i)
    pad = pad_ref[0]
    width = att.shape[0]
    span = GROUP * HEAD_DIM
    groups = width // span

    def exchange(group, k):
        part = pl.ds(pl.multiple_of(k * width + group * span, 16), span)
        return remote(dkvx.at[part], got.at[part], x_send.at[group, k], x_recv.at[group, k], p.id(p.sibling))

    def body(group, carry):
        for core in (0, 1):
            pl.when(p.core == core)(
                functools.partial(
                    attend_back_heads, core, group * GROUP, pad, qkv, kvx, do, att, lse,
                    (cos, sin, cosx, sinx), dqkv, dkvx,
                )
            )
        for k in (0, 1):
            exchange(group, k).start()
        if plan:

            @pl.when(group == 1)
            def _():
                for i in range(items):
                    line.middle(i)
                scatter.second(0)

            @pl.when(group == 2)
            def _():
                for i in range(1, units):
                    scatter.second(i)
                for i in range(items):
                    line.last(i)

        return carry

    lax.fori_loop(0, groups, body, 0)
    for i in range(units):
        scatter.third(i)
    for group in range(groups):
        for k in (0, 1):
            exchange(group, k).wait_recv()
    own = dqkv.at[pl.ds(width, 2 * width)]
    own[...] = (own[...].astype(F32) + got[...].astype(F32)).astype(BF)
    copies.save("dqkv", dqkv, pg_out)
    for i in range(items):
        line.end(i)
    for i in range(items):
        line.drain(i)
    for i in range(units):
        scatter.drain(i)
    for group in range(groups):
        for k in (0, 1):
            exchange(group, k).wait_send()
    if swapping:
        swap.arrive()
        swap.drain()
    copies.finish()


def attend_back(name, collective, layer, pad, qkv, kvx, do, att, lse, tables, hid, plan):
    _, width, rows = att.shape
    swapping = hid is not None
    args = [pad, qkv, kvx, do, att, lse, *tables] + ([hid] if swapping else []) + (plan.args() if plan else [])
    specs = [SM] + [ANY] * 4 + [VM] * 5 + [ANY] * (len(args) - 10)
    outs = [struct((3 * width, rows))]
    if swapping:
        outs.append(struct(hid.shape))
    outs += plan.outs() if plan else []
    scratch = [
        pltpu.VMEM((3 * width, rows), BF),
        pltpu.VMEM((2 * width, rows), BF),
        pltpu.VMEM((width, rows), BF),
        pltpu.VMEM((width, rows), BF),
        pltpu.VMEM((3 * width, rows), BF),
        pltpu.VMEM((2 * width, rows), BF),
        pltpu.VMEM((2 * width, rows), BF),
        pltpu.SemaphoreType.DMA((lse.shape[0], 2)),
        pltpu.SemaphoreType.DMA((lse.shape[0], 2)),
        pltpu.SemaphoreType.DMA((16,)),
    ]
    if swapping:
        scratch += swap_scratch()
    return pl.pallas_call(
        functools.partial(attend_back_kernel, plan, layer, swapping),
        in_specs=specs,
        out_specs=[ANY] * len(outs),
        out_shape=outs,
        scratch_shapes=scratch + (plan.scratch() if plan else []),
        compiler_params=kernel_params(collective),
        cost_estimate=pl.CostEstimate(flops=35 * 10**9, bytes_accessed=30 * 10**6, transcendentals=0),
        name=name,
    )(*args)


def project_back_kernel(plan, layer, swapping, *refs):
    refs = list(refs)
    take = lambda n: [refs.pop(0) for _ in range(n)]
    pg_in, xt_in, w_in, h_in, mg_in = take(5)
    xt_in, h_in = xt_in.at[layer], h_in.at[layer]
    inputs = take(len(plan.args())) if plan else []
    dw_out = None if swapping and plan else take(1)[0]
    g_out = take(1)[0]
    outputs = take(len(plan.outs())) if plan else []
    pg, xt, w, h, g, eg, dw, copy_sems = take(8)
    gb = take(1)[0] if swapping else None
    swap_sems = take(2) if swapping else None
    copies = Copies(copy_sems)
    width = xt.shape[0]
    quarter = xt.shape[1] // 2
    shard = dw.shape[3]
    p = Place()
    signals = plan.signals(p) if plan else []
    if swapping:
        swap = Swap(p, False, gb, g_out, *swap_sems)
        signals = signals + swap.came_from
    if signals:
        greet(p, signals, bool(plan and plan.z))
    load_pg = copies.start(pg_in, pg)
    load_xt = copies.start(xt_in, xt)
    held = earlier = shares = 0
    scatter = line = None
    if plan:
        scatter, line = plan.open(p, inputs, outputs, refs, dw)
        held = len(plan.xy)
        earlier = sum(src != "own" for src, _ in plan.xy)
        shares = sum(src != "sum" for src, _ in plan.z)
    for i in range(earlier):
        scatter.open(i)
    for i in range(shares):
        line.load(i).start()
    load_w = [copies.start(w_in.at[6 * layer + (2, 0, 1)[unit]], w.at[unit]) for unit in range(3)]
    load_h = copies.start(h_in, h)
    load_g = copies.start(mg_in, g)
    load_pg.wait()
    load_xt.wait()
    for i in range(shares):
        line.start(i)
    for i in range(min(earlier, 1)):
        scatter.first(i)

    def weight_grad(unit):
        for cols in tiles(width):
            value = dot(xt[...], pg[unit * width + cols.start : unit * width + cols.stop, :], 1, 1)
            for k in range(dw.shape[1]):
                for c in range(2):
                    at = (2 * k + c) * shard
                    dw[unit, k, c, :, cols] = value[at : at + shard].astype(BF)
        if dw_out is not None and not (plan and ("own", unit) in plan.xy):
            copies.save("dw", dw.at[unit], dw_out.at[unit])

    own = earlier
    weight_grad(1)
    for i in range(1, earlier):
        scatter.first(i)
    if own < held:
        scatter.open(own)
    weight_grad(2)
    if own < held:
        scatter.first(own)
    for i in range(shares):
        line.middle(i)
    if own + 1 < held:
        scatter.open(own + 1)
    weight_grad(0)
    if own + 2 < held:
        scatter.open(own + 2)
    for i in range(min(earlier, 1)):
        scatter.second(i)
    for load in load_w:
        load.wait()
    load_h.wait()
    r = rms(h[...])
    total = 0.0
    for n, cols in enumerate(tiles(width)):
        e = 0.0
        for unit in range(3):
            e = e + dot(pg[unit * width : (unit + 1) * width, :], w[unit, cols, :], 0, 1)
        eg[:, cols] = e
        total = total + jnp.sum(e * (h[:, cols] * r), axis=1, keepdims=True)
        if n == 1:
            for i in range(1, earlier):
                scatter.second(i)
        if n == 2 and own + 1 < held:
            scatter.first(own + 1)
        if n == 3:
            for i in range(shares):
                line.last(i)
    total = total / width
    load_g.wait()
    for cols in tiles(width):
        v = g[:, cols] + r * (eg[:, cols] - h[:, cols] * r * total)
        if swapping:
            for k in (0, 1):
                gb[k, :, cols] = v[k * quarter : (k + 1) * quarter].astype(BF)
        else:
            g[:, cols] = v
    if swapping:
        swap.start()
    else:
        copies.save("g", g, g_out)
    chain = bool(plan) and len(plan.z) > shares
    for i in range(own + 2, held):
        scatter.first(i)
    for i in range(earlier):
        scatter.third(i)
    steps = [[] for _ in range(held + 6)]
    for i in range(held):
        if i >= earlier:
            steps[i].append(functools.partial(scatter.second, i))
            steps[i + 1].append(functools.partial(scatter.third, i))
        if chain:
            j = shares + i
            base = i + 1
            steps[base].append(functools.partial(line.start, j))
            steps[base + 1].append(functools.partial(line.middle, j))
            steps[base + 2].append(functools.partial(line.last, j))
            steps[base + 3].append(functools.partial(line.end, j))
    for group in steps:
        for step in group:
            step()
    for i in range(shares):
        line.end(i)
    for i in range(len(plan.z) if plan else 0):
        line.drain(i)
    for i in range(held):
        scatter.drain(i)
    if swapping:
        swap.arrive()
        swap.drain()
    copies.finish()


def project_back(name, collective, layer, pg, xt, w, h, mg, chips, shard, swapping, plan):
    _, rows, width = h.shape
    nat, tr = (rows, width), (width, rows)
    grad = (3, chips, 2, shard, width)
    args = [pg, xt, w, h, mg] + (plan.args() if plan else [])
    outs = [] if swapping and plan else [struct(grad)]
    outs.append(struct((2, rows // 2, width)) if swapping else struct(nat, F32))
    outs += plan.outs() if plan else []
    scratch = [
        pltpu.VMEM((3 * width, rows), BF),
        pltpu.VMEM(tr, BF),
        pltpu.VMEM((3, width, width), BF),
        pltpu.VMEM(nat, F32),
        pltpu.VMEM(nat, F32),
        pltpu.VMEM(nat, F32),
        pltpu.VMEM(grad, BF),
        pltpu.SemaphoreType.DMA((16,)),
    ]
    if swapping:
        scratch += [pltpu.VMEM((2, rows // 2, width), BF)] + swap_scratch()
    return pl.pallas_call(
        functools.partial(project_back_kernel, plan, layer, swapping),
        in_specs=[ANY] * len(args),
        out_specs=[ANY] * len(outs),
        out_shape=outs,
        scratch_shapes=scratch + (plan.scratch() if plan else []),
        compiler_params=kernel_params(collective if plan or swapping else None),
        cost_estimate=pl.CostEstimate(flops=16 * 10**9, bytes_accessed=30 * 10**6, transcendentals=0),
        name=name,
    )(*args)


def local(nb, ns, inputs, lengths, wqkv, wout, wup, wdown, gain_attn, gain_mlp, cotangent):
    series, quarter, width = inputs.shape
    heads = width // HEAD_DIM
    rows = 2 * quarter
    shard = wout.shape[1]
    chips = nb // 2
    spread = nb == 8
    z = lax.axis_index("seq")
    core = lax.axis_index("batch") % 2

    other = lax.ppermute(
        lengths, AXES, [(b * ns + s, (b ^ 1) * ns + s) for b in range(nb) for s in range(ns)]
    )
    both = jnp.where(core == 0, jnp.concatenate([lengths, other]), jnp.concatenate([other, lengths]))
    which = jnp.where((z == 0) | (z == 3), 2, 0) + z // 2
    pad = SLOTS - lax.dynamic_index_in_dim(both, which, 0, keepdims=True)
    angle = (
        jnp.exp(jnp.arange(HALF, dtype=F32) * (-2.0 * math.log(10000.0) / HEAD_DIM))[:, None]
        * jnp.arange(SLOTS, dtype=F32)[None, :]
    )
    cos_all, sin_all = jnp.cos(angle), jnp.sin(angle)
    cos_pad = lax.dynamic_slice_in_dim(cos_all, pad[0], 1, axis=1)
    sin_pad = lax.dynamic_slice_in_dim(sin_all, pad[0], 1, axis=1)
    cos_four = (cos_all * cos_pad + sin_all * sin_pad).reshape(HALF, 4, quarter)
    sin_four = (sin_all * cos_pad - cos_all * sin_pad).reshape(HALF, 4, quarter)

    def pick(table):
        even = jnp.concatenate([table[:, 0], table[:, 3]], axis=1)
        odd = jnp.concatenate([table[:, 1], table[:, 2]], axis=1)
        return jnp.where(core == 0, even, odd), jnp.where(core == 0, odd, even)

    cos, cosx = pick(cos_four)
    sin, sinx = pick(sin_four)

    wqkv_g = (wqkv.astype(F32) * gain_attn.astype(F32)[:, :, None]).astype(BF)
    wup_g = (wup.astype(F32) * gain_mlp.astype(F32)[:, :, None]).astype(BF)

    stacked = (
        lambda array: array
        if spread
        else lax.all_gather(array, "batch", axis=1, tiled=True)
    )
    w_all, cot, hidden_0, hid_1, h_all, xt_all, qkv_all, kvx_all, att_all, lse_all, mid_all, mt_all, pre_all, act_all = forward(
        spread, 0, pad, cos, sin, inputs, cotangent, stacked(wqkv_g), stacked(wout), stacked(wup_g), stacked(wdown), shard
    )
    g = cot.reshape(rows, width)

    def plan(xy, xy_arrays, z, z_arrays):
        return Plan(xy, xy_arrays, z, z_arrays, shard, width) if spread else None

    tables = (cos, sin, cosx, sinx)
    ff_1, mg, do, *p_d1 = feed_back(
        "feed_back_1", 4, 1, g, w_all, act_all, mt_all, pre_all, mid_all, att_all, chips, shard, plan([("own", 2)], [], [], [])
    )
    pg, hidden_1, *sums = attend_back(
        "attend_back_1", 5, 1, pad, qkv_all, kvx_all, do, att_all, lse_all[1], tables, hid_1,
        plan([(0, 1), (0, 0)], [ff_1], [(0, 0)], p_d1),
    )
    p_uo1, r_d1 = sums if spread else (None, None)
    qkv_1, g, *sums = project_back(
        "project_back_1", 6, 1, pg, xt_all, w_all, h_all, mg, chips, shard, False,
        plan([("own", 1)], [], [(0, 0)], [p_uo1]),
    )
    p_k1, r_u1 = sums if spread else (None, None)
    ff_0, mg, do, *sums = feed_back(
        "feed_back_0", 7, 0, g, w_all, act_all, mt_all, pre_all, mid_all, att_all, chips, shard,
        plan([(0, 0)], [qkv_1], [(0, 1)], [p_uo1]),
    )
    p_q1, r_o1 = sums if spread else (None, None)
    pg, *sums = attend_back(
        "attend_back_0", 8, 0, pad, qkv_all, kvx_all, do, att_all, lse_all[0], tables, None,
        plan([(0, 2), (1, 2)], [qkv_1, ff_0], [(0, 0), (1, 0)], [p_k1, p_q1]),
    )
    p_vd, r_kq1 = sums if spread else (None, None)
    tail = project_back(
        "project_back_0", 9, 0, pg, xt_all, w_all, h_all, mg, chips, shard, True,
        plan(
            [(0, 1), (0, 0), ("own", 1), ("own", 2), ("own", 0)], [ff_0],
            [(0, 0), (0, 1)] + [("sum", i) for i in range(5)], [p_vd],
        ),
    )
    if spread:
        input_grad, r = tail
        s_qkv = [[r[6], r[4], r[5]], [r_kq1[1], r_kq1[0], r[0]]]
        s_ff = [[r[3], r[2], r[1]], [r_o1[0], r_u1[0], r_d1[0]]]
    else:
        qkv_0, input_grad = tail

        def over_all(grads):
            flat = grads.reshape(3, nb * shard, width)
            return lax.psum(lax.psum_scatter(flat, "batch", scatter_dimension=1, tiled=True), "seq")

        s_qkv = [over_all(qkv_0), over_all(qkv_1)]
        s_ff = [over_all(ff_0), over_all(ff_1)]
    input_grad = input_grad.astype(F32)
    hidden = [hidden_0, hidden_1]

    grad_qkv, grad_out, grad_up, grad_down, grad_ga, grad_gm = [], [], [], [], [], []
    for layer in range(LAYERS):
        ff = [part.astype(F32) for part in s_ff[layer]]
        qkv_sum = jnp.concatenate([part.astype(F32) for part in s_qkv[layer]], axis=1)
        grad_qkv.append(qkv_sum * gain_attn[layer].astype(F32)[:, None])
        grad_ga.append(jnp.sum(qkv_sum * wqkv[layer].astype(F32), axis=1))
        grad_out.append(ff[0])
        grad_up.append(ff[1] * gain_mlp[layer].astype(F32)[:, None])
        grad_gm.append(jnp.sum(ff[1] * wup[layer].astype(F32), axis=1))
        grad_down.append(ff[2])
    stack = jnp.stack
    return (
        stack(hidden), input_grad, stack(grad_qkv), stack(grad_out), stack(grad_up), stack(grad_down),
        stack(grad_ga), stack(grad_gm),
    )


def solution(mesh):
    nb, ns = mesh.shape["batch"], mesh.shape["seq"]
    rows = P("batch", "seq", None)
    weight = P(None, "batch", None)
    gain = P(None, "batch")
    return jax.shard_map(
        functools.partial(local, nb, ns),
        mesh=mesh,
        in_specs=(rows, P("batch"), weight, weight, weight, weight, gain, gain, rows),
        out_specs=(P(None, "batch", "seq", None), rows, weight, weight, weight, weight, gain, gain),
        check_vma=False,
    )
```

```python
import functools
import math

import jax
import jax.numpy as jnp
from jax import lax
from jax.experimental import pallas as pl
from jax.experimental.pallas import tpu as pltpu
from jax.sharding import PartitionSpec as P

HEAD_DIM = 80
HALF = HEAD_DIM // 2
LAYERS = 2
SLOTS = 1024
BF = jnp.bfloat16
F32 = jnp.float32
AXES = ("batch", "seq")
LOG2_SCALE = math.log2(math.e) / math.sqrt(HEAD_DIM)
NEG = -1e30
EPS = 1e-6
TILE = 256
MESH = pl.DeviceIdType.MESH
ANY = pl.BlockSpec(memory_space=pl.ANY)
VM = pl.BlockSpec(memory_space=pltpu.VMEM)
SM = pl.BlockSpec(memory_space=pltpu.SMEM)
GROUP = 4
LAG = 2
RATE = 2
DIRECT = (0, 1)
AHEAD = 2


def dot(a, b, i, j):
    return lax.dot_general(a, b, (((i,), (j,)), ((), ())), preferred_element_type=F32)


def struct(shape, dtype=BF):
    return jax.ShapeDtypeStruct(shape, dtype)


def tiles(extent):
    return [slice(at, at + TILE) for at in range(0, extent, TILE)]


class Place:
    def __init__(self):
        self.batch = lax.axis_index("batch")
        self.z = lax.axis_index("seq")
        self.core = self.batch % 2
        self.chip = self.batch // 2
        x = self.chip % 2
        y = (self.chip // 2) % 2
        self.to_x = 2 - 4 * x
        self.to_y = 4 - 8 * y
        self.x = self.batch + self.to_x
        self.y = self.batch + self.to_y
        self.diag = self.batch + self.to_x + self.to_y
        self.sibling = self.batch + 1 - 2 * self.core
        self.inner = (self.z == 1) | (self.z == 2)
        self.pair_z = self.z + 1 - 2 * (self.z % 2)
        self.owner = ((self.z + 1) // 2) % 2
        self.part = self.z // 2

    def id(self, batch):
        return (batch, self.z)

    def workers(self):
        return [
            (2 * self.chip + self.owner, (1 - self.core) * (1 + j) + self.core * 3 * j) for j in (0, 1)
        ]

    def holders(self):
        return [(2 * self.chip + 1 - self.owner, at) for at in (self.core, 3 - self.core)]


def greet(place, signals, line=False):
    barrier = pltpu.get_barrier_semaphore()
    for device in signals:
        pl.semaphore_signal(barrier, inc=1, device_id=device, device_id_type=MESH)
    if line:
        pl.semaphore_signal(barrier, inc=1, device_id=(place.batch, place.pair_z), device_id_type=MESH)

        @pl.when(place.inner)
        def _():
            pl.semaphore_signal(barrier, inc=1, device_id=(place.batch, 3 - place.z), device_id_type=MESH)

        pl.semaphore_wait(barrier, len(signals) + 1 + place.part + place.z % 2 - 2 * place.part * (place.z % 2))
    else:
        pl.semaphore_wait(barrier, len(signals))


class Swap:
    PIECES = 8

    def __init__(self, place, to_workers, src, landing, send, recv):
        self.src, self.landing, self.send, self.recv = src, landing, send, recv
        self.to = place.workers() if to_workers else place.holders()
        self.came_from = place.holders() if to_workers else place.workers()
        self.part = place.part
        self.sent = 0

    def copy(self, k, piece, part):
        count = self.src.shape[1] // self.PIECES
        rows = pl.ds(piece * count, count)
        return remote(
            self.src.at[k, rows], self.landing.at[part, rows], self.send.at[k, piece], self.recv.at[part, piece],
            self.to[k],
        )

    def start(self, pieces=PIECES):
        for _ in range(pieces):
            if self.sent < self.PIECES:
                for k in (0, 1):
                    self.copy(k, self.sent, self.part).start()
                self.sent += 1

    def arrive(self):
        for piece in range(self.PIECES):
            for k in (0, 1):
                self.copy(k, piece, k).wait_recv()

    def drain(self):
        for piece in range(self.PIECES):
            for k in (0, 1):
                self.copy(k, piece, self.part).wait_send()


def swap_scratch():
    return [pltpu.SemaphoreType.DMA((2, Swap.PIECES)), pltpu.SemaphoreType.DMA((2, Swap.PIECES))]


def remote(src, dst, send_sem, recv_sem, device):
    return pltpu.make_async_remote_copy(
        src_ref=src, dst_ref=dst, send_sem=send_sem, recv_sem=recv_sem, device_id=device,
        device_id_type=MESH,
    )


class Gather:
    SEMS = 13

    def __init__(self, place, spread, shards, full, slots, direct, send, recv, local):
        self.place, self.spread, self.direct = place, spread, direct
        self.shards, self.full, self.slots = shards, full, slots
        self.send, self.recv, self.local = send, recv, local
        self.stage = {}

    def rows(self, unit, index, start=0, count=None):
        size = self.shards[unit].shape[0]
        count = size if count is None else count
        return self.full.at[self.slots[unit], pl.ds(pl.multiple_of(index * size + start, 16), count)]

    def span(self, unit):
        size = self.shards[unit].shape[0]
        if unit in self.direct:
            return 0, 0, size
        hz = self.place.z % 2
        return hz * (size // 2), (1 - hz) * (size // 2), size // 2

    def cut(self, unit):
        _, _, half = self.span(unit)
        small = half // 32 * 16
        return small if unit % 2 else half - small

    def copy(self, unit, k):
        p = self.place
        near, far, half = self.span(unit)
        cut = self.cut(unit)
        src = self.shards[unit]
        whole = lambda index: self.rows(unit, index)
        x_part = lambda index, at: self.rows(unit, index, at, cut)
        y_part = lambda index, at: self.rows(unit, index, at + cut, half - cut)
        dst, to = (
            lambda: (whole(p.batch), p.id(p.x)),
            lambda: (whole(p.batch), p.id(p.y)),
            lambda: (whole(p.batch), p.id(p.sibling)),
            lambda: (x_part(p.y, near), p.id(p.x)),
            lambda: (y_part(p.x, near), p.id(p.y)),
            lambda: (whole(p.x), p.id(p.sibling)),
            lambda: (whole(p.y), p.id(p.sibling)),
            lambda: (x_part(p.diag, near), p.id(p.sibling)),
            lambda: (y_part(p.diag, near), p.id(p.sibling)),
            lambda: (x_part(p.diag, near), (p.batch, p.pair_z)),
            lambda: (y_part(p.diag, near), (p.batch, p.pair_z)),
            lambda: (x_part(p.diag, far), p.id(p.sibling)),
            lambda: (y_part(p.diag, far), p.id(p.sibling)),
        )[k]()
        return remote(src if k < 3 else dst, dst, self.send.at[unit, k], self.recv.at[unit, k], to)

    def own(self, unit):
        dst = self.rows(unit, self.place.batch) if self.spread else self.full.at[self.slots[unit]]
        return pltpu.make_async_copy(self.shards[unit], dst, self.local.at[unit])

    def at_stage(self, unit, stage):
        if self.stage.get(unit, 0) >= stage:
            return False
        assert self.stage.get(unit, 0) == stage - 1
        self.stage[unit] = stage
        return self.spread

    def open(self, unit):
        self.own(unit).start()
        if self.at_stage(unit, 1):
            for k in (0, 1, 2):
                self.copy(unit, k).start()

    def relay(self, unit):
        if self.at_stage(unit, 2):
            self.copy(unit, 0).wait_recv()
            self.copy(unit, 1).wait_recv()
            for k in (3, 4, 5, 6):
                self.copy(unit, k).start()

    def share(self, unit):
        if self.at_stage(unit, 3):
            for k in (3, 4):
                self.copy(unit, k).wait_recv()
                if unit not in self.direct:
                    self.copy(unit, k + 6).start()
                self.copy(unit, k + 4).start()

    def pass_on(self, unit):
        if self.at_stage(unit, 4) and unit not in self.direct:
            for k in (9, 10):
                self.arrival(unit, k).wait_recv()
                self.copy(unit, k + 2).start()

    def arrival(self, unit, k):
        p = self.place
        _, far, half = self.span(unit)
        cut = self.cut(unit)
        start, count = ((far, cut), (far + cut, half - cut))[k - 9]
        dst = self.rows(unit, p.diag, start, count)
        return remote(dst, dst, self.send.at[unit, k], self.recv.at[unit, k], (p.batch, p.pair_z))

    def need(self, unit):
        self.relay(unit)
        self.share(unit)
        self.pass_on(unit)
        self.own(unit).wait()
        if self.spread:
            for k in (2, 5, 6, 7, 8) + (() if unit in self.direct else (11, 12)):
                self.copy(unit, k).wait_recv()

    def drain(self, unit):
        if self.spread:
            for k in range(9 if unit in self.direct else self.SEMS):
                self.copy(unit, k).wait_send()


class Scatter:
    SEMS = 7

    def __init__(self, place, grads, out, keep, got_core, got_x, got_y, last_x, last_y, send, recv, local):
        self.p, self.grads, self.out = place, grads, out
        self.room, self.got_core = keep, got_core
        self.got_x, self.got_y, self.last_x, self.last_y = got_x, got_y, last_x, last_y
        self.send, self.recv, self.local = send, recv, local
        p = place
        self.chip_x = p.x // 2
        self.chip_y = p.y // 2
        self.chip_d = p.diag // 2

    def keep(self, unit):
        far, near = self.grads[unit]
        if far is None:
            return near.at[:, self.p.core]
        return self.room.at[unit]

    def piece(self, unit, chip, part):
        half = self.last_x.shape[1]
        return self.keep(unit).at[chip, pl.ds(part * half, half)]

    def copy(self, unit, k):
        p = self.p
        src, dst, to = (
            lambda: (self.source(unit).at[:, 1 - p.core], self.got_core.at[unit], p.sibling),
            lambda: (self.piece(unit, self.chip_x, 0), self.got_x.at[unit, 0], p.x),
            lambda: (self.piece(unit, self.chip_d, 0), self.got_x.at[unit, 1], p.x),
            lambda: (self.piece(unit, self.chip_y, 1), self.got_y.at[unit, 0], p.y),
            lambda: (self.piece(unit, self.chip_d, 1), self.got_y.at[unit, 1], p.y),
            lambda: (self.piece(unit, self.chip_y, 0), self.last_y.at[unit], p.y),
            lambda: (self.piece(unit, self.chip_x, 1), self.last_x.at[unit], p.x),
        )[k]()
        return remote(src, dst, self.send.at[unit, k], self.recv.at[unit, k], p.id(to))

    def source(self, unit):
        far, near = self.grads[unit]
        return near if far is None else far

    def load(self, unit):
        return pltpu.make_async_copy(self.grads[unit][0].at[:, self.p.core], self.room.at[unit], self.local.at[unit, 0])

    def store(self, unit):
        return pltpu.make_async_copy(self.keep(unit).at[self.p.chip], self.out.at[unit], self.local.at[unit, 1])

    def open(self, unit):
        self.copy(unit, 0).start()
        if self.grads[unit][0] is not None:
            self.load(unit).start()

    def add(self, ref, other):
        ref[...] = (ref[...].astype(F32) + other[...].astype(F32)).astype(BF)

    def first(self, unit):
        if self.grads[unit][0] is not None:
            self.load(unit).wait()
        self.copy(unit, 0).wait_recv()
        self.add(self.keep(unit), self.got_core.at[unit])
        for k in (1, 2, 3, 4):
            self.copy(unit, k).start()

    def second(self, unit):
        p = self.p
        self.copy(unit, 2).wait_recv()
        self.add(self.piece(unit, self.chip_y, 0), self.got_x.at[unit, 1])
        self.copy(unit, 5).start()
        self.copy(unit, 4).wait_recv()
        self.add(self.piece(unit, self.chip_x, 1), self.got_y.at[unit, 1])
        self.copy(unit, 6).start()
        self.copy(unit, 1).wait_recv()
        self.add(self.piece(unit, p.chip, 0), self.got_x.at[unit, 0])
        self.copy(unit, 3).wait_recv()
        self.add(self.piece(unit, p.chip, 1), self.got_y.at[unit, 0])

    def third(self, unit):
        p = self.p
        self.copy(unit, 5).wait_recv()
        self.add(self.piece(unit, p.chip, 0), self.last_y.at[unit])
        self.copy(unit, 6).wait_recv()
        self.add(self.piece(unit, p.chip, 1), self.last_x.at[unit])
        if self.out is not None:
            self.store(unit).start()

    def drain(self, unit):
        for k in range(self.SEMS):
            self.copy(unit, k).wait_send()
        if self.out is not None:
            self.store(unit).wait()


def scatter_scratch(units, loaded, shard, width):
    half = shard // 2
    return [
        pltpu.VMEM((max(loaded, 1), 4, shard, width) if loaded else (1, 1, 16, width), BF),
        pltpu.VMEM((units, 4, shard, width), BF),
        pltpu.VMEM((units, 2, half, width), BF),
        pltpu.VMEM((units, 2, half, width), BF),
        pltpu.VMEM((units, half, width), BF),
        pltpu.VMEM((units, half, width), BF),
        pltpu.SemaphoreType.DMA((units, Scatter.SEMS)),
        pltpu.SemaphoreType.DMA((units, Scatter.SEMS)),
        pltpu.SemaphoreType.DMA((units, 2)),
    ]


class Line:
    def __init__(self, place, shares, out, mine, got, other, send, recv, local):
        self.p, self.shares, self.out = place, shares, out
        self.room, self.got, self.other = mine, got, other
        self.send, self.recv, self.local = send, recv, local

    def copy(self, item, half, k):
        p = self.p
        size = self.got.shape[1] // 2
        part = lambda ref: ref.at[pl.ds(half * size, size)]
        mine, got, other = self.mine(item), self.got.at[item], self.other.at[item]
        src, dst, to_z = ((mine, got, p.pair_z), (mine, other, 3 - p.z), (got, got, p.pair_z))[k]
        at = 3 * half + k
        return remote(part(src), part(dst), self.send.at[item, at], self.recv.at[item, at], (p.batch, to_z))

    def mine(self, item):
        far, near = self.shares[item]
        return self.room.at[item] if near is None else near

    def part(self, ref, half):
        size = self.got.shape[1] // 2
        return ref.at[pl.ds(half * size, size)]

    def load(self, item):
        return pltpu.make_async_copy(self.shares[item][0], self.room.at[item], self.local.at[item, 0])

    def store(self, item):
        return pltpu.make_async_copy(self.got.at[item], self.out.at[item], self.local.at[item, 1])

    def start(self, item):
        if self.shares[item][0] is not None:
            self.load(item).wait()

        @pl.when(jnp.logical_not(self.p.inner))
        def _():
            for half in (0, 1):
                self.copy(item, half, 0).start()

    def middle(self, item):
        @pl.when(self.p.inner)
        def _():
            for half in (0, 1):
                mine = self.part(self.mine(item), half)
                got = self.part(self.got.at[item], half)
                self.copy(item, half, 0).wait_recv()
                mine[...] = (mine[...].astype(F32) + got[...].astype(F32)).astype(BF)
                self.copy(item, half, 1).start()

    def last(self, item):
        @pl.when(self.p.inner)
        def _():
            for half in (0, 1):
                mine = self.part(self.mine(item), half)
                got = self.part(self.got.at[item], half)
                other = self.part(self.other.at[item], half)
                self.copy(item, half, 1).wait_recv()
                got[...] = (mine[...].astype(F32) + other[...].astype(F32)).astype(BF)
                self.copy(item, half, 2).start()

    def end(self, item):
        @pl.when(jnp.logical_not(self.p.inner))
        def _():
            for half in (0, 1):
                self.copy(item, half, 2).wait_recv()

        self.store(item).start()

    def drain(self, item):
        @pl.when(self.p.inner)
        def _():
            for half in (0, 1):
                self.copy(item, half, 1).wait_send()
                self.copy(item, half, 2).wait_send()

        @pl.when(jnp.logical_not(self.p.inner))
        def _():
            for half in (0, 1):
                self.copy(item, half, 0).wait_send()

        self.store(item).wait()


def line_scratch(items, loaded, shard, width):
    return [
        pltpu.VMEM((loaded, shard, width) if loaded else (1, 16, width), BF),
        pltpu.VMEM((items, shard, width), BF),
        pltpu.VMEM((items, shard, width), BF),
        pltpu.SemaphoreType.DMA((items, 6)),
        pltpu.SemaphoreType.DMA((items, 6)),
        pltpu.SemaphoreType.DMA((items, 2)),
    ]


class Plan:
    def __init__(self, xy, xy_arrays, z, z_arrays, shard, width):
        self.xy, self.xy_arrays, self.z, self.z_arrays = xy, xy_arrays, z, z_arrays
        self.shard, self.width = shard, width
        self.keep_sums = bool(xy) and not any(src == "sum" for src, _ in z)

    def args(self):
        return [*self.xy_arrays, *self.z_arrays]

    def outs(self):
        out = []
        if self.keep_sums:
            out.append(struct((len(self.xy), self.shard, self.width)))
        if self.z:
            out.append(struct((len(self.z), self.shard, self.width)))
        return out

    def scratch(self):
        loaded = sum(src != "own" for src, _ in self.xy)
        shares = sum(src != "sum" for src, _ in self.z)
        return (scatter_scratch(len(self.xy), loaded, self.shard, self.width) if self.xy else []) + (
            line_scratch(len(self.z), shares, self.shard, self.width) if self.z else []
        )

    def signals(self, p):
        return [p.id(p.sibling), p.id(p.x), p.id(p.y)] if self.xy else []

    def open(self, p, inputs, outputs, scratch, own=None):
        outputs, scratch = list(outputs), list(scratch)
        arrays = inputs[: len(self.xy_arrays)]
        shares = inputs[len(self.xy_arrays) :]
        sums_out = outputs.pop(0) if self.keep_sums else None
        scatter = line = None
        if self.xy:
            grads = [
                (None, own.at[unit]) if src == "own" else (arrays[src].at[unit], None) for src, unit in self.xy
            ]
            scatter = Scatter(p, grads, sums_out, *scratch[:9])
            scratch = scratch[9:]
        if self.z:
            items = [
                (None, scatter.keep(i).at[p.chip]) if src == "sum" else (shares[src].at[i], None)
                for src, i in self.z
            ]
            line = Line(p, items, outputs.pop(0), *scratch)
        return scatter, line


def kernel_params(collective):
    params = dict(vmem_limit_bytes=63 * 2**20)
    if collective is not None:
        params.update(collective_id=collective, has_side_effects=True)
    return pltpu.CompilerParams(**params)


def rms(rows):
    return lax.rsqrt(jnp.mean(rows * rows, axis=-1, keepdims=True) + EPS)


def key_blocks(core):
    if core == 0:
        return [(0, [("o", 0, 0)]), (1, [("o", 0, 0), ("x", 0, 1), ("x", 1, 2), ("o", 1, 3)])]
    return [(0, [("x", 0, 0), ("o", 0, 1)]), (1, [("x", 0, 0), ("o", 0, 1), ("o", 1, 2)])]


def masked(scores, quarter, diagonal, pad):
    size = scores.shape[0]
    key = lax.broadcasted_iota(jnp.int32, scores.shape, 0)
    ok = key >= pad - quarter * size
    if diagonal:
        query = lax.broadcasted_iota(jnp.int32, scores.shape, 1)
        ok = ((key <= query) & ok) | (key == query)
    return jnp.where(ok, scores, NEG)


def attend_heads(core, base, pad, qkv, kvx, o_ref, lse_ref):
    width, rows = o_ref.shape
    size = rows // 2
    at = lambda off, hh: pl.ds(pl.multiple_of(off * width + (base + hh) * HEAD_DIM, 16), HEAD_DIM)
    for hh in range(GROUP):
        for block, keys in key_blocks(core):
            cols = slice(block * size, block * size + size)
            q = qkv[at(0, hh), cols]
            scores = []
            for i, (src, half, quarter) in enumerate(keys):
                span = slice(half * size, half * size + size)
                k = qkv[at(1, hh), span] if src == "o" else kvx[at(0, hh), span]
                scores.append(masked(dot(k, q, 0, 0), quarter, i == len(keys) - 1, pad))
            top = functools.reduce(jnp.maximum, [jnp.max(s, axis=0, keepdims=True) for s in scores])
            total = 0.0
            out = 0.0
            for s, (src, half, quarter) in zip(scores, keys):
                span = slice(half * size, half * size + size)
                v = qkv[at(2, hh), span] if src == "o" else kvx[at(1, hh), span]
                weight = jnp.exp2((s - top) * LOG2_SCALE)
                total = total + jnp.sum(weight, axis=0, keepdims=True)
                out = out + dot(v, weight.astype(BF), 1, 0)
            o_ref[at(0, hh), cols] = (out * (1.0 / total)).astype(BF)
            lse_ref[base // GROUP, hh : hh + 1, cols] = top * LOG2_SCALE + jnp.log2(total)


class Copies:
    def __init__(self, sems):
        self.sems, self.used, self.open = sems, 0, {}

    def start(self, src, dst):
        copy = pltpu.make_async_copy(src, dst, self.sems.at[self.used])
        self.used += 1
        copy.start()
        return copy

    def save(self, name, src, dst):
        self.open.setdefault(name, []).append(self.start(src, dst))

    def ready(self, *names):
        for name in names:
            for copy in self.open.pop(name, []):
                copy.wait()

    def finish(self):
        self.ready(*list(self.open))


def forward_kernel(spread, *refs):
    refs = list(refs)
    take = lambda n: [refs.pop(0) for _ in range(n)]
    pad_ref, cos, sin, rows_in, cot_in, wqkv, wout, wup, wdown = take(9)
    (w_out, cot_out, hid0_out, hid1_out, h_out, xt_out, qkv_out, kvx_out, att_out, lse_out, mid_out, mt_out, pre_out,
     act_out) = take(14)
    (full, g_send, g_recv, g_local, qkv, kvx, h, att, lse, mid, xhat, tp, tq, act, rows_buf, x_send, x_recv, s_send, s_recv,
     free, copy_sems) = refs
    p = Place()
    width = xhat.shape[1]
    rows = xhat.shape[0]
    quarter = rows // 2
    groups = width // (HEAD_DIM * GROUP)
    copies = Copies(copy_sems)
    swap_in = Swap(p, True, rows_in, rows_buf, s_send.at[0], s_recv.at[0])
    swap_cot = Swap(p, True, cot_in, cot_out, s_send.at[1], s_recv.at[1])
    swap_hid = Swap(p, False, rows_buf, hid0_out, s_send.at[2], s_recv.at[2])
    others = [p.id(p.x), p.id(p.y), p.id(p.sibling), (p.batch, p.pair_z)] if spread else [p.id(p.sibling)]
    greet(p, others + swap_in.came_from + swap_hid.came_from)
    shards = []
    for layer in range(LAYERS):
        shards += [wqkv.at[layer, :, pl.ds(u * width, width)] for u in (1, 2, 0)]
        shards += [w.at[layer] for w in (wout, wup, wdown)]
    units = len(shards)
    room = full.shape[0]
    slots = [unit % room for unit in range(units)]
    gather = Gather(p, spread, shards, full, slots, DIRECT, g_send, g_recv, g_local)

    moving = []

    def release():
        for unit in range(units - room):
            gather.drain(unit)
            copies.ready(("w", unit))
        if spread:
            for k, device in enumerate(others):
                pl.semaphore_signal(free.at[k], inc=1, device_id=device, device_id_type=MESH)

    def tick(unit):
        gather.relay(unit)
        if unit + AHEAD < units:
            if unit + AHEAD == room and spread:
                for k in range(len(others)):
                    pl.semaphore_wait(free.at[k], 1)
            gather.open(unit + AHEAD)
        if unit:
            gather.share(unit - 1)
        if unit >= LAG:
            gather.pass_on(unit - LAG)
        for swap in moving:
            swap.start(RATE)

    def need(unit):
        gather.need(unit)
        copies.save(("w", unit), full.at[slots[unit]], w_out.at[unit])

    swap_in.start()
    for unit in range(AHEAD):
        gather.open(unit)
    tick(0)
    swap_in.arrive()
    for k in (0, 1):
        h[k * quarter : (k + 1) * quarter, :] = rows_buf[k].astype(F32)
    pad = pad_ref[0]

    for layer in range(LAYERS):
        base = 6 * layer
        copies.save("h", h, h_out.at[layer])
        copies.ready("tp", "tq")
        xhat[...] = (h[...] * rms(h[...])).astype(BF)
        tp[...] = xhat[...].T
        copies.save("tp", tp, xt_out.at[layer])
        copies.ready("qkv")
        if layer == 0:
            tick(1)
            tick(2)

        def exchange(k):
            return remote(
                qkv.at[pl.ds((1 + k) * width, width)], kvx.at[layer, pl.ds(k * width, width)],
                x_send.at[layer, k], x_recv.at[layer, k], p.id(p.sibling),
            )

        for i, part in enumerate((1, 2, 0)):
            need(base + i)
            step = 8 * HEAD_DIM
            for at in range(0, width, step):
                y = dot(xhat[...], full[slots[base + i], :, at : at + step], 1, 0).T
                for head in range(0, step, HEAD_DIM):
                    to = part * width + at + head
                    if part == 2:
                        qkv[to : to + HEAD_DIM, :] = y[head : head + HEAD_DIM].astype(BF)
                    else:
                        a, b = y[head : head + HALF], y[head + HALF : head + HEAD_DIM]
                        qkv[to : to + HEAD_DIM, :] = jnp.concatenate(
                            [a * cos[...] - b * sin[...], b * cos[...] + a * sin[...]], axis=0
                        ).astype(BF)
            if i < 2:
                exchange(i).start()
                tick(base + 3 + i)
        copies.save("qkv", qkv, qkv_out.at[layer])
        if layer == 0:
            moving.append(swap_cot)
        for k in (0, 1):
            exchange(k).wait_recv()
        copies.save("kvx", kvx.at[layer], kvx_out.at[layer])
        copies.ready("att", "lse")

        def body(group, carry):
            for core in (0, 1):
                pl.when(p.core == core)(
                    functools.partial(attend_heads, core, group * GROUP, pad, qkv, kvx.at[layer], att, lse)
                )

            @pl.when(group == 1)
            def _():
                tick(base + 5)

            return carry

        lax.fori_loop(0, groups, body, 0)
        if layer == 0:
            release()
        if layer == 0:
            tick(base + 6)
        copies.save("att", att, att_out.at[layer])
        copies.save("lse", lse, lse_out.at[layer])
        for k in (0, 1):
            exchange(k).wait_send()
        copies.ready("mid")
        need(base + 3)
        square = 0.0
        for cols in tiles(width):
            m = h[:, cols] + dot(att[...], full[slots[base + 3], :, cols], 0, 0)
            mid[:, cols] = m
            square = square + jnp.sum(m * m, axis=1, keepdims=True)
        copies.save("mid", mid, mid_out.at[layer])
        scale = lax.rsqrt(square / width + EPS)
        for cols in tiles(width):
            m = (mid[:, cols] * scale).astype(BF)
            xhat[:, cols] = m
            tq[cols, :] = m.T
        copies.save("tq", tq, mt_out.at[layer])
        need(base + 4)
        copies.ready("h", "tp")
        for cols in tiles(width):
            v = dot(xhat[...], full[slots[base + 4], :, cols], 1, 0)
            h[:, cols] = v
            a = (v / (1.0 + jnp.exp(-v))).astype(BF)
            act[:, cols] = a
            tp[cols, :] = a.T
        copies.save("pre", h, pre_out.at[layer])
        copies.save("tp", tp, act_out.at[layer])
        last = layer == LAYERS - 1
        if not last:
            tick(base + 7)
        need(base + 5)
        copies.ready("pre")
        if last:
            swap_hid.start()
            swap_hid.drain()
        for cols in tiles(width):
            v = mid[:, cols] + dot(act[...], full[slots[base + 5], :, cols], 1, 0)
            if not last:
                h[:, cols] = v
            for k in (0, 1):
                rows_buf[k, :, cols] = v[k * quarter : (k + 1) * quarter].astype(BF)
        if last:
            copies.save("hid", rows_buf, hid1_out)
        else:
            moving.append(swap_hid)
            tick(base + 8)
    for unit in range(units - room, units):
        gather.drain(unit)
    for swap in moving:
        swap.start()
    swap_in.drain()
    swap_cot.arrive()
    swap_cot.drain()
    swap_hid.arrive()
    copies.finish()


def forward(spread, collective, pad, cos, sin, inputs, cotangent, wqkv, wout, wup, wdown, shard):
    _, quarter, width = inputs.shape
    rows = 2 * quarter
    groups = width // (HEAD_DIM * GROUP)
    nat, tr = (rows, width), (width, rows)
    lse = (groups, GROUP, rows)
    two = lambda shape, dtype=BF: struct((LAYERS,) + shape, dtype)
    units = 6 * LAYERS
    room = units - 3
    swapped = struct((2, quarter, width))
    outs = [
        struct((units, width, width)), swapped, swapped, swapped, two(nat, F32), two(tr), two((3 * width, rows)),
        two((2 * width, rows)), two(tr), two(lse, F32), two(nat, F32), two(tr), two(nat, F32), two(tr),
    ]
    scratch = [
        pltpu.VMEM((room, width, width), BF),
        pltpu.SemaphoreType.DMA((units, Gather.SEMS)),
        pltpu.SemaphoreType.DMA((units, Gather.SEMS)),
        pltpu.SemaphoreType.DMA((units,)),
        pltpu.VMEM((3 * width, rows), BF),
        pltpu.VMEM((LAYERS, 2 * width, rows), BF),
        pltpu.VMEM(nat, F32),
        pltpu.VMEM(tr, BF),
        pltpu.VMEM(lse, F32),
        pltpu.VMEM(nat, F32),
        pltpu.VMEM(nat, BF),
        pltpu.VMEM(tr, BF),
        pltpu.VMEM(tr, BF),
        pltpu.VMEM(nat, BF),
        pltpu.VMEM((2, quarter, width), BF),
        pltpu.SemaphoreType.DMA((LAYERS, 2)),
        pltpu.SemaphoreType.DMA((LAYERS, 2)),
        pltpu.SemaphoreType.DMA((3, 2, Swap.PIECES)),
        pltpu.SemaphoreType.DMA((3, 2, Swap.PIECES)),
        pltpu.SemaphoreType.REGULAR((4,)),
        pltpu.SemaphoreType.DMA((units + 10 * LAYERS + 2,)),
    ]
    return pl.pallas_call(
        functools.partial(forward_kernel, spread),
        in_specs=[SM, VM, VM] + [ANY] * 6,
        out_specs=[ANY] * len(outs),
        out_shape=outs,
        scratch_shapes=scratch,
        compiler_params=kernel_params(collective),
        cost_estimate=pl.CostEstimate(flops=180 * 10**9, bytes_accessed=100 * 10**6, transcendentals=0),
        name="forward",
    )(pad, cos, sin, inputs, cotangent, wqkv, wout, wup, wdown)


def feed_back_kernel(plan, layer, *refs):
    refs = list(refs)
    take = lambda n: [refs.pop(0) for _ in range(n)]
    g_in, w_in, *held = take(7)
    act_t_in, mt_in, pre_in, mid_in, att_in = [ref.at[layer] for ref in held]
    inputs = take(len(plan.args())) if plan else []
    dw_out, mg_out, do_out = take(3)
    outputs = take(len(plan.outs())) if plan else []
    g, w, act_t, mt, pre, mid, att, gb, dpre, eg, do, dw, copy_sems = take(13)
    copies = Copies(copy_sems)
    width = w.shape[1]
    shard = dw.shape[3]
    if plan:
        p = Place()
        greet(p, plan.signals(p), bool(plan.z))
        scatter, line = plan.open(p, inputs, outputs, refs, dw)
        if line:
            line.load(0).start()
        if plan.xy[0][0] != "own":
            scatter.open(0)
    load_g = copies.start(g_in, gb if g_in.dtype == BF else g)
    load_act = copies.start(act_t_in, act_t)
    load_w = [copies.start(w_in.at[6 * layer + 5], w.at[2])]
    load_pre = copies.start(pre_in, pre)
    load_mt = copies.start(mt_in, mt)
    load_w += [copies.start(w_in.at[6 * layer + 4], w.at[1])]
    load_mid = copies.start(mid_in, mid)
    load_att = copies.start(att_in, att)
    load_w += [copies.start(w_in.at[6 * layer + 3], w.at[0])]

    def put(unit, cols, value):
        for k in range(dw.shape[1]):
            for c in range(2):
                at = (2 * k + c) * shard
                dw[unit, k, c, :, cols] = value[at : at + shard].astype(BF)

    load_g.wait()
    if g_in.dtype == BF:
        g[...] = gb[...].astype(F32)
    else:
        gb[...] = g[...].astype(BF)
    load_act.wait()
    for cols in tiles(width):
        put(2, cols, dot(act_t[...], gb[:, cols], 1, 0))
    if plan and plan.xy[0][0] == "own":
        scatter.open(0)
    else:
        copies.save("dw", dw.at[2], dw_out.at[2])
    if plan:
        if line:
            line.start(0)
    load_w[0].wait()
    load_pre.wait()
    for cols in tiles(width):
        da = dot(gb[...], w[2, cols, :], 1, 1)
        v = pre[:, cols]
        s = 1.0 / (1.0 + jnp.exp(-v))
        dpre[:, cols] = (da * (s + v * s * (1.0 - s))).astype(BF)
    if plan:
        scatter.first(0)
    load_mt.wait()
    for cols in tiles(width):
        put(1, cols, dot(mt[...], dpre[:, cols], 1, 0))
    copies.save("dw", dw.at[1], dw_out.at[1])
    load_w[1].wait()
    load_mid.wait()
    r = rms(mid[...])
    total = 0.0
    for cols in tiles(width):
        e = dot(dpre[...], w[1, cols, :], 1, 1)
        eg[:, cols] = e
        total = total + jnp.sum(e * (mid[:, cols] * r), axis=1, keepdims=True)
    total = total / width
    if plan and line:
        line.middle(0)
    for cols in tiles(width):
        m = g[:, cols] + r * (eg[:, cols] - mid[:, cols] * r * total)
        g[:, cols] = m
        gb[:, cols] = m.astype(BF)
    copies.save("g", g, mg_out)
    load_att.wait()
    for cols in tiles(width):
        put(0, cols, dot(att[...], gb[:, cols], 1, 0))
    copies.save("dw", dw.at[0], dw_out.at[0])
    load_w[2].wait()
    if plan:
        scatter.second(0)
        if line:
            line.last(0)
    for cols in tiles(width):
        do[cols, :] = dot(w[0, cols, :], gb[...], 1, 1).astype(BF)
    copies.save("do", do, do_out)
    if plan:
        scatter.third(0)
        if line:
            line.end(0)
            line.drain(0)
        scatter.drain(0)
    copies.finish()


def feed_back(name, collective, layer, g, w, act_t, mt, pre, mid, att, chips, shard, plan):
    _, width, rows = act_t.shape
    nat, tr = (rows, width), (width, rows)
    grad = (3, chips, 2, shard, width)
    args = [g, w, act_t, mt, pre, mid, att] + (plan.args() if plan else [])
    outs = [struct(grad), struct(nat, F32), struct(tr)] + (plan.outs() if plan else [])
    return pl.pallas_call(
        functools.partial(feed_back_kernel, plan, layer),
        in_specs=[ANY] * len(args),
        out_specs=[ANY] * len(outs),
        out_shape=outs,
        scratch_shapes=[
            pltpu.VMEM(nat, F32),
            pltpu.VMEM((3, width, width), BF),
            pltpu.VMEM(tr, BF),
            pltpu.VMEM(tr, BF),
            pltpu.VMEM(nat, F32),
            pltpu.VMEM(nat, F32),
            pltpu.VMEM(tr, BF),
            pltpu.VMEM(nat, BF),
            pltpu.VMEM(nat, BF),
            pltpu.VMEM(nat, F32),
            pltpu.VMEM(tr, BF),
            pltpu.VMEM(grad, BF),
            pltpu.SemaphoreType.DMA((16,)),
        ] + (plan.scratch() if plan else []),
        compiler_params=kernel_params(collective if plan else None),
        cost_estimate=pl.CostEstimate(flops=16 * 10**9, bytes_accessed=30 * 10**6, transcendentals=0),
        name=name,
    )(*args)


def unrotate(t, cos, sin):
    a, b = t[:HALF], t[HALF:]
    return jnp.concatenate([a * cos + b * sin, b * cos - a * sin], axis=0)


def attend_back_heads(core, base, pad, qkv, kvx, do, o, lse, tables, dqkv, dkvx):
    width, rows = o.shape
    size = rows // 2
    scale = 1.0 / math.sqrt(HEAD_DIM)
    cos, sin, cosx, sinx = tables
    at = lambda off, hh: pl.ds(pl.multiple_of(off * width + (base + hh) * HEAD_DIM, 16), HEAD_DIM)
    for hh in range(GROUP):
        dk, dv = {}, {}
        for block, keys in key_blocks(core):
            cols = slice(block * size, block * size + size)
            q = qkv[at(0, hh), cols]
            d_out = do[at(0, hh), cols]
            delta = jnp.sum(d_out.astype(F32) * o[at(0, hh), cols].astype(F32), axis=0, keepdims=True)
            norm = lse[base // GROUP, hh : hh + 1, cols]
            dq = 0.0
            for i, (src, half, quarter) in enumerate(keys):
                span = slice(half * size, half * size + size)
                k = qkv[at(1, hh), span] if src == "o" else kvx[at(0, hh), span]
                v = qkv[at(2, hh), span] if src == "o" else kvx[at(1, hh), span]
                s = masked(dot(k, q, 0, 0), quarter, i == len(keys) - 1, pad)
                weight = jnp.exp2(s * LOG2_SCALE - norm)
                ds = (weight * (dot(v, d_out, 0, 0) - delta)).astype(BF)
                dq = dq + dot(k, ds, 1, 0)
                a, b = dot(q, ds, 1, 1), dot(d_out, weight.astype(BF), 1, 1)
                key = (src, half)
                dk[key] = dk[key] + a if key in dk else a
                dv[key] = dv[key] + b if key in dv else b
            dqkv[at(0, hh), cols] = unrotate(dq * scale, cos[:, cols], sin[:, cols]).astype(BF)
        for src, ref, k_off, ct, st in (("o", dqkv, 1, cos, sin), ("x", dkvx, 0, cosx, sinx)):
            for half in (0, 1):
                span = slice(half * size, half * size + size)
                if (src, half) in dk:
                    a = unrotate(dk[src, half] * scale, ct[:, span], st[:, span]).astype(BF)
                    b = dv[src, half].astype(BF)
                else:
                    a = b = jnp.zeros((HEAD_DIM, size), BF)
                ref[at(k_off, hh), span] = a
                ref[at(k_off + 1, hh), span] = b


def attend_back_kernel(plan, layer, swapping, *refs):
    refs = list(refs)
    take = lambda n: [refs.pop(0) for _ in range(n)]
    pad_ref, qkv_in, kvx_in, do_in, att_in, lse, cos, sin, cosx, sinx = take(10)
    qkv_in, kvx_in, att_in = qkv_in.at[layer], kvx_in.at[layer], att_in.at[layer]
    hid_in = take(1)[0] if swapping else None
    inputs = take(len(plan.args())) if plan else []
    pg_out = take(1)[0]
    swap_out = take(1)[0] if swapping else None
    outputs = take(len(plan.outs())) if plan else []
    qkv, kvx, do, att, dqkv, dkvx, got, x_send, x_recv, copy_sems = take(10)
    p = Place()
    copies = Copies(copy_sems)
    signals = [p.id(p.sibling)]
    if plan:
        signals = plan.signals(p)
    if swapping:
        swap = Swap(p, False, hid_in, swap_out, *take(2))
        signals = signals + swap.came_from
    greet(p, signals, bool(plan and plan.z))
    if swapping:
        swap.start()
    loads = [copies.start(a, b) for a, b in ((qkv_in, qkv), (kvx_in, kvx), (do_in, do), (att_in, att))]
    units = items = 0
    if plan:
        scatter, line = plan.open(p, inputs, outputs, refs)
        units, items = len(plan.xy), len(plan.z)
        for i in range(units):
            scatter.open(i)
        for i in range(items):
            line.load(i).start()
        for i in range(items):
            line.start(i)
    for load in loads:
        load.wait()
    for i in range(units):
        scatter.first(i)
    pad = pad_ref[0]
    width = att.shape[0]
    span = GROUP * HEAD_DIM
    groups = width // span

    def exchange(group, k):
        part = pl.ds(pl.multiple_of(k * width + group * span, 16), span)
        return remote(dkvx.at[part], got.at[part], x_send.at[group, k], x_recv.at[group, k], p.id(p.sibling))

    def body(group, carry):
        for core in (0, 1):
            pl.when(p.core == core)(
                functools.partial(
                    attend_back_heads, core, group * GROUP, pad, qkv, kvx, do, att, lse,
                    (cos, sin, cosx, sinx), dqkv, dkvx,
                )
            )
        for k in (0, 1):
            exchange(group, k).start()
        after = [[], [], []]
        if units:
            after[1] += [(scatter.second, 0)]
            after[2] += [(scatter.second, i) for i in range(1, units)]
        if items:
            after[0] += [(line.middle, 0)]
            after[1] += [(line.middle, i) for i in range(1, min(items, 2))] + [(line.last, 0)]
            after[2] += [(line.middle, i) for i in range(2, items)] + [(line.last, i) for i in range(1, min(items, 2))]
        for at, steps in enumerate(after):

            @pl.when(group == at)
            def _(steps=steps):
                for step, i in steps:
                    step(i)

        return carry

    lax.fori_loop(0, groups, body, 0)
    for group in range(groups):
        for k in (0, 1):
            exchange(group, k).wait_recv()
    own = dqkv.at[pl.ds(width, 2 * width)]
    own[...] = (own[...].astype(F32) + got[...].astype(F32)).astype(BF)
    copies.save("dqkv", dqkv, pg_out)
    for i in range(units):
        scatter.third(i)
    for i in range(2, items):
        line.last(i)
    for i in range(items):
        line.end(i)
    for i in range(items):
        line.drain(i)
    for i in range(units):
        scatter.drain(i)
    for group in range(groups):
        for k in (0, 1):
            exchange(group, k).wait_send()
    if swapping:
        swap.arrive()
        swap.drain()
    copies.finish()


def attend_back(name, collective, layer, pad, qkv, kvx, do, att, lse, tables, hid, plan):
    _, width, rows = att.shape
    swapping = hid is not None
    args = [pad, qkv, kvx, do, att, lse, *tables] + ([hid] if swapping else []) + (plan.args() if plan else [])
    specs = [SM] + [ANY] * 4 + [VM] * 5 + [ANY] * (len(args) - 10)
    outs = [struct((3 * width, rows))]
    if swapping:
        outs.append(struct(hid.shape))
    outs += plan.outs() if plan else []
    scratch = [
        pltpu.VMEM((3 * width, rows), BF),
        pltpu.VMEM((2 * width, rows), BF),
        pltpu.VMEM((width, rows), BF),
        pltpu.VMEM((width, rows), BF),
        pltpu.VMEM((3 * width, rows), BF),
        pltpu.VMEM((2 * width, rows), BF),
        pltpu.VMEM((2 * width, rows), BF),
        pltpu.SemaphoreType.DMA((lse.shape[0], 2)),
        pltpu.SemaphoreType.DMA((lse.shape[0], 2)),
        pltpu.SemaphoreType.DMA((16,)),
    ]
    if swapping:
        scratch += swap_scratch()
    return pl.pallas_call(
        functools.partial(attend_back_kernel, plan, layer, swapping),
        in_specs=specs,
        out_specs=[ANY] * len(outs),
        out_shape=outs,
        scratch_shapes=scratch + (plan.scratch() if plan else []),
        compiler_params=kernel_params(collective),
        cost_estimate=pl.CostEstimate(flops=35 * 10**9, bytes_accessed=30 * 10**6, transcendentals=0),
        name=name,
    )(*args)


def project_back_kernel(plan, layer, swapping, *refs):
    refs = list(refs)
    take = lambda n: [refs.pop(0) for _ in range(n)]
    pg_in, xt_in, w_in, h_in, mg_in = take(5)
    xt_in, h_in = xt_in.at[layer], h_in.at[layer]
    inputs = take(len(plan.args())) if plan else []
    dw_out = None if swapping and plan else take(1)[0]
    g_out = take(1)[0]
    outputs = take(len(plan.outs())) if plan else []
    pg, xt, w, h, g, eg, dw, copy_sems = take(8)
    gb = take(1)[0] if swapping else None
    swap_sems = take(2) if swapping else None
    copies = Copies(copy_sems)
    width = xt.shape[0]
    quarter = xt.shape[1] // 2
    shard = dw.shape[3]
    p = Place()
    signals = plan.signals(p) if plan else []
    if swapping:
        swap = Swap(p, False, gb, g_out, *swap_sems)
        signals = signals + swap.came_from
    if signals:
        greet(p, signals, bool(plan and plan.z))
    load_pg = copies.start(pg_in, pg)
    load_xt = copies.start(xt_in, xt)
    held = earlier = shares = 0
    scatter = line = None
    if plan:
        scatter, line = plan.open(p, inputs, outputs, refs, dw)
        held = len(plan.xy)
        earlier = sum(src != "own" for src, _ in plan.xy)
        shares = sum(src != "sum" for src, _ in plan.z)
    for i in range(earlier):
        scatter.open(i)
    for i in range(shares):
        line.load(i).start()
    load_w = [copies.start(w_in.at[6 * layer + (2, 0, 1)[unit]], w.at[unit]) for unit in range(3)]
    load_h = copies.start(h_in, h)
    load_g = copies.start(mg_in, g)
    load_pg.wait()
    load_xt.wait()
    for i in range(shares):
        line.start(i)
    for i in range(min(earlier, 1)):
        scatter.first(i)

    def weight_grad(unit):
        for cols in tiles(width):
            value = dot(xt[...], pg[unit * width + cols.start : unit * width + cols.stop, :], 1, 1)
            for k in range(dw.shape[1]):
                for c in range(2):
                    at = (2 * k + c) * shard
                    dw[unit, k, c, :, cols] = value[at : at + shard].astype(BF)
        if dw_out is not None and not (plan and ("own", unit) in plan.xy):
            copies.save("dw", dw.at[unit], dw_out.at[unit])

    own = earlier
    weight_grad(1)
    for i in range(1, earlier):
        scatter.first(i)
    if own < held:
        scatter.open(own)
    weight_grad(2)
    if own < held:
        scatter.first(own)
    for i in range(shares):
        line.middle(i)
    if own + 1 < held:
        scatter.open(own + 1)
    weight_grad(0)
    if own + 2 < held:
        scatter.open(own + 2)
    for i in range(min(earlier, 1)):
        scatter.second(i)
    for load in load_w:
        load.wait()
    load_h.wait()
    r = rms(h[...])
    total = 0.0
    for n, cols in enumerate(tiles(width)):
        e = 0.0
        for unit in range(3):
            e = e + dot(pg[unit * width : (unit + 1) * width, :], w[unit, cols, :], 0, 1)
        eg[:, cols] = e
        total = total + jnp.sum(e * (h[:, cols] * r), axis=1, keepdims=True)
        if n == 1:
            for i in range(1, earlier):
                scatter.second(i)
        if n == 2 and own + 1 < held:
            scatter.first(own + 1)
        if n == 3:
            for i in range(shares):
                line.last(i)
    total = total / width
    load_g.wait()
    for cols in tiles(width):
        v = g[:, cols] + r * (eg[:, cols] - h[:, cols] * r * total)
        if swapping:
            for k in (0, 1):
                gb[k, :, cols] = v[k * quarter : (k + 1) * quarter].astype(BF)
        else:
            g[:, cols] = v
    if swapping:
        swap.start()
    else:
        copies.save("g", g, g_out)
    chain = bool(plan) and len(plan.z) > shares
    for i in range(own + 2, held):
        scatter.first(i)
    for i in range(earlier):
        scatter.third(i)
    steps = [[] for _ in range(held + 6)]
    for i in range(held):
        if i >= earlier:
            steps[i].append(functools.partial(scatter.second, i))
            steps[i + 1].append(functools.partial(scatter.third, i))
        if chain:
            j = shares + i
            base = i + 1
            steps[base].append(functools.partial(line.start, j))
            steps[base + 1].append(functools.partial(line.middle, j))
            steps[base + 2].append(functools.partial(line.last, j))
            steps[base + 3].append(functools.partial(line.end, j))
    for group in steps:
        for step in group:
            step()
    for i in range(shares):
        line.end(i)
    for i in range(len(plan.z) if plan else 0):
        line.drain(i)
    for i in range(held):
        scatter.drain(i)
    if swapping:
        swap.arrive()
        swap.drain()
    copies.finish()


def project_back(name, collective, layer, pg, xt, w, h, mg, chips, shard, swapping, plan):
    _, rows, width = h.shape
    nat, tr = (rows, width), (width, rows)
    grad = (3, chips, 2, shard, width)
    args = [pg, xt, w, h, mg] + (plan.args() if plan else [])
    outs = [] if swapping and plan else [struct(grad)]
    outs.append(struct((2, rows // 2, width)) if swapping else struct(nat, F32))
    outs += plan.outs() if plan else []
    scratch = [
        pltpu.VMEM((3 * width, rows), BF),
        pltpu.VMEM(tr, BF),
        pltpu.VMEM((3, width, width), BF),
        pltpu.VMEM(nat, F32),
        pltpu.VMEM(nat, F32),
        pltpu.VMEM(nat, F32),
        pltpu.VMEM(grad, BF),
        pltpu.SemaphoreType.DMA((16,)),
    ]
    if swapping:
        scratch += [pltpu.VMEM((2, rows // 2, width), BF)] + swap_scratch()
    return pl.pallas_call(
        functools.partial(project_back_kernel, plan, layer, swapping),
        in_specs=[ANY] * len(args),
        out_specs=[ANY] * len(outs),
        out_shape=outs,
        scratch_shapes=scratch + (plan.scratch() if plan else []),
        compiler_params=kernel_params(collective if plan or swapping else None),
        cost_estimate=pl.CostEstimate(flops=16 * 10**9, bytes_accessed=30 * 10**6, transcendentals=0),
        name=name,
    )(*args)


def turn_kernel(plan, upper, lower, *refs):
    refs = list(refs)
    take = lambda n: [refs.pop(0) for _ in range(n)]
    pg_in, xt_in, w_in, h_in, mg_in, act_t_in, mt_in, pre_in, mid_in, att_in = take(10)
    inputs = take(len(plan.args())) if plan else []
    dqkv_out, dff_out, mg_out, do_out = take(4)
    outputs = take(len(plan.outs())) if plan else []
    pg, xt, w, h, g, eg, dw, act_t, mt, pre, att, gb, dpre, do, dw_more, copy_sems = take(16)
    copies = Copies(copy_sems)
    width = xt.shape[0]
    shard = dw.shape[3]
    if plan:
        p = Place()
        greet(p, plan.signals(p), True)
        scatter, line = plan.open(p, inputs, outputs, refs, dw)
        for i in (0, 1):
            line.load(i).start()
    load_pg = copies.start(pg_in, pg)
    load_xt = copies.start(xt_in.at[upper], xt)
    load_w = [copies.start(w_in.at[6 * upper + (2, 0, 1)[unit]], w.at[unit]) for unit in range(3)]
    load_h = copies.start(h_in.at[upper], h)
    load_g = copies.start(mg_in, g)
    load_act, load_mt, load_pre, load_att = [
        copies.start(src.at[lower], dst)
        for src, dst in ((act_t_in, act_t), (mt_in, mt), (pre_in, pre), (att_in, att))
    ]

    def put(to, cols, value):
        for k in range(dw.shape[1]):
            for c in range(2):
                at = (2 * k + c) * shard
                to[k, c, :, cols] = value[at : at + shard].astype(BF)

    def weight_grad(unit):
        for cols in tiles(width):
            put(dw.at[unit], cols, dot(xt[...], pg[unit * width + cols.start : unit * width + cols.stop, :], 1, 1))
        if not plan or ("own", unit) not in plan.xy:
            copies.save(("dw", unit), dw.at[unit], dqkv_out.at[unit])

    load_pg.wait()
    load_xt.wait()
    if plan:
        for i in (0, 1):
            line.start(i)
    weight_grad(1)
    if plan:
        scatter.open(0)
    weight_grad(0)
    if plan:
        scatter.open(1)
        scatter.first(0)
    weight_grad(2)
    if plan:
        scatter.first(1)
    for load in load_w:
        load.wait()
    load_h.wait()
    r = rms(h[...])
    total = 0.0
    for cols in tiles(width):
        e = 0.0
        for unit in range(3):
            e = e + dot(pg[unit * width : (unit + 1) * width, :], w[unit, cols, :], 0, 1)
        eg[:, cols] = e
        total = total + jnp.sum(e * (h[:, cols] * r), axis=1, keepdims=True)
    total = total / width
    if plan:
        line.middle(0)
    load_w = [copies.start(w_in.at[6 * lower + 3 + unit], w.at[unit]) for unit in (2, 1, 0)]
    load_g.wait()
    for cols in tiles(width):
        v = g[:, cols] + r * (eg[:, cols] - h[:, cols] * r * total)
        g[:, cols] = v
        gb[:, cols] = v.astype(BF)
    load_mid = copies.start(mid_in.at[lower], h)
    if plan:
        scatter.second(0)

    load_act.wait()
    copies.ready(("dw", 2))
    for cols in tiles(width):
        put(dw.at[2], cols, dot(act_t[...], gb[:, cols], 1, 0))
    copies.save("dff", dw.at[2], dff_out.at[2])
    load_w[0].wait()
    load_pre.wait()
    if plan:
        line.middle(1)
        line.last(0)
    for cols in tiles(width):
        da = dot(gb[...], w[2, cols, :], 1, 1)
        v = pre[:, cols]
        s = 1.0 / (1.0 + jnp.exp(-v))
        dpre[:, cols] = (da * (s + v * s * (1.0 - s))).astype(BF)
    if plan:
        scatter.second(1)
    load_mt.wait()
    for cols in tiles(width):
        put(dw_more.at[0], cols, dot(mt[...], dpre[:, cols], 1, 0))
    copies.save("dff", dw_more.at[0], dff_out.at[1])
    load_w[1].wait()
    load_mid.wait()
    if plan:
        scatter.third(0)
        line.last(1)
    r = rms(h[...])
    total = 0.0
    for cols in tiles(width):
        e = dot(dpre[...], w[1, cols, :], 1, 1)
        eg[:, cols] = e
        total = total + jnp.sum(e * (h[:, cols] * r), axis=1, keepdims=True)
    total = total / width
    for cols in tiles(width):
        m = g[:, cols] + r * (eg[:, cols] - h[:, cols] * r * total)
        g[:, cols] = m
        gb[:, cols] = m.astype(BF)
    copies.save("g", g, mg_out)
    load_att.wait()
    for cols in tiles(width):
        put(dw_more.at[1], cols, dot(att[...], gb[:, cols], 1, 0))
    copies.save("dff", dw_more.at[1], dff_out.at[0])
    load_w[2].wait()
    for cols in tiles(width):
        do[cols, :] = dot(w[0, cols, :], gb[...], 1, 1).astype(BF)
    copies.save("do", do, do_out)
    if plan:
        scatter.third(1)
        for i in (0, 1):
            line.end(i)
        for i in (0, 1):
            line.drain(i)
            scatter.drain(i)
    copies.finish()


def turn(name, collective, upper, lower, pg, xt, w, h, mg, act_t, mt, pre, mid, att, chips, shard, plan):
    _, rows, width = h.shape
    nat, tr = (rows, width), (width, rows)
    grad = (3, chips, 2, shard, width)
    args = [pg, xt, w, h, mg, act_t, mt, pre, mid, att] + (plan.args() if plan else [])
    outs = [struct(grad), struct(grad), struct(nat, F32), struct(tr)] + (plan.outs() if plan else [])
    scratch = [
        pltpu.VMEM((3 * width, rows), BF),
        pltpu.VMEM(tr, BF),
        pltpu.VMEM((3, width, width), BF),
        pltpu.VMEM(nat, F32),
        pltpu.VMEM(nat, F32),
        pltpu.VMEM(nat, F32),
        pltpu.VMEM(grad, BF),
        pltpu.VMEM(tr, BF),
        pltpu.VMEM(tr, BF),
        pltpu.VMEM(nat, F32),
        pltpu.VMEM(tr, BF),
        pltpu.VMEM(nat, BF),
        pltpu.VMEM(nat, BF),
        pltpu.VMEM(tr, BF),
        pltpu.VMEM((2,) + grad[1:], BF),
        pltpu.SemaphoreType.DMA((24,)),
    ]
    return pl.pallas_call(
        functools.partial(turn_kernel, plan, upper, lower),
        in_specs=[ANY] * len(args),
        out_specs=[ANY] * len(outs),
        out_shape=outs,
        scratch_shapes=scratch + (plan.scratch() if plan else []),
        compiler_params=kernel_params(collective if plan else None),
        cost_estimate=pl.CostEstimate(flops=32 * 10**9, bytes_accessed=60 * 10**6, transcendentals=0),
        name=name,
    )(*args)


def local(nb, ns, inputs, lengths, wqkv, wout, wup, wdown, gain_attn, gain_mlp, cotangent):
    series, quarter, width = inputs.shape
    heads = width // HEAD_DIM
    rows = 2 * quarter
    shard = wout.shape[1]
    chips = nb // 2
    spread = nb == 8
    z = lax.axis_index("seq")
    core = lax.axis_index("batch") % 2

    other = lax.ppermute(
        lengths, AXES, [(b * ns + s, (b ^ 1) * ns + s) for b in range(nb) for s in range(ns)]
    )
    both = jnp.where(core == 0, jnp.concatenate([lengths, other]), jnp.concatenate([other, lengths]))
    which = jnp.where((z == 0) | (z == 3), 2, 0) + z // 2
    pad = SLOTS - lax.dynamic_index_in_dim(both, which, 0, keepdims=True)
    angle = (
        jnp.exp(jnp.arange(HALF, dtype=F32) * (-2.0 * math.log(10000.0) / HEAD_DIM))[:, None]
        * jnp.arange(SLOTS, dtype=F32)[None, :]
    )
    cos_all, sin_all = jnp.cos(angle), jnp.sin(angle)
    cos_pad = lax.dynamic_slice_in_dim(cos_all, pad[0], 1, axis=1)
    sin_pad = lax.dynamic_slice_in_dim(sin_all, pad[0], 1, axis=1)
    cos_four = (cos_all * cos_pad + sin_all * sin_pad).reshape(HALF, 4, quarter)
    sin_four = (sin_all * cos_pad - cos_all * sin_pad).reshape(HALF, 4, quarter)

    def pick(table):
        even = jnp.concatenate([table[:, 0], table[:, 3]], axis=1)
        odd = jnp.concatenate([table[:, 1], table[:, 2]], axis=1)
        return jnp.where(core == 0, even, odd), jnp.where(core == 0, odd, even)

    cos, cosx = pick(cos_four)
    sin, sinx = pick(sin_four)

    wqkv_g = (wqkv.astype(F32) * gain_attn.astype(F32)[:, :, None]).astype(BF)
    wup_g = (wup.astype(F32) * gain_mlp.astype(F32)[:, :, None]).astype(BF)

    stacked = (
        lambda array: array
        if spread
        else lax.all_gather(array, "batch", axis=1, tiled=True)
    )
    w_all, cot, hidden_0, hid_1, h_all, xt_all, qkv_all, kvx_all, att_all, lse_all, mid_all, mt_all, pre_all, act_all = forward(
        spread, 0, pad, cos, sin, inputs, cotangent, stacked(wqkv_g), stacked(wout), stacked(wup_g), stacked(wdown), shard
    )
    g = cot.reshape(rows, width)

    def plan(xy, xy_arrays, z, z_arrays):
        return Plan(xy, xy_arrays, z, z_arrays, shard, width) if spread else None

    tables = (cos, sin, cosx, sinx)
    ff_1, mg, do, *sums = feed_back(
        "feed_back", 4, 1, g, w_all, act_all, mt_all, pre_all, mid_all, att_all, chips, shard,
        plan([("own", 2)], [], [], []),
    )
    p_d1 = sums
    pg, hidden_1, *sums = attend_back(
        "attend_back_1", 5, 1, pad, qkv_all, kvx_all, do, att_all, lse_all[1], tables, hid_1,
        plan([(0, 1), (0, 0)], [ff_1], [], []),
    )
    p_uo1 = sums[0] if spread else None
    qkv_1, ff_0, mg, do, *sums = turn(
        "turn", 6, 1, 0, pg, xt_all, w_all, h_all, mg, act_all, mt_all, pre_all, mid_all, att_all, chips, shard,
        plan([("own", 1), ("own", 0)], [], [(0, 0), (0, 1)], [p_uo1]),
    )
    p_kq1, r_uo1 = sums if spread else (None, None)
    pg, *sums = attend_back(
        "attend_back_0", 8, 0, pad, qkv_all, kvx_all, do, att_all, lse_all[0], tables, None,
        plan([(0, 2), (1, 2)], [qkv_1, ff_0], [(0, 0), (0, 1), (1, 0)], [p_kq1, *p_d1]),
    )
    p_vd, r_kqd1 = sums if spread else (None, None)
    tail = project_back(
        "project_back", 9, 0, pg, xt_all, w_all, h_all, mg, chips, shard, True,
        plan(
            [(0, 1), (0, 0), ("own", 1), ("own", 2), ("own", 0)], [ff_0],
            [(0, 0), (0, 1)] + [("sum", i) for i in range(5)], [p_vd],
        ),
    )
    if spread:
        input_grad, r = tail
        s_qkv = [[r[6], r[4], r[5]], [r_kqd1[1], r_kqd1[0], r[0]]]
        s_ff = [[r[3], r[2], r[1]], [r_uo1[1], r_uo1[0], r_kqd1[2]]]
    else:
        qkv_0, input_grad = tail

        def over_all(grads):
            flat = grads.reshape(3, nb * shard, width)
            return lax.psum(lax.psum_scatter(flat, "batch", scatter_dimension=1, tiled=True), "seq")

        s_qkv = [over_all(qkv_0), over_all(qkv_1)]
        s_ff = [over_all(ff_0), over_all(ff_1)]
    input_grad = input_grad.astype(F32)
    hidden = [hidden_0, hidden_1]

    grad_qkv, grad_out, grad_up, grad_down, grad_ga, grad_gm = [], [], [], [], [], []
    for layer in range(LAYERS):
        ff = [part.astype(F32) for part in s_ff[layer]]
        qkv_sum = jnp.concatenate([part.astype(F32) for part in s_qkv[layer]], axis=1)
        grad_qkv.append(qkv_sum * gain_attn[layer].astype(F32)[:, None])
        grad_ga.append(jnp.sum(qkv_sum * wqkv[layer].astype(F32), axis=1))
        grad_out.append(ff[0])
        grad_up.append(ff[1] * gain_mlp[layer].astype(F32)[:, None])
        grad_gm.append(jnp.sum(ff[1] * wup[layer].astype(F32), axis=1))
        grad_down.append(ff[2])
    stack = jnp.stack
    return (
        stack(hidden), input_grad, stack(grad_qkv), stack(grad_out), stack(grad_up), stack(grad_down),
        stack(grad_ga), stack(grad_gm),
    )


def solution(mesh):
    nb, ns = mesh.shape["batch"], mesh.shape["seq"]
    rows = P("batch", "seq", None)
    weight = P(None, "batch", None)
    gain = P(None, "batch")
    return jax.shard_map(
        functools.partial(local, nb, ns),
        mesh=mesh,
        in_specs=(rows, P("batch"), weight, weight, weight, weight, gain, gain, rows),
        out_specs=(P(None, "batch", "seq", None), rows, weight, weight, weight, weight, gain, gain),
        check_vma=False,
    )
```

```python
import functools
import math

import jax
import jax.numpy as jnp
from jax import lax
from jax.experimental import pallas as pl
from jax.experimental.pallas import tpu as pltpu
from jax.sharding import PartitionSpec as P

HEAD_DIM = 80
HALF = HEAD_DIM // 2
LAYERS = 2
SLOTS = 1024
BF = jnp.bfloat16
F32 = jnp.float32
AXES = ("batch", "seq")
LOG2_SCALE = math.log2(math.e) / math.sqrt(HEAD_DIM)
NEG = -1e30
EPS = 1e-6
TILE = 256
MESH = pl.DeviceIdType.MESH
ANY = pl.BlockSpec(memory_space=pl.ANY)
VM = pl.BlockSpec(memory_space=pltpu.VMEM)
SM = pl.BlockSpec(memory_space=pltpu.SMEM)
GROUP = 4
LAG = 2
RATE = 2
DIRECT = (0, 1)
AHEAD = 2


def dot(a, b, i, j):
    return lax.dot_general(a, b, (((i,), (j,)), ((), ())), preferred_element_type=F32)


def struct(shape, dtype=BF):
    return jax.ShapeDtypeStruct(shape, dtype)


def tiles(extent):
    return [slice(at, at + TILE) for at in range(0, extent, TILE)]


class Place:
    def __init__(self):
        self.batch = lax.axis_index("batch")
        self.z = lax.axis_index("seq")
        self.core = self.batch % 2
        self.chip = self.batch // 2
        x = self.chip % 2
        y = (self.chip // 2) % 2
        self.to_x = 2 - 4 * x
        self.to_y = 4 - 8 * y
        self.x = self.batch + self.to_x
        self.y = self.batch + self.to_y
        self.diag = self.batch + self.to_x + self.to_y
        self.sibling = self.batch + 1 - 2 * self.core
        self.inner = (self.z == 1) | (self.z == 2)
        self.pair_z = self.z + 1 - 2 * (self.z % 2)
        self.owner = ((self.z + 1) // 2) % 2
        self.part = self.z // 2

    def id(self, batch):
        return (batch, self.z)

    def workers(self):
        return [
            (2 * self.chip + self.owner, (1 - self.core) * (1 + j) + self.core * 3 * j) for j in (0, 1)
        ]

    def holders(self):
        return [(2 * self.chip + 1 - self.owner, at) for at in (self.core, 3 - self.core)]


def greet(place, signals, line=False):
    barrier = pltpu.get_barrier_semaphore()
    for device in signals:
        pl.semaphore_signal(barrier, inc=1, device_id=device, device_id_type=MESH)
    if line:
        pl.semaphore_signal(barrier, inc=1, device_id=(place.batch, place.pair_z), device_id_type=MESH)

        @pl.when(place.inner)
        def _():
            pl.semaphore_signal(barrier, inc=1, device_id=(place.batch, 3 - place.z), device_id_type=MESH)

        pl.semaphore_wait(barrier, len(signals) + 1 + place.part + place.z % 2 - 2 * place.part * (place.z % 2))
    else:
        pl.semaphore_wait(barrier, len(signals))


class Swap:
    PIECES = 8

    def __init__(self, place, to_workers, src, landing, send, recv):
        self.src, self.landing, self.send, self.recv = src, landing, send, recv
        self.to = place.workers() if to_workers else place.holders()
        self.came_from = place.holders() if to_workers else place.workers()
        self.part = place.part
        self.sent = 0

    def copy(self, k, piece, part):
        count = self.src.shape[1] // self.PIECES
        rows = pl.ds(piece * count, count)
        return remote(
            self.src.at[k, rows], self.landing.at[part, rows], self.send.at[k, piece], self.recv.at[part, piece],
            self.to[k],
        )

    def start(self, pieces=PIECES):
        for _ in range(pieces):
            if self.sent < self.PIECES:
                for k in (0, 1):
                    self.copy(k, self.sent, self.part).start()
                self.sent += 1

    def arrive(self):
        for piece in range(self.PIECES):
            for k in (0, 1):
                self.copy(k, piece, k).wait_recv()

    def drain(self):
        for piece in range(self.PIECES):
            for k in (0, 1):
                self.copy(k, piece, self.part).wait_send()


def swap_scratch():
    return [pltpu.SemaphoreType.DMA((2, Swap.PIECES)), pltpu.SemaphoreType.DMA((2, Swap.PIECES))]


def remote(src, dst, send_sem, recv_sem, device):
    return pltpu.make_async_remote_copy(
        src_ref=src, dst_ref=dst, send_sem=send_sem, recv_sem=recv_sem, device_id=device,
        device_id_type=MESH,
    )


class Gather:
    SEMS = 13

    def __init__(self, place, spread, shards, full, slots, direct, send, recv, local):
        self.place, self.spread, self.direct = place, spread, direct
        self.shards, self.full, self.slots = shards, full, slots
        self.send, self.recv, self.local = send, recv, local
        self.stage = {}

    def rows(self, unit, index, start=0, count=None):
        size = self.shards[unit].shape[0]
        count = size if count is None else count
        return self.full.at[self.slots[unit], pl.ds(pl.multiple_of(index * size + start, 16), count)]

    def span(self, unit):
        size = self.shards[unit].shape[0]
        if unit in self.direct:
            return 0, 0, size
        hz = self.place.z % 2
        return hz * (size // 2), (1 - hz) * (size // 2), size // 2

    def cut(self, unit):
        _, _, half = self.span(unit)
        small = half // 32 * 16
        return small if unit % 2 else half - small

    def copy(self, unit, k):
        p = self.place
        near, far, half = self.span(unit)
        cut = self.cut(unit)
        src = self.shards[unit]
        whole = lambda index: self.rows(unit, index)
        x_part = lambda index, at: self.rows(unit, index, at, cut)
        y_part = lambda index, at: self.rows(unit, index, at + cut, half - cut)
        dst, to = (
            lambda: (whole(p.batch), p.id(p.x)),
            lambda: (whole(p.batch), p.id(p.y)),
            lambda: (whole(p.batch), p.id(p.sibling)),
            lambda: (x_part(p.y, near), p.id(p.x)),
            lambda: (y_part(p.x, near), p.id(p.y)),
            lambda: (whole(p.x), p.id(p.sibling)),
            lambda: (whole(p.y), p.id(p.sibling)),
            lambda: (x_part(p.diag, near), p.id(p.sibling)),
            lambda: (y_part(p.diag, near), p.id(p.sibling)),
            lambda: (x_part(p.diag, near), (p.batch, p.pair_z)),
            lambda: (y_part(p.diag, near), (p.batch, p.pair_z)),
            lambda: (x_part(p.diag, far), p.id(p.sibling)),
            lambda: (y_part(p.diag, far), p.id(p.sibling)),
        )[k]()
        return remote(src if k < 3 else dst, dst, self.send.at[unit, k], self.recv.at[unit, k], to)

    def own(self, unit):
        dst = self.rows(unit, self.place.batch) if self.spread else self.full.at[self.slots[unit]]
        return pltpu.make_async_copy(self.shards[unit], dst, self.local.at[unit])

    def at_stage(self, unit, stage):
        if self.stage.get(unit, 0) >= stage:
            return False
        assert self.stage.get(unit, 0) == stage - 1
        self.stage[unit] = stage
        return self.spread

    def open(self, unit):
        self.own(unit).start()
        if self.at_stage(unit, 1):
            for k in (0, 1, 2):
                self.copy(unit, k).start()

    def relay(self, unit):
        if self.at_stage(unit, 2):
            self.copy(unit, 0).wait_recv()
            self.copy(unit, 1).wait_recv()
            for k in (3, 4, 5, 6):
                self.copy(unit, k).start()

    def share(self, unit):
        if self.at_stage(unit, 3):
            for k in (3, 4):
                self.copy(unit, k).wait_recv()
                if unit not in self.direct:
                    self.copy(unit, k + 6).start()
                self.copy(unit, k + 4).start()

    def pass_on(self, unit):
        if self.at_stage(unit, 4) and unit not in self.direct:
            for k in (9, 10):
                self.arrival(unit, k).wait_recv()
                self.copy(unit, k + 2).start()

    def arrival(self, unit, k):
        p = self.place
        _, far, half = self.span(unit)
        cut = self.cut(unit)
        start, count = ((far, cut), (far + cut, half - cut))[k - 9]
        dst = self.rows(unit, p.diag, start, count)
        return remote(dst, dst, self.send.at[unit, k], self.recv.at[unit, k], (p.batch, p.pair_z))

    def need(self, unit):
        self.relay(unit)
        self.share(unit)
        self.pass_on(unit)
        self.own(unit).wait()
        if self.spread:
            for k in (2, 5, 6, 7, 8) + (() if unit in self.direct else (11, 12)):
                self.copy(unit, k).wait_recv()

    def drain(self, unit):
        if self.spread:
            for k in range(9 if unit in self.direct else self.SEMS):
                self.copy(unit, k).wait_send()


class Scatter:
    SEMS = 7

    def __init__(self, place, grads, out, keep, got_core, got_x, got_y, last_x, last_y, send, recv, local):
        self.p, self.grads, self.out = place, grads, out
        self.room, self.got_core = keep, got_core
        self.got_x, self.got_y, self.last_x, self.last_y = got_x, got_y, last_x, last_y
        self.send, self.recv, self.local = send, recv, local
        p = place
        self.chip_x = p.x // 2
        self.chip_y = p.y // 2
        self.chip_d = p.diag // 2

    def keep(self, unit):
        far, near = self.grads[unit]
        if far is None:
            return near.at[:, self.p.core]
        return self.room.at[unit]

    def piece(self, unit, chip, part):
        half = self.last_x.shape[1]
        return self.keep(unit).at[chip, pl.ds(part * half, half)]

    def copy(self, unit, k):
        p = self.p
        src, dst, to = (
            lambda: (self.source(unit).at[:, 1 - p.core], self.got_core.at[unit], p.sibling),
            lambda: (self.piece(unit, self.chip_x, 0), self.got_x.at[unit, 0], p.x),
            lambda: (self.piece(unit, self.chip_d, 0), self.got_x.at[unit, 1], p.x),
            lambda: (self.piece(unit, self.chip_y, 1), self.got_y.at[unit, 0], p.y),
            lambda: (self.piece(unit, self.chip_d, 1), self.got_y.at[unit, 1], p.y),
            lambda: (self.piece(unit, self.chip_y, 0), self.last_y.at[unit], p.y),
            lambda: (self.piece(unit, self.chip_x, 1), self.last_x.at[unit], p.x),
        )[k]()
        return remote(src, dst, self.send.at[unit, k], self.recv.at[unit, k], p.id(to))

    def source(self, unit):
        far, near = self.grads[unit]
        return near if far is None else far

    def load(self, unit):
        return pltpu.make_async_copy(self.grads[unit][0].at[:, self.p.core], self.room.at[unit], self.local.at[unit, 0])

    def store(self, unit):
        return pltpu.make_async_copy(self.keep(unit).at[self.p.chip], self.out.at[unit], self.local.at[unit, 1])

    def open(self, unit):
        self.copy(unit, 0).start()
        if self.grads[unit][0] is not None:
            self.load(unit).start()

    def add(self, ref, other):
        ref[...] = (ref[...].astype(F32) + other[...].astype(F32)).astype(BF)

    def first(self, unit):
        if self.grads[unit][0] is not None:
            self.load(unit).wait()
        self.copy(unit, 0).wait_recv()
        self.add(self.keep(unit), self.got_core.at[unit])
        for k in (1, 2, 3, 4):
            self.copy(unit, k).start()

    def second(self, unit):
        p = self.p
        self.copy(unit, 2).wait_recv()
        self.add(self.piece(unit, self.chip_y, 0), self.got_x.at[unit, 1])
        self.copy(unit, 5).start()
        self.copy(unit, 4).wait_recv()
        self.add(self.piece(unit, self.chip_x, 1), self.got_y.at[unit, 1])
        self.copy(unit, 6).start()
        self.copy(unit, 1).wait_recv()
        self.add(self.piece(unit, p.chip, 0), self.got_x.at[unit, 0])
        self.copy(unit, 3).wait_recv()
        self.add(self.piece(unit, p.chip, 1), self.got_y.at[unit, 0])

    def third(self, unit):
        p = self.p
        self.copy(unit, 5).wait_recv()
        self.add(self.piece(unit, p.chip, 0), self.last_y.at[unit])
        self.copy(unit, 6).wait_recv()
        self.add(self.piece(unit, p.chip, 1), self.last_x.at[unit])
        if self.out is not None:
            self.store(unit).start()

    def drain(self, unit):
        for k in range(self.SEMS):
            self.copy(unit, k).wait_send()
        if self.out is not None:
            self.store(unit).wait()


def scatter_scratch(units, loaded, shard, width):
    half = shard // 2
    return [
        pltpu.VMEM((max(loaded, 1), 4, shard, width) if loaded else (1, 1, 16, width), BF),
        pltpu.VMEM((units, 4, shard, width), BF),
        pltpu.VMEM((units, 2, half, width), BF),
        pltpu.VMEM((units, 2, half, width), BF),
        pltpu.VMEM((units, half, width), BF),
        pltpu.VMEM((units, half, width), BF),
        pltpu.SemaphoreType.DMA((units, Scatter.SEMS)),
        pltpu.SemaphoreType.DMA((units, Scatter.SEMS)),
        pltpu.SemaphoreType.DMA((units, 2)),
    ]


class Line:
    def __init__(self, place, shares, out, mine, got, other, send, recv, local):
        self.p, self.shares, self.out = place, shares, out
        self.room, self.got, self.other = mine, got, other
        self.send, self.recv, self.local = send, recv, local

    def copy(self, item, half, k):
        p = self.p
        size = self.got.shape[1] // 2
        part = lambda ref: ref.at[pl.ds(half * size, size)]
        mine, got, other = self.mine(item), self.got.at[item], self.other.at[item]
        src, dst, to_z = ((mine, got, p.pair_z), (mine, other, 3 - p.z), (got, got, p.pair_z))[k]
        at = 3 * half + k
        return remote(part(src), part(dst), self.send.at[item, at], self.recv.at[item, at], (p.batch, to_z))

    def mine(self, item):
        far, near = self.shares[item]
        return self.room.at[item] if near is None else near

    def part(self, ref, half):
        size = self.got.shape[1] // 2
        return ref.at[pl.ds(half * size, size)]

    def load(self, item):
        return pltpu.make_async_copy(self.shares[item][0], self.room.at[item], self.local.at[item, 0])

    def store(self, item):
        return pltpu.make_async_copy(self.got.at[item], self.out.at[item], self.local.at[item, 1])

    def start(self, item):
        if self.shares[item][0] is not None:
            self.load(item).wait()

        @pl.when(jnp.logical_not(self.p.inner))
        def _():
            for half in (0, 1):
                self.copy(item, half, 0).start()

    def middle(self, item):
        @pl.when(self.p.inner)
        def _():
            for half in (0, 1):
                mine = self.part(self.mine(item), half)
                got = self.part(self.got.at[item], half)
                self.copy(item, half, 0).wait_recv()
                mine[...] = (mine[...].astype(F32) + got[...].astype(F32)).astype(BF)
                self.copy(item, half, 1).start()

    def last(self, item):
        @pl.when(self.p.inner)
        def _():
            for half in (0, 1):
                mine = self.part(self.mine(item), half)
                got = self.part(self.got.at[item], half)
                other = self.part(self.other.at[item], half)
                self.copy(item, half, 1).wait_recv()
                got[...] = (mine[...].astype(F32) + other[...].astype(F32)).astype(BF)
                self.copy(item, half, 2).start()

    def end(self, item):
        @pl.when(jnp.logical_not(self.p.inner))
        def _():
            for half in (0, 1):
                self.copy(item, half, 2).wait_recv()

        self.store(item).start()

    def drain(self, item):
        @pl.when(self.p.inner)
        def _():
            for half in (0, 1):
                self.copy(item, half, 1).wait_send()
                self.copy(item, half, 2).wait_send()

        @pl.when(jnp.logical_not(self.p.inner))
        def _():
            for half in (0, 1):
                self.copy(item, half, 0).wait_send()

        self.store(item).wait()


def line_scratch(items, loaded, shard, width):
    return [
        pltpu.VMEM((loaded, shard, width) if loaded else (1, 16, width), BF),
        pltpu.VMEM((items, shard, width), BF),
        pltpu.VMEM((items, shard, width), BF),
        pltpu.SemaphoreType.DMA((items, 6)),
        pltpu.SemaphoreType.DMA((items, 6)),
        pltpu.SemaphoreType.DMA((items, 2)),
    ]


class Plan:
    def __init__(self, xy, xy_arrays, z, z_arrays, shard, width):
        self.xy, self.xy_arrays, self.z, self.z_arrays = xy, xy_arrays, z, z_arrays
        self.shard, self.width = shard, width
        self.keep_sums = bool(xy) and not any(src == "sum" for src, _ in z)

    def args(self):
        return [*self.xy_arrays, *self.z_arrays]

    def outs(self):
        out = []
        if self.keep_sums:
            out.append(struct((len(self.xy), self.shard, self.width)))
        if self.z:
            out.append(struct((len(self.z), self.shard, self.width)))
        return out

    def scratch(self):
        loaded = sum(src != "own" for src, _ in self.xy)
        shares = sum(src != "sum" for src, _ in self.z)
        return (scatter_scratch(len(self.xy), loaded, self.shard, self.width) if self.xy else []) + (
            line_scratch(len(self.z), shares, self.shard, self.width) if self.z else []
        )

    def signals(self, p):
        return [p.id(p.sibling), p.id(p.x), p.id(p.y)] if self.xy else []

    def open(self, p, inputs, outputs, scratch, own=None):
        outputs, scratch = list(outputs), list(scratch)
        arrays = inputs[: len(self.xy_arrays)]
        shares = inputs[len(self.xy_arrays) :]
        sums_out = outputs.pop(0) if self.keep_sums else None
        scatter = line = None
        if self.xy:
            grads = [
                (None, own.at[unit]) if src == "own" else (arrays[src].at[unit], None) for src, unit in self.xy
            ]
            scatter = Scatter(p, grads, sums_out, *scratch[:9])
            scratch = scratch[9:]
        if self.z:
            items = [
                (None, scatter.keep(i).at[p.chip]) if src == "sum" else (shares[src].at[i], None)
                for src, i in self.z
            ]
            line = Line(p, items, outputs.pop(0), *scratch)
        return scatter, line


def kernel_params(collective):
    params = dict(vmem_limit_bytes=63 * 2**20)
    if collective is not None:
        params.update(collective_id=collective, has_side_effects=True)
    return pltpu.CompilerParams(**params)


def rms(rows):
    return lax.rsqrt(jnp.mean(rows * rows, axis=-1, keepdims=True) + EPS)


def key_blocks(core):
    if core == 0:
        return [(0, [("o", 0, 0)]), (1, [("o", 0, 0), ("x", 0, 1), ("x", 1, 2), ("o", 1, 3)])]
    return [(0, [("x", 0, 0), ("o", 0, 1)]), (1, [("x", 0, 0), ("o", 0, 1), ("o", 1, 2)])]


def masked(scores, quarter, diagonal, pad):
    size = scores.shape[0]
    key = lax.broadcasted_iota(jnp.int32, scores.shape, 0)
    ok = key >= pad - quarter * size
    if diagonal:
        query = lax.broadcasted_iota(jnp.int32, scores.shape, 1)
        ok = ((key <= query) & ok) | (key == query)
    return jnp.where(ok, scores, NEG)


def attend_heads(core, base, pad, qkv, kvx, o_ref, lse_ref):
    width, rows = o_ref.shape
    size = rows // 2
    at = lambda off, hh: pl.ds(pl.multiple_of(off * width + (base + hh) * HEAD_DIM, 16), HEAD_DIM)
    for hh in range(GROUP):
        for block, keys in key_blocks(core):
            cols = slice(block * size, block * size + size)
            q = qkv[at(0, hh), cols]
            scores = []
            for i, (src, half, quarter) in enumerate(keys):
                span = slice(half * size, half * size + size)
                k = qkv[at(1, hh), span] if src == "o" else kvx[at(0, hh), span]
                scores.append(masked(dot(k, q, 0, 0), quarter, i == len(keys) - 1, pad))
            top = functools.reduce(jnp.maximum, [jnp.max(s, axis=0, keepdims=True) for s in scores])
            total = 0.0
            out = 0.0
            for s, (src, half, quarter) in zip(scores, keys):
                span = slice(half * size, half * size + size)
                v = qkv[at(2, hh), span] if src == "o" else kvx[at(1, hh), span]
                weight = jnp.exp2((s - top) * LOG2_SCALE)
                total = total + jnp.sum(weight, axis=0, keepdims=True)
                out = out + dot(v, weight.astype(BF), 1, 0)
            o_ref[at(0, hh), cols] = (out * (1.0 / total)).astype(BF)
            lse_ref[base // GROUP, hh : hh + 1, cols] = top * LOG2_SCALE + jnp.log2(total)


class Copies:
    def __init__(self, sems):
        self.sems, self.used, self.open = sems, 0, {}

    def start(self, src, dst):
        copy = pltpu.make_async_copy(src, dst, self.sems.at[self.used])
        self.used += 1
        copy.start()
        return copy

    def save(self, name, src, dst):
        self.open.setdefault(name, []).append(self.start(src, dst))

    def ready(self, *names):
        for name in names:
            for copy in self.open.pop(name, []):
                copy.wait()

    def finish(self):
        self.ready(*list(self.open))


def forward_kernel(spread, *refs):
    refs = list(refs)
    take = lambda n: [refs.pop(0) for _ in range(n)]
    pad_ref, cos, sin, rows_in, cot_in, wqkv, wout, wup, wdown = take(9)
    (w_out, cot_out, hid0_out, hid1_out, h_out, xt_out, qkv_out, kvx_out, att_out, lse_out, mid_out, mt_out, pre_out,
     act_out) = take(14)
    (full, g_send, g_recv, g_local, qkv, kvx, h, att, lse, mid, xhat, tp, tq, act, rows_buf, x_send, x_recv, s_send, s_recv,
     free, copy_sems) = refs
    p = Place()
    width = xhat.shape[1]
    rows = xhat.shape[0]
    quarter = rows // 2
    groups = width // (HEAD_DIM * GROUP)
    copies = Copies(copy_sems)
    swap_in = Swap(p, True, rows_in, rows_buf, s_send.at[0], s_recv.at[0])
    swap_cot = Swap(p, True, cot_in, cot_out, s_send.at[1], s_recv.at[1])
    swap_hid = Swap(p, False, rows_buf, hid0_out, s_send.at[2], s_recv.at[2])
    others = [p.id(p.x), p.id(p.y), p.id(p.sibling), (p.batch, p.pair_z)] if spread else [p.id(p.sibling)]
    greet(p, others + swap_in.came_from + swap_hid.came_from)
    shards = []
    for layer in range(LAYERS):
        shards += [wqkv.at[layer, :, pl.ds(u * width, width)] for u in (1, 2, 0)]
        shards += [w.at[layer] for w in (wout, wup, wdown)]
    units = len(shards)
    room = full.shape[0]
    slots = [unit % room for unit in range(units)]
    gather = Gather(p, spread, shards, full, slots, DIRECT, g_send, g_recv, g_local)

    moving = []

    def release():
        for unit in range(units - room):
            gather.drain(unit)
            copies.ready(("w", unit))
        if spread:
            for k, device in enumerate(others):
                pl.semaphore_signal(free.at[k], inc=1, device_id=device, device_id_type=MESH)

    def tick(unit):
        gather.relay(unit)
        if unit + AHEAD < units:
            if unit + AHEAD == room and spread:
                for k in range(len(others)):
                    pl.semaphore_wait(free.at[k], 1)
            gather.open(unit + AHEAD)
        if unit:
            gather.share(unit - 1)
        if unit >= LAG:
            gather.pass_on(unit - LAG)
        for swap in moving:
            swap.start(RATE)

    def need(unit):
        gather.need(unit)
        copies.save(("w", unit), full.at[slots[unit]], w_out.at[unit])

    swap_in.start()
    for unit in range(AHEAD):
        gather.open(unit)
    tick(0)
    swap_in.arrive()
    for k in (0, 1):
        h[k * quarter : (k + 1) * quarter, :] = rows_buf[k].astype(F32)
    pad = pad_ref[0]

    for layer in range(LAYERS):
        base = 6 * layer
        copies.save("h", h, h_out.at[layer])
        copies.ready("tp", "tq")
        xhat[...] = (h[...] * rms(h[...])).astype(BF)
        tp[...] = xhat[...].T
        copies.save("tp", tp, xt_out.at[layer])
        copies.ready("qkv")
        if layer == 0:
            tick(1)
            tick(2)

        def exchange(k):
            return remote(
                qkv.at[pl.ds((1 + k) * width, width)], kvx.at[layer, pl.ds(k * width, width)],
                x_send.at[layer, k], x_recv.at[layer, k], p.id(p.sibling),
            )

        for i, part in enumerate((1, 2, 0)):
            need(base + i)
            step = 8 * HEAD_DIM
            for at in range(0, width, step):
                y = dot(xhat[...], full[slots[base + i], :, at : at + step], 1, 0).T
                for head in range(0, step, HEAD_DIM):
                    to = part * width + at + head
                    if part == 2:
                        qkv[to : to + HEAD_DIM, :] = y[head : head + HEAD_DIM].astype(BF)
                    else:
                        a, b = y[head : head + HALF], y[head + HALF : head + HEAD_DIM]
                        qkv[to : to + HEAD_DIM, :] = jnp.concatenate(
                            [a * cos[...] - b * sin[...], b * cos[...] + a * sin[...]], axis=0
                        ).astype(BF)
            if i < 2:
                exchange(i).start()
                tick(base + 3 + i)
        copies.save("qkv", qkv, qkv_out.at[layer])
        if layer == 0:
            moving.append(swap_cot)
        for k in (0, 1):
            exchange(k).wait_recv()
        copies.save("kvx", kvx.at[layer], kvx_out.at[layer])
        copies.ready("att", "lse")

        def body(group, carry):
            for core in (0, 1):
                pl.when(p.core == core)(
                    functools.partial(attend_heads, core, group * GROUP, pad, qkv, kvx.at[layer], att, lse)
                )

            @pl.when(group == 1)
            def _():
                tick(base + 5)

            return carry

        lax.fori_loop(0, groups, body, 0)
        if layer == 0:
            release()
        if layer == 0:
            tick(base + 6)
        copies.save("att", att, att_out.at[layer])
        copies.save("lse", lse, lse_out.at[layer])
        for k in (0, 1):
            exchange(k).wait_send()
        copies.ready("mid")
        if layer == LAYERS - 1:
            gather.pass_on(units - 2)
            gather.share(units - 1)
        need(base + 3)
        square = 0.0
        for cols in tiles(width):
            m = h[:, cols] + dot(att[...], full[slots[base + 3], :, cols], 0, 0)
            mid[:, cols] = m
            square = square + jnp.sum(m * m, axis=1, keepdims=True)
        copies.save("mid", mid, mid_out.at[layer])
        scale = lax.rsqrt(square / width + EPS)
        for cols in tiles(width):
            m = (mid[:, cols] * scale).astype(BF)
            xhat[:, cols] = m
            tq[cols, :] = m.T
        copies.save("tq", tq, mt_out.at[layer])
        if layer == LAYERS - 1:
            gather.pass_on(units - 1)
        need(base + 4)
        copies.ready("h", "tp")
        for cols in tiles(width):
            v = dot(xhat[...], full[slots[base + 4], :, cols], 1, 0)
            h[:, cols] = v
            a = (v / (1.0 + jnp.exp(-v))).astype(BF)
            act[:, cols] = a
            tp[cols, :] = a.T
        copies.save("pre", h, pre_out.at[layer])
        copies.save("tp", tp, act_out.at[layer])
        last = layer == LAYERS - 1
        if not last:
            tick(base + 7)
        need(base + 5)
        copies.ready("pre")
        if last:
            swap_hid.start()
            swap_hid.drain()
        for cols in tiles(width):
            v = mid[:, cols] + dot(act[...], full[slots[base + 5], :, cols], 1, 0)
            if not last:
                h[:, cols] = v
            for k in (0, 1):
                rows_buf[k, :, cols] = v[k * quarter : (k + 1) * quarter].astype(BF)
        if last:
            copies.save("hid", rows_buf, hid1_out)
        else:
            moving.append(swap_hid)
            tick(base + 8)
    for unit in range(units - room, units):
        gather.drain(unit)
    for swap in moving:
        swap.start()
    swap_in.drain()
    swap_cot.arrive()
    swap_cot.drain()
    swap_hid.arrive()
    copies.finish()


def forward(spread, collective, pad, cos, sin, inputs, cotangent, wqkv, wout, wup, wdown, shard):
    _, quarter, width = inputs.shape
    rows = 2 * quarter
    groups = width // (HEAD_DIM * GROUP)
    nat, tr = (rows, width), (width, rows)
    lse = (groups, GROUP, rows)
    two = lambda shape, dtype=BF: struct((LAYERS,) + shape, dtype)
    units = 6 * LAYERS
    room = units - 3
    swapped = struct((2, quarter, width))
    outs = [
        struct((units, width, width)), swapped, swapped, swapped, two(nat, F32), two(tr), two((3 * width, rows)),
        two((2 * width, rows)), two(tr), two(lse, F32), two(nat, F32), two(tr), two(nat, F32), two(tr),
    ]
    scratch = [
        pltpu.VMEM((room, width, width), BF),
        pltpu.SemaphoreType.DMA((units, Gather.SEMS)),
        pltpu.SemaphoreType.DMA((units, Gather.SEMS)),
        pltpu.SemaphoreType.DMA((units,)),
        pltpu.VMEM((3 * width, rows), BF),
        pltpu.VMEM((LAYERS, 2 * width, rows), BF),
        pltpu.VMEM(nat, F32),
        pltpu.VMEM(tr, BF),
        pltpu.VMEM(lse, F32),
        pltpu.VMEM(nat, F32),
        pltpu.VMEM(nat, BF),
        pltpu.VMEM(tr, BF),
        pltpu.VMEM(tr, BF),
        pltpu.VMEM(nat, BF),
        pltpu.VMEM((2, quarter, width), BF),
        pltpu.SemaphoreType.DMA((LAYERS, 2)),
        pltpu.SemaphoreType.DMA((LAYERS, 2)),
        pltpu.SemaphoreType.DMA((3, 2, Swap.PIECES)),
        pltpu.SemaphoreType.DMA((3, 2, Swap.PIECES)),
        pltpu.SemaphoreType.REGULAR((4,)),
        pltpu.SemaphoreType.DMA((units + 10 * LAYERS + 2,)),
    ]
    return pl.pallas_call(
        functools.partial(forward_kernel, spread),
        in_specs=[SM, VM, VM] + [ANY] * 6,
        out_specs=[ANY] * len(outs),
        out_shape=outs,
        scratch_shapes=scratch,
        compiler_params=kernel_params(collective),
        cost_estimate=pl.CostEstimate(flops=180 * 10**9, bytes_accessed=100 * 10**6, transcendentals=0),
        name="forward",
    )(pad, cos, sin, inputs, cotangent, wqkv, wout, wup, wdown)


def feed_back_kernel(plan, layer, *refs):
    refs = list(refs)
    take = lambda n: [refs.pop(0) for _ in range(n)]
    g_in, w_in, *held = take(7)
    act_t_in, mt_in, pre_in, mid_in, att_in = [ref.at[layer] for ref in held]
    inputs = take(len(plan.args())) if plan else []
    dw_out, mg_out, do_out = take(3)
    outputs = take(len(plan.outs())) if plan else []
    g, w, act_t, mt, pre, mid, att, gb, dpre, eg, do, dw, copy_sems = take(13)
    copies = Copies(copy_sems)
    width = w.shape[1]
    shard = dw.shape[3]
    if plan:
        p = Place()
        greet(p, plan.signals(p), bool(plan.z))
        scatter, line = plan.open(p, inputs, outputs, refs, dw)
        if line:
            line.load(0).start()
        if plan.xy[0][0] != "own":
            scatter.open(0)
    load_g = copies.start(g_in, gb if g_in.dtype == BF else g)
    load_act = copies.start(act_t_in, act_t)
    load_w = [copies.start(w_in.at[6 * layer + 5], w.at[2])]
    load_pre = copies.start(pre_in, pre)
    load_mt = copies.start(mt_in, mt)
    load_w += [copies.start(w_in.at[6 * layer + 4], w.at[1])]
    load_mid = copies.start(mid_in, mid)
    load_att = copies.start(att_in, att)
    load_w += [copies.start(w_in.at[6 * layer + 3], w.at[0])]

    def put(unit, cols, value):
        for k in range(dw.shape[1]):
            for c in range(2):
                at = (2 * k + c) * shard
                dw[unit, k, c, :, cols] = value[at : at + shard].astype(BF)

    load_g.wait()
    if g_in.dtype == BF:
        g[...] = gb[...].astype(F32)
    else:
        gb[...] = g[...].astype(BF)
    load_act.wait()
    for cols in tiles(width):
        put(2, cols, dot(act_t[...], gb[:, cols], 1, 0))
    if plan and plan.xy[0][0] == "own":
        scatter.open(0)
    else:
        copies.save("dw", dw.at[2], dw_out.at[2])
    if plan:
        if line:
            line.start(0)
    load_w[0].wait()
    load_pre.wait()
    for cols in tiles(width):
        da = dot(gb[...], w[2, cols, :], 1, 1)
        v = pre[:, cols]
        s = 1.0 / (1.0 + jnp.exp(-v))
        dpre[:, cols] = (da * (s + v * s * (1.0 - s))).astype(BF)
    if plan:
        scatter.first(0)
    load_mt.wait()
    for cols in tiles(width):
        put(1, cols, dot(mt[...], dpre[:, cols], 1, 0))
    copies.save("dw", dw.at[1], dw_out.at[1])
    load_w[1].wait()
    load_mid.wait()
    r = rms(mid[...])
    total = 0.0
    for cols in tiles(width):
        e = dot(dpre[...], w[1, cols, :], 1, 1)
        eg[:, cols] = e
        total = total + jnp.sum(e * (mid[:, cols] * r), axis=1, keepdims=True)
    total = total / width
    if plan and line:
        line.middle(0)
    for cols in tiles(width):
        m = g[:, cols] + r * (eg[:, cols] - mid[:, cols] * r * total)
        g[:, cols] = m
        gb[:, cols] = m.astype(BF)
    copies.save("g", g, mg_out)
    load_att.wait()
    for cols in tiles(width):
        put(0, cols, dot(att[...], gb[:, cols], 1, 0))
    copies.save("dw", dw.at[0], dw_out.at[0])
    load_w[2].wait()
    if plan:
        scatter.second(0)
        if line:
            line.last(0)
    for cols in tiles(width):
        do[cols, :] = dot(w[0, cols, :], gb[...], 1, 1).astype(BF)
    copies.save("do", do, do_out)
    if plan:
        scatter.third(0)
        if line:
            line.end(0)
            line.drain(0)
        scatter.drain(0)
    copies.finish()


def feed_back(name, collective, layer, g, w, act_t, mt, pre, mid, att, chips, shard, plan):
    _, width, rows = act_t.shape
    nat, tr = (rows, width), (width, rows)
    grad = (3, chips, 2, shard, width)
    args = [g, w, act_t, mt, pre, mid, att] + (plan.args() if plan else [])
    outs = [struct(grad), struct(nat, F32), struct(tr)] + (plan.outs() if plan else [])
    return pl.pallas_call(
        functools.partial(feed_back_kernel, plan, layer),
        in_specs=[ANY] * len(args),
        out_specs=[ANY] * len(outs),
        out_shape=outs,
        scratch_shapes=[
            pltpu.VMEM(nat, F32),
            pltpu.VMEM((3, width, width), BF),
            pltpu.VMEM(tr, BF),
            pltpu.VMEM(tr, BF),
            pltpu.VMEM(nat, F32),
            pltpu.VMEM(nat, F32),
            pltpu.VMEM(tr, BF),
            pltpu.VMEM(nat, BF),
            pltpu.VMEM(nat, BF),
            pltpu.VMEM(nat, F32),
            pltpu.VMEM(tr, BF),
            pltpu.VMEM(grad, BF),
            pltpu.SemaphoreType.DMA((16,)),
        ] + (plan.scratch() if plan else []),
        compiler_params=kernel_params(collective if plan else None),
        cost_estimate=pl.CostEstimate(flops=16 * 10**9, bytes_accessed=30 * 10**6, transcendentals=0),
        name=name,
    )(*args)


def unrotate(t, cos, sin):
    a, b = t[:HALF], t[HALF:]
    return jnp.concatenate([a * cos + b * sin, b * cos - a * sin], axis=0)


def attend_back_heads(core, base, pad, qkv, kvx, do, o, lse, tables, dqkv, dkvx):
    width, rows = o.shape
    size = rows // 2
    scale = 1.0 / math.sqrt(HEAD_DIM)
    cos, sin, cosx, sinx = tables
    at = lambda off, hh: pl.ds(pl.multiple_of(off * width + (base + hh) * HEAD_DIM, 16), HEAD_DIM)
    for hh in range(GROUP):
        dk, dv = {}, {}
        for block, keys in key_blocks(core):
            cols = slice(block * size, block * size + size)
            q = qkv[at(0, hh), cols]
            d_out = do[at(0, hh), cols]
            delta = jnp.sum(d_out.astype(F32) * o[at(0, hh), cols].astype(F32), axis=0, keepdims=True)
            norm = lse[base // GROUP, hh : hh + 1, cols]
            dq = 0.0
            for i, (src, half, quarter) in enumerate(keys):
                span = slice(half * size, half * size + size)
                k = qkv[at(1, hh), span] if src == "o" else kvx[at(0, hh), span]
                v = qkv[at(2, hh), span] if src == "o" else kvx[at(1, hh), span]
                s = masked(dot(k, q, 0, 0), quarter, i == len(keys) - 1, pad)
                weight = jnp.exp2(s * LOG2_SCALE - norm)
                ds = (weight * (dot(v, d_out, 0, 0) - delta)).astype(BF)
                dq = dq + dot(k, ds, 1, 0)
                a, b = dot(q, ds, 1, 1), dot(d_out, weight.astype(BF), 1, 1)
                key = (src, half)
                dk[key] = dk[key] + a if key in dk else a
                dv[key] = dv[key] + b if key in dv else b
            dqkv[at(0, hh), cols] = unrotate(dq * scale, cos[:, cols], sin[:, cols]).astype(BF)
        for src, ref, k_off, ct, st in (("o", dqkv, 1, cos, sin), ("x", dkvx, 0, cosx, sinx)):
            for half in (0, 1):
                span = slice(half * size, half * size + size)
                if (src, half) in dk:
                    a = unrotate(dk[src, half] * scale, ct[:, span], st[:, span]).astype(BF)
                    b = dv[src, half].astype(BF)
                else:
                    a = b = jnp.zeros((HEAD_DIM, size), BF)
                ref[at(k_off, hh), span] = a
                ref[at(k_off + 1, hh), span] = b


def attend_back_kernel(plan, layer, swapping, *refs):
    refs = list(refs)
    take = lambda n: [refs.pop(0) for _ in range(n)]
    pad_ref, qkv_in, kvx_in, do_in, att_in, lse, cos, sin, cosx, sinx = take(10)
    qkv_in, kvx_in, att_in = qkv_in.at[layer], kvx_in.at[layer], att_in.at[layer]
    hid_in = take(1)[0] if swapping else None
    inputs = take(len(plan.args())) if plan else []
    pg_out = take(1)[0]
    swap_out = take(1)[0] if swapping else None
    outputs = take(len(plan.outs())) if plan else []
    qkv, kvx, do, att, dqkv, dkvx, got, x_send, x_recv, copy_sems = take(10)
    p = Place()
    copies = Copies(copy_sems)
    signals = [p.id(p.sibling)]
    if plan:
        signals = plan.signals(p)
    if swapping:
        swap = Swap(p, False, hid_in, swap_out, *take(2))
        signals = signals + swap.came_from
    greet(p, signals, bool(plan and plan.z))
    if swapping:
        swap.start()
    loads = [copies.start(a, b) for a, b in ((qkv_in, qkv), (kvx_in, kvx), (do_in, do), (att_in, att))]
    units = items = 0
    if plan:
        scatter, line = plan.open(p, inputs, outputs, refs)
        units, items = len(plan.xy), len(plan.z)
        for i in range(units):
            scatter.open(i)
        for i in range(items):
            line.load(i).start()
        for i in range(items):
            line.start(i)
    for load in loads:
        load.wait()
    for i in range(units):
        scatter.first(i)
    pad = pad_ref[0]
    width = att.shape[0]
    span = GROUP * HEAD_DIM
    groups = width // span

    def exchange(group, k):
        part = pl.ds(pl.multiple_of(k * width + group * span, 16), span)
        return remote(dkvx.at[part], got.at[part], x_send.at[group, k], x_recv.at[group, k], p.id(p.sibling))

    def body(group, carry):
        for core in (0, 1):
            pl.when(p.core == core)(
                functools.partial(
                    attend_back_heads, core, group * GROUP, pad, qkv, kvx, do, att, lse,
                    (cos, sin, cosx, sinx), dqkv, dkvx,
                )
            )
        for k in (0, 1):
            exchange(group, k).start()
        after = [[], [], []]
        if units:
            after[1] += [(scatter.second, 0)]
            after[2] += [(scatter.second, i) for i in range(1, units)]
        if items:
            after[0] += [(line.middle, 0)]
            after[1] += [(line.middle, i) for i in range(1, min(items, 2))] + [(line.last, 0)]
            after[2] += [(line.middle, i) for i in range(2, items)] + [(line.last, i) for i in range(1, min(items, 2))]
        for at, steps in enumerate(after):

            @pl.when(group == at)
            def _(steps=steps):
                for step, i in steps:
                    step(i)

        return carry

    lax.fori_loop(0, groups, body, 0)
    for group in range(groups):
        for k in (0, 1):
            exchange(group, k).wait_recv()
    own = dqkv.at[pl.ds(width, 2 * width)]
    own[...] = (own[...].astype(F32) + got[...].astype(F32)).astype(BF)
    copies.save("dqkv", dqkv, pg_out)
    for i in range(units):
        scatter.third(i)
    for i in range(2, items):
        line.last(i)
    for i in range(items):
        line.end(i)
    for i in range(items):
        line.drain(i)
    for i in range(units):
        scatter.drain(i)
    for group in range(groups):
        for k in (0, 1):
            exchange(group, k).wait_send()
    if swapping:
        swap.arrive()
        swap.drain()
    copies.finish()


def attend_back(name, collective, layer, pad, qkv, kvx, do, att, lse, tables, hid, plan):
    _, width, rows = att.shape
    swapping = hid is not None
    args = [pad, qkv, kvx, do, att, lse, *tables] + ([hid] if swapping else []) + (plan.args() if plan else [])
    specs = [SM] + [ANY] * 4 + [VM] * 5 + [ANY] * (len(args) - 10)
    outs = [struct((3 * width, rows))]
    if swapping:
        outs.append(struct(hid.shape))
    outs += plan.outs() if plan else []
    scratch = [
        pltpu.VMEM((3 * width, rows), BF),
        pltpu.VMEM((2 * width, rows), BF),
        pltpu.VMEM((width, rows), BF),
        pltpu.VMEM((width, rows), BF),
        pltpu.VMEM((3 * width, rows), BF),
        pltpu.VMEM((2 * width, rows), BF),
        pltpu.VMEM((2 * width, rows), BF),
        pltpu.SemaphoreType.DMA((lse.shape[0], 2)),
        pltpu.SemaphoreType.DMA((lse.shape[0], 2)),
        pltpu.SemaphoreType.DMA((16,)),
    ]
    if swapping:
        scratch += swap_scratch()
    return pl.pallas_call(
        functools.partial(attend_back_kernel, plan, layer, swapping),
        in_specs=specs,
        out_specs=[ANY] * len(outs),
        out_shape=outs,
        scratch_shapes=scratch + (plan.scratch() if plan else []),
        compiler_params=kernel_params(collective),
        cost_estimate=pl.CostEstimate(flops=35 * 10**9, bytes_accessed=30 * 10**6, transcendentals=0),
        name=name,
    )(*args)


def project_back_kernel(plan, layer, swapping, *refs):
    refs = list(refs)
    take = lambda n: [refs.pop(0) for _ in range(n)]
    pg_in, xt_in, w_in, h_in, mg_in = take(5)
    xt_in, h_in = xt_in.at[layer], h_in.at[layer]
    inputs = take(len(plan.args())) if plan else []
    dw_out = None if swapping and plan else take(1)[0]
    g_out = take(1)[0]
    outputs = take(len(plan.outs())) if plan else []
    pg, xt, w, h, g, eg, dw, copy_sems = take(8)
    gb = take(1)[0] if swapping else None
    swap_sems = take(2) if swapping else None
    copies = Copies(copy_sems)
    width = xt.shape[0]
    quarter = xt.shape[1] // 2
    shard = dw.shape[3]
    p = Place()
    signals = plan.signals(p) if plan else []
    if swapping:
        swap = Swap(p, False, gb, g_out, *swap_sems)
        signals = signals + swap.came_from
    if signals:
        greet(p, signals, bool(plan and plan.z))
    load_pg = copies.start(pg_in, pg)
    load_xt = copies.start(xt_in, xt)
    held = earlier = shares = 0
    scatter = line = None
    if plan:
        scatter, line = plan.open(p, inputs, outputs, refs, dw)
        held = len(plan.xy)
        earlier = sum(src != "own" for src, _ in plan.xy)
        shares = sum(src != "sum" for src, _ in plan.z)
    for i in range(earlier):
        scatter.open(i)
    for i in range(shares):
        line.load(i).start()
    load_w = [copies.start(w_in.at[6 * layer + (2, 0, 1)[unit]], w.at[unit]) for unit in range(3)]
    load_h = copies.start(h_in, h)
    load_g = copies.start(mg_in, g)
    load_pg.wait()
    load_xt.wait()
    for i in range(shares):
        line.start(i)
    for i in range(min(earlier, 1)):
        scatter.first(i)

    def weight_grad(unit):
        for cols in tiles(width):
            value = dot(xt[...], pg[unit * width + cols.start : unit * width + cols.stop, :], 1, 1)
            for k in range(dw.shape[1]):
                for c in range(2):
                    at = (2 * k + c) * shard
                    dw[unit, k, c, :, cols] = value[at : at + shard].astype(BF)
        if dw_out is not None and not (plan and ("own", unit) in plan.xy):
            copies.save("dw", dw.at[unit], dw_out.at[unit])

    own = earlier
    weight_grad(1)
    for i in range(1, earlier):
        scatter.first(i)
    if own < held:
        scatter.open(own)
    weight_grad(2)
    if own < held:
        scatter.first(own)
    for i in range(shares):
        line.middle(i)
    if own + 1 < held:
        scatter.open(own + 1)
    weight_grad(0)
    if own + 2 < held:
        scatter.open(own + 2)
    for i in range(min(earlier, 1)):
        scatter.second(i)
    for load in load_w:
        load.wait()
    load_h.wait()
    r = rms(h[...])
    total = 0.0
    for n, cols in enumerate(tiles(width)):
        e = 0.0
        for unit in range(3):
            e = e + dot(pg[unit * width : (unit + 1) * width, :], w[unit, cols, :], 0, 1)
        eg[:, cols] = e
        total = total + jnp.sum(e * (h[:, cols] * r), axis=1, keepdims=True)
        if n == 1:
            for i in range(1, earlier):
                scatter.second(i)
        if n == 2 and own + 1 < held:
            scatter.first(own + 1)
        if n == 3:
            for i in range(shares):
                line.last(i)
    total = total / width
    load_g.wait()
    for cols in tiles(width):
        v = g[:, cols] + r * (eg[:, cols] - h[:, cols] * r * total)
        if swapping:
            for k in (0, 1):
                gb[k, :, cols] = v[k * quarter : (k + 1) * quarter].astype(BF)
        else:
            g[:, cols] = v
    if swapping:
        swap.start()
    else:
        copies.save("g", g, g_out)
    chain = bool(plan) and len(plan.z) > shares
    for i in range(own + 2, held):
        scatter.first(i)
    for i in range(earlier):
        scatter.third(i)
    steps = [[] for _ in range(held + 6)]
    for i in range(held):
        if i >= earlier:
            steps[i].append(functools.partial(scatter.second, i))
            steps[i + 1].append(functools.partial(scatter.third, i))
        if chain:
            j = shares + i
            base = i + 1
            steps[base].append(functools.partial(line.start, j))
            steps[base + 1].append(functools.partial(line.middle, j))
            steps[base + 2].append(functools.partial(line.last, j))
            steps[base + 3].append(functools.partial(line.end, j))
    for group in steps:
        for step in group:
            step()
    for i in range(shares):
        line.end(i)
    for i in range(len(plan.z) if plan else 0):
        line.drain(i)
    for i in range(held):
        scatter.drain(i)
    if swapping:
        swap.arrive()
        swap.drain()
    copies.finish()


def project_back(name, collective, layer, pg, xt, w, h, mg, chips, shard, swapping, plan):
    _, rows, width = h.shape
    nat, tr = (rows, width), (width, rows)
    grad = (3, chips, 2, shard, width)
    args = [pg, xt, w, h, mg] + (plan.args() if plan else [])
    outs = [] if swapping and plan else [struct(grad)]
    outs.append(struct((2, rows // 2, width)) if swapping else struct(nat, F32))
    outs += plan.outs() if plan else []
    scratch = [
        pltpu.VMEM((3 * width, rows), BF),
        pltpu.VMEM(tr, BF),
        pltpu.VMEM((3, width, width), BF),
        pltpu.VMEM(nat, F32),
        pltpu.VMEM(nat, F32),
        pltpu.VMEM(nat, F32),
        pltpu.VMEM(grad, BF),
        pltpu.SemaphoreType.DMA((16,)),
    ]
    if swapping:
        scratch += [pltpu.VMEM((2, rows // 2, width), BF)] + swap_scratch()
    return pl.pallas_call(
        functools.partial(project_back_kernel, plan, layer, swapping),
        in_specs=[ANY] * len(args),
        out_specs=[ANY] * len(outs),
        out_shape=outs,
        scratch_shapes=scratch + (plan.scratch() if plan else []),
        compiler_params=kernel_params(collective if plan or swapping else None),
        cost_estimate=pl.CostEstimate(flops=16 * 10**9, bytes_accessed=30 * 10**6, transcendentals=0),
        name=name,
    )(*args)


def turn_kernel(plan, upper, lower, *refs):
    refs = list(refs)
    take = lambda n: [refs.pop(0) for _ in range(n)]
    pg_in, xt_in, w_in, h_in, mg_in, act_t_in, mt_in, pre_in, mid_in, att_in = take(10)
    inputs = take(len(plan.args())) if plan else []
    dqkv_out, dff_out, mg_out, do_out = take(4)
    outputs = take(len(plan.outs())) if plan else []
    pg, xt, w, h, g, eg, dw, act_t, mt, pre, att, gb, dpre, do, dw_more, copy_sems = take(16)
    copies = Copies(copy_sems)
    width = xt.shape[0]
    shard = dw.shape[3]
    if plan:
        p = Place()
        greet(p, plan.signals(p), True)
        scatter, line = plan.open(p, inputs, outputs, refs, dw)
        for i in (0, 1):
            line.load(i).start()
    load_pg = copies.start(pg_in, pg)
    load_xt = copies.start(xt_in.at[upper], xt)
    load_w = [copies.start(w_in.at[6 * upper + (2, 0, 1)[unit]], w.at[unit]) for unit in range(3)]
    load_h = copies.start(h_in.at[upper], h)
    load_g = copies.start(mg_in, g)
    load_act, load_mt, load_pre, load_att = [
        copies.start(src.at[lower], dst)
        for src, dst in ((act_t_in, act_t), (mt_in, mt), (pre_in, pre), (att_in, att))
    ]

    def put(to, cols, value):
        for k in range(dw.shape[1]):
            for c in range(2):
                at = (2 * k + c) * shard
                to[k, c, :, cols] = value[at : at + shard].astype(BF)

    def weight_grad(unit):
        for cols in tiles(width):
            put(dw.at[unit], cols, dot(xt[...], pg[unit * width + cols.start : unit * width + cols.stop, :], 1, 1))
        if not plan or ("own", unit) not in plan.xy:
            copies.save(("dw", unit), dw.at[unit], dqkv_out.at[unit])

    load_pg.wait()
    load_xt.wait()
    if plan:
        for i in (0, 1):
            line.start(i)
    weight_grad(1)
    if plan:
        scatter.open(0)
    weight_grad(0)
    if plan:
        scatter.open(1)
        scatter.first(0)
    weight_grad(2)
    if plan:
        scatter.first(1)
    for load in load_w:
        load.wait()
    load_h.wait()
    r = rms(h[...])
    total = 0.0
    for n, cols in enumerate(tiles(width)):
        if plan and n == 3:
            line.middle(0)
        e = 0.0
        for unit in range(3):
            e = e + dot(pg[unit * width : (unit + 1) * width, :], w[unit, cols, :], 0, 1)
        eg[:, cols] = e
        total = total + jnp.sum(e * (h[:, cols] * r), axis=1, keepdims=True)
    total = total / width
    load_w = [copies.start(w_in.at[6 * lower + 3 + unit], w.at[unit]) for unit in (2, 1, 0)]
    load_g.wait()
    for cols in tiles(width):
        v = g[:, cols] + r * (eg[:, cols] - h[:, cols] * r * total)
        g[:, cols] = v
        gb[:, cols] = v.astype(BF)
    load_mid = copies.start(mid_in.at[lower], h)
    if plan:
        scatter.second(0)

    load_act.wait()
    copies.ready(("dw", 2))
    for cols in tiles(width):
        put(dw.at[2], cols, dot(act_t[...], gb[:, cols], 1, 0))
    copies.save("dff", dw.at[2], dff_out.at[2])
    load_w[0].wait()
    load_pre.wait()
    if plan:
        line.middle(1)
        line.last(0)
    for cols in tiles(width):
        da = dot(gb[...], w[2, cols, :], 1, 1)
        v = pre[:, cols]
        s = 1.0 / (1.0 + jnp.exp(-v))
        dpre[:, cols] = (da * (s + v * s * (1.0 - s))).astype(BF)
    if plan:
        scatter.second(1)
    load_mt.wait()
    for cols in tiles(width):
        put(dw_more.at[0], cols, dot(mt[...], dpre[:, cols], 1, 0))
    copies.save("dff", dw_more.at[0], dff_out.at[1])
    load_w[1].wait()
    load_mid.wait()
    if plan:
        line.last(1)
        scatter.third(0)
    r = rms(h[...])
    total = 0.0
    for cols in tiles(width):
        e = dot(dpre[...], w[1, cols, :], 1, 1)
        eg[:, cols] = e
        total = total + jnp.sum(e * (h[:, cols] * r), axis=1, keepdims=True)
    total = total / width
    for cols in tiles(width):
        m = g[:, cols] + r * (eg[:, cols] - h[:, cols] * r * total)
        g[:, cols] = m
        gb[:, cols] = m.astype(BF)
    copies.save("g", g, mg_out)
    load_att.wait()
    for cols in tiles(width):
        put(dw_more.at[1], cols, dot(att[...], gb[:, cols], 1, 0))
    copies.save("dff", dw_more.at[1], dff_out.at[0])
    load_w[2].wait()
    for cols in tiles(width):
        do[cols, :] = dot(w[0, cols, :], gb[...], 1, 1).astype(BF)
    copies.save("do", do, do_out)
    if plan:
        scatter.third(1)
        for i in (0, 1):
            line.end(i)
        for i in (0, 1):
            line.drain(i)
            scatter.drain(i)
    copies.finish()


def turn(name, collective, upper, lower, pg, xt, w, h, mg, act_t, mt, pre, mid, att, chips, shard, plan):
    _, rows, width = h.shape
    nat, tr = (rows, width), (width, rows)
    grad = (3, chips, 2, shard, width)
    args = [pg, xt, w, h, mg, act_t, mt, pre, mid, att] + (plan.args() if plan else [])
    outs = [struct(grad), struct(grad), struct(nat, F32), struct(tr)] + (plan.outs() if plan else [])
    scratch = [
        pltpu.VMEM((3 * width, rows), BF),
        pltpu.VMEM(tr, BF),
        pltpu.VMEM((3, width, width), BF),
        pltpu.VMEM(nat, F32),
        pltpu.VMEM(nat, F32),
        pltpu.VMEM(nat, F32),
        pltpu.VMEM(grad, BF),
        pltpu.VMEM(tr, BF),
        pltpu.VMEM(tr, BF),
        pltpu.VMEM(nat, F32),
        pltpu.VMEM(tr, BF),
        pltpu.VMEM(nat, BF),
        pltpu.VMEM(nat, BF),
        pltpu.VMEM(tr, BF),
        pltpu.VMEM((2,) + grad[1:], BF),
        pltpu.SemaphoreType.DMA((24,)),
    ]
    return pl.pallas_call(
        functools.partial(turn_kernel, plan, upper, lower),
        in_specs=[ANY] * len(args),
        out_specs=[ANY] * len(outs),
        out_shape=outs,
        scratch_shapes=scratch + (plan.scratch() if plan else []),
        compiler_params=kernel_params(collective if plan else None),
        cost_estimate=pl.CostEstimate(flops=32 * 10**9, bytes_accessed=60 * 10**6, transcendentals=0),
        name=name,
    )(*args)


def finish_kernel(places, *refs):
    count = len(places[0][0])
    refs = list(refs)
    take = lambda n: [refs.pop(0) for _ in range(n)]
    sums = take(3)
    wqkv, wup, gain_attn, gain_mlp, moved, hidden_0, hidden_1 = take(7)
    hid_out, in_out, qkv_out, out_out, up_out, down_out, ga, gm = take(8)
    grad_in, qkv, out, up, down, sems = refs
    copies = Copies(sems)
    copies.save("hid", hidden_0, hid_out.at[0])
    copies.save("hid", hidden_1, hid_out.at[1])
    grad_in[...] = moved[...].astype(F32)
    copies.save("in", grad_in, in_out)
    width = out.shape[2]
    get = lambda place: sums[place[0]][place[1]].astype(F32)
    for layer, (thirds, (out_at, up_at, down_at)) in enumerate(places):
        gain = gain_attn[layer]
        total = 0.0
        for part in range(count):
            cols = slice(part * width, part * width + width)
            value = get(thirds[part])
            qkv[layer, :, cols] = value * gain
            total = total + jnp.sum(value * wqkv[layer, :, cols].astype(F32), axis=1, keepdims=True)
        ga[layer] = total
        copies.save("qkv", qkv.at[layer], qkv_out.at[layer])
        out[layer] = get(out_at)
        copies.save("out", out.at[layer], out_out.at[layer])
        value = get(up_at)
        up[layer] = value * gain_mlp[layer]
        gm[layer] = jnp.sum(value * wup[layer].astype(F32), axis=1, keepdims=True)
        copies.save("up", up.at[layer], up_out.at[layer])
        down[layer] = get(down_at)
        copies.save("down", down.at[layer], down_out.at[layer])
    copies.finish()


def finish(places, sums, wqkv, wup, gain_attn, gain_mlp, moved, hidden_0, hidden_1):
    layers, shard, width = wup.shape
    grad = (layers, shard, width)
    wide = (layers, shard, 3 * width)
    column = (layers, shard, 1)
    return pl.pallas_call(
        functools.partial(finish_kernel, places),
        in_specs=[VM] * 10,
        out_specs=[ANY] * 6 + [VM] * 2,
        out_shape=[
            struct((layers,) + hidden_0.shape), struct(moved.shape, F32), struct(wide, F32), struct(grad, F32),
            struct(grad, F32), struct(grad, F32), struct(column, F32), struct(column, F32),
        ],
        scratch_shapes=[
            pltpu.VMEM(moved.shape, F32),
            pltpu.VMEM(wide, F32),
            pltpu.VMEM(grad, F32),
            pltpu.VMEM(grad, F32),
            pltpu.VMEM(grad, F32),
            pltpu.SemaphoreType.DMA((16,)),
        ],
        compiler_params=kernel_params(None),
        cost_estimate=pl.CostEstimate(flops=10**8, bytes_accessed=25 * 10**6, transcendentals=0),
        name="finish",
    )(*sums, wqkv, wup, gain_attn, gain_mlp, moved, hidden_0, hidden_1)


def local(nb, ns, inputs, lengths, wqkv, wout, wup, wdown, gain_attn, gain_mlp, cotangent):
    series, quarter, width = inputs.shape
    heads = width // HEAD_DIM
    rows = 2 * quarter
    shard = wout.shape[1]
    chips = nb // 2
    spread = nb == 8
    z = lax.axis_index("seq")
    core = lax.axis_index("batch") % 2

    other = lax.ppermute(
        lengths, AXES, [(b * ns + s, (b ^ 1) * ns + s) for b in range(nb) for s in range(ns)]
    )
    both = jnp.where(core == 0, jnp.concatenate([lengths, other]), jnp.concatenate([other, lengths]))
    which = jnp.where((z == 0) | (z == 3), 2, 0) + z // 2
    pad = SLOTS - lax.dynamic_index_in_dim(both, which, 0, keepdims=True)
    angle = (
        jnp.exp(jnp.arange(HALF, dtype=F32) * (-2.0 * math.log(10000.0) / HEAD_DIM))[:, None]
        * jnp.arange(SLOTS, dtype=F32)[None, :]
    )
    cos_all, sin_all = jnp.cos(angle), jnp.sin(angle)
    cos_pad = lax.dynamic_slice_in_dim(cos_all, pad[0], 1, axis=1)
    sin_pad = lax.dynamic_slice_in_dim(sin_all, pad[0], 1, axis=1)
    cos_four = (cos_all * cos_pad + sin_all * sin_pad).reshape(HALF, 4, quarter)
    sin_four = (sin_all * cos_pad - cos_all * sin_pad).reshape(HALF, 4, quarter)

    def pick(table):
        even = jnp.concatenate([table[:, 0], table[:, 3]], axis=1)
        odd = jnp.concatenate([table[:, 1], table[:, 2]], axis=1)
        return jnp.where(core == 0, even, odd), jnp.where(core == 0, odd, even)

    cos, cosx = pick(cos_four)
    sin, sinx = pick(sin_four)

    wqkv_g = (wqkv.astype(F32) * gain_attn.astype(F32)[:, :, None]).astype(BF)
    wup_g = (wup.astype(F32) * gain_mlp.astype(F32)[:, :, None]).astype(BF)

    stacked = (
        lambda array: array
        if spread
        else lax.all_gather(array, "batch", axis=1, tiled=True)
    )
    w_all, cot, hidden_0, hid_1, h_all, xt_all, qkv_all, kvx_all, att_all, lse_all, mid_all, mt_all, pre_all, act_all = forward(
        spread, 0, pad, cos, sin, inputs, cotangent, stacked(wqkv_g), stacked(wout), stacked(wup_g), stacked(wdown), shard
    )
    g = cot.reshape(rows, width)

    def plan(xy, xy_arrays, z, z_arrays):
        return Plan(xy, xy_arrays, z, z_arrays, shard, width) if spread else None

    tables = (cos, sin, cosx, sinx)
    ff_1, mg, do, *sums = feed_back(
        "feed_back", 4, 1, g, w_all, act_all, mt_all, pre_all, mid_all, att_all, chips, shard,
        plan([("own", 2)], [], [], []),
    )
    p_d1 = sums
    pg, hidden_1, *sums = attend_back(
        "attend_back_1", 5, 1, pad, qkv_all, kvx_all, do, att_all, lse_all[1], tables, hid_1,
        plan([(0, 1), (0, 0)], [ff_1], [], []),
    )
    p_uo1 = sums[0] if spread else None
    qkv_1, ff_0, mg, do, *sums = turn(
        "turn", 6, 1, 0, pg, xt_all, w_all, h_all, mg, act_all, mt_all, pre_all, mid_all, att_all, chips, shard,
        plan([("own", 1), ("own", 0)], [], [(0, 0), (0, 1)], [p_uo1]),
    )
    p_kq1, r_uo1 = sums if spread else (None, None)
    pg, *sums = attend_back(
        "attend_back_0", 8, 0, pad, qkv_all, kvx_all, do, att_all, lse_all[0], tables, None,
        plan([(0, 2), (1, 2)], [qkv_1, ff_0], [(0, 0), (0, 1), (1, 0)], [p_kq1, *p_d1]),
    )
    p_vd, r_kqd1 = sums if spread else (None, None)
    tail = project_back(
        "project_back", 9, 0, pg, xt_all, w_all, h_all, mg, chips, shard, True,
        plan(
            [(0, 1), (0, 0), ("own", 1), ("own", 2), ("own", 0)], [ff_0],
            [(0, 0), (0, 1)] + [("sum", i) for i in range(5)], [p_vd],
        ),
    )
    if spread:
        input_grad, r = tail
        places = (
            (((0, 6), (0, 4), (0, 5)), ((0, 3), (0, 2), (0, 1))),
            (((1, 1), (1, 0), (0, 0)), ((2, 1), (2, 0), (1, 2))),
        )
        column = lambda gain: gain.astype(F32)[:, :, None]
        *grads, grad_ga, grad_gm = finish(
            places, (r, r_kqd1, r_uo1), wqkv, wup, column(gain_attn), column(gain_mlp), input_grad, hidden_0, hidden_1
        )
        return (*grads, grad_ga[:, :, 0], grad_gm[:, :, 0])
    qkv_0, input_grad = tail

    def over_all(grads):
        flat = grads.reshape(3, nb * shard, width)
        return lax.psum(lax.psum_scatter(flat, "batch", scatter_dimension=1, tiled=True), "seq")

    s_qkv = [over_all(qkv_0), over_all(qkv_1)]
    s_ff = [over_all(ff_0), over_all(ff_1)]
    input_grad = input_grad.astype(F32)
    hidden = [hidden_0, hidden_1]

    grad_qkv, grad_out, grad_up, grad_down, grad_ga, grad_gm = [], [], [], [], [], []
    for layer in range(LAYERS):
        ff = [part.astype(F32) for part in s_ff[layer]]
        qkv_sum = jnp.concatenate([part.astype(F32) for part in s_qkv[layer]], axis=1)
        grad_qkv.append(qkv_sum * gain_attn[layer].astype(F32)[:, None])
        grad_ga.append(jnp.sum(qkv_sum * wqkv[layer].astype(F32), axis=1))
        grad_out.append(ff[0])
        grad_up.append(ff[1] * gain_mlp[layer].astype(F32)[:, None])
        grad_gm.append(jnp.sum(ff[1] * wup[layer].astype(F32), axis=1))
        grad_down.append(ff[2])
    stack = jnp.stack
    return (
        stack(hidden), input_grad, stack(grad_qkv), stack(grad_out), stack(grad_up), stack(grad_down),
        stack(grad_ga), stack(grad_gm),
    )


def solution(mesh):
    nb, ns = mesh.shape["batch"], mesh.shape["seq"]
    rows = P("batch", "seq", None)
    weight = P(None, "batch", None)
    gain = P(None, "batch")
    return jax.shard_map(
        functools.partial(local, nb, ns),
        mesh=mesh,
        in_specs=(rows, P("batch"), weight, weight, weight, weight, gain, gain, rows),
        out_specs=(P(None, "batch", "seq", None), rows, weight, weight, weight, weight, gain, gain),
        check_vma=False,
    )
```

```python
import functools
import math

import jax
import jax.numpy as jnp
from jax import lax
from jax.experimental import pallas as pl
from jax.experimental.pallas import tpu as pltpu
from jax.sharding import PartitionSpec as P

HEAD_DIM = 80
HALF = HEAD_DIM // 2
LAYERS = 2
SLOTS = 1024
BF = jnp.bfloat16
F32 = jnp.float32
AXES = ("batch", "seq")
LOG2_SCALE = math.log2(math.e) / math.sqrt(HEAD_DIM)
NEG = -1e30
EPS = 1e-6
TILE = 256
MESH = pl.DeviceIdType.MESH
ANY = pl.BlockSpec(memory_space=pl.ANY)
VM = pl.BlockSpec(memory_space=pltpu.VMEM)
SM = pl.BlockSpec(memory_space=pltpu.SMEM)
GROUP = 4
LAG = 2
RATE = 2
DIRECT = (0, 1, 2, 10, 11)
AHEAD = 2


def dot(a, b, i, j):
    return lax.dot_general(a, b, (((i,), (j,)), ((), ())), preferred_element_type=F32)


def struct(shape, dtype=BF):
    return jax.ShapeDtypeStruct(shape, dtype)


def tiles(extent):
    return [slice(at, at + TILE) for at in range(0, extent, TILE)]


class Place:
    def __init__(self):
        self.batch = lax.axis_index("batch")
        self.z = lax.axis_index("seq")
        self.core = self.batch % 2
        self.chip = self.batch // 2
        x = self.chip % 2
        y = (self.chip // 2) % 2
        self.to_x = 2 - 4 * x
        self.to_y = 4 - 8 * y
        self.x = self.batch + self.to_x
        self.y = self.batch + self.to_y
        self.diag = self.batch + self.to_x + self.to_y
        self.sibling = self.batch + 1 - 2 * self.core
        self.inner = (self.z == 1) | (self.z == 2)
        self.pair_z = self.z + 1 - 2 * (self.z % 2)
        self.owner = ((self.z + 1) // 2) % 2
        self.part = self.z // 2

    def id(self, batch):
        return (batch, self.z)

    def workers(self):
        return [
            (2 * self.chip + self.owner, (1 - self.core) * (1 + j) + self.core * 3 * j) for j in (0, 1)
        ]

    def holders(self):
        return [(2 * self.chip + 1 - self.owner, at) for at in (self.core, 3 - self.core)]


def greet(place, signals, line=False):
    barrier = pltpu.get_barrier_semaphore()
    for device in signals:
        pl.semaphore_signal(barrier, inc=1, device_id=device, device_id_type=MESH)
    if line:
        pl.semaphore_signal(barrier, inc=1, device_id=(place.batch, place.pair_z), device_id_type=MESH)

        @pl.when(place.inner)
        def _():
            pl.semaphore_signal(barrier, inc=1, device_id=(place.batch, 3 - place.z), device_id_type=MESH)

        pl.semaphore_wait(barrier, len(signals) + 1 + place.part + place.z % 2 - 2 * place.part * (place.z % 2))
    else:
        pl.semaphore_wait(barrier, len(signals))


class Swap:
    PIECES = 8

    def __init__(self, place, to_workers, src, landing, send, recv):
        self.src, self.landing, self.send, self.recv = src, landing, send, recv
        self.to = place.workers() if to_workers else place.holders()
        self.came_from = place.holders() if to_workers else place.workers()
        self.part = place.part
        self.sent = 0

    def copy(self, k, piece, part):
        count = self.src.shape[1] // self.PIECES
        rows = pl.ds(piece * count, count)
        return remote(
            self.src.at[k, rows], self.landing.at[part, rows], self.send.at[k, piece], self.recv.at[part, piece],
            self.to[k],
        )

    def start(self, pieces=PIECES):
        for _ in range(pieces):
            if self.sent < self.PIECES:
                for k in (0, 1):
                    self.copy(k, self.sent, self.part).start()
                self.sent += 1

    def arrive(self):
        for piece in range(self.PIECES):
            for k in (0, 1):
                self.copy(k, piece, k).wait_recv()

    def drain(self):
        for piece in range(self.PIECES):
            for k in (0, 1):
                self.copy(k, piece, self.part).wait_send()


def swap_scratch():
    return [pltpu.SemaphoreType.DMA((2, Swap.PIECES)), pltpu.SemaphoreType.DMA((2, Swap.PIECES))]


def remote(src, dst, send_sem, recv_sem, device):
    return pltpu.make_async_remote_copy(
        src_ref=src, dst_ref=dst, send_sem=send_sem, recv_sem=recv_sem, device_id=device,
        device_id_type=MESH,
    )


class Gather:
    SEMS = 13

    def __init__(self, place, spread, shards, full, slots, direct, send, recv, local):
        self.place, self.spread, self.direct = place, spread, direct
        self.shards, self.full, self.slots = shards, full, slots
        self.send, self.recv, self.local = send, recv, local
        self.stage = {}

    def rows(self, unit, index, start=0, count=None):
        size = self.shards[unit].shape[0]
        count = size if count is None else count
        return self.full.at[self.slots[unit], pl.ds(pl.multiple_of(index * size + start, 16), count)]

    def span(self, unit):
        size = self.shards[unit].shape[0]
        if unit in self.direct:
            return 0, 0, size
        hz = self.place.z % 2
        return hz * (size // 2), (1 - hz) * (size // 2), size // 2

    def cut(self, unit):
        _, _, half = self.span(unit)
        small = half // 32 * 16
        return small if unit % 2 else half - small

    def copy(self, unit, k):
        p = self.place
        near, far, half = self.span(unit)
        cut = self.cut(unit)
        src = self.shards[unit]
        whole = lambda index: self.rows(unit, index)
        x_part = lambda index, at: self.rows(unit, index, at, cut)
        y_part = lambda index, at: self.rows(unit, index, at + cut, half - cut)
        dst, to = (
            lambda: (whole(p.batch), p.id(p.x)),
            lambda: (whole(p.batch), p.id(p.y)),
            lambda: (whole(p.batch), p.id(p.sibling)),
            lambda: (x_part(p.y, near), p.id(p.x)),
            lambda: (y_part(p.x, near), p.id(p.y)),
            lambda: (whole(p.x), p.id(p.sibling)),
            lambda: (whole(p.y), p.id(p.sibling)),
            lambda: (x_part(p.diag, near), p.id(p.sibling)),
            lambda: (y_part(p.diag, near), p.id(p.sibling)),
            lambda: (x_part(p.diag, near), (p.batch, p.pair_z)),
            lambda: (y_part(p.diag, near), (p.batch, p.pair_z)),
            lambda: (x_part(p.diag, far), p.id(p.sibling)),
            lambda: (y_part(p.diag, far), p.id(p.sibling)),
        )[k]()
        return remote(src if k < 3 else dst, dst, self.send.at[unit, k], self.recv.at[unit, k], to)

    def own(self, unit):
        dst = self.rows(unit, self.place.batch) if self.spread else self.full.at[self.slots[unit]]
        return pltpu.make_async_copy(self.shards[unit], dst, self.local.at[unit])

    def at_stage(self, unit, stage):
        if self.stage.get(unit, 0) >= stage:
            return False
        assert self.stage.get(unit, 0) == stage - 1
        self.stage[unit] = stage
        return self.spread

    def open(self, unit):
        self.own(unit).start()
        if self.at_stage(unit, 1):
            for k in (0, 1, 2):
                self.copy(unit, k).start()

    def relay(self, unit):
        if self.at_stage(unit, 2):
            self.copy(unit, 0).wait_recv()
            self.copy(unit, 1).wait_recv()
            for k in (3, 4, 5, 6):
                self.copy(unit, k).start()

    def share(self, unit):
        if self.at_stage(unit, 3):
            for k in (3, 4):
                self.copy(unit, k).wait_recv()
                if unit not in self.direct:
                    self.copy(unit, k + 6).start()
                self.copy(unit, k + 4).start()

    def pass_on(self, unit):
        if self.at_stage(unit, 4) and unit not in self.direct:
            for k in (9, 10):
                self.arrival(unit, k).wait_recv()
                self.copy(unit, k + 2).start()

    def arrival(self, unit, k):
        p = self.place
        _, far, half = self.span(unit)
        cut = self.cut(unit)
        start, count = ((far, cut), (far + cut, half - cut))[k - 9]
        dst = self.rows(unit, p.diag, start, count)
        return remote(dst, dst, self.send.at[unit, k], self.recv.at[unit, k], (p.batch, p.pair_z))

    def need(self, unit):
        self.relay(unit)
        self.share(unit)
        self.pass_on(unit)
        self.own(unit).wait()
        if self.spread:
            for k in (2, 5, 6, 7, 8) + (() if unit in self.direct else (11, 12)):
                self.copy(unit, k).wait_recv()

    def drain(self, unit):
        if self.spread:
            for k in range(9 if unit in self.direct else self.SEMS):
                self.copy(unit, k).wait_send()


class Scatter:
    SEMS = 7

    def __init__(self, place, grads, out, keep, got_core, got_x, got_y, last_x, last_y, send, recv, local):
        self.p, self.grads, self.out = place, grads, out
        self.room, self.got_core = keep, got_core
        self.got_x, self.got_y, self.last_x, self.last_y = got_x, got_y, last_x, last_y
        self.send, self.recv, self.local = send, recv, local
        p = place
        self.chip_x = p.x // 2
        self.chip_y = p.y // 2
        self.chip_d = p.diag // 2

    def keep(self, unit):
        far, near = self.grads[unit]
        if far is None:
            return near.at[:, self.p.core]
        return self.room.at[unit]

    def piece(self, unit, chip, part):
        half = self.last_x.shape[1]
        return self.keep(unit).at[chip, pl.ds(part * half, half)]

    def copy(self, unit, k):
        p = self.p
        src, dst, to = (
            lambda: (self.source(unit).at[:, 1 - p.core], self.got_core.at[unit], p.sibling),
            lambda: (self.piece(unit, self.chip_x, 0), self.got_x.at[unit, 0], p.x),
            lambda: (self.piece(unit, self.chip_d, 0), self.got_x.at[unit, 1], p.x),
            lambda: (self.piece(unit, self.chip_y, 1), self.got_y.at[unit, 0], p.y),
            lambda: (self.piece(unit, self.chip_d, 1), self.got_y.at[unit, 1], p.y),
            lambda: (self.piece(unit, self.chip_y, 0), self.last_y.at[unit], p.y),
            lambda: (self.piece(unit, self.chip_x, 1), self.last_x.at[unit], p.x),
        )[k]()
        return remote(src, dst, self.send.at[unit, k], self.recv.at[unit, k], p.id(to))

    def source(self, unit):
        far, near = self.grads[unit]
        return near if far is None else far

    def load(self, unit):
        return pltpu.make_async_copy(self.grads[unit][0].at[:, self.p.core], self.room.at[unit], self.local.at[unit, 0])

    def store(self, unit):
        return pltpu.make_async_copy(self.keep(unit).at[self.p.chip], self.out.at[unit], self.local.at[unit, 1])

    def open(self, unit):
        self.copy(unit, 0).start()
        if self.grads[unit][0] is not None:
            self.load(unit).start()

    def add(self, ref, other):
        ref[...] = (ref[...].astype(F32) + other[...].astype(F32)).astype(BF)

    def first(self, unit):
        if self.grads[unit][0] is not None:
            self.load(unit).wait()
        self.copy(unit, 0).wait_recv()
        self.add(self.keep(unit), self.got_core.at[unit])
        for k in (1, 2, 3, 4):
            self.copy(unit, k).start()

    def second(self, unit):
        p = self.p
        self.copy(unit, 2).wait_recv()
        self.add(self.piece(unit, self.chip_y, 0), self.got_x.at[unit, 1])
        self.copy(unit, 5).start()
        self.copy(unit, 4).wait_recv()
        self.add(self.piece(unit, self.chip_x, 1), self.got_y.at[unit, 1])
        self.copy(unit, 6).start()
        self.copy(unit, 1).wait_recv()
        self.add(self.piece(unit, p.chip, 0), self.got_x.at[unit, 0])
        self.copy(unit, 3).wait_recv()
        self.add(self.piece(unit, p.chip, 1), self.got_y.at[unit, 0])

    def third(self, unit):
        p = self.p
        self.copy(unit, 5).wait_recv()
        self.add(self.piece(unit, p.chip, 0), self.last_y.at[unit])
        self.copy(unit, 6).wait_recv()
        self.add(self.piece(unit, p.chip, 1), self.last_x.at[unit])
        if self.out is not None:
            self.store(unit).start()

    def drain(self, unit):
        for k in range(self.SEMS):
            self.copy(unit, k).wait_send()
        if self.out is not None:
            self.store(unit).wait()


def scatter_scratch(units, loaded, shard, width):
    half = shard // 2
    return [
        pltpu.VMEM((max(loaded, 1), 4, shard, width) if loaded else (1, 1, 16, width), BF),
        pltpu.VMEM((units, 4, shard, width), BF),
        pltpu.VMEM((units, 2, half, width), BF),
        pltpu.VMEM((units, 2, half, width), BF),
        pltpu.VMEM((units, half, width), BF),
        pltpu.VMEM((units, half, width), BF),
        pltpu.SemaphoreType.DMA((units, Scatter.SEMS)),
        pltpu.SemaphoreType.DMA((units, Scatter.SEMS)),
        pltpu.SemaphoreType.DMA((units, 2)),
    ]


class Line:
    def __init__(self, place, shares, out, mine, got, other, send, recv, local):
        self.p, self.shares, self.out = place, shares, out
        self.room, self.got, self.other = mine, got, other
        self.send, self.recv, self.local = send, recv, local

    def copy(self, item, half, k):
        p = self.p
        size = self.got.shape[1] // 2
        part = lambda ref: ref.at[pl.ds(half * size, size)]
        mine, got, other = self.mine(item), self.got.at[item], self.other.at[item]
        src, dst, to_z = ((mine, got, p.pair_z), (mine, other, 3 - p.z), (got, got, p.pair_z))[k]
        at = 3 * half + k
        return remote(part(src), part(dst), self.send.at[item, at], self.recv.at[item, at], (p.batch, to_z))

    def mine(self, item):
        far, near = self.shares[item]
        return self.room.at[item] if near is None else near

    def part(self, ref, half):
        size = self.got.shape[1] // 2
        return ref.at[pl.ds(half * size, size)]

    def load(self, item):
        return pltpu.make_async_copy(self.shares[item][0], self.room.at[item], self.local.at[item, 0])

    def store(self, item):
        return pltpu.make_async_copy(self.got.at[item], self.out.at[item], self.local.at[item, 1])

    def start(self, item):
        if self.shares[item][0] is not None:
            self.load(item).wait()

        @pl.when(jnp.logical_not(self.p.inner))
        def _():
            for half in (0, 1):
                self.copy(item, half, 0).start()

    def middle(self, item):
        @pl.when(self.p.inner)
        def _():
            for half in (0, 1):
                mine = self.part(self.mine(item), half)
                got = self.part(self.got.at[item], half)
                self.copy(item, half, 0).wait_recv()
                mine[...] = (mine[...].astype(F32) + got[...].astype(F32)).astype(BF)
                self.copy(item, half, 1).start()

    def last(self, item):
        @pl.when(self.p.inner)
        def _():
            for half in (0, 1):
                mine = self.part(self.mine(item), half)
                got = self.part(self.got.at[item], half)
                other = self.part(self.other.at[item], half)
                self.copy(item, half, 1).wait_recv()
                got[...] = (mine[...].astype(F32) + other[...].astype(F32)).astype(BF)
                self.copy(item, half, 2).start()

    def end(self, item):
        @pl.when(jnp.logical_not(self.p.inner))
        def _():
            for half in (0, 1):
                self.copy(item, half, 2).wait_recv()

        self.store(item).start()

    def drain(self, item):
        @pl.when(self.p.inner)
        def _():
            for half in (0, 1):
                self.copy(item, half, 1).wait_send()
                self.copy(item, half, 2).wait_send()

        @pl.when(jnp.logical_not(self.p.inner))
        def _():
            for half in (0, 1):
                self.copy(item, half, 0).wait_send()

        self.store(item).wait()


def line_scratch(items, loaded, shard, width):
    return [
        pltpu.VMEM((loaded, shard, width) if loaded else (1, 16, width), BF),
        pltpu.VMEM((items, shard, width), BF),
        pltpu.VMEM((items, shard, width), BF),
        pltpu.SemaphoreType.DMA((items, 6)),
        pltpu.SemaphoreType.DMA((items, 6)),
        pltpu.SemaphoreType.DMA((items, 2)),
    ]


class Plan:
    def __init__(self, xy, xy_arrays, z, z_arrays, shard, width):
        self.xy, self.xy_arrays, self.z, self.z_arrays = xy, xy_arrays, z, z_arrays
        self.shard, self.width = shard, width
        self.keep_sums = bool(xy) and not any(src == "sum" for src, _ in z)

    def args(self):
        return [*self.xy_arrays, *self.z_arrays]

    def outs(self):
        out = []
        if self.keep_sums:
            out.append(struct((len(self.xy), self.shard, self.width)))
        if self.z:
            out.append(struct((len(self.z), self.shard, self.width)))
        return out

    def scratch(self):
        loaded = sum(src != "own" for src, _ in self.xy)
        shares = sum(src != "sum" for src, _ in self.z)
        return (scatter_scratch(len(self.xy), loaded, self.shard, self.width) if self.xy else []) + (
            line_scratch(len(self.z), shares, self.shard, self.width) if self.z else []
        )

    def signals(self, p):
        return [p.id(p.sibling), p.id(p.x), p.id(p.y)] if self.xy else []

    def open(self, p, inputs, outputs, scratch, own=None):
        outputs, scratch = list(outputs), list(scratch)
        arrays = inputs[: len(self.xy_arrays)]
        shares = inputs[len(self.xy_arrays) :]
        sums_out = outputs.pop(0) if self.keep_sums else None
        scatter = line = None
        if self.xy:
            grads = [
                (None, own.at[unit]) if src == "own" else (arrays[src].at[unit], None) for src, unit in self.xy
            ]
            scatter = Scatter(p, grads, sums_out, *scratch[:9])
            scratch = scratch[9:]
        if self.z:
            items = [
                (None, scatter.keep(i).at[p.chip]) if src == "sum" else (shares[src].at[i], None)
                for src, i in self.z
            ]
            line = Line(p, items, outputs.pop(0), *scratch)
        return scatter, line


def kernel_params(collective):
    params = dict(vmem_limit_bytes=63 * 2**20)
    if collective is not None:
        params.update(collective_id=collective, has_side_effects=True)
    return pltpu.CompilerParams(**params)


def rms(rows):
    return lax.rsqrt(jnp.mean(rows * rows, axis=-1, keepdims=True) + EPS)


def key_blocks(core):
    if core == 0:
        return [(0, [("o", 0, 0)]), (1, [("o", 0, 0), ("x", 0, 1), ("x", 1, 2), ("o", 1, 3)])]
    return [(0, [("x", 0, 0), ("o", 0, 1)]), (1, [("x", 0, 0), ("o", 0, 1), ("o", 1, 2)])]


def masked(scores, quarter, diagonal, pad):
    size = scores.shape[0]
    key = lax.broadcasted_iota(jnp.int32, scores.shape, 0)
    ok = key >= pad - quarter * size
    if diagonal:
        query = lax.broadcasted_iota(jnp.int32, scores.shape, 1)
        ok = ((key <= query) & ok) | (key == query)
    return jnp.where(ok, scores, NEG)


def attend_heads(core, base, pad, qkv, kvx, o_ref, lse_ref):
    width, rows = o_ref.shape
    size = rows // 2
    at = lambda off, hh: pl.ds(pl.multiple_of(off * width + (base + hh) * HEAD_DIM, 16), HEAD_DIM)
    for hh in range(GROUP):
        for block, keys in key_blocks(core):
            cols = slice(block * size, block * size + size)
            q = qkv[at(0, hh), cols]
            scores = []
            for i, (src, half, quarter) in enumerate(keys):
                span = slice(half * size, half * size + size)
                k = qkv[at(1, hh), span] if src == "o" else kvx[at(0, hh), span]
                scores.append(masked(dot(k, q, 0, 0), quarter, i == len(keys) - 1, pad))
            top = functools.reduce(jnp.maximum, [jnp.max(s, axis=0, keepdims=True) for s in scores])
            total = 0.0
            out = 0.0
            for s, (src, half, quarter) in zip(scores, keys):
                span = slice(half * size, half * size + size)
                v = qkv[at(2, hh), span] if src == "o" else kvx[at(1, hh), span]
                weight = jnp.exp2((s - top) * LOG2_SCALE)
                total = total + jnp.sum(weight, axis=0, keepdims=True)
                out = out + dot(v, weight.astype(BF), 1, 0)
            o_ref[at(0, hh), cols] = (out * (1.0 / total)).astype(BF)
            lse_ref[base // GROUP, hh : hh + 1, cols] = top * LOG2_SCALE + jnp.log2(total)


class Copies:
    def __init__(self, sems):
        self.sems, self.used, self.open = sems, 0, {}

    def start(self, src, dst):
        copy = pltpu.make_async_copy(src, dst, self.sems.at[self.used])
        self.used += 1
        copy.start()
        return copy

    def save(self, name, src, dst):
        self.open.setdefault(name, []).append(self.start(src, dst))

    def ready(self, *names):
        for name in names:
            for copy in self.open.pop(name, []):
                copy.wait()

    def finish(self):
        self.ready(*list(self.open))


def forward_kernel(spread, *refs):
    refs = list(refs)
    take = lambda n: [refs.pop(0) for _ in range(n)]
    pad_ref, cos, sin, rows_in, cot_in, wqkv, wout, wup, wdown = take(9)
    (w_out, cot_out, hid0_out, hid1_out, h_out, xt_out, qkv_out, kvx_out, att_out, lse_out, mid_out, mt_out, pre_out,
     act_out) = take(14)
    (full, g_send, g_recv, g_local, qkv, kvx, h, att, lse, mid, xhat, tp, tq, act, rows_buf, x_send, x_recv, s_send, s_recv,
     free, copy_sems) = refs
    p = Place()
    width = xhat.shape[1]
    rows = xhat.shape[0]
    quarter = rows // 2
    groups = width // (HEAD_DIM * GROUP)
    copies = Copies(copy_sems)
    swap_in = Swap(p, True, rows_in, rows_buf, s_send.at[0], s_recv.at[0])
    swap_cot = Swap(p, True, cot_in, cot_out, s_send.at[1], s_recv.at[1])
    swap_hid = Swap(p, False, rows_buf, hid0_out, s_send.at[2], s_recv.at[2])
    others = [p.id(p.x), p.id(p.y), p.id(p.sibling), (p.batch, p.pair_z)] if spread else [p.id(p.sibling)]
    greet(p, others + swap_in.came_from + swap_hid.came_from)
    shards = []
    for layer in range(LAYERS):
        shards += [wqkv.at[layer, :, pl.ds(u * width, width)] for u in (1, 2, 0)]
        shards += [w.at[layer] for w in (wout, wup, wdown)]
    units = len(shards)
    room = full.shape[0]
    slots = [unit % room for unit in range(units)]
    gather = Gather(p, spread, shards, full, slots, DIRECT, g_send, g_recv, g_local)

    moving = []

    def release():
        for unit in range(units - room):
            gather.drain(unit)
            copies.ready(("w", unit))
        if spread:
            for k, device in enumerate(others):
                pl.semaphore_signal(free.at[k], inc=1, device_id=device, device_id_type=MESH)

    def tick(unit):
        gather.relay(unit)
        if unit + AHEAD < units:
            if unit + AHEAD == room and spread:
                for k in range(len(others)):
                    pl.semaphore_wait(free.at[k], 1)
            gather.open(unit + AHEAD)
        if unit:
            gather.share(unit - 1)
        if unit >= LAG:
            gather.pass_on(unit - LAG)
        for swap in moving:
            swap.start(RATE)

    def need(unit):
        gather.need(unit)
        copies.save(("w", unit), full.at[slots[unit]], w_out.at[unit])

    swap_in.start()
    for unit in range(AHEAD):
        gather.open(unit)
    tick(0)
    swap_in.arrive()
    for k in (0, 1):
        h[k * quarter : (k + 1) * quarter, :] = rows_buf[k].astype(F32)
    pad = pad_ref[0]

    for layer in range(LAYERS):
        base = 6 * layer
        copies.save("h", h, h_out.at[layer])
        copies.ready("tp", "tq")
        xhat[...] = (h[...] * rms(h[...])).astype(BF)
        tp[...] = xhat[...].T
        copies.save("tp", tp, xt_out.at[layer])
        copies.ready("qkv")
        if layer == 0:
            tick(1)
            tick(2)

        def exchange(k):
            return remote(
                qkv.at[pl.ds((1 + k) * width, width)], kvx.at[layer, pl.ds(k * width, width)],
                x_send.at[layer, k], x_recv.at[layer, k], p.id(p.sibling),
            )

        for i, part in enumerate((1, 2, 0)):
            need(base + i)
            step = 8 * HEAD_DIM
            for at in range(0, width, step):
                y = dot(xhat[...], full[slots[base + i], :, at : at + step], 1, 0).T
                for head in range(0, step, HEAD_DIM):
                    to = part * width + at + head
                    if part == 2:
                        qkv[to : to + HEAD_DIM, :] = y[head : head + HEAD_DIM].astype(BF)
                    else:
                        a, b = y[head : head + HALF], y[head + HALF : head + HEAD_DIM]
                        qkv[to : to + HEAD_DIM, :] = jnp.concatenate(
                            [a * cos[...] - b * sin[...], b * cos[...] + a * sin[...]], axis=0
                        ).astype(BF)
            if i < 2:
                exchange(i).start()
                tick(base + 3 + i)
        copies.save("qkv", qkv, qkv_out.at[layer])
        if layer == 0:
            moving.append(swap_cot)
        for k in (0, 1):
            exchange(k).wait_recv()
        copies.save("kvx", kvx.at[layer], kvx_out.at[layer])
        copies.ready("att", "lse")

        def body(group, carry):
            for core in (0, 1):
                pl.when(p.core == core)(
                    functools.partial(attend_heads, core, group * GROUP, pad, qkv, kvx.at[layer], att, lse)
                )

            @pl.when(group == 1)
            def _():
                tick(base + 5)

            return carry

        lax.fori_loop(0, groups, body, 0)
        if layer == 0:
            release()
        if layer == 0:
            tick(base + 6)
        copies.save("att", att, att_out.at[layer])
        copies.save("lse", lse, lse_out.at[layer])
        for k in (0, 1):
            exchange(k).wait_send()
        copies.ready("mid")
        if layer == LAYERS - 1:
            gather.pass_on(units - 2)
            gather.share(units - 1)
        need(base + 3)
        square = 0.0
        for cols in tiles(width):
            m = h[:, cols] + dot(att[...], full[slots[base + 3], :, cols], 0, 0)
            mid[:, cols] = m
            square = square + jnp.sum(m * m, axis=1, keepdims=True)
        copies.save("mid", mid, mid_out.at[layer])
        scale = lax.rsqrt(square / width + EPS)
        for cols in tiles(width):
            m = (mid[:, cols] * scale).astype(BF)
            xhat[:, cols] = m
            tq[cols, :] = m.T
        copies.save("tq", tq, mt_out.at[layer])
        if layer == LAYERS - 1:
            gather.pass_on(units - 1)
        need(base + 4)
        copies.ready("h", "tp")
        for cols in tiles(width):
            v = dot(xhat[...], full[slots[base + 4], :, cols], 1, 0)
            h[:, cols] = v
            a = (v / (1.0 + jnp.exp(-v))).astype(BF)
            act[:, cols] = a
            tp[cols, :] = a.T
        copies.save("pre", h, pre_out.at[layer])
        copies.save("tp", tp, act_out.at[layer])
        last = layer == LAYERS - 1
        if not last:
            tick(base + 7)
        need(base + 5)
        copies.ready("pre")
        if last:
            swap_hid.start()
            swap_hid.drain()
        for cols in tiles(width):
            v = mid[:, cols] + dot(act[...], full[slots[base + 5], :, cols], 1, 0)
            if not last:
                h[:, cols] = v
            for k in (0, 1):
                rows_buf[k, :, cols] = v[k * quarter : (k + 1) * quarter].astype(BF)
        if last:
            copies.save("hid", rows_buf, hid1_out)
        else:
            moving.append(swap_hid)
            tick(base + 8)
    for unit in range(units - room, units):
        gather.drain(unit)
    for swap in moving:
        swap.start()
    swap_in.drain()
    swap_cot.arrive()
    swap_cot.drain()
    swap_hid.arrive()
    copies.finish()


def forward(spread, collective, pad, cos, sin, inputs, cotangent, wqkv, wout, wup, wdown, shard):
    _, quarter, width = inputs.shape
    rows = 2 * quarter
    groups = width // (HEAD_DIM * GROUP)
    nat, tr = (rows, width), (width, rows)
    lse = (groups, GROUP, rows)
    two = lambda shape, dtype=BF: struct((LAYERS,) + shape, dtype)
    units = 6 * LAYERS
    room = units - 3
    swapped = struct((2, quarter, width))
    outs = [
        struct((units, width, width)), swapped, swapped, swapped, two(nat, F32), two(tr), two((3 * width, rows)),
        two((2 * width, rows)), two(tr), two(lse, F32), two(nat, F32), two(tr), two(nat, F32), two(tr),
    ]
    scratch = [
        pltpu.VMEM((room, width, width), BF),
        pltpu.SemaphoreType.DMA((units, Gather.SEMS)),
        pltpu.SemaphoreType.DMA((units, Gather.SEMS)),
        pltpu.SemaphoreType.DMA((units,)),
        pltpu.VMEM((3 * width, rows), BF),
        pltpu.VMEM((LAYERS, 2 * width, rows), BF),
        pltpu.VMEM(nat, F32),
        pltpu.VMEM(tr, BF),
        pltpu.VMEM(lse, F32),
        pltpu.VMEM(nat, F32),
        pltpu.VMEM(nat, BF),
        pltpu.VMEM(tr, BF),
        pltpu.VMEM(tr, BF),
        pltpu.VMEM(nat, BF),
        pltpu.VMEM((2, quarter, width), BF),
        pltpu.SemaphoreType.DMA((LAYERS, 2)),
        pltpu.SemaphoreType.DMA((LAYERS, 2)),
        pltpu.SemaphoreType.DMA((3, 2, Swap.PIECES)),
        pltpu.SemaphoreType.DMA((3, 2, Swap.PIECES)),
        pltpu.SemaphoreType.REGULAR((4,)),
        pltpu.SemaphoreType.DMA((units + 10 * LAYERS + 2,)),
    ]
    return pl.pallas_call(
        functools.partial(forward_kernel, spread),
        in_specs=[SM, VM, VM] + [ANY] * 6,
        out_specs=[ANY] * len(outs),
        out_shape=outs,
        scratch_shapes=scratch,
        compiler_params=kernel_params(collective),
        cost_estimate=pl.CostEstimate(flops=180 * 10**9, bytes_accessed=100 * 10**6, transcendentals=0),
        name="forward",
    )(pad, cos, sin, inputs, cotangent, wqkv, wout, wup, wdown)


def feed_back_kernel(plan, layer, *refs):
    refs = list(refs)
    take = lambda n: [refs.pop(0) for _ in range(n)]
    g_in, w_in, *held = take(7)
    act_t_in, mt_in, pre_in, mid_in, att_in = [ref.at[layer] for ref in held]
    inputs = take(len(plan.args())) if plan else []
    dw_out, mg_out, do_out = take(3)
    outputs = take(len(plan.outs())) if plan else []
    g, w, act_t, mt, pre, mid, att, gb, dpre, eg, do, dw, copy_sems = take(13)
    copies = Copies(copy_sems)
    width = w.shape[1]
    shard = dw.shape[3]
    if plan:
        p = Place()
        greet(p, plan.signals(p), bool(plan.z))
        scatter, line = plan.open(p, inputs, outputs, refs, dw)
        if line:
            line.load(0).start()
        if plan.xy[0][0] != "own":
            scatter.open(0)
    load_g = copies.start(g_in, gb if g_in.dtype == BF else g)
    load_act = copies.start(act_t_in, act_t)
    load_w = [copies.start(w_in.at[6 * layer + 5], w.at[2])]
    load_pre = copies.start(pre_in, pre)
    load_mt = copies.start(mt_in, mt)
    load_w += [copies.start(w_in.at[6 * layer + 4], w.at[1])]
    load_mid = copies.start(mid_in, mid)
    load_att = copies.start(att_in, att)
    load_w += [copies.start(w_in.at[6 * layer + 3], w.at[0])]

    def put(unit, cols, value):
        for k in range(dw.shape[1]):
            for c in range(2):
                at = (2 * k + c) * shard
                dw[unit, k, c, :, cols] = value[at : at + shard].astype(BF)

    load_g.wait()
    if g_in.dtype == BF:
        g[...] = gb[...].astype(F32)
    else:
        gb[...] = g[...].astype(BF)
    load_act.wait()
    for cols in tiles(width):
        put(2, cols, dot(act_t[...], gb[:, cols], 1, 0))
    if plan and plan.xy[0][0] == "own":
        scatter.open(0)
    else:
        copies.save("dw", dw.at[2], dw_out.at[2])
    if plan:
        if line:
            line.start(0)
    load_w[0].wait()
    load_pre.wait()
    for cols in tiles(width):
        da = dot(gb[...], w[2, cols, :], 1, 1)
        v = pre[:, cols]
        s = 1.0 / (1.0 + jnp.exp(-v))
        dpre[:, cols] = (da * (s + v * s * (1.0 - s))).astype(BF)
    if plan:
        scatter.first(0)
    load_mt.wait()
    for cols in tiles(width):
        put(1, cols, dot(mt[...], dpre[:, cols], 1, 0))
    copies.save("dw", dw.at[1], dw_out.at[1])
    load_w[1].wait()
    load_mid.wait()
    r = rms(mid[...])
    total = 0.0
    for cols in tiles(width):
        e = dot(dpre[...], w[1, cols, :], 1, 1)
        eg[:, cols] = e
        total = total + jnp.sum(e * (mid[:, cols] * r), axis=1, keepdims=True)
    total = total / width
    if plan and line:
        line.middle(0)
    for cols in tiles(width):
        m = g[:, cols] + r * (eg[:, cols] - mid[:, cols] * r * total)
        g[:, cols] = m
        gb[:, cols] = m.astype(BF)
    copies.save("g", g, mg_out)
    load_att.wait()
    for cols in tiles(width):
        put(0, cols, dot(att[...], gb[:, cols], 1, 0))
    copies.save("dw", dw.at[0], dw_out.at[0])
    load_w[2].wait()
    if plan:
        scatter.second(0)
        if line:
            line.last(0)
    for cols in tiles(width):
        do[cols, :] = dot(w[0, cols, :], gb[...], 1, 1).astype(BF)
    copies.save("do", do, do_out)
    if plan:
        scatter.third(0)
        if line:
            line.end(0)
            line.drain(0)
        scatter.drain(0)
    copies.finish()


def feed_back(name, collective, layer, g, w, act_t, mt, pre, mid, att, chips, shard, plan):
    _, width, rows = act_t.shape
    nat, tr = (rows, width), (width, rows)
    grad = (3, chips, 2, shard, width)
    args = [g, w, act_t, mt, pre, mid, att] + (plan.args() if plan else [])
    outs = [struct(grad), struct(nat, F32), struct(tr)] + (plan.outs() if plan else [])
    return pl.pallas_call(
        functools.partial(feed_back_kernel, plan, layer),
        in_specs=[ANY] * len(args),
        out_specs=[ANY] * len(outs),
        out_shape=outs,
        scratch_shapes=[
            pltpu.VMEM(nat, F32),
            pltpu.VMEM((3, width, width), BF),
            pltpu.VMEM(tr, BF),
            pltpu.VMEM(tr, BF),
            pltpu.VMEM(nat, F32),
            pltpu.VMEM(nat, F32),
            pltpu.VMEM(tr, BF),
            pltpu.VMEM(nat, BF),
            pltpu.VMEM(nat, BF),
            pltpu.VMEM(nat, F32),
            pltpu.VMEM(tr, BF),
            pltpu.VMEM(grad, BF),
            pltpu.SemaphoreType.DMA((16,)),
        ] + (plan.scratch() if plan else []),
        compiler_params=kernel_params(collective if plan else None),
        cost_estimate=pl.CostEstimate(flops=16 * 10**9, bytes_accessed=30 * 10**6, transcendentals=0),
        name=name,
    )(*args)


def unrotate(t, cos, sin):
    a, b = t[:HALF], t[HALF:]
    return jnp.concatenate([a * cos + b * sin, b * cos - a * sin], axis=0)


def attend_back_heads(core, base, pad, qkv, kvx, do, o, lse, tables, dqkv, dkvx):
    width, rows = o.shape
    size = rows // 2
    scale = 1.0 / math.sqrt(HEAD_DIM)
    cos, sin, cosx, sinx = tables
    at = lambda off, hh: pl.ds(pl.multiple_of(off * width + (base + hh) * HEAD_DIM, 16), HEAD_DIM)
    for hh in range(GROUP):
        dk, dv = {}, {}
        for block, keys in key_blocks(core):
            cols = slice(block * size, block * size + size)
            q = qkv[at(0, hh), cols]
            d_out = do[at(0, hh), cols]
            delta = jnp.sum(d_out.astype(F32) * o[at(0, hh), cols].astype(F32), axis=0, keepdims=True)
            norm = lse[base // GROUP, hh : hh + 1, cols]
            dq = 0.0
            for i, (src, half, quarter) in enumerate(keys):
                span = slice(half * size, half * size + size)
                k = qkv[at(1, hh), span] if src == "o" else kvx[at(0, hh), span]
                v = qkv[at(2, hh), span] if src == "o" else kvx[at(1, hh), span]
                s = masked(dot(k, q, 0, 0), quarter, i == len(keys) - 1, pad)
                weight = jnp.exp2(s * LOG2_SCALE - norm)
                ds = (weight * (dot(v, d_out, 0, 0) - delta)).astype(BF)
                dq = dq + dot(k, ds, 1, 0)
                a, b = dot(q, ds, 1, 1), dot(d_out, weight.astype(BF), 1, 1)
                key = (src, half)
                dk[key] = dk[key] + a if key in dk else a
                dv[key] = dv[key] + b if key in dv else b
            dqkv[at(0, hh), cols] = unrotate(dq * scale, cos[:, cols], sin[:, cols]).astype(BF)
        for src, ref, k_off, ct, st in (("o", dqkv, 1, cos, sin), ("x", dkvx, 0, cosx, sinx)):
            for half in (0, 1):
                span = slice(half * size, half * size + size)
                if (src, half) in dk:
                    a = unrotate(dk[src, half] * scale, ct[:, span], st[:, span]).astype(BF)
                    b = dv[src, half].astype(BF)
                else:
                    a = b = jnp.zeros((HEAD_DIM, size), BF)
                ref[at(k_off, hh), span] = a
                ref[at(k_off + 1, hh), span] = b


def attend_back_kernel(plan, layer, swapping, *refs):
    refs = list(refs)
    take = lambda n: [refs.pop(0) for _ in range(n)]
    pad_ref, qkv_in, kvx_in, do_in, att_in, lse, cos, sin, cosx, sinx = take(10)
    qkv_in, kvx_in, att_in = qkv_in.at[layer], kvx_in.at[layer], att_in.at[layer]
    hid_in = take(1)[0] if swapping else None
    inputs = take(len(plan.args())) if plan else []
    pg_out = take(1)[0]
    swap_out = take(1)[0] if swapping else None
    outputs = take(len(plan.outs())) if plan else []
    qkv, kvx, do, att, dqkv, dkvx, got, x_send, x_recv, copy_sems = take(10)
    p = Place()
    copies = Copies(copy_sems)
    signals = [p.id(p.sibling)]
    if plan:
        signals = plan.signals(p)
    if swapping:
        swap = Swap(p, False, hid_in, swap_out, *take(2))
        signals = signals + swap.came_from
    greet(p, signals, bool(plan and plan.z))
    if swapping:
        swap.start()
    loads = [copies.start(a, b) for a, b in ((qkv_in, qkv), (kvx_in, kvx), (do_in, do), (att_in, att))]
    units = items = 0
    if plan:
        scatter, line = plan.open(p, inputs, outputs, refs)
        units, items = len(plan.xy), len(plan.z)
        for i in range(units):
            scatter.open(i)
        for i in range(items):
            line.load(i).start()
        for i in range(items):
            line.start(i)
    for load in loads:
        load.wait()
    for i in range(units):
        scatter.first(i)
    pad = pad_ref[0]
    width = att.shape[0]
    span = GROUP * HEAD_DIM
    groups = width // span

    def exchange(group, k):
        part = pl.ds(pl.multiple_of(k * width + group * span, 16), span)
        return remote(dkvx.at[part], got.at[part], x_send.at[group, k], x_recv.at[group, k], p.id(p.sibling))

    def body(group, carry):
        for core in (0, 1):
            pl.when(p.core == core)(
                functools.partial(
                    attend_back_heads, core, group * GROUP, pad, qkv, kvx, do, att, lse,
                    (cos, sin, cosx, sinx), dqkv, dkvx,
                )
            )
        for k in (0, 1):
            exchange(group, k).start()
        after = [[], [], []]
        if units:
            after[1] += [(scatter.second, 0)]
            after[2] += [(scatter.second, i) for i in range(1, units)]
        if items:
            after[0] += [(line.middle, 0)]
            after[1] += [(line.middle, i) for i in range(1, min(items, 2))] + [(line.last, 0)]
            after[2] += [(line.middle, i) for i in range(2, items)] + [(line.last, i) for i in range(1, min(items, 2))]
        for at, steps in enumerate(after):

            @pl.when(group == at)
            def _(steps=steps):
                for step, i in steps:
                    step(i)

        return carry

    lax.fori_loop(0, groups, body, 0)
    for group in range(groups):
        for k in (0, 1):
            exchange(group, k).wait_recv()
    own = dqkv.at[pl.ds(width, 2 * width)]
    own[...] = (own[...].astype(F32) + got[...].astype(F32)).astype(BF)
    copies.save("dqkv", dqkv, pg_out)
    for i in range(units):
        scatter.third(i)
    for i in range(2, items):
        line.last(i)
    for i in range(items):
        line.end(i)
    for i in range(items):
        line.drain(i)
    for i in range(units):
        scatter.drain(i)
    for group in range(groups):
        for k in (0, 1):
            exchange(group, k).wait_send()
    if swapping:
        swap.arrive()
        swap.drain()
    copies.finish()


def attend_back(name, collective, layer, pad, qkv, kvx, do, att, lse, tables, hid, plan):
    _, width, rows = att.shape
    swapping = hid is not None
    args = [pad, qkv, kvx, do, att, lse, *tables] + ([hid] if swapping else []) + (plan.args() if plan else [])
    specs = [SM] + [ANY] * 4 + [VM] * 5 + [ANY] * (len(args) - 10)
    outs = [struct((3 * width, rows))]
    if swapping:
        outs.append(struct(hid.shape))
    outs += plan.outs() if plan else []
    scratch = [
        pltpu.VMEM((3 * width, rows), BF),
        pltpu.VMEM((2 * width, rows), BF),
        pltpu.VMEM((width, rows), BF),
        pltpu.VMEM((width, rows), BF),
        pltpu.VMEM((3 * width, rows), BF),
        pltpu.VMEM((2 * width, rows), BF),
        pltpu.VMEM((2 * width, rows), BF),
        pltpu.SemaphoreType.DMA((lse.shape[0], 2)),
        pltpu.SemaphoreType.DMA((lse.shape[0], 2)),
        pltpu.SemaphoreType.DMA((16,)),
    ]
    if swapping:
        scratch += swap_scratch()
    return pl.pallas_call(
        functools.partial(attend_back_kernel, plan, layer, swapping),
        in_specs=specs,
        out_specs=[ANY] * len(outs),
        out_shape=outs,
        scratch_shapes=scratch + (plan.scratch() if plan else []),
        compiler_params=kernel_params(collective),
        cost_estimate=pl.CostEstimate(flops=35 * 10**9, bytes_accessed=30 * 10**6, transcendentals=0),
        name=name,
    )(*args)


def project_back_kernel(plan, layer, swapping, *refs):
    refs = list(refs)
    take = lambda n: [refs.pop(0) for _ in range(n)]
    pg_in, xt_in, w_in, h_in, mg_in = take(5)
    xt_in, h_in = xt_in.at[layer], h_in.at[layer]
    inputs = take(len(plan.args())) if plan else []
    dw_out = None if swapping and plan else take(1)[0]
    g_out = take(1)[0]
    outputs = take(len(plan.outs())) if plan else []
    pg, xt, w, h, g, dw, copy_sems = take(7)
    gb = take(1)[0] if swapping else None
    swap_sems = take(2) if swapping else None
    copies = Copies(copy_sems)
    width = xt.shape[0]
    quarter = xt.shape[1] // 2
    shard = dw.shape[3]
    p = Place()
    signals = plan.signals(p) if plan else []
    if swapping:
        swap = Swap(p, False, gb, g_out, *swap_sems)
        signals = signals + swap.came_from
    if signals:
        greet(p, signals, bool(plan and plan.z))
    load_pg = copies.start(pg_in, pg)
    load_xt = copies.start(xt_in, xt)
    held = earlier = shares = 0
    scatter = line = None
    if plan:
        scatter, line = plan.open(p, inputs, outputs, refs, dw)
        held = len(plan.xy)
        earlier = sum(src != "own" for src, _ in plan.xy)
        shares = sum(src != "sum" for src, _ in plan.z)
    for i in range(earlier):
        scatter.open(i)
    for i in range(shares):
        line.load(i).start()
    load_w = [copies.start(w_in.at[6 * layer + (2, 0, 1)[unit]], w.at[unit]) for unit in range(3)]
    load_h = copies.start(h_in, h)
    load_g = copies.start(mg_in, g)
    load_pg.wait()
    load_xt.wait()
    for i in range(shares):
        line.start(i)
    for i in range(min(earlier, 1)):
        scatter.first(i)

    def weight_grad(unit):
        for cols in tiles(width):
            value = dot(xt[...], pg[unit * width + cols.start : unit * width + cols.stop, :], 1, 1)
            for k in range(dw.shape[1]):
                for c in range(2):
                    at = (2 * k + c) * shard
                    dw[unit, k, c, :, cols] = value[at : at + shard].astype(BF)
        if dw_out is not None and not (plan and ("own", unit) in plan.xy):
            copies.save("dw", dw.at[unit], dw_out.at[unit])

    own = earlier
    weight_grad(1)
    for i in range(1, earlier):
        scatter.first(i)
    if own < held:
        scatter.open(own)
    weight_grad(2)
    if own < held:
        scatter.first(own)
    wait_for = lambda step, i: getattr(line, step)(i) if i < shares else None
    wait_for("middle", 0)
    if own + 1 < held:
        scatter.open(own + 1)
    weight_grad(0)
    if own + 2 < held:
        scatter.open(own + 2)
    for i in range(min(earlier, 1)):
        scatter.second(i)
    wait_for("middle", 1)
    wait_for("last", 0)
    for load in load_w:
        load.wait()
    load_h.wait()
    load_g.wait()
    r = rms(h[...])
    total = 0.0
    for n, cols in enumerate(tiles(width)):
        e = 0.0
        for unit in range(3):
            e = e + dot(pg[unit * width : (unit + 1) * width, :], w[unit, cols, :], 0, 1)
        g[:, cols] = g[:, cols] + r * e
        total = total + jnp.sum(e * (h[:, cols] * r), axis=1, keepdims=True)
        if n == 1:
            for i in range(1, earlier):
                scatter.second(i)
        if n == 2 and own + 1 < held:
            scatter.first(own + 1)
        if n == 3:
            wait_for("middle", 2)
            wait_for("last", 1)
    total = total / width
    for cols in tiles(width):
        v = g[:, cols] - h[:, cols] * (r * r * total)
        if swapping:
            for k in (0, 1):
                gb[k, :, cols] = v[k * quarter : (k + 1) * quarter].astype(BF)
        else:
            g[:, cols] = v
    if swapping:
        swap.start()
    else:
        copies.save("g", g, g_out)
    chain = bool(plan) and len(plan.z) > shares
    for i in range(own + 2, held):
        scatter.first(i)
    for i in range(earlier):
        scatter.third(i)
    wait_for("middle", 3)
    wait_for("last", 2)
    steps = [[] for _ in range(held + 6)]
    for i in range(held):
        if i >= earlier:
            steps[i].append(functools.partial(scatter.second, i))
            steps[i + 1].append(functools.partial(scatter.third, i))
        if chain:
            j = shares + i
            base = i + 1
            steps[base].append(functools.partial(line.start, j))
            steps[base + 1].append(functools.partial(line.middle, j))
            steps[base + 2].append(functools.partial(line.last, j))
            steps[base + 3].append(functools.partial(line.end, j))
    if shares > 3:
        steps[2].append(functools.partial(line.last, 3))
    for group in steps:
        for step in group:
            step()
    for i in range(shares):
        line.end(i)
    for i in range(len(plan.z) if plan else 0):
        line.drain(i)
    for i in range(held):
        scatter.drain(i)
    if swapping:
        swap.arrive()
        swap.drain()
    copies.finish()


def project_back(name, collective, layer, pg, xt, w, h, mg, chips, shard, swapping, plan):
    _, rows, width = h.shape
    nat, tr = (rows, width), (width, rows)
    grad = (3, chips, 2, shard, width)
    args = [pg, xt, w, h, mg] + (plan.args() if plan else [])
    outs = [] if swapping and plan else [struct(grad)]
    outs.append(struct((2, rows // 2, width)) if swapping else struct(nat, F32))
    outs += plan.outs() if plan else []
    scratch = [
        pltpu.VMEM((3 * width, rows), BF),
        pltpu.VMEM(tr, BF),
        pltpu.VMEM((3, width, width), BF),
        pltpu.VMEM(nat, F32),
        pltpu.VMEM(nat, F32),
        pltpu.VMEM(grad, BF),
        pltpu.SemaphoreType.DMA((16,)),
    ]
    if swapping:
        scratch += [pltpu.VMEM((2, rows // 2, width), BF)] + swap_scratch()
    return pl.pallas_call(
        functools.partial(project_back_kernel, plan, layer, swapping),
        in_specs=[ANY] * len(args),
        out_specs=[ANY] * len(outs),
        out_shape=outs,
        scratch_shapes=scratch + (plan.scratch() if plan else []),
        compiler_params=kernel_params(collective if plan or swapping else None),
        cost_estimate=pl.CostEstimate(flops=16 * 10**9, bytes_accessed=30 * 10**6, transcendentals=0),
        name=name,
    )(*args)


def turn_kernel(plan, upper, lower, *refs):
    refs = list(refs)
    take = lambda n: [refs.pop(0) for _ in range(n)]
    pg_in, xt_in, w_in, h_in, mg_in, act_t_in, mt_in, pre_in, mid_in, att_in = take(10)
    inputs = take(len(plan.args())) if plan else []
    dqkv_out, dff_out, mg_out, do_out = take(4)
    outputs = take(len(plan.outs())) if plan else []
    pg, xt, w, h, g, eg, dw, act_t, mt, pre, att, gb, dpre, do, dw_more, copy_sems = take(16)
    copies = Copies(copy_sems)
    width = xt.shape[0]
    shard = dw.shape[3]
    if plan:
        p = Place()
        greet(p, plan.signals(p), True)
        scatter, line = plan.open(p, inputs, outputs, refs, dw)
        for i in (0, 1):
            line.load(i).start()
    load_pg = copies.start(pg_in, pg)
    load_xt = copies.start(xt_in.at[upper], xt)
    load_w = [copies.start(w_in.at[6 * upper + (2, 0, 1)[unit]], w.at[unit]) for unit in range(3)]
    load_h = copies.start(h_in.at[upper], h)
    load_g = copies.start(mg_in, g)
    load_act, load_mt, load_pre, load_att = [
        copies.start(src.at[lower], dst)
        for src, dst in ((act_t_in, act_t), (mt_in, mt), (pre_in, pre), (att_in, att))
    ]

    def put(to, cols, value):
        for k in range(dw.shape[1]):
            for c in range(2):
                at = (2 * k + c) * shard
                to[k, c, :, cols] = value[at : at + shard].astype(BF)

    def weight_grad(unit):
        for cols in tiles(width):
            put(dw.at[unit], cols, dot(xt[...], pg[unit * width + cols.start : unit * width + cols.stop, :], 1, 1))
        if not plan or ("own", unit) not in plan.xy:
            copies.save(("dw", unit), dw.at[unit], dqkv_out.at[unit])

    load_pg.wait()
    load_xt.wait()
    if plan:
        for i in (0, 1):
            line.start(i)
    weight_grad(1)
    if plan:
        scatter.open(0)
    weight_grad(0)
    if plan:
        scatter.open(1)
        scatter.first(0)
    weight_grad(2)
    if plan:
        scatter.first(1)
    for load in load_w:
        load.wait()
    load_h.wait()
    r = rms(h[...])
    total = 0.0
    for n, cols in enumerate(tiles(width)):
        if plan and n == 3:
            line.middle(0)
        e = 0.0
        for unit in range(3):
            e = e + dot(pg[unit * width : (unit + 1) * width, :], w[unit, cols, :], 0, 1)
        eg[:, cols] = e
        total = total + jnp.sum(e * (h[:, cols] * r), axis=1, keepdims=True)
    total = total / width
    load_w = [copies.start(w_in.at[6 * lower + 3 + unit], w.at[unit]) for unit in (2, 1, 0)]
    load_g.wait()
    for cols in tiles(width):
        v = g[:, cols] + r * (eg[:, cols] - h[:, cols] * r * total)
        g[:, cols] = v
        gb[:, cols] = v.astype(BF)
    load_mid = copies.start(mid_in.at[lower], h)
    if plan:
        scatter.second(0)

    load_act.wait()
    copies.ready(("dw", 2))
    for cols in tiles(width):
        put(dw.at[2], cols, dot(act_t[...], gb[:, cols], 1, 0))
    copies.save("dff", dw.at[2], dff_out.at[2])
    load_w[0].wait()
    load_pre.wait()
    if plan:
        line.middle(1)
        line.last(0)
    for cols in tiles(width):
        da = dot(gb[...], w[2, cols, :], 1, 1)
        v = pre[:, cols]
        s = 1.0 / (1.0 + jnp.exp(-v))
        dpre[:, cols] = (da * (s + v * s * (1.0 - s))).astype(BF)
    if plan:
        scatter.second(1)
    load_mt.wait()
    for cols in tiles(width):
        put(dw_more.at[0], cols, dot(mt[...], dpre[:, cols], 1, 0))
    copies.save("dff", dw_more.at[0], dff_out.at[1])
    load_w[1].wait()
    load_mid.wait()
    if plan:
        line.last(1)
        scatter.third(0)
    r = rms(h[...])
    total = 0.0
    for cols in tiles(width):
        e = dot(dpre[...], w[1, cols, :], 1, 1)
        eg[:, cols] = e
        total = total + jnp.sum(e * (h[:, cols] * r), axis=1, keepdims=True)
    total = total / width
    for cols in tiles(width):
        m = g[:, cols] + r * (eg[:, cols] - h[:, cols] * r * total)
        g[:, cols] = m
        gb[:, cols] = m.astype(BF)
    copies.save("g", g, mg_out)
    load_att.wait()
    for cols in tiles(width):
        put(dw_more.at[1], cols, dot(att[...], gb[:, cols], 1, 0))
    copies.save("dff", dw_more.at[1], dff_out.at[0])
    load_w[2].wait()
    for cols in tiles(width):
        do[cols, :] = dot(w[0, cols, :], gb[...], 1, 1).astype(BF)
    copies.save("do", do, do_out)
    if plan:
        scatter.third(1)
        for i in (0, 1):
            line.end(i)
        for i in (0, 1):
            line.drain(i)
            scatter.drain(i)
    copies.finish()


def turn(name, collective, upper, lower, pg, xt, w, h, mg, act_t, mt, pre, mid, att, chips, shard, plan):
    _, rows, width = h.shape
    nat, tr = (rows, width), (width, rows)
    grad = (3, chips, 2, shard, width)
    args = [pg, xt, w, h, mg, act_t, mt, pre, mid, att] + (plan.args() if plan else [])
    outs = [struct(grad), struct(grad), struct(nat, F32), struct(tr)] + (plan.outs() if plan else [])
    scratch = [
        pltpu.VMEM((3 * width, rows), BF),
        pltpu.VMEM(tr, BF),
        pltpu.VMEM((3, width, width), BF),
        pltpu.VMEM(nat, F32),
        pltpu.VMEM(nat, F32),
        pltpu.VMEM(nat, F32),
        pltpu.VMEM(grad, BF),
        pltpu.VMEM(tr, BF),
        pltpu.VMEM(tr, BF),
        pltpu.VMEM(nat, F32),
        pltpu.VMEM(tr, BF),
        pltpu.VMEM(nat, BF),
        pltpu.VMEM(nat, BF),
        pltpu.VMEM(tr, BF),
        pltpu.VMEM((2,) + grad[1:], BF),
        pltpu.SemaphoreType.DMA((24,)),
    ]
    return pl.pallas_call(
        functools.partial(turn_kernel, plan, upper, lower),
        in_specs=[ANY] * len(args),
        out_specs=[ANY] * len(outs),
        out_shape=outs,
        scratch_shapes=scratch + (plan.scratch() if plan else []),
        compiler_params=kernel_params(collective if plan else None),
        cost_estimate=pl.CostEstimate(flops=32 * 10**9, bytes_accessed=60 * 10**6, transcendentals=0),
        name=name,
    )(*args)


def finish_kernel(places, *refs):
    count = len(places[0][0])
    refs = list(refs)
    take = lambda n: [refs.pop(0) for _ in range(n)]
    sums = take(3)
    wqkv, wup, gain_attn, gain_mlp, moved, hidden_0, hidden_1 = take(7)
    hid_out, in_out, qkv_out, out_out, up_out, down_out, ga, gm = take(8)
    grad_in, qkv, out, up, down, sems = refs
    copies = Copies(sems)
    copies.save("hid", hidden_0, hid_out.at[0])
    copies.save("hid", hidden_1, hid_out.at[1])
    grad_in[...] = moved[...].astype(F32)
    copies.save("in", grad_in, in_out)
    width = out.shape[2]
    get = lambda place: sums[place[0]][place[1]].astype(F32)
    for layer, (thirds, (out_at, up_at, down_at)) in enumerate(places):
        gain = gain_attn[layer]
        total = 0.0
        for part in range(count):
            cols = slice(part * width, part * width + width)
            value = get(thirds[part])
            qkv[layer, :, cols] = value * gain
            total = total + jnp.sum(value * wqkv[layer, :, cols].astype(F32), axis=1, keepdims=True)
        ga[layer] = total
        copies.save("qkv", qkv.at[layer], qkv_out.at[layer])
        out[layer] = get(out_at)
        copies.save("out", out.at[layer], out_out.at[layer])
        value = get(up_at)
        up[layer] = value * gain_mlp[layer]
        gm[layer] = jnp.sum(value * wup[layer].astype(F32), axis=1, keepdims=True)
        copies.save("up", up.at[layer], up_out.at[layer])
        down[layer] = get(down_at)
        copies.save("down", down.at[layer], down_out.at[layer])
    copies.finish()


def finish(places, sums, wqkv, wup, gain_attn, gain_mlp, moved, hidden_0, hidden_1):
    layers, shard, width = wup.shape
    grad = (layers, shard, width)
    wide = (layers, shard, 3 * width)
    column = (layers, shard, 1)
    return pl.pallas_call(
        functools.partial(finish_kernel, places),
        in_specs=[VM] * 10,
        out_specs=[ANY] * 6 + [VM] * 2,
        out_shape=[
            struct((layers,) + hidden_0.shape), struct(moved.shape, F32), struct(wide, F32), struct(grad, F32),
            struct(grad, F32), struct(grad, F32), struct(column, F32), struct(column, F32),
        ],
        scratch_shapes=[
            pltpu.VMEM(moved.shape, F32),
            pltpu.VMEM(wide, F32),
            pltpu.VMEM(grad, F32),
            pltpu.VMEM(grad, F32),
            pltpu.VMEM(grad, F32),
            pltpu.SemaphoreType.DMA((16,)),
        ],
        compiler_params=kernel_params(None),
        cost_estimate=pl.CostEstimate(flops=10**8, bytes_accessed=25 * 10**6, transcendentals=0),
        name="finish",
    )(*sums, wqkv, wup, gain_attn, gain_mlp, moved, hidden_0, hidden_1)


def local(nb, ns, inputs, lengths, wqkv, wout, wup, wdown, gain_attn, gain_mlp, cotangent):
    series, quarter, width = inputs.shape
    heads = width // HEAD_DIM
    rows = 2 * quarter
    shard = wout.shape[1]
    chips = nb // 2
    spread = nb == 8
    z = lax.axis_index("seq")
    core = lax.axis_index("batch") % 2

    other = lax.ppermute(
        lengths, AXES, [(b * ns + s, (b ^ 1) * ns + s) for b in range(nb) for s in range(ns)]
    )
    both = jnp.where(core == 0, jnp.concatenate([lengths, other]), jnp.concatenate([other, lengths]))
    which = jnp.where((z == 0) | (z == 3), 2, 0) + z // 2
    pad = SLOTS - lax.dynamic_index_in_dim(both, which, 0, keepdims=True)
    angle = (
        jnp.exp(jnp.arange(HALF, dtype=F32) * (-2.0 * math.log(10000.0) / HEAD_DIM))[:, None]
        * jnp.arange(SLOTS, dtype=F32)[None, :]
    )
    cos_all, sin_all = jnp.cos(angle), jnp.sin(angle)
    cos_pad = lax.dynamic_slice_in_dim(cos_all, pad[0], 1, axis=1)
    sin_pad = lax.dynamic_slice_in_dim(sin_all, pad[0], 1, axis=1)
    cos_four = (cos_all * cos_pad + sin_all * sin_pad).reshape(HALF, 4, quarter)
    sin_four = (sin_all * cos_pad - cos_all * sin_pad).reshape(HALF, 4, quarter)

    def pick(table):
        even = jnp.concatenate([table[:, 0], table[:, 3]], axis=1)
        odd = jnp.concatenate([table[:, 1], table[:, 2]], axis=1)
        return jnp.where(core == 0, even, odd), jnp.where(core == 0, odd, even)

    cos, cosx = pick(cos_four)
    sin, sinx = pick(sin_four)

    wqkv_g = (wqkv.astype(F32) * gain_attn.astype(F32)[:, :, None]).astype(BF)
    wup_g = (wup.astype(F32) * gain_mlp.astype(F32)[:, :, None]).astype(BF)

    stacked = (
        lambda array: array
        if spread
        else lax.all_gather(array, "batch", axis=1, tiled=True)
    )
    w_all, cot, hidden_0, hid_1, h_all, xt_all, qkv_all, kvx_all, att_all, lse_all, mid_all, mt_all, pre_all, act_all = forward(
        spread, 0, pad, cos, sin, inputs, cotangent, stacked(wqkv_g), stacked(wout), stacked(wup_g), stacked(wdown), shard
    )
    g = cot.reshape(rows, width)

    def plan(xy, xy_arrays, z, z_arrays):
        return Plan(xy, xy_arrays, z, z_arrays, shard, width) if spread else None

    tables = (cos, sin, cosx, sinx)
    ff_1, mg, do, *sums = feed_back(
        "feed_back", 4, 1, g, w_all, act_all, mt_all, pre_all, mid_all, att_all, chips, shard,
        plan([("own", 2)], [], [], []),
    )
    p_d1 = sums
    pg, hidden_1, *sums = attend_back(
        "attend_back_1", 5, 1, pad, qkv_all, kvx_all, do, att_all, lse_all[1], tables, hid_1,
        plan([(0, 1), (0, 0)], [ff_1], [], []),
    )
    p_uo1 = sums[0] if spread else None
    qkv_1, ff_0, mg, do, *sums = turn(
        "turn", 6, 1, 0, pg, xt_all, w_all, h_all, mg, act_all, mt_all, pre_all, mid_all, att_all, chips, shard,
        plan([("own", 1), ("own", 0)], [], [(0, 0), (0, 1)], [p_uo1]),
    )
    p_kq1, r_uo1 = sums if spread else (None, None)
    pg, *sums = attend_back(
        "attend_back_0", 8, 0, pad, qkv_all, kvx_all, do, att_all, lse_all[0], tables, None,
        plan([(0, 2), (1, 2)], [qkv_1, ff_0], [(0, 0), (0, 1)], [p_kq1]),
    )
    p_vd, r_kq1 = sums if spread else (None, None)
    tail = project_back(
        "project_back", 9, 0, pg, xt_all, w_all, h_all, mg, chips, shard, True,
        plan(
            [(0, 1), (0, 0), ("own", 1), ("own", 2), ("own", 0)], [ff_0],
            [(0, 0), (0, 1), (1, 0)] + [("sum", i) for i in range(5)], [p_vd, *p_d1],
        ),
    )
    if spread:
        input_grad, r = tail
        places = (
            (((0, 7), (0, 5), (0, 6)), ((0, 4), (0, 3), (0, 1))),
            (((1, 1), (1, 0), (0, 0)), ((2, 1), (2, 0), (0, 2))),
        )
        column = lambda gain: gain.astype(F32)[:, :, None]
        *grads, grad_ga, grad_gm = finish(
            places, (r, r_kq1, r_uo1), wqkv, wup, column(gain_attn), column(gain_mlp), input_grad, hidden_0, hidden_1
        )
        return (*grads, grad_ga[:, :, 0], grad_gm[:, :, 0])
    qkv_0, input_grad = tail

    def over_all(grads):
        flat = grads.reshape(3, nb * shard, width)
        return lax.psum(lax.psum_scatter(flat, "batch", scatter_dimension=1, tiled=True), "seq")

    s_qkv = [over_all(qkv_0), over_all(qkv_1)]
    s_ff = [over_all(ff_0), over_all(ff_1)]
    input_grad = input_grad.astype(F32)
    hidden = [hidden_0, hidden_1]

    grad_qkv, grad_out, grad_up, grad_down, grad_ga, grad_gm = [], [], [], [], [], []
    for layer in range(LAYERS):
        ff = [part.astype(F32) for part in s_ff[layer]]
        qkv_sum = jnp.concatenate([part.astype(F32) for part in s_qkv[layer]], axis=1)
        grad_qkv.append(qkv_sum * gain_attn[layer].astype(F32)[:, None])
        grad_ga.append(jnp.sum(qkv_sum * wqkv[layer].astype(F32), axis=1))
        grad_out.append(ff[0])
        grad_up.append(ff[1] * gain_mlp[layer].astype(F32)[:, None])
        grad_gm.append(jnp.sum(ff[1] * wup[layer].astype(F32), axis=1))
        grad_down.append(ff[2])
    stack = jnp.stack
    return (
        stack(hidden), input_grad, stack(grad_qkv), stack(grad_out), stack(grad_up), stack(grad_down),
        stack(grad_ga), stack(grad_gm),
    )


def solution(mesh):
    nb, ns = mesh.shape["batch"], mesh.shape["seq"]
    rows = P("batch", "seq", None)
    weight = P(None, "batch", None)
    gain = P(None, "batch")
    return jax.shard_map(
        functools.partial(local, nb, ns),
        mesh=mesh,
        in_specs=(rows, P("batch"), weight, weight, weight, weight, gain, gain, rows),
        out_specs=(P(None, "batch", "seq", None), rows, weight, weight, weight, weight, gain, gain),
        check_vma=False,
    )
```

```python
import functools
import math

import jax
import jax.numpy as jnp
from jax import lax
from jax.experimental import pallas as pl
from jax.experimental.pallas import tpu as pltpu
from jax.sharding import PartitionSpec as P

HEAD_DIM = 80
HALF = HEAD_DIM // 2
LAYERS = 2
SLOTS = 1024
BF = jnp.bfloat16
F32 = jnp.float32
AXES = ("batch", "seq")
LOG2_SCALE = math.log2(math.e) / math.sqrt(HEAD_DIM)
NEG = -1e30
EPS = 1e-6
TILE = 256
MESH = pl.DeviceIdType.MESH
ANY = pl.BlockSpec(memory_space=pl.ANY)
VM = pl.BlockSpec(memory_space=pltpu.VMEM)
SM = pl.BlockSpec(memory_space=pltpu.SMEM)
GROUP = 4
LAG = 2
RATE = 2
DIRECT = (0, 1, 2, 9, 10, 11)
AHEAD = 2


def dot(a, b, i, j):
    return lax.dot_general(a, b, (((i,), (j,)), ((), ())), preferred_element_type=F32)


def struct(shape, dtype=BF):
    return jax.ShapeDtypeStruct(shape, dtype)


def tiles(extent):
    return [slice(at, at + TILE) for at in range(0, extent, TILE)]


class Place:
    def __init__(self):
        self.batch = lax.axis_index("batch")
        self.z = lax.axis_index("seq")
        self.core = self.batch % 2
        self.chip = self.batch // 2
        x = self.chip % 2
        y = (self.chip // 2) % 2
        self.to_x = 2 - 4 * x
        self.to_y = 4 - 8 * y
        self.x = self.batch + self.to_x
        self.y = self.batch + self.to_y
        self.diag = self.batch + self.to_x + self.to_y
        self.sibling = self.batch + 1 - 2 * self.core
        self.inner = (self.z == 1) | (self.z == 2)
        self.pair_z = self.z + 1 - 2 * (self.z % 2)
        self.owner = ((self.z + 1) // 2) % 2
        self.part = self.z // 2

    def id(self, batch):
        return (batch, self.z)

    def workers(self):
        return [
            (2 * self.chip + self.owner, (1 - self.core) * (1 + j) + self.core * 3 * j) for j in (0, 1)
        ]

    def holders(self):
        return [(2 * self.chip + 1 - self.owner, at) for at in (self.core, 3 - self.core)]


def greet(place, signals, line=False):
    barrier = pltpu.get_barrier_semaphore()
    for device in signals:
        pl.semaphore_signal(barrier, inc=1, device_id=device, device_id_type=MESH)
    if line:
        pl.semaphore_signal(barrier, inc=1, device_id=(place.batch, place.pair_z), device_id_type=MESH)

        @pl.when(place.inner)
        def _():
            pl.semaphore_signal(barrier, inc=1, device_id=(place.batch, 3 - place.z), device_id_type=MESH)

        pl.semaphore_wait(barrier, len(signals) + 1 + place.part + place.z % 2 - 2 * place.part * (place.z % 2))
    else:
        pl.semaphore_wait(barrier, len(signals))


class Swap:
    PIECES = 8

    def __init__(self, place, to_workers, src, landing, send, recv):
        self.src, self.landing, self.send, self.recv = src, landing, send, recv
        self.to = place.workers() if to_workers else place.holders()
        self.came_from = place.holders() if to_workers else place.workers()
        self.part = place.part
        self.sent = 0

    def copy(self, k, piece, part):
        count = self.src.shape[1] // self.PIECES
        rows = pl.ds(piece * count, count)
        return remote(
            self.src.at[k, rows], self.landing.at[part, rows], self.send.at[k, piece], self.recv.at[part, piece],
            self.to[k],
        )

    def start(self, pieces=PIECES):
        for _ in range(pieces):
            if self.sent < self.PIECES:
                for k in (0, 1):
                    self.copy(k, self.sent, self.part).start()
                self.sent += 1

    def arrive(self):
        for piece in range(self.PIECES):
            for k in (0, 1):
                self.copy(k, piece, k).wait_recv()

    def drain(self):
        for piece in range(self.PIECES):
            for k in (0, 1):
                self.copy(k, piece, self.part).wait_send()


def swap_scratch():
    return [pltpu.SemaphoreType.DMA((2, Swap.PIECES)), pltpu.SemaphoreType.DMA((2, Swap.PIECES))]


def remote(src, dst, send_sem, recv_sem, device):
    return pltpu.make_async_remote_copy(
        src_ref=src, dst_ref=dst, send_sem=send_sem, recv_sem=recv_sem, device_id=device,
        device_id_type=MESH,
    )


class Gather:
    SEMS = 13

    def __init__(self, place, spread, shards, full, slots, direct, send, recv, local):
        self.place, self.spread, self.direct = place, spread, direct
        self.shards, self.full, self.slots = shards, full, slots
        self.send, self.recv, self.local = send, recv, local
        self.stage = {}

    def rows(self, unit, index, start=0, count=None):
        size = self.shards[unit].shape[0]
        count = size if count is None else count
        return self.full.at[self.slots[unit], pl.ds(pl.multiple_of(index * size + start, 16), count)]

    def span(self, unit):
        size = self.shards[unit].shape[0]
        if unit in self.direct:
            return 0, 0, size
        hz = self.place.z % 2
        return hz * (size // 2), (1 - hz) * (size // 2), size // 2

    def cut(self, unit):
        _, _, half = self.span(unit)
        small = half // 32 * 16
        return small if unit % 2 else half - small

    def copy(self, unit, k):
        p = self.place
        near, far, half = self.span(unit)
        cut = self.cut(unit)
        src = self.shards[unit]
        whole = lambda index: self.rows(unit, index)
        x_part = lambda index, at: self.rows(unit, index, at, cut)
        y_part = lambda index, at: self.rows(unit, index, at + cut, half - cut)
        dst, to = (
            lambda: (whole(p.batch), p.id(p.x)),
            lambda: (whole(p.batch), p.id(p.y)),
            lambda: (whole(p.batch), p.id(p.sibling)),
            lambda: (x_part(p.y, near), p.id(p.x)),
            lambda: (y_part(p.x, near), p.id(p.y)),
            lambda: (whole(p.x), p.id(p.sibling)),
            lambda: (whole(p.y), p.id(p.sibling)),
            lambda: (x_part(p.diag, near), p.id(p.sibling)),
            lambda: (y_part(p.diag, near), p.id(p.sibling)),
            lambda: (x_part(p.diag, near), (p.batch, p.pair_z)),
            lambda: (y_part(p.diag, near), (p.batch, p.pair_z)),
            lambda: (x_part(p.diag, far), p.id(p.sibling)),
            lambda: (y_part(p.diag, far), p.id(p.sibling)),
        )[k]()
        return remote(src if k < 3 else dst, dst, self.send.at[unit, k], self.recv.at[unit, k], to)

    def own(self, unit):
        dst = self.rows(unit, self.place.batch) if self.spread else self.full.at[self.slots[unit]]
        return pltpu.make_async_copy(self.shards[unit], dst, self.local.at[unit])

    def at_stage(self, unit, stage):
        if self.stage.get(unit, 0) >= stage:
            return False
        assert self.stage.get(unit, 0) == stage - 1
        self.stage[unit] = stage
        return self.spread

    def open(self, unit):
        self.own(unit).start()
        if self.at_stage(unit, 1):
            for k in (0, 1, 2):
                self.copy(unit, k).start()

    def relay(self, unit):
        if self.at_stage(unit, 2):
            self.copy(unit, 0).wait_recv()
            self.copy(unit, 1).wait_recv()
            for k in (3, 4, 5, 6):
                self.copy(unit, k).start()

    def share(self, unit):
        if self.at_stage(unit, 3):
            for k in (3, 4):
                self.copy(unit, k).wait_recv()
                if unit not in self.direct:
                    self.copy(unit, k + 6).start()
                self.copy(unit, k + 4).start()

    def pass_on(self, unit):
        if self.at_stage(unit, 4) and unit not in self.direct:
            for k in (9, 10):
                self.arrival(unit, k).wait_recv()
                self.copy(unit, k + 2).start()

    def arrival(self, unit, k):
        p = self.place
        _, far, half = self.span(unit)
        cut = self.cut(unit)
        start, count = ((far, cut), (far + cut, half - cut))[k - 9]
        dst = self.rows(unit, p.diag, start, count)
        return remote(dst, dst, self.send.at[unit, k], self.recv.at[unit, k], (p.batch, p.pair_z))

    def need(self, unit):
        self.relay(unit)
        self.share(unit)
        self.pass_on(unit)
        self.own(unit).wait()
        if self.spread:
            for k in (2, 5, 6, 7, 8) + (() if unit in self.direct else (11, 12)):
                self.copy(unit, k).wait_recv()

    def drain(self, unit):
        if self.spread:
            for k in range(9 if unit in self.direct else self.SEMS):
                self.copy(unit, k).wait_send()


class Scatter:
    SEMS = 7

    def __init__(self, place, grads, out, keep, got_core, got_x, got_y, last_x, last_y, send, recv, local):
        self.p, self.grads, self.out = place, grads, out
        self.room, self.got_core = keep, got_core
        self.got_x, self.got_y, self.last_x, self.last_y = got_x, got_y, last_x, last_y
        self.send, self.recv, self.local = send, recv, local
        p = place
        self.chip_x = p.x // 2
        self.chip_y = p.y // 2
        self.chip_d = p.diag // 2

    def keep(self, unit):
        far, near = self.grads[unit]
        if far is None:
            return near.at[:, self.p.core]
        return self.room.at[unit]

    def piece(self, unit, chip, part):
        half = self.last_x.shape[1]
        return self.keep(unit).at[chip, pl.ds(part * half, half)]

    def copy(self, unit, k):
        p = self.p
        src, dst, to = (
            lambda: (self.source(unit).at[:, 1 - p.core], self.got_core.at[unit], p.sibling),
            lambda: (self.piece(unit, self.chip_x, 0), self.got_x.at[unit, 0], p.x),
            lambda: (self.piece(unit, self.chip_d, 0), self.got_x.at[unit, 1], p.x),
            lambda: (self.piece(unit, self.chip_y, 1), self.got_y.at[unit, 0], p.y),
            lambda: (self.piece(unit, self.chip_d, 1), self.got_y.at[unit, 1], p.y),
            lambda: (self.piece(unit, self.chip_y, 0), self.last_y.at[unit], p.y),
            lambda: (self.piece(unit, self.chip_x, 1), self.last_x.at[unit], p.x),
        )[k]()
        return remote(src, dst, self.send.at[unit, k], self.recv.at[unit, k], p.id(to))

    def source(self, unit):
        far, near = self.grads[unit]
        return near if far is None else far

    def load(self, unit):
        return pltpu.make_async_copy(self.grads[unit][0].at[:, self.p.core], self.room.at[unit], self.local.at[unit, 0])

    def store(self, unit):
        return pltpu.make_async_copy(self.keep(unit).at[self.p.chip], self.out.at[unit], self.local.at[unit, 1])

    def open(self, unit):
        self.copy(unit, 0).start()
        if self.grads[unit][0] is not None:
            self.load(unit).start()

    def add(self, ref, other):
        ref[...] = (ref[...].astype(F32) + other[...].astype(F32)).astype(BF)

    def first(self, unit):
        if self.grads[unit][0] is not None:
            self.load(unit).wait()
        self.copy(unit, 0).wait_recv()
        self.add(self.keep(unit), self.got_core.at[unit])
        for k in (1, 2, 3, 4):
            self.copy(unit, k).start()

    def second(self, unit):
        p = self.p
        self.copy(unit, 2).wait_recv()
        self.add(self.piece(unit, self.chip_y, 0), self.got_x.at[unit, 1])
        self.copy(unit, 5).start()
        self.copy(unit, 4).wait_recv()
        self.add(self.piece(unit, self.chip_x, 1), self.got_y.at[unit, 1])
        self.copy(unit, 6).start()
        self.copy(unit, 1).wait_recv()
        self.add(self.piece(unit, p.chip, 0), self.got_x.at[unit, 0])
        self.copy(unit, 3).wait_recv()
        self.add(self.piece(unit, p.chip, 1), self.got_y.at[unit, 0])

    def third(self, unit):
        p = self.p
        self.copy(unit, 5).wait_recv()
        self.add(self.piece(unit, p.chip, 0), self.last_y.at[unit])
        self.copy(unit, 6).wait_recv()
        self.add(self.piece(unit, p.chip, 1), self.last_x.at[unit])
        if self.out is not None:
            self.store(unit).start()

    def drain(self, unit):
        for k in range(self.SEMS):
            self.copy(unit, k).wait_send()
        if self.out is not None:
            self.store(unit).wait()


def scatter_scratch(units, loaded, shard, width):
    half = shard // 2
    return [
        pltpu.VMEM((max(loaded, 1), 4, shard, width) if loaded else (1, 1, 16, width), BF),
        pltpu.VMEM((units, 4, shard, width), BF),
        pltpu.VMEM((units, 2, half, width), BF),
        pltpu.VMEM((units, 2, half, width), BF),
        pltpu.VMEM((units, half, width), BF),
        pltpu.VMEM((units, half, width), BF),
        pltpu.SemaphoreType.DMA((units, Scatter.SEMS)),
        pltpu.SemaphoreType.DMA((units, Scatter.SEMS)),
        pltpu.SemaphoreType.DMA((units, 2)),
    ]


class Line:
    def __init__(self, place, shares, out, mine, got, other, send, recv, local):
        self.p, self.shares, self.out = place, shares, out
        self.room, self.got, self.other = mine, got, other
        self.send, self.recv, self.local = send, recv, local

    def copy(self, item, half, k):
        p = self.p
        size = self.got.shape[1] // 2
        part = lambda ref: ref.at[pl.ds(half * size, size)]
        mine, got, other = self.mine(item), self.got.at[item], self.other.at[item]
        src, dst, to_z = ((mine, got, p.pair_z), (mine, other, 3 - p.z), (got, got, p.pair_z))[k]
        at = 3 * half + k
        return remote(part(src), part(dst), self.send.at[item, at], self.recv.at[item, at], (p.batch, to_z))

    def mine(self, item):
        far, near = self.shares[item]
        return self.room.at[item] if near is None else near

    def part(self, ref, half):
        size = self.got.shape[1] // 2
        return ref.at[pl.ds(half * size, size)]

    def load(self, item):
        return pltpu.make_async_copy(self.shares[item][0], self.room.at[item], self.local.at[item, 0])

    def store(self, item):
        return pltpu.make_async_copy(self.got.at[item], self.out.at[item], self.local.at[item, 1])

    def start(self, item):
        if self.shares[item][0] is not None:
            self.load(item).wait()

        @pl.when(jnp.logical_not(self.p.inner))
        def _():
            for half in (0, 1):
                self.copy(item, half, 0).start()

    def middle(self, item):
        @pl.when(self.p.inner)
        def _():
            for half in (0, 1):
                mine = self.part(self.mine(item), half)
                got = self.part(self.got.at[item], half)
                self.copy(item, half, 0).wait_recv()
                mine[...] = (mine[...].astype(F32) + got[...].astype(F32)).astype(BF)
                self.copy(item, half, 1).start()

    def last(self, item):
        @pl.when(self.p.inner)
        def _():
            for half in (0, 1):
                mine = self.part(self.mine(item), half)
                got = self.part(self.got.at[item], half)
                other = self.part(self.other.at[item], half)
                self.copy(item, half, 1).wait_recv()
                got[...] = (mine[...].astype(F32) + other[...].astype(F32)).astype(BF)
                self.copy(item, half, 2).start()

    def end(self, item):
        @pl.when(jnp.logical_not(self.p.inner))
        def _():
            for half in (0, 1):
                self.copy(item, half, 2).wait_recv()

        self.store(item).start()

    def drain(self, item):
        @pl.when(self.p.inner)
        def _():
            for half in (0, 1):
                self.copy(item, half, 1).wait_send()
                self.copy(item, half, 2).wait_send()

        @pl.when(jnp.logical_not(self.p.inner))
        def _():
            for half in (0, 1):
                self.copy(item, half, 0).wait_send()

        self.store(item).wait()


def line_scratch(items, loaded, shard, width):
    return [
        pltpu.VMEM((loaded, shard, width) if loaded else (1, 16, width), BF),
        pltpu.VMEM((items, shard, width), BF),
        pltpu.VMEM((items, shard, width), BF),
        pltpu.SemaphoreType.DMA((items, 6)),
        pltpu.SemaphoreType.DMA((items, 6)),
        pltpu.SemaphoreType.DMA((items, 2)),
    ]


class Plan:
    def __init__(self, xy, xy_arrays, z, z_arrays, shard, width):
        self.xy, self.xy_arrays, self.z, self.z_arrays = xy, xy_arrays, z, z_arrays
        self.shard, self.width = shard, width
        self.keep_sums = bool(xy) and not any(src == "sum" for src, _ in z)

    def args(self):
        return [*self.xy_arrays, *self.z_arrays]

    def outs(self):
        out = []
        if self.keep_sums:
            out.append(struct((len(self.xy), self.shard, self.width)))
        if self.z:
            out.append(struct((len(self.z), self.shard, self.width)))
        return out

    def scratch(self):
        loaded = sum(src != "own" for src, _ in self.xy)
        shares = sum(src != "sum" for src, _ in self.z)
        return (scatter_scratch(len(self.xy), loaded, self.shard, self.width) if self.xy else []) + (
            line_scratch(len(self.z), shares, self.shard, self.width) if self.z else []
        )

    def signals(self, p):
        return [p.id(p.sibling), p.id(p.x), p.id(p.y)] if self.xy else []

    def open(self, p, inputs, outputs, scratch, own=None):
        outputs, scratch = list(outputs), list(scratch)
        arrays = inputs[: len(self.xy_arrays)]
        shares = inputs[len(self.xy_arrays) :]
        sums_out = outputs.pop(0) if self.keep_sums else None
        scatter = line = None
        if self.xy:
            grads = [
                (None, own.at[unit]) if src == "own" else (arrays[src].at[unit], None) for src, unit in self.xy
            ]
            scatter = Scatter(p, grads, sums_out, *scratch[:9])
            scratch = scratch[9:]
        if self.z:
            items = [
                (None, scatter.keep(i).at[p.chip]) if src == "sum" else (shares[src].at[i], None)
                for src, i in self.z
            ]
            line = Line(p, items, outputs.pop(0), *scratch)
        return scatter, line


def kernel_params(collective):
    params = dict(vmem_limit_bytes=63 * 2**20)
    if collective is not None:
        params.update(collective_id=collective, has_side_effects=True)
    return pltpu.CompilerParams(**params)


def rms(rows):
    return lax.rsqrt(jnp.mean(rows * rows, axis=-1, keepdims=True) + EPS)


def key_blocks(core):
    if core == 0:
        return [(0, [("o", 0, 0)]), (1, [("o", 0, 0), ("x", 0, 1), ("x", 1, 2), ("o", 1, 3)])]
    return [(0, [("x", 0, 0), ("o", 0, 1)]), (1, [("x", 0, 0), ("o", 0, 1), ("o", 1, 2)])]


def masked(scores, quarter, diagonal, pad):
    size = scores.shape[0]
    key = lax.broadcasted_iota(jnp.int32, scores.shape, 0)
    ok = key >= pad - quarter * size
    if diagonal:
        query = lax.broadcasted_iota(jnp.int32, scores.shape, 1)
        ok = ((key <= query) & ok) | (key == query)
    return jnp.where(ok, scores, NEG)


def attend_heads(core, base, pad, qkv, kvx, o_ref, lse_ref):
    width, rows = o_ref.shape
    size = rows // 2
    at = lambda off, hh: pl.ds(pl.multiple_of(off * width + (base + hh) * HEAD_DIM, 16), HEAD_DIM)
    for hh in range(GROUP):
        for block, keys in key_blocks(core):
            cols = slice(block * size, block * size + size)
            q = qkv[at(0, hh), cols]
            scores = []
            for i, (src, half, quarter) in enumerate(keys):
                span = slice(half * size, half * size + size)
                k = qkv[at(1, hh), span] if src == "o" else kvx[at(0, hh), span]
                scores.append(masked(dot(k, q, 0, 0), quarter, i == len(keys) - 1, pad))
            top = functools.reduce(jnp.maximum, [jnp.max(s, axis=0, keepdims=True) for s in scores])
            total = 0.0
            out = 0.0
            for s, (src, half, quarter) in zip(scores, keys):
                span = slice(half * size, half * size + size)
                v = qkv[at(2, hh), span] if src == "o" else kvx[at(1, hh), span]
                weight = jnp.exp2((s - top) * LOG2_SCALE)
                total = total + jnp.sum(weight, axis=0, keepdims=True)
                out = out + dot(v, weight.astype(BF), 1, 0)
            o_ref[at(0, hh), cols] = (out * (1.0 / total)).astype(BF)
            lse_ref[base // GROUP, hh : hh + 1, cols] = top * LOG2_SCALE + jnp.log2(total)


class Copies:
    def __init__(self, sems):
        self.sems, self.used, self.open = sems, 0, {}

    def start(self, src, dst):
        copy = pltpu.make_async_copy(src, dst, self.sems.at[self.used])
        self.used += 1
        copy.start()
        return copy

    def save(self, name, src, dst):
        self.open.setdefault(name, []).append(self.start(src, dst))

    def ready(self, *names):
        for name in names:
            for copy in self.open.pop(name, []):
                copy.wait()

    def finish(self):
        self.ready(*list(self.open))


def forward_kernel(spread, *refs):
    refs = list(refs)
    take = lambda n: [refs.pop(0) for _ in range(n)]
    pad_ref, cos, sin, rows_in, cot_in, wqkv, wout, wup, wdown = take(9)
    (w_out, cot_out, hid0_out, hid1_out, h_out, xt_out, qkv_out, kvx_out, att_out, lse_out, mid_out, mt_out, pre_out,
     act_out) = take(14)
    (full, g_send, g_recv, g_local, qkv, kvx, h, att, lse, mid, xhat, tp, tq, act, rows_buf, x_send, x_recv, s_send, s_recv,
     free, copy_sems) = refs
    p = Place()
    width = xhat.shape[1]
    rows = xhat.shape[0]
    quarter = rows // 2
    groups = width // (HEAD_DIM * GROUP)
    copies = Copies(copy_sems)
    swap_in = Swap(p, True, rows_in, rows_buf, s_send.at[0], s_recv.at[0])
    swap_cot = Swap(p, True, cot_in, cot_out, s_send.at[1], s_recv.at[1])
    swap_hid = Swap(p, False, rows_buf, hid0_out, s_send.at[2], s_recv.at[2])
    others = [p.id(p.x), p.id(p.y), p.id(p.sibling), (p.batch, p.pair_z)] if spread else [p.id(p.sibling)]
    greet(p, others + swap_in.came_from + swap_hid.came_from)
    shards = []
    for layer in range(LAYERS):
        shards += [wqkv.at[layer, :, pl.ds(u * width, width)] for u in (1, 2, 0)]
        shards += [w.at[layer] for w in (wout, wup, wdown)]
    units = len(shards)
    room = full.shape[0]
    slots = [unit % room for unit in range(units)]
    gather = Gather(p, spread, shards, full, slots, DIRECT, g_send, g_recv, g_local)

    moving = []

    def release():
        for unit in range(units - room):
            gather.drain(unit)
            copies.ready(("w", unit))
        if spread:
            for k, device in enumerate(others):
                pl.semaphore_signal(free.at[k], inc=1, device_id=device, device_id_type=MESH)

    def tick(unit):
        gather.relay(unit)
        if unit + AHEAD < units:
            if unit + AHEAD == room and spread:
                for k in range(len(others)):
                    pl.semaphore_wait(free.at[k], 1)
            gather.open(unit + AHEAD)
        if unit:
            gather.share(unit - 1)
        if unit >= LAG:
            gather.pass_on(unit - LAG)
        for swap in moving:
            swap.start(RATE)

    def need(unit):
        gather.need(unit)
        copies.save(("w", unit), full.at[slots[unit]], w_out.at[unit])

    swap_in.start()
    for unit in range(AHEAD):
        gather.open(unit)
    tick(0)
    swap_in.arrive()
    for k in (0, 1):
        h[k * quarter : (k + 1) * quarter, :] = rows_buf[k].astype(F32)
    pad = pad_ref[0]

    for layer in range(LAYERS):
        base = 6 * layer
        copies.save("h", h, h_out.at[layer])
        copies.ready("tp", "tq")
        xhat[...] = (h[...] * rms(h[...])).astype(BF)
        tp[...] = xhat[...].T
        copies.save("tp", tp, xt_out.at[layer])
        copies.ready("qkv")
        if layer == 0:
            tick(1)
            tick(2)

        def exchange(k):
            return remote(
                qkv.at[pl.ds((1 + k) * width, width)], kvx.at[layer, pl.ds(k * width, width)],
                x_send.at[layer, k], x_recv.at[layer, k], p.id(p.sibling),
            )

        for i, part in enumerate((1, 2, 0)):
            need(base + i)
            step = 8 * HEAD_DIM
            for at in range(0, width, step):
                y = dot(xhat[...], full[slots[base + i], :, at : at + step], 1, 0).T
                for head in range(0, step, HEAD_DIM):
                    to = part * width + at + head
                    if part == 2:
                        qkv[to : to + HEAD_DIM, :] = y[head : head + HEAD_DIM].astype(BF)
                    else:
                        a, b = y[head : head + HALF], y[head + HALF : head + HEAD_DIM]
                        qkv[to : to + HEAD_DIM, :] = jnp.concatenate(
                            [a * cos[...] - b * sin[...], b * cos[...] + a * sin[...]], axis=0
                        ).astype(BF)
            if i < 2:
                exchange(i).start()
                tick(base + 3 + i)
        copies.save("qkv", qkv, qkv_out.at[layer])
        if layer == 0:
            moving.append(swap_cot)
        for k in (0, 1):
            exchange(k).wait_recv()
        copies.save("kvx", kvx.at[layer], kvx_out.at[layer])
        copies.ready("att", "lse")

        def body(group, carry):
            for core in (0, 1):
                pl.when(p.core == core)(
                    functools.partial(attend_heads, core, group * GROUP, pad, qkv, kvx.at[layer], att, lse)
                )

            @pl.when(group == 1)
            def _():
                tick(base + 5)

            return carry

        lax.fori_loop(0, groups, body, 0)
        if layer == 0:
            release()
        if layer == 0:
            tick(base + 6)
        copies.save("att", att, att_out.at[layer])
        copies.save("lse", lse, lse_out.at[layer])
        for k in (0, 1):
            exchange(k).wait_send()
        copies.ready("mid")
        if layer == LAYERS - 1:
            gather.pass_on(units - 2)
            gather.share(units - 1)
        need(base + 3)
        square = 0.0
        for cols in tiles(width):
            m = h[:, cols] + dot(att[...], full[slots[base + 3], :, cols], 0, 0)
            mid[:, cols] = m
            square = square + jnp.sum(m * m, axis=1, keepdims=True)
        copies.save("mid", mid, mid_out.at[layer])
        scale = lax.rsqrt(square / width + EPS)
        for cols in tiles(width):
            m = (mid[:, cols] * scale).astype(BF)
            xhat[:, cols] = m
            tq[cols, :] = m.T
        copies.save("tq", tq, mt_out.at[layer])
        if layer == LAYERS - 1:
            gather.pass_on(units - 1)
        need(base + 4)
        copies.ready("h", "tp")
        for cols in tiles(width):
            v = dot(xhat[...], full[slots[base + 4], :, cols], 1, 0)
            h[:, cols] = v
            a = (v / (1.0 + jnp.exp(-v))).astype(BF)
            act[:, cols] = a
            tp[cols, :] = a.T
        copies.save("pre", h, pre_out.at[layer])
        copies.save("tp", tp, act_out.at[layer])
        last = layer == LAYERS - 1
        if not last:
            tick(base + 7)
        need(base + 5)
        copies.ready("pre")
        if last:
            swap_hid.start()
            swap_hid.drain()
        for cols in tiles(width):
            v = mid[:, cols] + dot(act[...], full[slots[base + 5], :, cols], 1, 0)
            if not last:
                h[:, cols] = v
            for k in (0, 1):
                rows_buf[k, :, cols] = v[k * quarter : (k + 1) * quarter].astype(BF)
        if last:
            copies.save("hid", rows_buf, hid1_out)
        else:
            moving.append(swap_hid)
            tick(base + 8)
    for unit in range(units - room, units):
        gather.drain(unit)
    for swap in moving:
        swap.start()
    swap_in.drain()
    swap_cot.arrive()
    swap_cot.drain()
    swap_hid.arrive()
    copies.finish()


def forward(spread, collective, pad, cos, sin, inputs, cotangent, wqkv, wout, wup, wdown, shard):
    _, quarter, width = inputs.shape
    rows = 2 * quarter
    groups = width // (HEAD_DIM * GROUP)
    nat, tr = (rows, width), (width, rows)
    lse = (groups, GROUP, rows)
    two = lambda shape, dtype=BF: struct((LAYERS,) + shape, dtype)
    units = 6 * LAYERS
    room = units - 3
    swapped = struct((2, quarter, width))
    outs = [
        struct((units, width, width)), swapped, swapped, swapped, two(nat, F32), two(tr), two((3 * width, rows)),
        two((2 * width, rows)), two(tr), two(lse, F32), two(nat, F32), two(tr), two(nat, F32), two(tr),
    ]
    scratch = [
        pltpu.VMEM((room, width, width), BF),
        pltpu.SemaphoreType.DMA((units, Gather.SEMS)),
        pltpu.SemaphoreType.DMA((units, Gather.SEMS)),
        pltpu.SemaphoreType.DMA((units,)),
        pltpu.VMEM((3 * width, rows), BF),
        pltpu.VMEM((LAYERS, 2 * width, rows), BF),
        pltpu.VMEM(nat, F32),
        pltpu.VMEM(tr, BF),
        pltpu.VMEM(lse, F32),
        pltpu.VMEM(nat, F32),
        pltpu.VMEM(nat, BF),
        pltpu.VMEM(tr, BF),
        pltpu.VMEM(tr, BF),
        pltpu.VMEM(nat, BF),
        pltpu.VMEM((2, quarter, width), BF),
        pltpu.SemaphoreType.DMA((LAYERS, 2)),
        pltpu.SemaphoreType.DMA((LAYERS, 2)),
        pltpu.SemaphoreType.DMA((3, 2, Swap.PIECES)),
        pltpu.SemaphoreType.DMA((3, 2, Swap.PIECES)),
        pltpu.SemaphoreType.REGULAR((4,)),
        pltpu.SemaphoreType.DMA((units + 10 * LAYERS + 2,)),
    ]
    return pl.pallas_call(
        functools.partial(forward_kernel, spread),
        in_specs=[SM, VM, VM] + [ANY] * 6,
        out_specs=[ANY] * len(outs),
        out_shape=outs,
        scratch_shapes=scratch,
        compiler_params=kernel_params(collective),
        cost_estimate=pl.CostEstimate(flops=180 * 10**9, bytes_accessed=100 * 10**6, transcendentals=0),
        name="forward",
    )(pad, cos, sin, inputs, cotangent, wqkv, wout, wup, wdown)


def feed_back_kernel(plan, layer, *refs):
    refs = list(refs)
    take = lambda n: [refs.pop(0) for _ in range(n)]
    g_in, w_in, *held = take(7)
    act_t_in, mt_in, pre_in, mid_in, att_in = [ref.at[layer] for ref in held]
    inputs = take(len(plan.args())) if plan else []
    dw_out, mg_out, do_out = take(3)
    outputs = take(len(plan.outs())) if plan else []
    g, w, act_t, mt, pre, mid, att, gb, dpre, eg, do, dw, copy_sems = take(13)
    copies = Copies(copy_sems)
    width = w.shape[1]
    shard = dw.shape[3]
    if plan:
        p = Place()
        greet(p, plan.signals(p), bool(plan.z))
        scatter, line = plan.open(p, inputs, outputs, refs, dw)
        if line:
            line.load(0).start()
        if plan.xy[0][0] != "own":
            scatter.open(0)
    load_g = copies.start(g_in, gb if g_in.dtype == BF else g)
    load_act = copies.start(act_t_in, act_t)
    load_w = [copies.start(w_in.at[6 * layer + 5], w.at[2])]
    load_pre = copies.start(pre_in, pre)
    load_mt = copies.start(mt_in, mt)
    load_w += [copies.start(w_in.at[6 * layer + 4], w.at[1])]
    load_mid = copies.start(mid_in, mid)
    load_att = copies.start(att_in, att)
    load_w += [copies.start(w_in.at[6 * layer + 3], w.at[0])]

    def put(unit, cols, value):
        for k in range(dw.shape[1]):
            for c in range(2):
                at = (2 * k + c) * shard
                dw[unit, k, c, :, cols] = value[at : at + shard].astype(BF)

    load_g.wait()
    if g_in.dtype == BF:
        g[...] = gb[...].astype(F32)
    else:
        gb[...] = g[...].astype(BF)
    load_act.wait()
    for cols in tiles(width):
        put(2, cols, dot(act_t[...], gb[:, cols], 1, 0))
    if plan and plan.xy[0][0] == "own":
        scatter.open(0)
    else:
        copies.save("dw", dw.at[2], dw_out.at[2])
    if plan:
        if line:
            line.start(0)
    load_w[0].wait()
    load_pre.wait()
    for cols in tiles(width):
        da = dot(gb[...], w[2, cols, :], 1, 1)
        v = pre[:, cols]
        s = 1.0 / (1.0 + jnp.exp(-v))
        dpre[:, cols] = (da * (s + v * s * (1.0 - s))).astype(BF)
    if plan:
        scatter.first(0)
    load_mt.wait()
    for cols in tiles(width):
        put(1, cols, dot(mt[...], dpre[:, cols], 1, 0))
    copies.save("dw", dw.at[1], dw_out.at[1])
    load_w[1].wait()
    load_mid.wait()
    r = rms(mid[...])
    total = 0.0
    for cols in tiles(width):
        e = dot(dpre[...], w[1, cols, :], 1, 1)
        eg[:, cols] = e
        total = total + jnp.sum(e * (mid[:, cols] * r), axis=1, keepdims=True)
    total = total / width
    if plan and line:
        line.middle(0)
    for cols in tiles(width):
        m = g[:, cols] + r * (eg[:, cols] - mid[:, cols] * r * total)
        g[:, cols] = m
        gb[:, cols] = m.astype(BF)
    copies.save("g", g, mg_out)
    load_att.wait()
    for cols in tiles(width):
        put(0, cols, dot(att[...], gb[:, cols], 1, 0))
    copies.save("dw", dw.at[0], dw_out.at[0])
    load_w[2].wait()
    if plan:
        scatter.second(0)
        if line:
            line.last(0)
    for cols in tiles(width):
        do[cols, :] = dot(w[0, cols, :], gb[...], 1, 1).astype(BF)
    copies.save("do", do, do_out)
    if plan:
        scatter.third(0)
        if line:
            line.end(0)
            line.drain(0)
        scatter.drain(0)
    copies.finish()


def feed_back(name, collective, layer, g, w, act_t, mt, pre, mid, att, chips, shard, plan):
    _, width, rows = act_t.shape
    nat, tr = (rows, width), (width, rows)
    grad = (3, chips, 2, shard, width)
    args = [g, w, act_t, mt, pre, mid, att] + (plan.args() if plan else [])
    outs = [struct(grad), struct(nat, F32), struct(tr)] + (plan.outs() if plan else [])
    return pl.pallas_call(
        functools.partial(feed_back_kernel, plan, layer),
        in_specs=[ANY] * len(args),
        out_specs=[ANY] * len(outs),
        out_shape=outs,
        scratch_shapes=[
            pltpu.VMEM(nat, F32),
            pltpu.VMEM((3, width, width), BF),
            pltpu.VMEM(tr, BF),
            pltpu.VMEM(tr, BF),
            pltpu.VMEM(nat, F32),
            pltpu.VMEM(nat, F32),
            pltpu.VMEM(tr, BF),
            pltpu.VMEM(nat, BF),
            pltpu.VMEM(nat, BF),
            pltpu.VMEM(nat, F32),
            pltpu.VMEM(tr, BF),
            pltpu.VMEM(grad, BF),
            pltpu.SemaphoreType.DMA((16,)),
        ] + (plan.scratch() if plan else []),
        compiler_params=kernel_params(collective if plan else None),
        cost_estimate=pl.CostEstimate(flops=16 * 10**9, bytes_accessed=30 * 10**6, transcendentals=0),
        name=name,
    )(*args)


def unrotate(t, cos, sin):
    a, b = t[:HALF], t[HALF:]
    return jnp.concatenate([a * cos + b * sin, b * cos - a * sin], axis=0)


def attend_back_heads(core, base, pad, qkv, kvx, do, o, lse, tables, dqkv, dkvx):
    width, rows = o.shape
    size = rows // 2
    scale = 1.0 / math.sqrt(HEAD_DIM)
    cos, sin, cosx, sinx = tables
    at = lambda off, hh: pl.ds(pl.multiple_of(off * width + (base + hh) * HEAD_DIM, 16), HEAD_DIM)
    for hh in range(GROUP):
        dk, dv = {}, {}
        for block, keys in key_blocks(core):
            cols = slice(block * size, block * size + size)
            q = qkv[at(0, hh), cols]
            d_out = do[at(0, hh), cols]
            delta = jnp.sum(d_out.astype(F32) * o[at(0, hh), cols].astype(F32), axis=0, keepdims=True)
            norm = lse[base // GROUP, hh : hh + 1, cols]
            dq = 0.0
            for i, (src, half, quarter) in enumerate(keys):
                span = slice(half * size, half * size + size)
                k = qkv[at(1, hh), span] if src == "o" else kvx[at(0, hh), span]
                v = qkv[at(2, hh), span] if src == "o" else kvx[at(1, hh), span]
                s = masked(dot(k, q, 0, 0), quarter, i == len(keys) - 1, pad)
                weight = jnp.exp2(s * LOG2_SCALE - norm)
                ds = (weight * (dot(v, d_out, 0, 0) - delta)).astype(BF)
                dq = dq + dot(k, ds, 1, 0)
                a, b = dot(q, ds, 1, 1), dot(d_out, weight.astype(BF), 1, 1)
                key = (src, half)
                dk[key] = dk[key] + a if key in dk else a
                dv[key] = dv[key] + b if key in dv else b
            dqkv[at(0, hh), cols] = unrotate(dq * scale, cos[:, cols], sin[:, cols]).astype(BF)
        for src, ref, k_off, ct, st in (("o", dqkv, 1, cos, sin), ("x", dkvx, 0, cosx, sinx)):
            for half in (0, 1):
                span = slice(half * size, half * size + size)
                if (src, half) in dk:
                    a = unrotate(dk[src, half] * scale, ct[:, span], st[:, span]).astype(BF)
                    b = dv[src, half].astype(BF)
                else:
                    a = b = jnp.zeros((HEAD_DIM, size), BF)
                ref[at(k_off, hh), span] = a
                ref[at(k_off + 1, hh), span] = b


def attend_back_kernel(plan, layer, swapping, *refs):
    refs = list(refs)
    take = lambda n: [refs.pop(0) for _ in range(n)]
    pad_ref, qkv_in, kvx_in, do_in, att_in, lse, cos, sin, cosx, sinx = take(10)
    qkv_in, kvx_in, att_in = qkv_in.at[layer], kvx_in.at[layer], att_in.at[layer]
    hid_in = take(1)[0] if swapping else None
    inputs = take(len(plan.args())) if plan else []
    pg_out = take(1)[0]
    swap_out = take(1)[0] if swapping else None
    outputs = take(len(plan.outs())) if plan else []
    qkv, kvx, do, att, dqkv, dkvx, got, x_send, x_recv, copy_sems = take(10)
    p = Place()
    copies = Copies(copy_sems)
    signals = [p.id(p.sibling)]
    if plan:
        signals = plan.signals(p)
    if swapping:
        swap = Swap(p, False, hid_in, swap_out, *take(2))
        signals = signals + swap.came_from
    greet(p, signals, bool(plan and plan.z))
    if swapping:
        swap.start()
    loads = [copies.start(a, b) for a, b in ((qkv_in, qkv), (kvx_in, kvx), (do_in, do), (att_in, att))]
    units = items = 0
    if plan:
        scatter, line = plan.open(p, inputs, outputs, refs)
        units, items = len(plan.xy), len(plan.z)
        for i in range(units):
            scatter.open(i)
        for i in range(items):
            line.load(i).start()
        for i in range(items):
            line.start(i)
    for load in loads:
        load.wait()
    for i in range(units):
        scatter.first(i)
    pad = pad_ref[0]
    width = att.shape[0]
    span = GROUP * HEAD_DIM
    groups = width // span

    def exchange(group, k):
        part = pl.ds(pl.multiple_of(k * width + group * span, 16), span)
        return remote(dkvx.at[part], got.at[part], x_send.at[group, k], x_recv.at[group, k], p.id(p.sibling))

    def body(group, carry):
        for core in (0, 1):
            pl.when(p.core == core)(
                functools.partial(
                    attend_back_heads, core, group * GROUP, pad, qkv, kvx, do, att, lse,
                    (cos, sin, cosx, sinx), dqkv, dkvx,
                )
            )
        for k in (0, 1):
            exchange(group, k).start()
        after = [[], [], []]
        if units:
            after[1] += [(scatter.second, 0)]
            after[2] += [(scatter.second, i) for i in range(1, units)]
        if items:
            after[0] += [(line.middle, 0)]
            after[1] += [(line.middle, i) for i in range(1, min(items, 2))] + [(line.last, 0)]
            after[2] += [(line.middle, i) for i in range(2, items)] + [(line.last, i) for i in range(1, min(items, 2))]
        for at, steps in enumerate(after):

            @pl.when(group == at)
            def _(steps=steps):
                for step, i in steps:
                    step(i)

        return carry

    lax.fori_loop(0, groups, body, 0)
    for group in range(groups):
        for k in (0, 1):
            exchange(group, k).wait_recv()
    own = dqkv.at[pl.ds(width, 2 * width)]
    own[...] = (own[...].astype(F32) + got[...].astype(F32)).astype(BF)
    copies.save("dqkv", dqkv, pg_out)
    for i in range(units):
        scatter.third(i)
    for i in range(2, items):
        line.last(i)
    for i in range(items):
        line.end(i)
    for i in range(items):
        line.drain(i)
    for i in range(units):
        scatter.drain(i)
    for group in range(groups):
        for k in (0, 1):
            exchange(group, k).wait_send()
    if swapping:
        swap.arrive()
        swap.drain()
    copies.finish()


def attend_back(name, collective, layer, pad, qkv, kvx, do, att, lse, tables, hid, plan):
    _, width, rows = att.shape
    swapping = hid is not None
    args = [pad, qkv, kvx, do, att, lse, *tables] + ([hid] if swapping else []) + (plan.args() if plan else [])
    specs = [SM] + [ANY] * 4 + [VM] * 5 + [ANY] * (len(args) - 10)
    outs = [struct((3 * width, rows))]
    if swapping:
        outs.append(struct(hid.shape))
    outs += plan.outs() if plan else []
    scratch = [
        pltpu.VMEM((3 * width, rows), BF),
        pltpu.VMEM((2 * width, rows), BF),
        pltpu.VMEM((width, rows), BF),
        pltpu.VMEM((width, rows), BF),
        pltpu.VMEM((3 * width, rows), BF),
        pltpu.VMEM((2 * width, rows), BF),
        pltpu.VMEM((2 * width, rows), BF),
        pltpu.SemaphoreType.DMA((lse.shape[0], 2)),
        pltpu.SemaphoreType.DMA((lse.shape[0], 2)),
        pltpu.SemaphoreType.DMA((16,)),
    ]
    if swapping:
        scratch += swap_scratch()
    return pl.pallas_call(
        functools.partial(attend_back_kernel, plan, layer, swapping),
        in_specs=specs,
        out_specs=[ANY] * len(outs),
        out_shape=outs,
        scratch_shapes=scratch + (plan.scratch() if plan else []),
        compiler_params=kernel_params(collective),
        cost_estimate=pl.CostEstimate(flops=35 * 10**9, bytes_accessed=30 * 10**6, transcendentals=0),
        name=name,
    )(*args)


def project_back_kernel(plan, layer, swapping, *refs):
    refs = list(refs)
    take = lambda n: [refs.pop(0) for _ in range(n)]
    pg_in, xt_in, w_in, h_in, mg_in = take(5)
    xt_in, h_in = xt_in.at[layer], h_in.at[layer]
    inputs = take(len(plan.args())) if plan else []
    dw_out = None if swapping and plan else take(1)[0]
    g_out = take(1)[0]
    outputs = take(len(plan.outs())) if plan else []
    pg, xt, w, h, g, dw, copy_sems = take(7)
    gb = take(1)[0] if swapping else None
    swap_sems = take(2) if swapping else None
    copies = Copies(copy_sems)
    width = xt.shape[0]
    quarter = xt.shape[1] // 2
    shard = dw.shape[3]
    p = Place()
    signals = plan.signals(p) if plan else []
    if swapping:
        swap = Swap(p, False, gb, g_out, *swap_sems)
        signals = signals + swap.came_from
    if signals:
        greet(p, signals, bool(plan and plan.z))
    load_pg = copies.start(pg_in, pg)
    load_xt = copies.start(xt_in, xt)
    held = earlier = shares = 0
    scatter = line = None
    if plan:
        scatter, line = plan.open(p, inputs, outputs, refs, dw)
        held = len(plan.xy)
        earlier = sum(src != "own" for src, _ in plan.xy)
        shares = sum(src != "sum" for src, _ in plan.z)
    for i in range(earlier):
        scatter.open(i)
    for i in range(shares):
        line.load(i).start()
    load_w = [copies.start(w_in.at[6 * layer + (2, 0, 1)[unit]], w.at[unit]) for unit in range(3)]
    load_h = copies.start(h_in, h)
    load_g = copies.start(mg_in, g)
    load_pg.wait()
    load_xt.wait()
    for i in range(shares):
        line.start(i)
    for i in range(min(earlier, 1)):
        scatter.first(i)

    def weight_grad(unit):
        for cols in tiles(width):
            value = dot(xt[...], pg[unit * width + cols.start : unit * width + cols.stop, :], 1, 1)
            for k in range(dw.shape[1]):
                for c in range(2):
                    at = (2 * k + c) * shard
                    dw[unit, k, c, :, cols] = value[at : at + shard].astype(BF)
        if dw_out is not None and not (plan and ("own", unit) in plan.xy):
            copies.save("dw", dw.at[unit], dw_out.at[unit])

    own = earlier
    weight_grad(1)
    for i in range(1, earlier):
        scatter.first(i)
    if own < held:
        scatter.open(own)
    weight_grad(2)
    if own < held:
        scatter.first(own)
    wait_for = lambda step, i: getattr(line, step)(i) if i < shares else None
    wait_for("middle", 0)
    if own + 1 < held:
        scatter.open(own + 1)
    weight_grad(0)
    if own + 2 < held:
        scatter.open(own + 2)
    for i in range(min(earlier, 1)):
        scatter.second(i)
    wait_for("middle", 1)
    wait_for("last", 0)
    for load in load_w:
        load.wait()
    load_h.wait()
    load_g.wait()
    r = rms(h[...])
    total = 0.0
    for n, cols in enumerate(tiles(width)):
        e = 0.0
        for unit in range(3):
            e = e + dot(pg[unit * width : (unit + 1) * width, :], w[unit, cols, :], 0, 1)
        g[:, cols] = g[:, cols] + r * e
        total = total + jnp.sum(e * (h[:, cols] * r), axis=1, keepdims=True)
        if n == 1:
            for i in range(1, earlier):
                scatter.second(i)
        if n == 2 and own + 1 < held:
            scatter.first(own + 1)
        if n == 3:
            wait_for("middle", 2)
            wait_for("last", 1)
    total = total / width
    for cols in tiles(width):
        v = g[:, cols] - h[:, cols] * (r * r * total)
        if swapping:
            for k in (0, 1):
                gb[k, :, cols] = v[k * quarter : (k + 1) * quarter].astype(BF)
        else:
            g[:, cols] = v
    if swapping:
        swap.start()
    else:
        copies.save("g", g, g_out)
    chain = bool(plan) and len(plan.z) > shares
    for i in range(own + 2, held):
        scatter.first(i)
    for i in range(earlier):
        scatter.third(i)
    wait_for("middle", 3)
    wait_for("last", 2)
    steps = [[] for _ in range(held + 6)]
    for i in range(held):
        if i >= earlier:
            steps[i].append(functools.partial(scatter.second, i))
            steps[i + 1].append(functools.partial(scatter.third, i))
        if chain:
            j = shares + i
            base = i + 1
            steps[base].append(functools.partial(line.start, j))
            steps[base + 1].append(functools.partial(line.middle, j))
            steps[base + 2].append(functools.partial(line.last, j))
            steps[base + 3].append(functools.partial(line.end, j))
    if shares > 3:
        steps[2].append(functools.partial(line.last, 3))
    for group in steps:
        for step in group:
            step()
    for i in range(shares):
        line.end(i)
    for i in range(len(plan.z) if plan else 0):
        line.drain(i)
    for i in range(held):
        scatter.drain(i)
    if swapping:
        swap.arrive()
        swap.drain()
    copies.finish()


def project_back(name, collective, layer, pg, xt, w, h, mg, chips, shard, swapping, plan):
    _, rows, width = h.shape
    nat, tr = (rows, width), (width, rows)
    grad = (3, chips, 2, shard, width)
    args = [pg, xt, w, h, mg] + (plan.args() if plan else [])
    outs = [] if swapping and plan else [struct(grad)]
    outs.append(struct((2, rows // 2, width)) if swapping else struct(nat, F32))
    outs += plan.outs() if plan else []
    scratch = [
        pltpu.VMEM((3 * width, rows), BF),
        pltpu.VMEM(tr, BF),
        pltpu.VMEM((3, width, width), BF),
        pltpu.VMEM(nat, F32),
        pltpu.VMEM(nat, F32),
        pltpu.VMEM(grad, BF),
        pltpu.SemaphoreType.DMA((16,)),
    ]
    if swapping:
        scratch += [pltpu.VMEM((2, rows // 2, width), BF)] + swap_scratch()
    return pl.pallas_call(
        functools.partial(project_back_kernel, plan, layer, swapping),
        in_specs=[ANY] * len(args),
        out_specs=[ANY] * len(outs),
        out_shape=outs,
        scratch_shapes=scratch + (plan.scratch() if plan else []),
        compiler_params=kernel_params(collective if plan or swapping else None),
        cost_estimate=pl.CostEstimate(flops=16 * 10**9, bytes_accessed=30 * 10**6, transcendentals=0),
        name=name,
    )(*args)


def turn_kernel(plan, upper, lower, *refs):
    refs = list(refs)
    take = lambda n: [refs.pop(0) for _ in range(n)]
    pg_in, xt_in, w_in, h_in, mg_in, act_t_in, mt_in, pre_in, mid_in, att_in = take(10)
    inputs = take(len(plan.args())) if plan else []
    dqkv_out, dff_out, mg_out, do_out = take(4)
    outputs = take(len(plan.outs())) if plan else []
    pg, xt, w, h, g, eg, dw, act_t, mt, pre, att, gb, dpre, do, dw_more, copy_sems = take(16)
    copies = Copies(copy_sems)
    width = xt.shape[0]
    shard = dw.shape[3]
    if plan:
        p = Place()
        greet(p, plan.signals(p), True)
        scatter, line = plan.open(p, inputs, outputs, refs, dw)
        for i in (0, 1):
            line.load(i).start()
    load_pg = copies.start(pg_in, pg)
    load_xt = copies.start(xt_in.at[upper], xt)
    load_w = [copies.start(w_in.at[6 * upper + (2, 0, 1)[unit]], w.at[unit]) for unit in range(3)]
    load_h = copies.start(h_in.at[upper], h)
    load_g = copies.start(mg_in, g)
    load_act, load_mt, load_pre, load_att = [
        copies.start(src.at[lower], dst)
        for src, dst in ((act_t_in, act_t), (mt_in, mt), (pre_in, pre), (att_in, att))
    ]

    def put(to, cols, value):
        for k in range(dw.shape[1]):
            for c in range(2):
                at = (2 * k + c) * shard
                to[k, c, :, cols] = value[at : at + shard].astype(BF)

    def weight_grad(unit):
        for cols in tiles(width):
            put(dw.at[unit], cols, dot(xt[...], pg[unit * width + cols.start : unit * width + cols.stop, :], 1, 1))
        if not plan or ("own", unit) not in plan.xy:
            copies.save(("dw", unit), dw.at[unit], dqkv_out.at[unit])

    load_pg.wait()
    load_xt.wait()
    if plan:
        for i in (0, 1):
            line.start(i)
    weight_grad(1)
    if plan:
        scatter.open(0)
    weight_grad(0)
    if plan:
        scatter.open(1)
        scatter.first(0)
    weight_grad(2)
    if plan:
        scatter.first(1)
    for load in load_w:
        load.wait()
    load_h.wait()
    r = rms(h[...])
    total = 0.0
    for n, cols in enumerate(tiles(width)):
        if plan and n == 3:
            line.middle(0)
        e = 0.0
        for unit in range(3):
            e = e + dot(pg[unit * width : (unit + 1) * width, :], w[unit, cols, :], 0, 1)
        eg[:, cols] = e
        total = total + jnp.sum(e * (h[:, cols] * r), axis=1, keepdims=True)
    total = total / width
    load_w = [copies.start(w_in.at[6 * lower + 3 + unit], w.at[unit]) for unit in (2, 1, 0)]
    load_g.wait()
    for cols in tiles(width):
        v = g[:, cols] + r * (eg[:, cols] - h[:, cols] * r * total)
        g[:, cols] = v
        gb[:, cols] = v.astype(BF)
    load_mid = copies.start(mid_in.at[lower], h)
    if plan:
        scatter.second(0)

    load_act.wait()
    copies.ready(("dw", 2))
    for cols in tiles(width):
        put(dw.at[2], cols, dot(act_t[...], gb[:, cols], 1, 0))
    copies.save("dff", dw.at[2], dff_out.at[2])
    load_w[0].wait()
    load_pre.wait()
    if plan:
        line.middle(1)
        line.last(0)
    for cols in tiles(width):
        da = dot(gb[...], w[2, cols, :], 1, 1)
        v = pre[:, cols]
        s = 1.0 / (1.0 + jnp.exp(-v))
        dpre[:, cols] = (da * (s + v * s * (1.0 - s))).astype(BF)
    if plan:
        scatter.second(1)
    load_mt.wait()
    for cols in tiles(width):
        put(dw_more.at[0], cols, dot(mt[...], dpre[:, cols], 1, 0))
    copies.save("dff", dw_more.at[0], dff_out.at[1])
    load_w[1].wait()
    load_mid.wait()
    if plan:
        line.last(1)
        scatter.third(0)
    r = rms(h[...])
    total = 0.0
    for cols in tiles(width):
        e = dot(dpre[...], w[1, cols, :], 1, 1)
        eg[:, cols] = e
        total = total + jnp.sum(e * (h[:, cols] * r), axis=1, keepdims=True)
    total = total / width
    for cols in tiles(width):
        m = g[:, cols] + r * (eg[:, cols] - h[:, cols] * r * total)
        g[:, cols] = m
        gb[:, cols] = m.astype(BF)
    copies.save("g", g, mg_out)
    load_att.wait()
    for cols in tiles(width):
        put(dw_more.at[1], cols, dot(att[...], gb[:, cols], 1, 0))
    copies.save("dff", dw_more.at[1], dff_out.at[0])
    load_w[2].wait()
    for cols in tiles(width):
        do[cols, :] = dot(w[0, cols, :], gb[...], 1, 1).astype(BF)
    copies.save("do", do, do_out)
    if plan:
        scatter.third(1)
        for i in (0, 1):
            line.end(i)
        for i in (0, 1):
            line.drain(i)
            scatter.drain(i)
    copies.finish()


def turn(name, collective, upper, lower, pg, xt, w, h, mg, act_t, mt, pre, mid, att, chips, shard, plan):
    _, rows, width = h.shape
    nat, tr = (rows, width), (width, rows)
    grad = (3, chips, 2, shard, width)
    args = [pg, xt, w, h, mg, act_t, mt, pre, mid, att] + (plan.args() if plan else [])
    outs = [struct(grad), struct(grad), struct(nat, F32), struct(tr)] + (plan.outs() if plan else [])
    scratch = [
        pltpu.VMEM((3 * width, rows), BF),
        pltpu.VMEM(tr, BF),
        pltpu.VMEM((3, width, width), BF),
        pltpu.VMEM(nat, F32),
        pltpu.VMEM(nat, F32),
        pltpu.VMEM(nat, F32),
        pltpu.VMEM(grad, BF),
        pltpu.VMEM(tr, BF),
        pltpu.VMEM(tr, BF),
        pltpu.VMEM(nat, F32),
        pltpu.VMEM(tr, BF),
        pltpu.VMEM(nat, BF),
        pltpu.VMEM(nat, BF),
        pltpu.VMEM(tr, BF),
        pltpu.VMEM((2,) + grad[1:], BF),
        pltpu.SemaphoreType.DMA((24,)),
    ]
    return pl.pallas_call(
        functools.partial(turn_kernel, plan, upper, lower),
        in_specs=[ANY] * len(args),
        out_specs=[ANY] * len(outs),
        out_shape=outs,
        scratch_shapes=scratch + (plan.scratch() if plan else []),
        compiler_params=kernel_params(collective if plan else None),
        cost_estimate=pl.CostEstimate(flops=32 * 10**9, bytes_accessed=60 * 10**6, transcendentals=0),
        name=name,
    )(*args)


def finish_kernel(places, *refs):
    count = len(places[0][0])
    refs = list(refs)
    take = lambda n: [refs.pop(0) for _ in range(n)]
    sums = take(3)
    wqkv, wup, gain_attn, gain_mlp, moved, hidden_0, hidden_1 = take(7)
    hid_out, in_out, qkv_out, out_out, up_out, down_out, ga, gm = take(8)
    grad_in, qkv, out, up, down, sems = refs
    copies = Copies(sems)
    copies.save("hid", hidden_0, hid_out.at[0])
    copies.save("hid", hidden_1, hid_out.at[1])
    grad_in[...] = moved[...].astype(F32)
    copies.save("in", grad_in, in_out)
    width = out.shape[2]
    get = lambda place: sums[place[0]][place[1]].astype(F32)
    for layer, (thirds, (out_at, up_at, down_at)) in enumerate(places):
        gain = gain_attn[layer]
        total = 0.0
        for part in range(count):
            cols = slice(part * width, part * width + width)
            value = get(thirds[part])
            qkv[layer, :, cols] = value * gain
            total = total + jnp.sum(value * wqkv[layer, :, cols].astype(F32), axis=1, keepdims=True)
        ga[layer] = total
        copies.save("qkv", qkv.at[layer], qkv_out.at[layer])
        out[layer] = get(out_at)
        copies.save("out", out.at[layer], out_out.at[layer])
        value = get(up_at)
        up[layer] = value * gain_mlp[layer]
        gm[layer] = jnp.sum(value * wup[layer].astype(F32), axis=1, keepdims=True)
        copies.save("up", up.at[layer], up_out.at[layer])
        down[layer] = get(down_at)
        copies.save("down", down.at[layer], down_out.at[layer])
    copies.finish()


def finish(places, sums, wqkv, wup, gain_attn, gain_mlp, moved, hidden_0, hidden_1):
    layers, shard, width = wup.shape
    grad = (layers, shard, width)
    wide = (layers, shard, 3 * width)
    column = (layers, shard, 1)
    return pl.pallas_call(
        functools.partial(finish_kernel, places),
        in_specs=[VM] * 10,
        out_specs=[ANY] * 6 + [VM] * 2,
        out_shape=[
            struct((layers,) + hidden_0.shape), struct(moved.shape, F32), struct(wide, F32), struct(grad, F32),
            struct(grad, F32), struct(grad, F32), struct(column, F32), struct(column, F32),
        ],
        scratch_shapes=[
            pltpu.VMEM(moved.shape, F32),
            pltpu.VMEM(wide, F32),
            pltpu.VMEM(grad, F32),
            pltpu.VMEM(grad, F32),
            pltpu.VMEM(grad, F32),
            pltpu.SemaphoreType.DMA((16,)),
        ],
        compiler_params=kernel_params(None),
        cost_estimate=pl.CostEstimate(flops=10**8, bytes_accessed=25 * 10**6, transcendentals=0),
        name="finish",
    )(*sums, wqkv, wup, gain_attn, gain_mlp, moved, hidden_0, hidden_1)


def local(nb, ns, inputs, lengths, wqkv, wout, wup, wdown, gain_attn, gain_mlp, cotangent):
    series, quarter, width = inputs.shape
    heads = width // HEAD_DIM
    rows = 2 * quarter
    shard = wout.shape[1]
    chips = nb // 2
    spread = nb == 8
    z = lax.axis_index("seq")
    core = lax.axis_index("batch") % 2

    other = lax.ppermute(
        lengths, AXES, [(b * ns + s, (b ^ 1) * ns + s) for b in range(nb) for s in range(ns)]
    )
    both = jnp.where(core == 0, jnp.concatenate([lengths, other]), jnp.concatenate([other, lengths]))
    which = jnp.where((z == 0) | (z == 3), 2, 0) + z // 2
    pad = SLOTS - lax.dynamic_index_in_dim(both, which, 0, keepdims=True)
    angle = (
        jnp.exp(jnp.arange(HALF, dtype=F32) * (-2.0 * math.log(10000.0) / HEAD_DIM))[:, None]
        * jnp.arange(SLOTS, dtype=F32)[None, :]
    )
    cos_all, sin_all = jnp.cos(angle), jnp.sin(angle)
    cos_pad = lax.dynamic_slice_in_dim(cos_all, pad[0], 1, axis=1)
    sin_pad = lax.dynamic_slice_in_dim(sin_all, pad[0], 1, axis=1)
    cos_four = (cos_all * cos_pad + sin_all * sin_pad).reshape(HALF, 4, quarter)
    sin_four = (sin_all * cos_pad - cos_all * sin_pad).reshape(HALF, 4, quarter)

    def pick(table):
        even = jnp.concatenate([table[:, 0], table[:, 3]], axis=1)
        odd = jnp.concatenate([table[:, 1], table[:, 2]], axis=1)
        return jnp.where(core == 0, even, odd), jnp.where(core == 0, odd, even)

    cos, cosx = pick(cos_four)
    sin, sinx = pick(sin_four)

    wqkv_g = (wqkv.astype(F32) * gain_attn.astype(F32)[:, :, None]).astype(BF)
    wup_g = (wup.astype(F32) * gain_mlp.astype(F32)[:, :, None]).astype(BF)

    stacked = (
        lambda array: array
        if spread
        else lax.all_gather(array, "batch", axis=1, tiled=True)
    )
    w_all, cot, hidden_0, hid_1, h_all, xt_all, qkv_all, kvx_all, att_all, lse_all, mid_all, mt_all, pre_all, act_all = forward(
        spread, 0, pad, cos, sin, inputs, cotangent, stacked(wqkv_g), stacked(wout), stacked(wup_g), stacked(wdown), shard
    )
    g = cot.reshape(rows, width)

    def plan(xy, xy_arrays, z, z_arrays):
        return Plan(xy, xy_arrays, z, z_arrays, shard, width) if spread else None

    tables = (cos, sin, cosx, sinx)
    ff_1, mg, do, *sums = feed_back(
        "feed_back", 4, 1, g, w_all, act_all, mt_all, pre_all, mid_all, att_all, chips, shard,
        plan([("own", 2)], [], [], []),
    )
    p_d1 = sums
    pg, hidden_1, *sums = attend_back(
        "attend_back_1", 5, 1, pad, qkv_all, kvx_all, do, att_all, lse_all[1], tables, hid_1,
        plan([(0, 1), (0, 0)], [ff_1], [], []),
    )
    p_uo1 = sums[0] if spread else None
    qkv_1, ff_0, mg, do, *sums = turn(
        "turn", 6, 1, 0, pg, xt_all, w_all, h_all, mg, act_all, mt_all, pre_all, mid_all, att_all, chips, shard,
        plan([("own", 1), ("own", 0)], [], [(0, 0), (0, 1)], [p_uo1]),
    )
    p_kq1, r_uo1 = sums if spread else (None, None)
    pg, *sums = attend_back(
        "attend_back_0", 8, 0, pad, qkv_all, kvx_all, do, att_all, lse_all[0], tables, None,
        plan([(0, 2), (1, 2)], [qkv_1, ff_0], [(0, 0), (0, 1)], [p_kq1]),
    )
    p_vd, r_kq1 = sums if spread else (None, None)
    tail = project_back(
        "project_back", 9, 0, pg, xt_all, w_all, h_all, mg, chips, shard, True,
        plan(
            [(0, 1), (0, 0), ("own", 1), ("own", 2), ("own", 0)], [ff_0],
            [(0, 0), (0, 1), (1, 0)] + [("sum", i) for i in range(5)], [p_vd, *p_d1],
        ),
    )
    if spread:
        input_grad, r = tail
        places = (
            (((0, 7), (0, 5), (0, 6)), ((0, 4), (0, 3), (0, 1))),
            (((1, 1), (1, 0), (0, 0)), ((2, 1), (2, 0), (0, 2))),
        )
        column = lambda gain: gain.astype(F32)[:, :, None]
        *grads, grad_ga, grad_gm = finish(
            places, (r, r_kq1, r_uo1), wqkv, wup, column(gain_attn), column(gain_mlp), input_grad, hidden_0, hidden_1
        )
        return (*grads, grad_ga[:, :, 0], grad_gm[:, :, 0])
    qkv_0, input_grad = tail

    def over_all(grads):
        flat = grads.reshape(3, nb * shard, width)
        return lax.psum(lax.psum_scatter(flat, "batch", scatter_dimension=1, tiled=True), "seq")

    s_qkv = [over_all(qkv_0), over_all(qkv_1)]
    s_ff = [over_all(ff_0), over_all(ff_1)]
    input_grad = input_grad.astype(F32)
    hidden = [hidden_0, hidden_1]

    grad_qkv, grad_out, grad_up, grad_down, grad_ga, grad_gm = [], [], [], [], [], []
    for layer in range(LAYERS):
        ff = [part.astype(F32) for part in s_ff[layer]]
        qkv_sum = jnp.concatenate([part.astype(F32) for part in s_qkv[layer]], axis=1)
        grad_qkv.append(qkv_sum * gain_attn[layer].astype(F32)[:, None])
        grad_ga.append(jnp.sum(qkv_sum * wqkv[layer].astype(F32), axis=1))
        grad_out.append(ff[0])
        grad_up.append(ff[1] * gain_mlp[layer].astype(F32)[:, None])
        grad_gm.append(jnp.sum(ff[1] * wup[layer].astype(F32), axis=1))
        grad_down.append(ff[2])
    stack = jnp.stack
    return (
        stack(hidden), input_grad, stack(grad_qkv), stack(grad_out), stack(grad_up), stack(grad_down),
        stack(grad_ga), stack(grad_gm),
    )


def solution(mesh):
    nb, ns = mesh.shape["batch"], mesh.shape["seq"]
    rows = P("batch", "seq", None)
    weight = P(None, "batch", None)
    gain = P(None, "batch")
    return jax.shard_map(
        functools.partial(local, nb, ns),
        mesh=mesh,
        in_specs=(rows, P("batch"), weight, weight, weight, weight, gain, gain, rows),
        out_specs=(P(None, "batch", "seq", None), rows, weight, weight, weight, weight, gain, gain),
        check_vma=False,
    )
```
